32 devices in a mesh: batch: 8 (over y, x, core), seq: 4 (over z).
Axes of the slice: x: 2, y: 2, z: 4, core: 2. Of those that a mesh axis runs over, the one named last changes fastest.
Arguments:
- tokens: bfloat16 [8, 8192, 512], P('batch', 'seq'), may hold values from -6 to 6
- cotangent: bfloat16 [8, 8192, 512], P('batch', 'seq'), may hold values from -6 to 6
- segment: int32 [8, 8192], P('batch', 'seq'), may hold values from 0 to 65, as said below
- keep_mask: int32 [8, 8192], P('batch', 'seq'), may hold values from 0 to 1, as said below
- attn_master: float32 [512, 1536], P(('batch', 'seq')), may hold values from -0.25 to 0.25
- out_master: float32 [512, 512], P(('batch', 'seq')), may hold values from -2 to 2
- in_master: float32 [512, 2048], P(('batch', 'seq')), may hold values from -0.25 to 0.25
- back_master: float32 [2048, 512], P(('batch', 'seq')), may hold values from -0.125 to 0.125
- vec_master: float32 [12, 512], P(None, ('batch', 'seq')), may hold values from -0.6 to 1.4
- attn_first: float32 [512, 1536], P(('batch', 'seq')), may hold values from -160 to 160
- out_first: float32 [512, 512], P(('batch', 'seq')), may hold values from -32 to 32
- in_first: float32 [512, 2048], P(('batch', 'seq')), may hold values from -40 to 40
- back_first: float32 [2048, 512], P(('batch', 'seq')), may hold values from -96 to 96
- vec_first: float32 [12, 512], P(None, ('batch', 'seq')), may hold values from -160 to 160
- attn_second: float32 [512, 1536], P(('batch', 'seq')), may hold values from 32.768 to 524.288
- out_second: float32 [512, 512], P(('batch', 'seq')), may hold values from 1.31072 to 20.97152
- in_second: float32 [512, 2048], P(('batch', 'seq')), may hold values from 1.96608 to 32.768
- back_second: float32 [2048, 512], P(('batch', 'seq')), may hold values from 11.79648 to 190.0544
- vec_second: float32 [12, 512], P(None, ('batch', 'seq')), may hold values from 32.768 to 524.288
Outputs:
- output: bfloat16 [8, 8192, 512], P('batch', 'seq')
- input_grad: float32 [8, 8192, 512], P('batch', 'seq')
- attn_first_new: float32 [512, 1536], P(('batch', 'seq'))
- out_first_new: float32 [512, 512], P(('batch', 'seq'))
- in_first_new: float32 [512, 2048], P(('batch', 'seq'))
- back_first_new: float32 [2048, 512], P(('batch', 'seq'))
- vec_first_new: float32 [12, 512], P(None, ('batch', 'seq'))
- attn_second_new: float32 [512, 1536], P(('batch', 'seq'))
- out_second_new: float32 [512, 512], P(('batch', 'seq'))
- in_second_new: float32 [512, 2048], P(('batch', 'seq'))
- back_second_new: float32 [2048, 512], P(('batch', 'seq'))
- vec_second_new: float32 [12, 512], P(None, ('batch', 'seq'))
- attn_master_new: float32 [512, 1536], P(('batch', 'seq'))
- out_master_new: float32 [512, 512], P(('batch', 'seq'))
- in_master_new: float32 [512, 2048], P(('batch', 'seq'))
- back_master_new: float32 [2048, 512], P(('batch', 'seq'))
- vec_master_new: float32 [12, 512], P(None, ('batch', 'seq'))
- attn_copy: bfloat16 [512, 1536], P(None, 'seq')
- out_copy: bfloat16 [512, 512], P(None, 'seq')
- in_copy: bfloat16 [512, 2048], P(None, 'seq')
- back_copy: bfloat16 [2048, 512], P(None, 'seq')
- vec_copy: bfloat16 [12, 512], P(None, 'seq')
The draws below stay inside these ranges and needn't reach their ends.
Inputs may be any that keep to these rules, and one draw needn't show every extreme that they name: Segment numbers of a stream start at 0 and rise by one from a segment to the next; each segment holds 5 to 250 positions, and the first segment of every stream holds exactly 250. Segments come in consecutive pairs (0 and 1, 2 and 3, ...) of 255 positions together; the stream's last position lies in the last segment, which every stream reaches. keep_mask is 1 at the first position of every segment, and within a segment no 1 follows a 0.
All inputs are finite; a program needn't handle non-finite values.
Results may differ from the reference program's by a relative error of at most 0.012.
The reference program's roundings to bfloat16 on the way count: a program that leaves them out, or rounds other values in their place, can miss the bound.
Values may be sent and summed in bfloat16 or wider, within the bound.
A program may use at most 320 MiB of HBM per device.

```python
import math
import jax
import jax.numpy as jnp
from jax import lax

D = 512
HEADS = 8
HEAD_DIM = 64
FF = 2048
MAXLEN = 250
STEP = 10
VROWS = 12
STREAM = 8192
STREAMS = 8
TOKENS = 65536


def stream_layout(key):
    length_key, cut_key = jax.random.split(key)
    pair_span = MAXLEN + 5
    pair_count = STREAM // pair_span + 1
    seg_count = 2 * pair_count
    last_pair = (STREAM - 1) // pair_span
    leading = jax.random.randint(length_key, (STREAMS, pair_count), 5, MAXLEN + 1)
    leading = leading.at[:, 0].set(MAXLEN)
    leading = leading.at[:, last_pair].set(5)
    lengths = jnp.stack([leading, pair_span - leading], axis=2).reshape(STREAMS, seg_count)
    seg_ends = jnp.cumsum(lengths, axis=1)
    begins = seg_ends - lengths
    position = jnp.arange(STREAM, dtype=jnp.int32)

    def row_search(row_ends):
        return jnp.searchsorted(row_ends, position, side='right')
    segment = jax.vmap(row_search)(seg_ends).astype(jnp.int32)
    cut_sizes = jax.random.randint(cut_key, (STREAMS, seg_count), 0, MAXLEN)
    kept_lengths = lengths - cut_sizes % (lengths // 2 + 1)
    seg_begin = jnp.take_along_axis(begins, segment, axis=1)
    seg_kept = jnp.take_along_axis(kept_lengths, segment, axis=1)
    keep_mask = (position[None, :] - seg_begin < seg_kept).astype(jnp.int32)
    return (segment, keep_mask)


def draw_segment(key, part):
    segment, keep_mask = stream_layout(key)
    return segment


def draw_keep_mask(key, part):
    segment, keep_mask = stream_layout(key)
    return keep_mask


def draw_vec_master(key, part):
    key = jax.random.fold_in(key, 3)
    bias_key, gain_key = jax.random.split(key)
    biases = jax.random.uniform(bias_key, (VROWS, D), jnp.float32, -0.6, 0.6)
    gain_rows = jax.random.uniform(gain_key, (VROWS, D), jnp.float32, 0.6, 1.4)
    row_index = jnp.arange(VROWS)[:, None]
    return jnp.where((row_index == 4) | (row_index == 6), gain_rows, biases)


def steps_of(own_key, shape, cuts, smallest, largest):
    def one(dim, shards_of):
        draws = jax.random.uniform(jax.random.fold_in(jax.random.fold_in(own_key, 6), dim), (shards_of,), jnp.float32, smallest / len(cuts), largest / len(cuts))
        return jnp.repeat(jnp.exp(draws), shape[dim] // shards_of).reshape((-1,) + (1,) * (len(shape) - dim - 1))

    factor_of = one(*cuts[0])
    for cut in cuts[1:]:
        factor_of = factor_of * one(*cut)
    return factor_of


def centred(stream_key, dims, scale, reach, cuts=(), held_as=jnp.bfloat16):
    values = scale * jax.random.normal(stream_key, dims, jnp.float32)
    if cuts:
        values = values * steps_of(stream_key, dims, cuts, -0.22, 0.18)
    return jnp.clip(values, -reach, reach).astype(held_as)


def setup_inputs(seed: int = 0) -> dict:
    seeds = jax.random.split(jax.random.key(seed), 20)
    tokens = centred(seeds[0], (STREAMS, STREAM, D), 1.0, 6.0, ((0, 8), (1, 4)))
    cotangent = centred(seeds[1], (STREAMS, STREAM, D), 1.0, 6.0, ((0, 8), (1, 4)))
    segment = draw_segment(jax.random.fold_in(seeds[19], 71), 0)
    keep_mask = draw_keep_mask(jax.random.fold_in(seeds[19], 71), 0)
    attn_master = centred(seeds[4], (D, 3 * D), D ** -0.5, 0.25, ((0, 32),), jnp.float32)
    out_master = centred(seeds[5], (D, D), (D // 64) ** -0.5, 2.0, ((0, 32),), jnp.float32)
    in_master = centred(seeds[6], (D, FF), D ** -0.5, 0.25, ((0, 32),), jnp.float32)
    back_master = centred(seeds[7], (FF, D), FF ** -0.5, 0.125, ((0, 32),), jnp.float32)
    vec_master = draw_vec_master(jax.random.fold_in(seeds[19], 71), 0)
    attn_first = centred(seeds[9], (D, 3 * D), (0.11 * TOKENS ** 0.5), 160.0, ((0, 32),), jnp.float32)
    out_first = centred(seeds[10], (D, D), (0.022 * TOKENS ** 0.5), 32.0, ((0, 32),), jnp.float32)
    in_first = centred(seeds[11], (D, FF), (0.028 * TOKENS ** 0.5), 40.0, ((0, 32),), jnp.float32)
    back_first = centred(seeds[12], (FF, D), (0.066 * TOKENS ** 0.5), 96.0, ((0, 32),), jnp.float32)
    vec_first = centred(seeds[13], (VROWS, D), (0.11 * TOKENS ** 0.5), 160.0, ((1, 32),), jnp.float32)
    attn_second = jnp.clip(jnp.exp(math.log(524.288) - 2.7725887 * jax.random.uniform(seeds[14], (D, 3 * D), jnp.float32) ** steps_of(seeds[14], (D, 3 * D), ((0, 32),), -0.2, 0.2)), 32.768, 524.288)
    out_second = jnp.clip(jnp.exp(math.log(20.97152) - 2.7725887 * jax.random.uniform(seeds[15], (D, D), jnp.float32) ** steps_of(seeds[15], (D, D), ((0, 32),), -0.2, 0.2)), 1.31072, 20.97152)
    in_second = jnp.clip(jnp.exp(math.log(32.768) - 2.8134108 * jax.random.uniform(seeds[16], (D, FF), jnp.float32) ** steps_of(seeds[16], (D, FF), ((0, 32),), -0.2, 0.2)), 1.96608, 32.768)
    back_second = jnp.clip(jnp.exp(math.log(190.0544) - 2.779509 * jax.random.uniform(seeds[17], (FF, D), jnp.float32) ** steps_of(seeds[17], (FF, D), ((0, 32),), -0.2, 0.2)), 11.79648, 190.0544)
    vec_second = jnp.clip(jnp.exp(math.log(524.288) - 2.7725887 * jax.random.uniform(seeds[18], (VROWS, D), jnp.float32) ** steps_of(seeds[18], (VROWS, D), ((1, 32),), -0.2, 0.2)), 32.768, 524.288)
    return {"tokens": tokens, "cotangent": cotangent, "segment": segment, "keep_mask": keep_mask, "attn_master": attn_master, "out_master": out_master, "in_master": in_master, "back_master": back_master, "vec_master": vec_master, "attn_first": attn_first, "out_first": out_first, "in_first": in_first, "back_first": back_first, "vec_first": vec_first, "attn_second": attn_second, "out_second": out_second, "in_second": in_second, "back_second": back_second, "vec_second": vec_second}


highest = lax.Precision.HIGHEST
norm_epsilon = 1e-05
beta_first = 0.9
beta_second = 0.999
adam_epsilon = 1e-08
weight_decay = 0.01
learn_rates = (0.03, 0.2, 0.03, 0.02, 0.5)
masked_value = -1e+30

@jax.custom_vjp
def low(v):
    return lax.optimization_barrier(v.astype(jnp.bfloat16)).astype(jnp.float32)

@jax.custom_vjp
def low_back(v):
    return v

def low_keep(v):
    return (low(v), None)

def low_pass(kept, grad):
    return (grad,)

def back_keep(v):
    return (v, None)

def back_low(kept, grad):
    return (low(grad),)
low.defvjp(low_keep, low_pass)
low_back.defvjp(back_keep, back_low)

def layer_norm(value, gain, shift):
    average = lax.optimization_barrier(jnp.mean(value, axis=-1, keepdims=True))
    centered = value - average
    spread = lax.optimization_barrier(jnp.mean(centered * centered, axis=-1, keepdims=True))
    return centered * lax.rsqrt(spread + norm_epsilon) * gain + shift

def gelu_exact(value):
    return 0.5 * value * (1.0 + jax.scipy.special.erf(value * 0.7071067811865476))

def stream_attention(queries, key_proj, values, segment, keep_mask):
    block_rows = min(512, STREAM)
    key_span = block_rows + 2 * MAXLEN
    score_scale = HEAD_DIM ** (-0.5)
    pad_keys = jnp.pad(key_proj, ((MAXLEN, MAXLEN), (0, 0), (0, 0)))
    pad_values = jnp.pad(values, ((MAXLEN, MAXLEN), (0, 0), (0, 0)))
    pad_segment = jnp.pad(segment, (MAXLEN, MAXLEN), constant_values=-1)
    pad_keep = jnp.pad(keep_mask, (MAXLEN, MAXLEN))

    def one_block(block_index):
        offset = block_index * block_rows
        query_block = lax.dynamic_slice_in_dim(queries, offset, block_rows, 0)
        key_block = lax.dynamic_slice_in_dim(pad_keys, offset, key_span, 0)
        value_block = lax.dynamic_slice_in_dim(pad_values, offset, key_span, 0)
        query_seg = lax.dynamic_slice_in_dim(segment, offset, block_rows, 0)
        key_seg = lax.dynamic_slice_in_dim(pad_segment, offset, key_span, 0)
        key_keep = lax.dynamic_slice_in_dim(pad_keep, offset, key_span, 0)
        raw_scores = low_back(score_scale * jnp.einsum('qhd,khd->hqk', query_block, key_block, precision=highest))
        allowed = (query_seg[:, None] == key_seg[None, :]) & (key_keep[None, :] == 1)
        masked_scores = jnp.where(allowed[None], raw_scores, masked_value)
        row_top = lax.optimization_barrier(jnp.max(masked_scores, axis=-1, keepdims=True))
        exponent = jnp.exp(masked_scores - row_top)
        weights_soft = exponent / lax.optimization_barrier(jnp.sum(exponent, axis=-1, keepdims=True))
        return jnp.einsum('hqk,khd->qhd', low(weights_soft), value_block, precision=highest)
    blocks = lax.map(jax.checkpoint(one_block), jnp.arange(STREAM // block_rows, dtype=jnp.int32))
    return blocks.reshape(STREAM, D)

def forward(tokens_f, attn_w, out_w, in_w, back_w, vec_w, segment, keep_mask):
    bias_query = vec_w[0]
    bias_value = vec_w[1]
    bias_out = vec_w[2]
    bias_back = vec_w[3]
    gain_one = vec_w[4]
    shift_one = vec_w[5]
    gain_two = vec_w[6]
    shift_two = vec_w[7]
    bias_inner = vec_w[8:].reshape(FF)
    project = jnp.dot(tokens_f, attn_w, precision=highest)
    queries = low_back(low(project[:, :D] + bias_query))
    key_proj = low_back(low(project[:, D:2 * D]))
    values = low_back(low(project[:, 2 * D:] + bias_value))
    context = stream_attention(queries.reshape(STREAM, HEADS, HEAD_DIM), key_proj.reshape(STREAM, HEADS, HEAD_DIM), values.reshape(STREAM, HEADS, HEAD_DIM), segment, keep_mask)
    context = low_back(low(context))
    branch = low_back(jnp.dot(context, out_w, precision=highest) + bias_out)
    middle = layer_norm(tokens_f + branch, gain_one, shift_one)
    inner_pre = low_back(jnp.dot(low(middle), in_w, precision=highest) + bias_inner)
    active = low(gelu_exact(inner_pre))
    feed_out = low_back(jnp.dot(active, back_w, precision=highest) + bias_back)
    return layer_norm(middle + feed_out, gain_two, shift_two)

def reference(tokens, cotangent, segment, keep_mask, attn_master, out_master, in_master, back_master, vec_master, attn_first, out_first, in_first, back_first, vec_first, attn_second, out_second, in_second, back_second, vec_second):
    masters = (attn_master, out_master, in_master, back_master, vec_master)
    firsts = (attn_first, out_first, in_first, back_first, vec_first)
    seconds = (attn_second, out_second, in_second, back_second, vec_second)
    weights = tuple((master.astype(jnp.bfloat16).astype(jnp.float32) for master in masters))

    def one_stream(summed, stream_items):
        stream_tokens, stream_cot, stream_seg, stream_keep = stream_items

        def layer(tokens_f, attn_w, out_w, in_w, back_w, vec_w):
            return forward(tokens_f, attn_w, out_w, in_w, back_w, vec_w, stream_seg, stream_keep)
        result, pullback = jax.vjp(layer, stream_tokens.astype(jnp.float32), weights[0], weights[1], weights[2], weights[3], weights[4])
        gradients = pullback(stream_cot.astype(jnp.float32))
        summed = tuple((summed[number] + gradients[number + 1] for number in range(5)))
        return (summed, (result.astype(jnp.bfloat16), gradients[0]))
    initial = tuple((jnp.zeros_like(weight) for weight in weights))
    summed, (output, input_grad) = lax.scan(one_stream, initial, (tokens, cotangent, segment, keep_mask))
    new_firsts = []
    new_seconds = []
    new_masters = []
    copies = []
    for number in range(5):
        gradient = summed[number]
        first_new = beta_first * firsts[number] + (1.0 - beta_first) * gradient
        second_new = beta_second * seconds[number] + (1.0 - beta_second) * gradient * gradient
        first_hat = first_new / (1.0 - beta_first ** STEP)
        second_hat = second_new / (1.0 - beta_second ** STEP)
        master_new = masters[number] - learn_rates[number] * (first_hat / (jnp.sqrt(second_hat) + adam_epsilon) + weight_decay * masters[number])
        new_firsts.append(first_new)
        new_seconds.append(second_new)
        new_masters.append(master_new)
        copies.append(master_new.astype(jnp.bfloat16))
    return (output, input_grad, new_firsts[0], new_firsts[1], new_firsts[2], new_firsts[3], new_firsts[4], new_seconds[0], new_seconds[1], new_seconds[2], new_seconds[3], new_seconds[4], new_masters[0], new_masters[1], new_masters[2], new_masters[3], new_masters[4], copies[0], copies[1], copies[2], copies[3], copies[4])
```

```python
import jax
import jax.numpy as jnp
from jax import lax
from jax.experimental import pallas as pl
from jax.experimental.pallas import tpu as pltpu
from jax.sharding import PartitionSpec as P

D = 512
HEADS = 8
HEAD_DIM = 64
FF = 2048
STEP = 10
PAIR = 255
SLOT = 256
HALO = 64
TILES = 4
TAIL = 64
PIECE = TAIL // TILES
TILE = 2 * SLOT + PIECE
ROWS = TILES * TILE
LANES = 8 * SLOT + 128
AUG = 16
MIB = 1 << 20

norm_epsilon = 1e-05
beta_first = 0.9
beta_second = 0.999
adam_epsilon = 1e-08
weight_decay = 0.01
learn_rates = (0.03, 0.2, 0.03, 0.02, 0.5)
big = 1e30

f32 = jnp.float32
bf16 = jnp.bfloat16


def dot(a, b, ca, cb):
    return lax.dot_general(a, b, (((ca,), (cb,)), ((), ())), preferred_element_type=f32)


def adam_update(master, first, second, gradient, rate):
    first_new = beta_first * first + (1.0 - beta_first) * gradient
    second_new = beta_second * second + (1.0 - beta_second) * gradient * gradient
    first_hat = first_new / (1.0 - beta_first**STEP)
    second_hat = second_new / (1.0 - beta_second**STEP)
    master_new = master - rate * (
        first_hat / (jnp.sqrt(second_hat) + adam_epsilon) + weight_decay * master
    )
    return (first_new, second_new, master_new)


def slot_row(j):
    return pl.multiple_of((j // 2) * TILE + (j % 2) * SLOT, 16)


def first_row(j, seq):
    return HALO + PAIR * j - 8 * seq


def staged(ref, start):
    base = pl.multiple_of((start // 16) * 16, 16)
    rest = start - base
    wide = ref[pl.ds(base, SLOT + 16), :].astype(f32)
    wide = jnp.where(rest >= 8, wide[8:], wide[:-8])
    shift = rest % 8
    groups = (SLOT + 8) // 8
    wide = wide.reshape(groups, 8, D)
    turned = pltpu.roll(wide, lax.rem(8 - shift, 8), 1)
    place = lax.broadcasted_iota(jnp.int32, (groups - 1, 8, D), 1)
    block = jnp.where(place < 8 - shift, turned[:-1], turned[1:]).reshape(SLOT, D)
    row = lax.broadcasted_iota(jnp.int32, (SLOT, D), 0)
    return jnp.where(row < PAIR, block, 0.0).astype(bf16)


def unstage(ref, start, block):
    base = pl.multiple_of((start // 8) * 8, 8)
    shift = start - base
    turned = pltpu.roll(block.reshape(SLOT // 8, 8, D), shift, 1)
    place = lax.broadcasted_iota(jnp.int32, (1, 8, D), 1)
    keep = ref[pl.ds(base, 8), :].reshape(1, 8, D)
    low = jnp.concatenate([keep, turned], 0)
    high = jnp.concatenate([turned, turned[-1:]], 0)
    place = lax.broadcasted_iota(jnp.int32, low.shape, 1)
    ref[pl.ds(base, SLOT + 8), :] = jnp.where(place < shift, low, high).reshape(SLOT + 8, D)


def tail_rows(ref, count, is_last):
    kept = ref[HALO + 2048 - count : HALO + 2048, :].astype(f32)
    if count < TAIL:
        kept = jnp.concatenate([kept, jnp.zeros((TAIL - count, D), f32)], 0)
    return jnp.where(is_last, kept, 0.0).astype(bf16)


def tag_rows(tag, pair):
    width = tag.shape[1]
    number = tag // 2 - 2 * pair
    kept = tag % 2
    row = lax.broadcasted_iota(jnp.int32, (AUG, width), 0)
    match = row == number
    query = jnp.where(match, 1.0, 0.0).astype(bf16)
    key = jnp.where(match & (kept == 1), 0.0, -big)
    key = jnp.where(row < 4, key, 0.0).astype(bf16)
    return query, key


def attn_forward_kernel(
    seq_count, x_ref, e_ref, tag_ref, w_ref, bias_ref,
    xs_ref, es_ref, xt_ref, qt_ref, kt_ref, vt_ref, c_ref, lse_ref, wt_ref,
):
    seq = lax.axis_index("seq")
    is_last = seq == seq_count - 1
    for part in range(3):
        wt_ref[part * D : (part + 1) * D, :] = w_ref[:, part * D : (part + 1) * D].T

    def block(xb, tag, pair, lane, width):
        lanes = pl.ds(lane, width)
        xt_ref[:D, lanes] = xb.T
        bias = bias_ref[...]
        q = dot(wt_ref[:D, :], xb, 1, 1) + bias[:D, :1]
        q = (q.astype(bf16).astype(f32) * HEAD_DIM**-0.5).astype(bf16)
        k = dot(wt_ref[D : 2 * D, :], xb, 1, 1).astype(bf16)
        v = (dot(wt_ref[2 * D :, :], xb, 1, 1) + bias[D:, :1]).astype(bf16)
        query_tag, key_tag = tag_rows(tag, pair)
        vt_ref[:, lanes] = v
        context = []
        for h in range(HEADS):
            rows = slice(h * HEAD_DIM, (h + 1) * HEAD_DIM)
            qh = jnp.concatenate([q[rows], query_tag], 0)
            kh = jnp.concatenate([k[rows], key_tag], 0)
            qt_ref[h, :, lanes] = qh
            kt_ref[h, :, lanes] = kh
            s = dot(kh, qh, 0, 0)
            top = jnp.max(s, axis=0, keepdims=True)
            ex = jnp.exp(s - top)
            total = jnp.sum(ex, axis=0, keepdims=True)
            lse_ref[h : h + 1, lanes] = top + jnp.log(total)
            a = (ex * (1.0 / total)).astype(bf16)
            context.append(dot(v[rows], a, 1, 0))
        return jnp.concatenate(context, 0).astype(bf16).T

    def one(j, carry):
        start = first_row(j, seq)
        row = slot_row(j)
        xb = staged(x_ref, start)
        xs_ref[pl.ds(row, SLOT), :] = xb
        es_ref[pl.ds(row, SLOT), :] = staged(e_ref, start)
        wide = tag_ref[:, pl.ds(pl.multiple_of(j * SLOT, 128), SLOT + 128)]
        width = SLOT + 128
        tag = pltpu.roll(wide, width - (start - j * SLOT), 1)[:1, :SLOT]
        c_ref[pl.ds(row, SLOT), :] = block(
            xb, tag, 8 * seq + j, pl.multiple_of(j * SLOT, 128), SLOT
        )
        return carry

    lax.fori_loop(0, 8, one, 0)
    count = 8 * seq_count
    xt_ref[:, 8 * SLOT :] = jnp.zeros((D + AUG, 128), bf16)
    xb = tail_rows(x_ref, count, is_last)
    eb = tail_rows(e_ref, count, is_last)
    tag = tag_ref[:1, 2048:2176]
    tag = pltpu.roll(tag_ref[:, 2048:2176], 128 - (64 - count), 1)[:1, :TAIL] if count < 64 else tag[:, :TAIL]
    place = lax.broadcasted_iota(jnp.int32, (1, TAIL), 1)
    tag = jnp.where(place < count, tag, (2 * 8 * seq_count + 3) * 2)
    cb = block(xb, tag, 8 * seq_count, 8 * SLOT, TAIL)
    for t in range(TILES):
        rows = slice(t * PIECE, (t + 1) * PIECE)
        at = slice(t * TILE + 2 * SLOT, (t + 1) * TILE)
        xs_ref[at, :] = xb[rows]
        es_ref[at, :] = eb[rows]
        c_ref[at, :] = cb[rows]
    ones = lax.broadcasted_iota(jnp.int32, (AUG, LANES), 0) == 0
    xt_ref[D:, :] = jnp.where(ones, 1.0, 0.0).astype(bf16)


def attn_forward(seq_count, x, e, tag, attn_w, bias):
    shape = jax.ShapeDtypeStruct
    import functools
    return pl.pallas_call(
        functools.partial(attn_forward_kernel, seq_count),
        out_shape=(
            shape((ROWS, D), bf16),
            shape((ROWS, D), bf16),
            shape((D + AUG, LANES), bf16),
            shape((HEADS, HEAD_DIM + AUG, LANES), bf16),
            shape((HEADS, HEAD_DIM + AUG, LANES), bf16),
            shape((D, LANES), bf16),
            shape((ROWS, D), bf16),
            shape((HEADS, LANES), f32),
        ),
        in_specs=[pl.BlockSpec(memory_space=pltpu.VMEM)] * 5,
        out_specs=[pl.BlockSpec(memory_space=pltpu.VMEM)] * 8,
        scratch_shapes=[pltpu.VMEM((3 * D, D), bf16)],
        compiler_params=pltpu.CompilerParams(vmem_limit_bytes=56 * MIB),
        name="attn_forward",
    )(x, e, tag, attn_w, bias)


def feed_kernel(
    xs_ref, c_ref, es_ref, wo_ref, w1_ref, w2_ref, vec_ref, b1_ref,
    z_ref, dh_ref, dr_ref, gwo_ref, gw1_ref, gw2_ref, gvec_ref, gb1_ref,
    u_ref, g_ref, awo_ref, aw1_ref, aw2_ref,
):
    step = pl.program_id(0)

    @pl.when(step == 0)
    def _():
        awo_ref[...] = jnp.zeros_like(awo_ref)
        aw1_ref[...] = jnp.zeros_like(aw1_ref)
        aw2_ref[...] = jnp.zeros_like(aw2_ref)
        gvec_ref[...] = jnp.zeros_like(gvec_ref)
        gb1_ref[...] = jnp.zeros_like(gb1_ref)

    def mean(v):
        return jnp.mean(v, axis=-1, keepdims=True)

    def row_sum(v):
        return jnp.sum(v, axis=0, keepdims=True)

    bo, b2, g1, c1, g2, c2 = (vec_ref[i : i + 1, :] for i in range(2, 8))
    h1 = xs_ref[...].astype(f32) + (dot(c_ref[...], wo_ref[...], 1, 0) + bo)
    mid = h1 - mean(h1)
    inv1 = lax.rsqrt(mean(mid * mid) + norm_epsilon)
    n1 = mid * inv1
    y = n1 * g1 + c1
    yb = y.astype(bf16)
    chunk = D
    f = None
    for k in range(FF // chunk):
        cols = slice(k * chunk, (k + 1) * chunk)
        u = dot(yb, w1_ref[:, cols], 1, 0) + b1_ref[:1, cols]
        cdf = 0.5 * (1.0 + lax.erf(u * 0.7071067811865476))
        gk = (u * cdf).astype(bf16)
        u_ref[:, cols] = cdf + u * jnp.exp(u * u * -0.5) * 0.3989422804014327
        g_ref[:, cols] = gk
        part = dot(gk, w2_ref[cols, :], 1, 0)
        f = part if f is None else f + part
    h2 = y + (f + b2)
    mid2 = h2 - mean(h2)
    inv2 = lax.rsqrt(mean(mid2 * mid2) + norm_epsilon)
    n2 = mid2 * inv2
    z_ref[...] = (n2 * g2 + c2).astype(bf16)
    e = es_ref[...].astype(f32)
    gvec_ref[7:8, :] += row_sum(e)
    gvec_ref[6:7, :] += row_sum(e * n2)
    eg = e * g2
    dh2 = (eg - mean(eg) - n2 * mean(eg * n2)) * inv2
    df = dh2.astype(bf16)
    gvec_ref[3:4, :] += row_sum(df.astype(f32))
    dft = df.T
    ybt = yb.T
    dy = dh2
    for k in range(FF // chunk):
        cols = slice(k * chunk, (k + 1) * chunk)
        aw2_ref[:, cols] += dot(dft, g_ref[:, cols], 1, 0)
        dg = dot(df, w2_ref[cols, :], 1, 1)
        du = (dg * u_ref[:, cols]).astype(bf16)
        gb1_ref[:1, cols] += row_sum(du.astype(f32))
        aw1_ref[:, cols] += dot(ybt, du, 1, 0)
        dy = dy + dot(du, w1_ref[:, cols], 1, 1)
    gvec_ref[5:6, :] += row_sum(dy)
    gvec_ref[4:5, :] += row_sum(dy * n1)
    eg = dy * g1
    dh1 = (eg - mean(eg) - n1 * mean(eg * n1)) * inv1
    dh_ref[...] = dh1
    dr = dh1.astype(bf16)
    dr_ref[...] = dr
    gvec_ref[2:3, :] += row_sum(dr.astype(f32))
    awo_ref[...] += dot(c_ref[...].T, dr, 1, 0)

    @pl.when(step == TILES - 1)
    def _():
        gwo_ref[...] = awo_ref[...].astype(bf16)
        gw1_ref[...] = aw1_ref[...].astype(bf16)
        for k in range(FF // chunk):
            cols = slice(k * chunk, (k + 1) * chunk)
            gw2_ref[cols, :] = aw2_ref[:, cols].astype(bf16).T


def feed(xs, c, es, wo, w1, w2, vec, b1):
    shape = jax.ShapeDtypeStruct
    tile = pl.BlockSpec((TILE, D), lambda i: (i, 0))

    def whole(*dims):
        return pl.BlockSpec(dims, lambda i: (0,) * len(dims), pipeline_mode=pl.Buffered(1))

    return pl.pallas_call(
        feed_kernel,
        grid=(TILES,),
        out_shape=(
            shape((ROWS, D), bf16),
            shape((ROWS, D), f32),
            shape((ROWS, D), bf16),
            shape((D, D), bf16),
            shape((D, FF), bf16),
            shape((FF, D), bf16),
            shape((8, D), f32),
            shape((8, FF), f32),
        ),
        in_specs=[tile, tile, tile, whole(D, D), whole(D, FF), whole(FF, D), whole(8, D), whole(8, FF)],
        out_specs=[tile, tile, tile, whole(D, D), whole(D, FF), whole(FF, D), whole(8, D), whole(8, FF)],
        scratch_shapes=[
            pltpu.VMEM((TILE, FF), f32),
            pltpu.VMEM((TILE, FF), bf16),
            pltpu.VMEM((D, D), f32),
            pltpu.VMEM((D, FF), f32),
            pltpu.VMEM((D, FF), f32),
        ],
        compiler_params=pltpu.CompilerParams(vmem_limit_bytes=60 * MIB),
        name="feed",
    )(xs, c, es, wo, w1, w2, vec, b1)


def attn_backward_kernel(
    seq_count, xt_ref, qt_ref, kt_ref, vt_ref, lse_ref, dr_ref, dh_ref, z_ref, w_ref, wo_ref,
    out_ref, out_halo_ref, in_ref, in_halo_ref, gwa_ref, gbias_ref,
    dpt_ref, ext_ref,
):
    seq = lax.axis_index("seq")
    is_last = seq == seq_count - 1

    def block(dr, lane, width):
        lanes = pl.ds(lane, width)
        dct = dot(wo_ref[...], dr, 1, 1).astype(bf16)
        for h in range(HEADS):
            rows = slice(h * HEAD_DIM, (h + 1) * HEAD_DIM)
            qh = qt_ref[h, :, lanes]
            kh = kt_ref[h, :, lanes]
            vh = vt_ref[rows, lanes]
            dch = dct[rows]
            a = jnp.exp(dot(kh, qh, 0, 0) - lse_ref[h : h + 1, lanes])
            da = dot(vh, dch, 0, 0)
            ada = a * da
            ds = (ada - a * jnp.sum(ada, axis=0, keepdims=True)).astype(bf16)
            dv = dot(dch, a.astype(bf16), 1, 1)
            dk = dot(qh[:HEAD_DIM], ds, 1, 1)
            dq = dot(kh[:HEAD_DIM], ds, 1, 0) * HEAD_DIM**-0.5
            dpt_ref[rows, lanes] = dq.astype(bf16)
            dpt_ref[slice(D + h * HEAD_DIM, D + (h + 1) * HEAD_DIM), lanes] = dk.astype(bf16)
            dpt_ref[slice(2 * D + h * HEAD_DIM, 2 * D + (h + 1) * HEAD_DIM), lanes] = dv.astype(bf16)
        return dot(w_ref[...], dpt_ref[:, lanes], 1, 0).T

    dpt_ref[:, 8 * SLOT :] = jnp.zeros((3 * D, 128), bf16)

    def one(j, carry):
        row = slot_row(j)
        grad = block(dr_ref[pl.ds(row, SLOT), :], pl.multiple_of(j * SLOT, 128), SLOT)
        unstage(ext_ref, first_row(j, seq), grad + dh_ref[pl.ds(row, SLOT), :])
        return carry

    lax.fori_loop(0, 8, one, 0)
    count = 8 * seq_count

    def tail_of(ref):
        return jnp.concatenate(
            [ref[t * TILE + 2 * SLOT : (t + 1) * TILE, :] for t in range(TILES)], 0
        )

    grad = block(tail_of(dr_ref), 8 * SLOT, TAIL) + tail_of(dh_ref)

    @pl.when(is_last)
    def _():
        ext_ref[HALO + 2048 - count : HALO + 2048, :] = grad[:count]

    in_halo_ref[...] = ext_ref[:HALO, :]
    in_ref[...] = ext_ref[HALO : HALO + 2048, :]

    def two(j, carry):
        unstage(ext_ref, first_row(j, seq), z_ref[pl.ds(slot_row(j), SLOT), :].astype(f32))
        return carry

    lax.fori_loop(0, 8, two, 0)
    tail = tail_of(z_ref).astype(f32)

    @pl.when(is_last)
    def _():
        ext_ref[HALO + 2048 - count : HALO + 2048, :] = tail[:count]

    out_halo_ref[...] = ext_ref[:HALO, :].astype(bf16)
    out_ref[...] = ext_ref[HALO : HALO + 2048, :].astype(bf16)
    for part in range(3):
        cols = slice(part * D, (part + 1) * D)
        g = dot(xt_ref[...], dpt_ref[cols, :], 1, 1)
        gwa_ref[:, cols] = g[:D].astype(bf16)
        gbias_ref[:, cols] = g[D : D + 8]


def attn_backward(seq_count, *operands):
    shape = jax.ShapeDtypeStruct
    import functools
    return pl.pallas_call(
        functools.partial(attn_backward_kernel, seq_count),
        out_shape=(
            shape((2048, D), bf16),
            shape((HALO, D), bf16),
            shape((2048, D), f32),
            shape((HALO, D), f32),
            shape((D, 3 * D), bf16),
            shape((8, 3 * D), f32),
        ),
        in_specs=[pl.BlockSpec(memory_space=pltpu.VMEM)] * len(operands),
        out_specs=[pl.BlockSpec(memory_space=pltpu.VMEM)] * 6,
        scratch_shapes=[
            pltpu.VMEM((3 * D, LANES), bf16),
            pltpu.VMEM((HALO + 2048 + 16, D), f32),
        ],
        compiler_params=pltpu.CompilerParams(vmem_limit_bytes=60 * MIB),
        name="attn_backward",
    )(*operands)


def on_device(
    tokens,
    cotangent,
    segment,
    keep_mask,
    attn_master,
    out_master,
    in_master,
    back_master,
    vec_master,
    attn_first,
    out_first,
    in_first,
    back_first,
    vec_first,
    attn_second,
    out_second,
    in_second,
    back_second,
    vec_second,
):
    seq = lax.axis_index("seq")
    seq_count = lax.axis_size("seq")
    both = ("batch", "seq")
    attn_w, out_w, in_w, back_w, vec_low = (
        lax.all_gather(attn_master.astype(bf16), both, axis=0, tiled=True),
        lax.all_gather(out_master.astype(bf16), both, axis=0, tiled=True),
        lax.all_gather(in_master.astype(bf16), both, axis=0, tiled=True),
        lax.all_gather(back_master.astype(bf16), both, axis=0, tiled=True),
        lax.all_gather(vec_master.astype(bf16), both, axis=1, tiled=True),
    )
    vec_w = vec_low.astype(f32)
    bias_col = jnp.broadcast_to(vec_w[:2].reshape(2 * D, 1), (2 * D, 128))
    b1 = jnp.broadcast_to(vec_w[8:].reshape(1, FF), (8, FF))

    forward = [(i, i + 1) for i in range(seq_count - 1)]
    backward = [(i + 1, i) for i in range(seq_count - 1)]
    rows = tokens.shape[1]
    local_tag = segment[0] * 2 + keep_mask[0]
    sent_tag = jnp.clip(local_tag[rows - HALO :] - 32 * (seq + 1), 0, 7).astype(bf16)
    halo = jnp.concatenate(
        [tokens[0, rows - HALO :], cotangent[0, rows - HALO :],
         jnp.broadcast_to(sent_tag[:, None], (HALO, 128))], 1
    )
    halo = lax.ppermute(halo, "seq", forward)
    x = jnp.concatenate([halo[:, :D], tokens[0]], 0)
    e = jnp.concatenate([halo[:, D : 2 * D], cotangent[0]], 0)
    tag = jnp.concatenate(
        [halo[:, 2 * D].astype(jnp.int32) + 32 * seq, local_tag, jnp.zeros((64,), jnp.int32)]
    )
    tag = jnp.broadcast_to(tag[None], (8, tag.shape[0]))

    xs, es, xt, qt, kt, vt, c, lse = attn_forward(seq_count, x, e, tag, attn_w, bias_col)
    z, dh, dr, gwo, gw1, gw2, gvec, gb1 = feed(xs, c, es, out_w, in_w, back_w, vec_w[:8], b1)
    out, out_halo, grad_in, grad_in_halo, gwa, gbias = attn_backward(
        seq_count, xt, qt, kt, vt, lse, dr, dh, z, attn_w, out_w
    )
    out_back = lax.ppermute(out_halo, "seq", backward)
    grad_back = lax.ppermute(grad_in_halo, "seq", backward)
    place = lax.broadcasted_iota(jnp.int32, (HALO, 1), 0)
    theirs = (place >= HALO - 8 * (seq + 1)) & (seq < seq_count - 1)
    out = out.at[rows - HALO :].set(jnp.where(theirs, out_back, out[rows - HALO :]))
    grad_in = grad_in.at[rows - HALO :].set(
        jnp.where(theirs, grad_back, grad_in[rows - HALO :])
    )
    grad_vec = jnp.concatenate(
        [gbias[:1, :D], gbias[:1, 2 * D :], gvec[2:8], gb1[0].reshape(FF // D, D)], 0
    )
    sums = (
        lax.psum_scatter(gwa.astype(f32), both, scatter_dimension=0, tiled=True),
        lax.psum_scatter(gwo.astype(f32), both, scatter_dimension=0, tiled=True),
        lax.psum_scatter(gw1.astype(f32), both, scatter_dimension=0, tiled=True),
        lax.psum_scatter(gw2.astype(f32), both, scatter_dimension=0, tiled=True),
        lax.psum_scatter(grad_vec, both, scatter_dimension=1, tiled=True),
    )
    masters = (attn_master, out_master, in_master, back_master, vec_master)
    firsts = (attn_first, out_first, in_first, back_first, vec_first)
    seconds = (attn_second, out_second, in_second, back_second, vec_second)
    new = [
        adam_update(masters[i], firsts[i], seconds[i], sums[i], learn_rates[i]) for i in range(5)
    ]

    def own_columns(i):
        whole = lax.all_gather(new[i][2].astype(bf16), both, axis=1 if i == 4 else 0, tiled=True)
        count = whole.shape[1] // seq_count
        return lax.dynamic_slice_in_dim(whole, seq * count, count, 1)

    return (
        (out[None], grad_in[None])
        + tuple(new[i][0] for i in range(5))
        + tuple(new[i][1] for i in range(5))
        + tuple(new[i][2] for i in range(5))
        + tuple(own_columns(i) for i in range(5))
    )


def solution(mesh):
    stream = P("batch", "seq", None)
    rows = P(("batch", "seq"), None)
    vector = P(None, ("batch", "seq"))
    five = (rows, rows, rows, rows, vector)
    return jax.shard_map(
        on_device,
        mesh=mesh,
        in_specs=(stream, stream, P("batch", "seq"), P("batch", "seq")) + five * 3,
        out_specs=(stream, stream) + five * 3 + (P(None, "seq"),) * 5,
        check_vma=False,
    )
```

```python
import functools

import jax
import jax.numpy as jnp
from jax import lax
from jax.experimental import pallas as pl
from jax.experimental.pallas import tpu as pltpu
from jax.sharding import PartitionSpec as P

D = 512
HEADS = 8
HEAD_DIM = 64
FF = 2048
STEP = 10
PAIR = 255
SLOT = 256
HALO = 64
TILES = 4
TAIL = 64
PIECE = TAIL // TILES
TILE = 2 * SLOT + PIECE
ROWS = TILES * TILE
LANES = 8 * SLOT + 128
AUG = 16
MIB = 1 << 20

norm_epsilon = 1e-05
beta_first = 0.9
beta_second = 0.999
adam_epsilon = 1e-08
weight_decay = 0.01
learn_rates = (0.03, 0.2, 0.03, 0.02, 0.5)
big = 1e30

f32 = jnp.float32
bf16 = jnp.bfloat16


def dot(a, b, ca, cb):
    return lax.dot_general(a, b, (((ca,), (cb,)), ((), ())), preferred_element_type=f32)


def adam_update(master, first, second, gradient, rate):
    first_new = beta_first * first + (1.0 - beta_first) * gradient
    second_new = beta_second * second + (1.0 - beta_second) * gradient * gradient
    first_hat = first_new / (1.0 - beta_first**STEP)
    second_hat = second_new / (1.0 - beta_second**STEP)
    master_new = master - rate * (
        first_hat / (jnp.sqrt(second_hat) + adam_epsilon) + weight_decay * master
    )
    return (first_new, second_new, master_new)


def slot_row(j):
    return pl.multiple_of((j // 2) * TILE + (j % 2) * SLOT, 16)


def first_row(j, seq):
    return HALO + PAIR * j - 8 * seq


def staged(ref, start):
    base = pl.multiple_of((start // 16) * 16, 16)
    rest = start - base
    wide = ref[pl.ds(base, SLOT + 16), :].astype(f32)
    wide = jnp.where(rest >= 8, wide[8:], wide[:-8])
    shift = rest % 8
    groups = (SLOT + 8) // 8
    wide = wide.reshape(groups, 8, D)
    turned = pltpu.roll(wide, lax.rem(8 - shift, 8), 1)
    place = lax.broadcasted_iota(jnp.int32, (groups - 1, 8, D), 1)
    block = jnp.where(place < 8 - shift, turned[:-1], turned[1:]).reshape(SLOT, D)
    row = lax.broadcasted_iota(jnp.int32, (SLOT, D), 0)
    return jnp.where(row < PAIR, block, 0.0).astype(bf16)


def unstage(ref, start, block):
    base = pl.multiple_of((start // 8) * 8, 8)
    shift = start - base
    turned = pltpu.roll(block.reshape(SLOT // 8, 8, D), shift, 1)
    place = lax.broadcasted_iota(jnp.int32, (1, 8, D), 1)
    keep = ref[pl.ds(base, 8), :].reshape(1, 8, D)
    low = jnp.concatenate([keep, turned], 0)
    high = jnp.concatenate([turned, turned[-1:]], 0)
    place = lax.broadcasted_iota(jnp.int32, low.shape, 1)
    ref[pl.ds(base, SLOT + 8), :] = jnp.where(place < shift, low, high).reshape(SLOT + 8, D)


def tail_rows(ref, count, is_last):
    kept = ref[HALO + 2048 - count : HALO + 2048, :].astype(f32)
    if count < TAIL:
        kept = jnp.concatenate([kept, jnp.zeros((TAIL - count, D), f32)], 0)
    return jnp.where(is_last, kept, 0.0).astype(bf16)


def tag_rows(tag, pair):
    width = tag.shape[1]
    number = tag // 2 - 2 * pair
    kept = tag % 2
    row = lax.broadcasted_iota(jnp.int32, (AUG, width), 0)
    match = row == number
    query = jnp.where(match, 1.0, 0.0).astype(bf16)
    key = jnp.where(match & (kept == 1), 0.0, -big)
    key = jnp.where(row < 4, key, 0.0).astype(bf16)
    return query, key


def attn_forward_kernel(
    seq_count, tok_ref, cot_ref, tok_halo, cot_halo, seg_ref, keep_ref, seg_halo, keep_halo,
    w_ref, vec_ref,
    xs_ref, es_ref, xt_ref, qt_ref, kt_ref, vt_ref, c_ref, lse_ref,
    wt_ref, x_ref, e_ref, tag_ref, sems,
):
    seq = lax.axis_index("seq")
    is_last = seq == seq_count - 1
    rows = tok_ref.shape[1]
    loads = []
    for i, (whole, halo, ext) in enumerate(((tok_ref, tok_halo, x_ref), (cot_ref, cot_halo, e_ref))):
        loads.append(pltpu.make_async_copy(whole.at[0], ext.at[pl.ds(HALO, rows)], sems.at[2 * i]))
        loads.append(pltpu.make_async_copy(halo, ext.at[pl.ds(0, HALO)], sems.at[2 * i + 1]))
    for load in loads:
        load.start()
    for part in range(3):
        wt_ref[part * D : (part + 1) * D, :] = w_ref[:, part * D : (part + 1) * D].T
    tag_ref[...] = jnp.zeros_like(tag_ref)
    edge = seg_halo[...] * 2 + keep_halo[...]
    tag_ref[:, :HALO] = jnp.broadcast_to(edge[:, 128 - HALO :], (8, HALO))
    tag_ref[:, HALO : HALO + rows] = jnp.broadcast_to(seg_ref[...] * 2 + keep_ref[...], (8, rows))
    query_bias = vec_ref[:, 0:1].astype(f32)
    value_bias = vec_ref[:, 1:2].astype(f32)
    for load in loads:
        load.wait()

    def block(xb, tag, pair, lane, width):
        lanes = pl.ds(lane, width)
        xt_ref[:D, lanes] = xb.T
        q = dot(wt_ref[:D, :], xb, 1, 1) + query_bias
        q = (q.astype(bf16).astype(f32) * HEAD_DIM**-0.5).astype(bf16)
        k = dot(wt_ref[D : 2 * D, :], xb, 1, 1).astype(bf16)
        v = (dot(wt_ref[2 * D :, :], xb, 1, 1) + value_bias).astype(bf16)
        query_tag, key_tag = tag_rows(tag, pair)
        vt_ref[:, lanes] = v
        context = []
        for h in range(HEADS):
            rows = slice(h * HEAD_DIM, (h + 1) * HEAD_DIM)
            qh = jnp.concatenate([q[rows], query_tag], 0)
            kh = jnp.concatenate([k[rows], key_tag], 0)
            qt_ref[h, :, lanes] = qh
            kt_ref[h, :, lanes] = kh
            s = dot(kh, qh, 0, 0)
            top = jnp.max(s, axis=0, keepdims=True)
            ex = jnp.exp(s - top)
            total = jnp.sum(ex, axis=0, keepdims=True)
            lse_ref[h : h + 1, lanes] = top + jnp.log(total)
            a = (ex * (1.0 / total)).astype(bf16)
            context.append(dot(v[rows], a, 1, 0))
        return jnp.concatenate(context, 0).astype(bf16).T

    def one(j, carry):
        start = first_row(j, seq)
        row = slot_row(j)
        xb = staged(x_ref, start)
        xs_ref[pl.ds(row, SLOT), :] = xb
        es_ref[pl.ds(row, SLOT), :] = staged(e_ref, start)
        wide = tag_ref[:, pl.ds(pl.multiple_of(j * SLOT, 128), SLOT + 128)]
        width = SLOT + 128
        tag = pltpu.roll(wide, width - (start - j * SLOT), 1)[:1, :SLOT]
        c_ref[pl.ds(row, SLOT), :] = block(
            xb, tag, 8 * seq + j, pl.multiple_of(j * SLOT, 128), SLOT
        )
        return carry

    lax.fori_loop(0, 8, one, 0)
    count = 8 * seq_count
    xt_ref[:, 8 * SLOT :] = jnp.zeros((D + AUG, 128), bf16)
    xb = tail_rows(x_ref, count, is_last)
    eb = tail_rows(e_ref, count, is_last)
    tag = tag_ref[:1, 2048:2176]
    tag = pltpu.roll(tag_ref[:, 2048:2176], 128 - (64 - count), 1)[:1, :TAIL] if count < 64 else tag[:, :TAIL]
    place = lax.broadcasted_iota(jnp.int32, (1, TAIL), 1)
    tag = jnp.where(place < count, tag, (2 * 8 * seq_count + 3) * 2)
    cb = block(xb, tag, 8 * seq_count, 8 * SLOT, TAIL)
    for t in range(TILES):
        rows = slice(t * PIECE, (t + 1) * PIECE)
        at = slice(t * TILE + 2 * SLOT, (t + 1) * TILE)
        xs_ref[at, :] = xb[rows]
        es_ref[at, :] = eb[rows]
        c_ref[at, :] = cb[rows]
    ones = lax.broadcasted_iota(jnp.int32, (AUG, LANES), 0) == 0
    xt_ref[D:, :] = jnp.where(ones, 1.0, 0.0).astype(bf16)


def attn_forward(seq_count, tokens, cotangent, *others):
    shape = jax.ShapeDtypeStruct
    vmem = pl.BlockSpec(memory_space=pltpu.VMEM)
    hbm = pl.BlockSpec(memory_space=pl.ANY)
    return pl.pallas_call(
        functools.partial(attn_forward_kernel, seq_count),
        out_shape=(
            shape((ROWS, D), bf16),
            shape((ROWS, D), bf16),
            shape((D + AUG, LANES), bf16),
            shape((HEADS, HEAD_DIM + AUG, LANES), bf16),
            shape((HEADS, HEAD_DIM + AUG, LANES), bf16),
            shape((D, LANES), bf16),
            shape((ROWS, D), bf16),
            shape((HEADS, LANES), f32),
        ),
        in_specs=[hbm, hbm] + [vmem] * len(others),
        out_specs=[vmem] * 8,
        scratch_shapes=[
            pltpu.VMEM((3 * D, D), bf16),
            pltpu.VMEM((HALO + tokens.shape[1], D), bf16),
            pltpu.VMEM((HALO + tokens.shape[1], D), bf16),
            pltpu.VMEM((8, LANES), jnp.int32),
            pltpu.SemaphoreType.DMA((4,)),
        ],
        compiler_params=pltpu.CompilerParams(vmem_limit_bytes=56 * MIB),
        name="attn_forward",
    )(tokens, cotangent, *others)


def feed_kernel(
    xs_ref, c_ref, es_ref, wo_ref, w1_ref, w2_ref, vect_ref,
    z_ref, dh_ref, dr_ref, gwo_ref, gw1_ref, gw2_ref, gvec_ref, gb1_ref,
    u_ref, g_ref, awo_ref, aw1_ref, aw2_ref, vec_ref,
):
    step = pl.program_id(0)

    @pl.when(step == 0)
    def _():
        awo_ref[...] = jnp.zeros_like(awo_ref)
        aw1_ref[...] = jnp.zeros_like(aw1_ref)
        aw2_ref[...] = jnp.zeros_like(aw2_ref)
        gvec_ref[...] = jnp.zeros_like(gvec_ref)
        gb1_ref[...] = jnp.zeros_like(gb1_ref)
        vec_ref[...] = vect_ref[...].astype(f32).T

    def mean(v):
        return jnp.mean(v, axis=-1, keepdims=True)

    def row_sum(v):
        return jnp.sum(v, axis=0, keepdims=True)

    bo, b2, g1, c1, g2, c2 = (vec_ref[i : i + 1, :] for i in range(2, 8))
    h1 = xs_ref[...].astype(f32) + (dot(c_ref[...], wo_ref[...], 1, 0) + bo)
    mid = h1 - mean(h1)
    inv1 = lax.rsqrt(mean(mid * mid) + norm_epsilon)
    n1 = mid * inv1
    y = n1 * g1 + c1
    yb = y.astype(bf16)
    chunk = D
    f = None
    for k in range(FF // chunk):
        cols = slice(k * chunk, (k + 1) * chunk)
        u = dot(yb, w1_ref[:, cols], 1, 0) + vec_ref[8 + k : 9 + k, :]
        cdf = 0.5 * (1.0 + lax.erf(u * 0.7071067811865476))
        gk = (u * cdf).astype(bf16)
        u_ref[:, cols] = cdf + u * jnp.exp(u * u * -0.5) * 0.3989422804014327
        g_ref[:, cols] = gk
        part = dot(gk, w2_ref[cols, :], 1, 0)
        f = part if f is None else f + part
    h2 = y + (f + b2)
    mid2 = h2 - mean(h2)
    inv2 = lax.rsqrt(mean(mid2 * mid2) + norm_epsilon)
    n2 = mid2 * inv2
    z_ref[...] = (n2 * g2 + c2).astype(bf16)
    e = es_ref[...].astype(f32)
    gvec_ref[7:8, :] += row_sum(e)
    gvec_ref[6:7, :] += row_sum(e * n2)
    eg = e * g2
    dh2 = (eg - mean(eg) - n2 * mean(eg * n2)) * inv2
    df = dh2.astype(bf16)
    gvec_ref[3:4, :] += row_sum(df.astype(f32))
    dft = df.T
    ybt = yb.T
    dy = dh2
    for k in range(FF // chunk):
        cols = slice(k * chunk, (k + 1) * chunk)
        aw2_ref[:, cols] += dot(dft, g_ref[:, cols], 1, 0)
        dg = dot(df, w2_ref[cols, :], 1, 1)
        du = (dg * u_ref[:, cols]).astype(bf16)
        gb1_ref[:1, cols] += row_sum(du.astype(f32))
        aw1_ref[:, cols] += dot(ybt, du, 1, 0)
        dy = dy + dot(du, w1_ref[:, cols], 1, 1)
    gvec_ref[5:6, :] += row_sum(dy)
    gvec_ref[4:5, :] += row_sum(dy * n1)
    eg = dy * g1
    dh1 = (eg - mean(eg) - n1 * mean(eg * n1)) * inv1
    dh_ref[...] = dh1
    dr = dh1.astype(bf16)
    dr_ref[...] = dr
    gvec_ref[2:3, :] += row_sum(dr.astype(f32))
    awo_ref[...] += dot(c_ref[...].T, dr, 1, 0)

    @pl.when(step == TILES - 1)
    def _():
        gwo_ref[...] = awo_ref[...].astype(bf16)
        gw1_ref[...] = aw1_ref[...].astype(bf16)
        for k in range(FF // chunk):
            cols = slice(k * chunk, (k + 1) * chunk)
            gw2_ref[cols, :] = aw2_ref[:, cols].astype(bf16).T


def feed(xs, c, es, wo, w1, w2, vec_t):
    shape = jax.ShapeDtypeStruct
    tile = pl.BlockSpec((TILE, D), lambda i: (i, 0))

    def whole(*dims):
        return pl.BlockSpec(dims, lambda i: (0,) * len(dims), pipeline_mode=pl.Buffered(1))

    return pl.pallas_call(
        feed_kernel,
        grid=(TILES,),
        out_shape=(
            shape((ROWS, D), bf16),
            shape((ROWS, D), f32),
            shape((ROWS, D), bf16),
            shape((D, D), bf16),
            shape((D, FF), bf16),
            shape((FF, D), bf16),
            shape((8, D), f32),
            shape((8, FF), f32),
        ),
        in_specs=[tile, tile, tile, whole(D, D), whole(D, FF), whole(FF, D), whole(D, 128)],
        out_specs=[tile, tile, tile, whole(D, D), whole(D, FF), whole(FF, D), whole(8, D), whole(8, FF)],
        scratch_shapes=[
            pltpu.VMEM((TILE, FF), f32),
            pltpu.VMEM((TILE, FF), bf16),
            pltpu.VMEM((D, D), f32),
            pltpu.VMEM((D, FF), f32),
            pltpu.VMEM((D, FF), f32),
            pltpu.VMEM((128, D), f32),
        ],
        compiler_params=pltpu.CompilerParams(vmem_limit_bytes=60 * MIB),
        name="feed",
    )(xs, c, es, wo, w1, w2, vec_t)


def attn_backward_kernel(
    seq_count, xt_ref, qt_ref, kt_ref, vt_ref, lse_ref, dr_ref, dh_ref, z_ref, w_ref, wo_ref,
    out_ref, out_halo_ref, in_ref, in_halo_ref, gwa_ref, gbias_ref,
    dpt_ref, ext_ref,
):
    seq = lax.axis_index("seq")
    is_last = seq == seq_count - 1

    def block(dr, lane, width):
        lanes = pl.ds(lane, width)
        dct = dot(wo_ref[...], dr, 1, 1).astype(bf16)
        for h in range(HEADS):
            rows = slice(h * HEAD_DIM, (h + 1) * HEAD_DIM)
            qh = qt_ref[h, :, lanes]
            kh = kt_ref[h, :, lanes]
            vh = vt_ref[rows, lanes]
            dch = dct[rows]
            a = jnp.exp(dot(kh, qh, 0, 0) - lse_ref[h : h + 1, lanes])
            da = dot(vh, dch, 0, 0)
            ada = a * da
            ds = (ada - a * jnp.sum(ada, axis=0, keepdims=True)).astype(bf16)
            dv = dot(dch, a.astype(bf16), 1, 1)
            dk = dot(qh[:HEAD_DIM], ds, 1, 1)
            dq = dot(kh[:HEAD_DIM], ds, 1, 0) * HEAD_DIM**-0.5
            dpt_ref[rows, lanes] = dq.astype(bf16)
            dpt_ref[slice(D + h * HEAD_DIM, D + (h + 1) * HEAD_DIM), lanes] = dk.astype(bf16)
            dpt_ref[slice(2 * D + h * HEAD_DIM, 2 * D + (h + 1) * HEAD_DIM), lanes] = dv.astype(bf16)
        return dot(w_ref[...], dpt_ref[:, lanes], 1, 0).T

    dpt_ref[:, 8 * SLOT :] = jnp.zeros((3 * D, 128), bf16)

    def one(j, carry):
        row = slot_row(j)
        grad = block(dr_ref[pl.ds(row, SLOT), :], pl.multiple_of(j * SLOT, 128), SLOT)
        unstage(ext_ref, first_row(j, seq), grad + dh_ref[pl.ds(row, SLOT), :])
        return carry

    lax.fori_loop(0, 8, one, 0)
    count = 8 * seq_count

    def tail_of(ref):
        return jnp.concatenate(
            [ref[t * TILE + 2 * SLOT : (t + 1) * TILE, :] for t in range(TILES)], 0
        )

    grad = block(tail_of(dr_ref), 8 * SLOT, TAIL) + tail_of(dh_ref)

    @pl.when(is_last)
    def _():
        ext_ref[HALO + 2048 - count : HALO + 2048, :] = grad[:count]

    in_halo_ref[...] = ext_ref[:HALO, :]
    in_ref[...] = ext_ref[HALO : HALO + 2048, :]

    def two(j, carry):
        unstage(ext_ref, first_row(j, seq), z_ref[pl.ds(slot_row(j), SLOT), :].astype(f32))
        return carry

    lax.fori_loop(0, 8, two, 0)
    tail = tail_of(z_ref).astype(f32)

    @pl.when(is_last)
    def _():
        ext_ref[HALO + 2048 - count : HALO + 2048, :] = tail[:count]

    out_halo_ref[...] = ext_ref[:HALO, :].astype(bf16)
    out_ref[...] = ext_ref[HALO : HALO + 2048, :].astype(bf16)
    for part in range(3):
        cols = slice(part * D, (part + 1) * D)
        g = dot(xt_ref[...], dpt_ref[cols, :], 1, 1)
        gwa_ref[:, cols] = g[:D].astype(bf16)
        gbias_ref[:, cols] = g[D : D + 8]


def attn_backward(seq_count, *operands):
    shape = jax.ShapeDtypeStruct
    return pl.pallas_call(
        functools.partial(attn_backward_kernel, seq_count),
        out_shape=(
            shape((2048, D), bf16),
            shape((HALO, D), bf16),
            shape((2048, D), f32),
            shape((HALO, D), f32),
            shape((D, 3 * D), bf16),
            shape((8, 3 * D), f32),
        ),
        in_specs=[pl.BlockSpec(memory_space=pltpu.VMEM)] * len(operands),
        out_specs=[pl.BlockSpec(memory_space=pltpu.VMEM)] * 6,
        scratch_shapes=[
            pltpu.VMEM((3 * D, LANES), bf16),
            pltpu.VMEM((HALO + 2048 + 16, D), f32),
        ],
        compiler_params=pltpu.CompilerParams(vmem_limit_bytes=60 * MIB),
        name="attn_backward",
    )(*operands)


MESH = pl.DeviceIdType.MESH
PLANE = 4
DEPTH = 4


class Place:
    def __init__(self):
        self.batch = lax.axis_index("batch")
        self.z = lax.axis_index("seq")
        self.core = self.batch % 2
        self.plane = self.batch // 2

    def plane_at(self, k):
        x = (self.plane % 2 + k % 2) % 2
        y = (self.plane // 2 + k // 2) % 2
        return y * 2 + x

    def in_plane(self, k):
        return {"batch": self.plane_at(k) * 2 + self.core, "seq": self.z}

    def depth_at(self, k):
        return (self.z + k) % DEPTH

    def in_depth(self, k):
        return {"batch": self.batch, "seq": self.depth_at(k)}

    def sibling(self):
        return {"batch": self.plane * 2 + 1 - self.core, "seq": self.z}

    def greet(self):
        barrier = pltpu.get_barrier_semaphore()
        for k in range(1, 4):
            pl.semaphore_signal(barrier, inc=1, device_id=self.in_plane(k), device_id_type=MESH)
            pl.semaphore_signal(barrier, inc=1, device_id=self.in_depth(k), device_id_type=MESH)
        pl.semaphore_signal(barrier, inc=1, device_id=self.sibling(), device_id_type=MESH)
        pl.semaphore_wait(barrier, 7)


def remote(src, dst, send, recv, device):
    return pltpu.make_async_remote_copy(
        src_ref=src, dst_ref=dst, send_sem=send, recv_sem=recv, device_id=device, device_id_type=MESH
    )


class Gather:
    def __init__(self, place, whole, send, recv, parts=None):
        self.place, self.whole, self.send, self.recv, self.parts = place, whole, send, recv, parts

    def depth(self, k):
        at = self.place
        here = self.whole.at[at.batch, at.z]
        source = here if self.parts is None else self.parts.at[at.depth_at(k)]
        return remote(source, here, self.send.at[k - 1], self.recv.at[k - 1], at.in_depth(k))

    def plane(self, k):
        block = self.whole.at[self.place.batch]
        return remote(block, block, self.send.at[2 + k], self.recv.at[2 + k], self.place.in_plane(k))

    def core(self, k):
        block = self.whole.at[self.place.plane_at(k) * 2 + self.place.core]
        return remote(block, block, self.send.at[6 + k], self.recv.at[6 + k], self.place.sibling())

    def first(self):
        for k in range(1, 4):
            self.depth(k).start()

    def second(self):
        for k in range(1, 4):
            self.depth(k).wait_recv()
        for k in range(1, 4):
            self.plane(k).start()
        self.core(0).start()

    def third(self):
        for k in range(1, 4):
            self.plane(k).wait_recv()
            self.core(k).start()

    def finish(self):
        for k in range(4):
            self.core(k).wait_recv()
        for k in range(1, 4):
            self.depth(k).wait_send()
            self.plane(k).wait_send()
        for k in range(4):
            self.core(k).wait_send()


class Scatter:
    def __init__(self, place, grad, twin, half, across, line, along, send, recv):
        self.place, self.grad, self.twin, self.half = place, grad, twin, half
        self.across, self.line, self.along, self.send, self.recv = across, line, along, send, recv

    def core(self):
        return remote(
            self.grad.at[:, 1 - self.place.core], self.twin, self.send.at[0], self.recv.at[0],
            self.place.sibling(),
        )

    def plane(self, k):
        return remote(
            self.half.at[self.place.plane_at(k)], self.across.at[k - 1], self.send.at[k],
            self.recv.at[k], self.place.in_plane(k),
        )

    def depth(self, k):
        return remote(
            self.line.at[self.place.depth_at(k)], self.along.at[k - 1], self.send.at[3 + k],
            self.recv.at[3 + k], self.place.in_depth(k),
        )

    def first(self):
        self.core().start()

    def second(self):
        self.core().wait_recv()
        own = self.place.core

        def one(i, carry):
            p, q = i // DEPTH, i % DEPTH
            total = self.grad[p, own, q].astype(f32) + self.twin[p, q].astype(f32)
            self.half[p, q] = total.astype(self.half.dtype)
            return carry

        lax.fori_loop(0, PLANE * DEPTH, one, 0)
        for k in range(1, 4):
            self.plane(k).start()

    def third(self):
        for k in range(1, 4):
            self.plane(k).wait_recv()
        own = self.place.plane

        def one(q, carry):
            total = self.half[own, q].astype(f32)
            for k in range(3):
                total = total + self.across[k, q].astype(f32)
            self.line[q] = total.astype(self.line.dtype)
            return carry

        lax.fori_loop(0, DEPTH, one, 0)
        for k in range(1, 4):
            self.depth(k).start()

    def total(self):
        for k in range(1, 4):
            self.depth(k).wait_recv()
        total = self.line[self.place.z].astype(f32)
        for k in range(3):
            total = total + self.along[k].astype(f32)
        return total

    def finish(self):
        self.core().wait_send()
        for k in range(1, 4):
            self.plane(k).wait_send()
            self.depth(k).wait_send()


def turned(ref, value):
    ref[...] = jnp.zeros_like(ref)
    ref[: value.shape[0], : value.shape[1]] = value
    return ref[...].T


def gather_kernel(
    attn_ref, out_ref, in_ref, back_ref, vec_ref, tok_ref, cot_ref, seg_ref, keep_ref,
    wa_ref, wo_ref, w1_ref, w2_ref, wv_ref, tok_halo, cot_halo, seg_halo, keep_halo,
    square, send, recv, edge_send, edge_recv,
):
    place = Place()
    place.greet()
    rows = tok_ref.shape[1]
    edge = []
    for i, (src, dst) in enumerate((
        (tok_ref.at[0, pl.ds(rows - HALO, HALO)], tok_halo),
        (cot_ref.at[0, pl.ds(rows - HALO, HALO)], cot_halo),
        (seg_ref.at[:, pl.ds(rows - 128, 128)], seg_halo),
        (keep_ref.at[:, pl.ds(rows - 128, 128)], keep_halo),
    )):
        edge.append(remote(src, dst, edge_send.at[i], edge_recv.at[i], place.in_depth(1)))
    own = (
        (wv_ref, turned(square, vec_ref[...])[: vec_ref.shape[1]]),
        (wa_ref, attn_ref[...]),
        (wo_ref, out_ref[...]),
        (w1_ref, in_ref[...]),
        (w2_ref, back_ref[...]),
    )
    gathers = []
    for i, (whole, shard) in enumerate(own):
        whole[place.batch, place.z] = shard.astype(bf16)
        gathers.append(Gather(place, whole, send.at[i], recv.at[i]))
        gathers[-1].first()
    for copy in edge:
        copy.start()
    for g in gathers:
        g.second()
    for g in gathers:
        g.third()
    for g in gathers:
        g.finish()
    for copy in edge:
        copy.wait()


def gather(attn, out, into, back, vec, tokens, cotangent, segment, keep):
    shape = jax.ShapeDtypeStruct
    vmem = pl.BlockSpec(memory_space=pltpu.VMEM)
    hbm = pl.BlockSpec(memory_space=pl.ANY)

    def whole(rows, cols):
        return shape((8, DEPTH, rows, cols), bf16)

    r = attn.shape[0]
    return pl.pallas_call(
        gather_kernel,
        out_shape=(
            whole(r, 3 * D), whole(r, D), whole(r, FF), whole(4 * r, D), whole(r, 128),
            shape((HALO, D), bf16), shape((HALO, D), bf16),
            shape((1, 128), jnp.int32), shape((1, 128), jnp.int32),
        ),
        in_specs=[vmem] * 5 + [hbm, hbm, vmem, vmem],
        out_specs=[vmem] * 9,
        scratch_shapes=[
            pltpu.VMEM((128, 128), f32),
            pltpu.SemaphoreType.DMA((5, 10)),
            pltpu.SemaphoreType.DMA((5, 10)),
            pltpu.SemaphoreType.DMA((4,)),
            pltpu.SemaphoreType.DMA((4,)),
        ],
        compiler_params=pltpu.CompilerParams(
            collective_id=0, has_side_effects=True, vmem_limit_bytes=40 * MIB
        ),
        name="gather",
    )(attn, out, into, back, vec, tokens, cotangent, segment, keep)


def step_kernel(shapes, *refs):
    refs = list(refs)

    def take(count):
        taken = refs[:count]
        del refs[:count]
        return taken

    grads = take(4)
    gvec_ref, gb1_ref, gbias_ref = take(3)
    edge_in = take(2)
    masters, firsts, seconds = take(5), take(5), take(5)
    first_out, second_out, master_out, copies = take(5), take(5), take(5), take(5)
    edge_out = take(2)
    grad_vec, wide, square, whole_vec = take(4)
    twins, halves, acrosses, lines, alongs = take(5), take(5), take(5), take(5), take(5)
    parts = take(4)
    send, recv, copy_send, copy_recv, edge_send, edge_recv = refs
    place = Place()
    place.greet()
    edge = [
        remote(edge_in[i], edge_out[i], edge_send.at[i], edge_recv.at[i], place.in_depth(3))
        for i in range(2)
    ]
    for copy in edge:
        copy.start()
    wide[...] = jnp.zeros_like(wide)
    wide[0:1] = gbias_ref[:1, :D]
    wide[1:2] = gbias_ref[:1, 2 * D :]
    wide[2:8] = gvec_ref[2:8]
    for k in range(FF // D):
        wide[8 + k : 9 + k] = gb1_ref[:1, k * D : (k + 1) * D]
    grad_vec[...] = wide[...].T.reshape(grad_vec.shape)
    grads = grads + [grad_vec]
    order = (3, 2, 1, 0, 4)
    scatters = {
        i: Scatter(
            place, grads[i], twins[i], halves[i], acrosses[i], lines[i], alongs[i],
            send.at[i], recv.at[i],
        )
        for i in order
    }
    for i in order:
        scatters[i].first()
    for i in order:
        scatters[i].second()
    for i in order:
        scatters[i].third()
    gathers = {}
    for i in order:
        total = scatters[i].total()
        if i == 4:
            square[...] = jnp.zeros_like(square)
            square[: total.shape[0], :] = total
            rows, cols = masters[4].shape
            total = square[...].T[:rows, :cols]
        new = adam_update(
            masters[i][...], firsts[i][...], seconds[i][...], total, learn_rates[i]
        )
        first_out[i][...], second_out[i][...], master_out[i][...] = new
        if i == 4:
            shard = turned(square, new[2])[: new[2].shape[1]].astype(bf16)
            whole_vec[place.batch, place.z] = shard
            gathers[i] = Gather(place, whole_vec, copy_send.at[i], copy_recv.at[i])
        else:
            low = new[2].astype(bf16)
            width = low.shape[1] // DEPTH
            for q in range(DEPTH):
                parts[i][q] = low[:, q * width : (q + 1) * width]
            copies[i][place.batch, place.z] = parts[i][place.z]
            gathers[i] = Gather(place, copies[i], copy_send.at[i], copy_recv.at[i], parts[i])
        gathers[i].first()
    for i in order:
        gathers[i].second()
    for i in order:
        gathers[i].third()
    for i in order:
        gathers[i].finish()
        scatters[i].finish()
    rows = masters[4].shape[0]
    mine = jnp.concatenate([whole_vec[place.z * 2 + q // 4, q % 4] for q in range(8)], 0)
    copies[4][...] = mine.astype(f32).T[:rows].astype(bf16)
    for copy in edge:
        copy.wait()


def step(grads, vectors, edges, masters, firsts, seconds):
    shape = jax.ShapeDtypeStruct
    r = masters[0].shape[0]
    shapes = ((r, 3 * D), (r, D), (r, FF), (4 * r, D))
    vmem = pl.BlockSpec(memory_space=pltpu.VMEM)
    grads = [
        g.reshape((PLANE, 2, DEPTH) + s) for g, s in zip(grads, shapes)
    ]
    operands = (*grads, *vectors, *edges, *masters, *firsts, *seconds)
    like = [shape(m.shape, f32) for m in masters]
    copies = [shape((8, DEPTH, s[0], s[1] // DEPTH), bf16) for s in shapes]
    copies.append(shape((masters[4].shape[0], 128), bf16))
    out_shape = (*like, *like, *like, *copies, *[shape(e.shape, e.dtype) for e in edges])
    five = [(s, bf16) for s in shapes] + [((r, 128), f32)]
    scratch = [
        pltpu.VMEM((PLANE, 2, DEPTH, r, 128), f32),
        pltpu.VMEM((128, D), f32),
        pltpu.VMEM((128, 128), f32),
        pltpu.VMEM((8, DEPTH, r, 128), bf16),
    ]
    for lead in ((PLANE, DEPTH), (PLANE, DEPTH), (3, DEPTH), (DEPTH,), (3,)):
        scratch += [pltpu.VMEM(lead + s, t) for s, t in five]
    scratch += [pltpu.VMEM((DEPTH, s[0], s[1] // DEPTH), bf16) for s in shapes]
    scratch += [
        pltpu.SemaphoreType.DMA((5, 7)),
        pltpu.SemaphoreType.DMA((5, 7)),
        pltpu.SemaphoreType.DMA((5, 10)),
        pltpu.SemaphoreType.DMA((5, 10)),
        pltpu.SemaphoreType.DMA((2,)),
        pltpu.SemaphoreType.DMA((2,)),
    ]
    return pl.pallas_call(
        functools.partial(step_kernel, shapes),
        out_shape=out_shape,
        in_specs=[vmem] * len(operands),
        out_specs=[vmem] * len(out_shape),
        scratch_shapes=scratch,
        compiler_params=pltpu.CompilerParams(
            collective_id=1, has_side_effects=True, vmem_limit_bytes=56 * MIB
        ),
        name="step",
    )(*operands)


def last_kernel(*refs):
    count = 22
    seq_count = 4
    out_ref, in_ref, out_back, in_back = refs[:4]
    results = refs[4 : 4 + 20]
    ends = refs[4 + 20 : 4 + 20 + count]
    out_low, in_low, sems = refs[4 + 20 + count :]
    copies = []
    for i in range(20):
        copies.append(pltpu.make_async_copy(results[i], ends[2 + i], sems.at[i]))
        copies[-1].start()
    rows = out_ref.shape[0]
    seq = lax.axis_index("seq")
    place = lax.broadcasted_iota(jnp.int32, (HALO, 1), 0)
    theirs = (place >= HALO - 8 * (seq + 1)) & (seq < lax.axis_size("seq") - 1)
    for n, (whole, back, low, end) in enumerate((
        (out_ref, out_back, out_low, ends[0]), (in_ref, in_back, in_low, ends[1])
    )):
        at = pl.ds(rows - HALO, HALO)
        load = pltpu.make_async_copy(whole.at[at], low, sems.at[20 + n])
        load.start()
        load.wait()
        low[...] = jnp.where(theirs, back[...].astype(f32), low[...].astype(f32)).astype(low.dtype)
        store = pltpu.make_async_copy(low, end.at[at], sems.at[20 + n])
        store.start()
        store.wait()
    for copy in copies:
        copy.wait()


def last(out, grad_in, out_back, in_back, results):
    shape = jax.ShapeDtypeStruct
    vmem = pl.BlockSpec(memory_space=pltpu.VMEM)
    hbm = pl.BlockSpec(memory_space=pl.ANY)
    same = [shape(a.shape, a.dtype) for a in (out, grad_in, *results)]
    return pl.pallas_call(
        last_kernel,
        out_shape=same,
        in_specs=[hbm, hbm, vmem, vmem] + [hbm] * len(results),
        out_specs=[hbm] * len(same),
        scratch_shapes=[
            pltpu.VMEM((HALO, D), bf16),
            pltpu.VMEM((HALO, D), f32),
            pltpu.SemaphoreType.DMA((22,)),
        ],
        input_output_aliases={0: 0, 1: 1},
        compiler_params=pltpu.CompilerParams(vmem_limit_bytes=8 * MIB),
        name="last",
    )(out, grad_in, out_back, in_back, *results)


def on_device(
    tokens,
    cotangent,
    segment,
    keep_mask,
    attn_master,
    out_master,
    in_master,
    back_master,
    vec_master,
    attn_first,
    out_first,
    in_first,
    back_first,
    vec_first,
    attn_second,
    out_second,
    in_second,
    back_second,
    vec_second,
):
    seq = lax.axis_index("seq")
    seq_count = lax.axis_size("seq")
    both = ("batch", "seq")
    rows = tokens.shape[1]
    masters = (attn_master, out_master, in_master, back_master, vec_master)
    firsts = (attn_first, out_first, in_first, back_first, vec_first)
    seconds = (attn_second, out_second, in_second, back_second, vec_second)
    direct = seq_count == DEPTH and lax.axis_size("batch") == 2 * PLANE
    forward = [(i, i + 1) for i in range(seq_count - 1)]
    backward = [(i + 1, i) for i in range(seq_count - 1)]
    if direct:
        *whole, x_halo, e_halo, seg_halo, keep_halo = gather(
            *masters, tokens, cotangent, segment, keep_mask
        )
        attn_w, out_w, in_w, back_w, vec_t = (w.reshape(-1, w.shape[-1]) for w in whole)
    else:
        low = [w.astype(bf16) for w in masters]
        low[4] = jnp.pad(low[4].T, ((0, 0), (0, 128 - low[4].shape[0])))
        attn_w, out_w, in_w, back_w, vec_t = (
            lax.all_gather(w, both, axis=0, tiled=True) for w in low
        )
        x_halo, e_halo, seg_halo, keep_halo = (
            lax.ppermute(a, "seq", forward)
            for a in (
                tokens[0, rows - HALO :], cotangent[0, rows - HALO :],
                segment[:, rows - 128 :], keep_mask[:, rows - 128 :],
            )
        )
    xs, es, xt, qt, kt, vt, c, lse = attn_forward(
        seq_count, tokens, cotangent, x_halo, e_halo, segment, keep_mask, seg_halo, keep_halo,
        attn_w, vec_t,
    )
    z, dh, dr, gwo, gw1, gw2, gvec, gb1 = feed(xs, c, es, out_w, in_w, back_w, vec_t)
    out, out_halo, grad_in, grad_in_halo, gwa, gbias = attn_backward(
        seq_count, xt, qt, kt, vt, lse, dr, dh, z, attn_w, out_w
    )
    grads = (gwa, gwo, gw1, gw2)
    if direct:
        *results, out_back, grad_back = step(
            grads, (gvec, gb1, gbias), (out_halo, grad_in_halo), masters, firsts, seconds
        )
        for i in range(15, 19):
            results[i] = results[i].reshape(-1, results[i].shape[-1])
    else:
        grad_vec = jnp.concatenate(
            [gbias[:1, :D], gbias[:1, 2 * D :], gvec[2:8], gb1[0].reshape(FF // D, D)], 0
        )
        sums = [lax.psum_scatter(g.astype(f32), both, scatter_dimension=0, tiled=True) for g in grads]
        sums.append(lax.psum_scatter(grad_vec, both, scatter_dimension=1, tiled=True))
        new = [
            adam_update(masters[i], firsts[i], seconds[i], sums[i], learn_rates[i])
            for i in range(5)
        ]

        def own_columns(i):
            whole = lax.all_gather(new[i][2].astype(bf16), both, axis=1 if i == 4 else 0, tiled=True)
            count = whole.shape[1] // seq_count
            return lax.dynamic_slice_in_dim(whole, seq * count, count, 1)

        results = [new[i][part] for part in range(3) for i in range(5)]
        results += [own_columns(i) for i in range(5)]
        out_back = lax.ppermute(out_halo, "seq", backward)
        grad_back = lax.ppermute(grad_in_halo, "seq", backward)
    ends = last(out, grad_in, out_back, grad_back, results)
    return (ends[0][None], ends[1][None], *ends[2:])


def solution(mesh):
    stream = P("batch", "seq", None)
    rows = P(("batch", "seq"), None)
    vector = P(None, ("batch", "seq"))
    five = (rows, rows, rows, rows, vector)
    return jax.shard_map(
        on_device,
        mesh=mesh,
        in_specs=(stream, stream, P("batch", "seq"), P("batch", "seq")) + five * 3,
        out_specs=(stream, stream) + five * 3 + (P(None, "seq"),) * 5,
        check_vma=False,
    )
```

```python
import functools

import jax
import jax.numpy as jnp
from jax import lax
from jax.experimental import pallas as pl
from jax.experimental.pallas import tpu as pltpu
from jax.sharding import PartitionSpec as P

D = 512
HEADS = 8
HEAD_DIM = 64
FF = 2048
STEP = 10
PAIR = 255
SLOT = 256
HALO = 64
TILES = 4
TAIL = 64
PIECE = TAIL // TILES
TILE = 2 * SLOT + PIECE
ROWS = TILES * TILE
LANES = 8 * SLOT + 128
AUG = 16
MIB = 1 << 20

norm_epsilon = 1e-05
beta_first = 0.9
beta_second = 0.999
adam_epsilon = 1e-08
weight_decay = 0.01
learn_rates = (0.03, 0.2, 0.03, 0.02, 0.5)
big = 1e30

f32 = jnp.float32
bf16 = jnp.bfloat16


def dot(a, b, ca, cb):
    return lax.dot_general(a, b, (((ca,), (cb,)), ((), ())), preferred_element_type=f32)


def adam_update(master, first, second, gradient, rate):
    first_new = beta_first * first + (1.0 - beta_first) * gradient
    second_new = beta_second * second + (1.0 - beta_second) * gradient * gradient
    first_hat = first_new / (1.0 - beta_first**STEP)
    second_hat = second_new / (1.0 - beta_second**STEP)
    master_new = master - rate * (
        first_hat / (jnp.sqrt(second_hat) + adam_epsilon) + weight_decay * master
    )
    return (first_new, second_new, master_new)


def slot_row(j):
    return pl.multiple_of((j // 2) * TILE + (j % 2) * SLOT, 16)


def first_row(j, seq):
    return HALO + PAIR * j - 8 * seq


def staged(ref, start):
    base = pl.multiple_of((start // 16) * 16, 16)
    rest = start - base
    wide = ref[pl.ds(base, SLOT + 16), :].astype(f32)
    wide = jnp.where(rest >= 8, wide[8:], wide[:-8])
    shift = rest % 8
    groups = (SLOT + 8) // 8
    wide = wide.reshape(groups, 8, D)
    turned = pltpu.roll(wide, lax.rem(8 - shift, 8), 1)
    place = lax.broadcasted_iota(jnp.int32, (groups - 1, 8, D), 1)
    block = jnp.where(place < 8 - shift, turned[:-1], turned[1:]).reshape(SLOT, D)
    row = lax.broadcasted_iota(jnp.int32, (SLOT, D), 0)
    return jnp.where(row < PAIR, block, 0.0).astype(bf16)


def unstage(ref, start, block):
    base = pl.multiple_of((start // 8) * 8, 8)
    shift = start - base
    turned = pltpu.roll(block.reshape(SLOT // 8, 8, D), shift, 1)
    place = lax.broadcasted_iota(jnp.int32, (1, 8, D), 1)
    keep = ref[pl.ds(base, 8), :].reshape(1, 8, D)
    low = jnp.concatenate([keep, turned], 0)
    high = jnp.concatenate([turned, turned[-1:]], 0)
    place = lax.broadcasted_iota(jnp.int32, low.shape, 1)
    ref[pl.ds(base, SLOT + 8), :] = jnp.where(place < shift, low, high).reshape(SLOT + 8, D)


def tail_rows(ref, count, is_last):
    kept = ref[HALO + 2048 - count : HALO + 2048, :].astype(f32)
    if count < TAIL:
        kept = jnp.concatenate([kept, jnp.zeros((TAIL - count, D), f32)], 0)
    return jnp.where(is_last, kept, 0.0).astype(bf16)


def tag_rows(tag, pair):
    width = tag.shape[1]
    number = tag // 2 - 2 * pair
    kept = tag % 2
    row = lax.broadcasted_iota(jnp.int32, (AUG, width), 0)
    match = row == number
    query = jnp.where(match, 1.0, 0.0).astype(bf16)
    key = jnp.where(match & (kept == 1), 0.0, -big)
    key = jnp.where(row < 4, key, 0.0).astype(bf16)
    return query, key


def attn_forward_kernel(
    seq_count, tok_ref, cot_ref, tok_halo, cot_halo, seg_ref, keep_ref, seg_halo, keep_halo,
    w_ref, vec_ref,
    xs_ref, es_ref, xt_ref, qt_ref, kt_ref, vt_ref, c_ref, lse_ref,
    wt_ref, x_ref, e_ref, tag_ref, sems,
):
    seq = lax.axis_index("seq")
    is_last = seq == seq_count - 1
    rows = tok_ref.shape[1]
    loads = []
    for i, (whole, halo, ext) in enumerate(((tok_ref, tok_halo, x_ref), (cot_ref, cot_halo, e_ref))):
        loads.append(pltpu.make_async_copy(whole.at[0], ext.at[pl.ds(HALO, rows)], sems.at[2 * i]))
        loads.append(pltpu.make_async_copy(halo, ext.at[pl.ds(0, HALO)], sems.at[2 * i + 1]))
    for load in loads:
        load.start()
    for part in range(3):
        wt_ref[part * D : (part + 1) * D, :] = w_ref[:, part * D : (part + 1) * D].T
    tag_ref[...] = jnp.zeros_like(tag_ref)
    edge = seg_halo[...] * 2 + keep_halo[...]
    tag_ref[:, :HALO] = jnp.broadcast_to(edge[:, 128 - HALO :], (8, HALO))
    tag_ref[:, HALO : HALO + rows] = jnp.broadcast_to(seg_ref[...] * 2 + keep_ref[...], (8, rows))
    query_bias = vec_ref[:, 0:1].astype(f32)
    value_bias = vec_ref[:, 1:2].astype(f32)
    for load in loads:
        load.wait()

    def block(xb, tag, pair, lane, width):
        lanes = pl.ds(lane, width)
        xt_ref[:D, lanes] = xb.T
        q = dot(wt_ref[:D, :], xb, 1, 1) + query_bias
        q = (q.astype(bf16).astype(f32) * HEAD_DIM**-0.5).astype(bf16)
        k = dot(wt_ref[D : 2 * D, :], xb, 1, 1).astype(bf16)
        v = (dot(wt_ref[2 * D :, :], xb, 1, 1) + value_bias).astype(bf16)
        query_tag, key_tag = tag_rows(tag, pair)
        vt_ref[:, lanes] = v
        context = []
        for h in range(HEADS):
            rows = slice(h * HEAD_DIM, (h + 1) * HEAD_DIM)
            qh = jnp.concatenate([q[rows], query_tag], 0)
            kh = jnp.concatenate([k[rows], key_tag], 0)
            qt_ref[h, :, lanes] = qh
            kt_ref[h, :, lanes] = kh
            s = dot(kh, qh, 0, 0)
            top = jnp.max(s, axis=0, keepdims=True)
            ex = jnp.exp(s - top)
            total = jnp.sum(ex, axis=0, keepdims=True)
            lse_ref[h : h + 1, lanes] = top + jnp.log(total)
            a = (ex * (1.0 / total)).astype(bf16)
            context.append(dot(v[rows], a, 1, 0))
        return jnp.concatenate(context, 0).astype(bf16).T

    def one(j, carry):
        start = first_row(j, seq)
        row = slot_row(j)
        xb = staged(x_ref, start)
        xs_ref[pl.ds(row, SLOT), :] = xb
        es_ref[pl.ds(row, SLOT), :] = staged(e_ref, start)
        wide = tag_ref[:, pl.ds(pl.multiple_of(j * SLOT, 128), SLOT + 128)]
        width = SLOT + 128
        tag = pltpu.roll(wide, width - (start - j * SLOT), 1)[:1, :SLOT]
        c_ref[pl.ds(row, SLOT), :] = block(
            xb, tag, 8 * seq + j, pl.multiple_of(j * SLOT, 128), SLOT
        )
        return carry

    lax.fori_loop(0, 8, one, 0)
    count = 8 * seq_count
    xt_ref[:, 8 * SLOT :] = jnp.zeros((D + AUG, 128), bf16)
    xb = tail_rows(x_ref, count, is_last)
    eb = tail_rows(e_ref, count, is_last)
    tag = tag_ref[:1, 2048:2176]
    tag = pltpu.roll(tag_ref[:, 2048:2176], 128 - (64 - count), 1)[:1, :TAIL] if count < 64 else tag[:, :TAIL]
    place = lax.broadcasted_iota(jnp.int32, (1, TAIL), 1)
    tag = jnp.where(place < count, tag, (2 * 8 * seq_count + 3) * 2)
    cb = block(xb, tag, 8 * seq_count, 8 * SLOT, TAIL)
    for t in range(TILES):
        rows = slice(t * PIECE, (t + 1) * PIECE)
        at = slice(t * TILE + 2 * SLOT, (t + 1) * TILE)
        xs_ref[at, :] = xb[rows]
        es_ref[at, :] = eb[rows]
        c_ref[at, :] = cb[rows]
    ones = lax.broadcasted_iota(jnp.int32, (AUG, LANES), 0) == 0
    xt_ref[D:, :] = jnp.where(ones, 1.0, 0.0).astype(bf16)


def attn_forward(seq_count, tokens, cotangent, *others):
    shape = jax.ShapeDtypeStruct
    vmem = pl.BlockSpec(memory_space=pltpu.VMEM)
    hbm = pl.BlockSpec(memory_space=pl.ANY)
    return pl.pallas_call(
        functools.partial(attn_forward_kernel, seq_count),
        out_shape=(
            shape((ROWS, D), bf16),
            shape((ROWS, D), bf16),
            shape((D + AUG, LANES), bf16),
            shape((HEADS, HEAD_DIM + AUG, LANES), bf16),
            shape((HEADS, HEAD_DIM + AUG, LANES), bf16),
            shape((D, LANES), bf16),
            shape((ROWS, D), bf16),
            shape((HEADS, LANES), f32),
        ),
        in_specs=[hbm, hbm] + [vmem] * len(others),
        out_specs=[vmem] * 8,
        scratch_shapes=[
            pltpu.VMEM((3 * D, D), bf16),
            pltpu.VMEM((HALO + tokens.shape[1], D), bf16),
            pltpu.VMEM((HALO + tokens.shape[1], D), bf16),
            pltpu.VMEM((8, LANES), jnp.int32),
            pltpu.SemaphoreType.DMA((4,)),
        ],
        compiler_params=pltpu.CompilerParams(vmem_limit_bytes=56 * MIB),
        name="attn_forward",
    )(tokens, cotangent, *others)


def feed_kernel(
    xs_ref, c_ref, es_ref, wo_ref, w1_ref, w2_ref, vect_ref,
    z_ref, dh_ref, dr_ref, gwo_ref, gw1_ref, gw2_ref, gvec_ref, gb1_ref,
    u_ref, g_ref, awo_ref, aw1_ref, aw2_ref, vec_ref,
):
    step = pl.program_id(0)

    @pl.when(step == 0)
    def _():
        awo_ref[...] = jnp.zeros_like(awo_ref)
        aw1_ref[...] = jnp.zeros_like(aw1_ref)
        aw2_ref[...] = jnp.zeros_like(aw2_ref)
        gvec_ref[...] = jnp.zeros_like(gvec_ref)
        gb1_ref[...] = jnp.zeros_like(gb1_ref)
        vec_ref[...] = vect_ref[...].astype(f32).T

    def mean(v):
        return jnp.mean(v, axis=-1, keepdims=True)

    def row_sum(v):
        return jnp.sum(v, axis=0, keepdims=True)

    bo, b2, g1, c1, g2, c2 = (vec_ref[i : i + 1, :] for i in range(2, 8))
    h1 = xs_ref[...].astype(f32) + (dot(c_ref[...], wo_ref[...], 1, 0) + bo)
    mid = h1 - mean(h1)
    inv1 = lax.rsqrt(mean(mid * mid) + norm_epsilon)
    n1 = mid * inv1
    y = n1 * g1 + c1
    yb = y.astype(bf16)
    chunk = D
    f = None
    for k in range(FF // chunk):
        cols = slice(k * chunk, (k + 1) * chunk)
        u = dot(yb, w1_ref[:, cols], 1, 0) + vec_ref[8 + k : 9 + k, :]
        cdf = 0.5 * (1.0 + lax.erf(u * 0.7071067811865476))
        gk = (u * cdf).astype(bf16)
        u_ref[:, cols] = cdf + u * jnp.exp(u * u * -0.5) * 0.3989422804014327
        g_ref[:, cols] = gk
        part = dot(gk, w2_ref[cols, :], 1, 0)
        f = part if f is None else f + part
    h2 = y + (f + b2)
    mid2 = h2 - mean(h2)
    inv2 = lax.rsqrt(mean(mid2 * mid2) + norm_epsilon)
    n2 = mid2 * inv2
    z_ref[...] = (n2 * g2 + c2).astype(bf16)
    e = es_ref[...].astype(f32)
    gvec_ref[7:8, :] += row_sum(e)
    gvec_ref[6:7, :] += row_sum(e * n2)
    eg = e * g2
    dh2 = (eg - mean(eg) - n2 * mean(eg * n2)) * inv2
    df = dh2.astype(bf16)
    gvec_ref[3:4, :] += row_sum(df.astype(f32))
    dft = df.T
    ybt = yb.T
    dy = dh2
    for k in range(FF // chunk):
        cols = slice(k * chunk, (k + 1) * chunk)
        aw2_ref[:, cols] += dot(dft, g_ref[:, cols], 1, 0)
        dg = dot(df, w2_ref[cols, :], 1, 1)
        du = (dg * u_ref[:, cols]).astype(bf16)
        gb1_ref[:1, cols] += row_sum(du.astype(f32))
        aw1_ref[:, cols] += dot(ybt, du, 1, 0)
        dy = dy + dot(du, w1_ref[:, cols], 1, 1)
    gvec_ref[5:6, :] += row_sum(dy)
    gvec_ref[4:5, :] += row_sum(dy * n1)
    eg = dy * g1
    dh1 = (eg - mean(eg) - n1 * mean(eg * n1)) * inv1
    dh_ref[...] = dh1
    dr = dh1.astype(bf16)
    dr_ref[...] = dr
    gvec_ref[2:3, :] += row_sum(dr.astype(f32))
    awo_ref[...] += dot(c_ref[...].T, dr, 1, 0)

    @pl.when(step == TILES - 1)
    def _():
        gwo_ref[...] = awo_ref[...].astype(bf16)
        gw1_ref[...] = aw1_ref[...].astype(bf16)
        for k in range(FF // chunk):
            cols = slice(k * chunk, (k + 1) * chunk)
            gw2_ref[cols, :] = aw2_ref[:, cols].astype(bf16).T


def feed(xs, c, es, wo, w1, w2, vec_t):
    shape = jax.ShapeDtypeStruct
    tile = pl.BlockSpec((TILE, D), lambda i: (i, 0))

    def whole(*dims):
        return pl.BlockSpec(dims, lambda i: (0,) * len(dims), pipeline_mode=pl.Buffered(1))

    return pl.pallas_call(
        feed_kernel,
        grid=(TILES,),
        out_shape=(
            shape((ROWS, D), bf16),
            shape((ROWS, D), f32),
            shape((ROWS, D), bf16),
            shape((D, D), bf16),
            shape((D, FF), bf16),
            shape((FF, D), bf16),
            shape((8, D), f32),
            shape((8, FF), f32),
        ),
        in_specs=[tile, tile, tile, whole(D, D), whole(D, FF), whole(FF, D), whole(D, 128)],
        out_specs=[tile, tile, tile, whole(D, D), whole(D, FF), whole(FF, D), whole(8, D), whole(8, FF)],
        scratch_shapes=[
            pltpu.VMEM((TILE, FF), f32),
            pltpu.VMEM((TILE, FF), bf16),
            pltpu.VMEM((D, D), f32),
            pltpu.VMEM((D, FF), f32),
            pltpu.VMEM((D, FF), f32),
            pltpu.VMEM((128, D), f32),
        ],
        compiler_params=pltpu.CompilerParams(vmem_limit_bytes=60 * MIB),
        name="feed",
    )(xs, c, es, wo, w1, w2, vec_t)


def attn_backward_kernel(
    seq_count, xt_ref, qt_ref, kt_ref, vt_ref, lse_ref, dr_ref, dh_ref, z_ref, w_ref, wo_ref,
    out_ref, out_halo_ref, in_ref, in_halo_ref, gwa_ref, gbias_ref,
    dpt_ref, ext_ref,
):
    seq = lax.axis_index("seq")
    is_last = seq == seq_count - 1

    def block(dr, lane, width):
        lanes = pl.ds(lane, width)
        dct = dot(wo_ref[...], dr, 1, 1).astype(bf16)
        for h in range(HEADS):
            rows = slice(h * HEAD_DIM, (h + 1) * HEAD_DIM)
            qh = qt_ref[h, :, lanes]
            kh = kt_ref[h, :, lanes]
            vh = vt_ref[rows, lanes]
            dch = dct[rows]
            a = jnp.exp(dot(kh, qh, 0, 0) - lse_ref[h : h + 1, lanes])
            da = dot(vh, dch, 0, 0)
            ada = a * da
            ds = (ada - a * jnp.sum(ada, axis=0, keepdims=True)).astype(bf16)
            dv = dot(dch, a.astype(bf16), 1, 1)
            dk = dot(qh[:HEAD_DIM], ds, 1, 1)
            dq = dot(kh[:HEAD_DIM], ds, 1, 0) * HEAD_DIM**-0.5
            dpt_ref[rows, lanes] = dq.astype(bf16)
            dpt_ref[slice(D + h * HEAD_DIM, D + (h + 1) * HEAD_DIM), lanes] = dk.astype(bf16)
            dpt_ref[slice(2 * D + h * HEAD_DIM, 2 * D + (h + 1) * HEAD_DIM), lanes] = dv.astype(bf16)
        return dot(w_ref[...], dpt_ref[:, lanes], 1, 0).T

    dpt_ref[:, 8 * SLOT :] = jnp.zeros((3 * D, 128), bf16)

    def one(j, carry):
        row = slot_row(j)
        grad = block(dr_ref[pl.ds(row, SLOT), :], pl.multiple_of(j * SLOT, 128), SLOT)
        unstage(ext_ref, first_row(j, seq), grad + dh_ref[pl.ds(row, SLOT), :])
        return carry

    lax.fori_loop(0, 8, one, 0)
    count = 8 * seq_count

    def tail_of(ref):
        return jnp.concatenate(
            [ref[t * TILE + 2 * SLOT : (t + 1) * TILE, :] for t in range(TILES)], 0
        )

    grad = block(tail_of(dr_ref), 8 * SLOT, TAIL) + tail_of(dh_ref)

    @pl.when(is_last)
    def _():
        ext_ref[HALO + 2048 - count : HALO + 2048, :] = grad[:count]

    in_halo_ref[...] = ext_ref[:HALO, :]
    in_ref[...] = ext_ref[HALO : HALO + 2048, :]

    def two(j, carry):
        unstage(ext_ref, first_row(j, seq), z_ref[pl.ds(slot_row(j), SLOT), :].astype(f32))
        return carry

    lax.fori_loop(0, 8, two, 0)
    tail = tail_of(z_ref).astype(f32)

    @pl.when(is_last)
    def _():
        ext_ref[HALO + 2048 - count : HALO + 2048, :] = tail[:count]

    out_halo_ref[...] = ext_ref[:HALO, :].astype(bf16)
    out_ref[...] = ext_ref[HALO : HALO + 2048, :].astype(bf16)
    for part in range(3):
        cols = slice(part * D, (part + 1) * D)
        g = dot(xt_ref[...], dpt_ref[cols, :], 1, 1)
        gwa_ref[:, cols] = g[:D].astype(bf16)
        gbias_ref[:, cols] = g[D : D + 8]


def attn_backward(seq_count, *operands):
    shape = jax.ShapeDtypeStruct
    return pl.pallas_call(
        functools.partial(attn_backward_kernel, seq_count),
        out_shape=(
            shape((2048, D), bf16),
            shape((HALO, D), bf16),
            shape((2048, D), f32),
            shape((HALO, D), f32),
            shape((D, 3 * D), bf16),
            shape((8, 3 * D), f32),
        ),
        in_specs=[pl.BlockSpec(memory_space=pltpu.VMEM)] * len(operands),
        out_specs=[pl.BlockSpec(memory_space=pltpu.VMEM)] * 6,
        scratch_shapes=[
            pltpu.VMEM((3 * D, LANES), bf16),
            pltpu.VMEM((HALO + 2048 + 16, D), f32),
        ],
        compiler_params=pltpu.CompilerParams(vmem_limit_bytes=60 * MIB),
        name="attn_backward",
    )(*operands)


MESH = pl.DeviceIdType.MESH
PLANE = 4
DEPTH = 4


class Place:
    def __init__(self):
        self.batch = lax.axis_index("batch")
        self.z = lax.axis_index("seq")
        self.core = self.batch % 2
        self.plane = self.batch // 2

    def plane_at(self, k):
        x = (self.plane % 2 + k % 2) % 2
        y = (self.plane // 2 + k // 2) % 2
        return y * 2 + x

    def in_plane(self, k):
        return {"batch": self.plane_at(k) * 2 + self.core, "seq": self.z}

    def depth_at(self, k):
        return (self.z + k) % DEPTH

    def in_depth(self, k):
        return {"batch": self.batch, "seq": self.depth_at(k)}

    def sibling(self):
        return {"batch": self.plane * 2 + 1 - self.core, "seq": self.z}

    def greet(self):
        barrier = pltpu.get_barrier_semaphore()
        for k in range(1, 4):
            pl.semaphore_signal(barrier, inc=1, device_id=self.in_plane(k), device_id_type=MESH)
            pl.semaphore_signal(barrier, inc=1, device_id=self.in_depth(k), device_id_type=MESH)
        pl.semaphore_signal(barrier, inc=1, device_id=self.sibling(), device_id_type=MESH)
        pl.semaphore_wait(barrier, 7)


def remote(src, dst, send, recv, device):
    return pltpu.make_async_remote_copy(
        src_ref=src, dst_ref=dst, send_sem=send, recv_sem=recv, device_id=device, device_id_type=MESH
    )


class Gather:
    def __init__(self, place, whole, send, recv, parts=None):
        self.place, self.whole, self.send, self.recv, self.parts = place, whole, send, recv, parts

    def depth(self, k):
        at = self.place
        here = self.whole.at[at.batch, at.z]
        source = here if self.parts is None else self.parts.at[at.depth_at(k)]
        return remote(source, here, self.send.at[k - 1], self.recv.at[k - 1], at.in_depth(k))

    def plane(self, k):
        block = self.whole.at[self.place.batch]
        return remote(block, block, self.send.at[2 + k], self.recv.at[2 + k], self.place.in_plane(k))

    def core(self, k):
        block = self.whole.at[self.place.plane_at(k) * 2 + self.place.core]
        return remote(block, block, self.send.at[6 + k], self.recv.at[6 + k], self.place.sibling())

    def first(self):
        for k in range(1, 4):
            self.depth(k).start()

    def second(self):
        for k in range(1, 4):
            self.depth(k).wait_recv()
        for k in range(1, 4):
            self.plane(k).start()
        self.core(0).start()

    def third(self):
        for k in range(1, 4):
            self.plane(k).wait_recv()
            self.core(k).start()

    def finish(self):
        for k in range(4):
            self.core(k).wait_recv()
        for k in range(1, 4):
            self.depth(k).wait_send()
            self.plane(k).wait_send()
        for k in range(4):
            self.core(k).wait_send()


class Scatter:
    def __init__(self, place, grad, twin, across, along, send, recv):
        self.place, self.grad, self.twin = place, grad, twin
        self.across, self.along, self.send, self.recv = across, along, send, recv
        shape = grad.shape
        if len(shape) == 4:
            self.at = lambda p, c: grad.at[p * 2 + c]
        else:
            self.at = lambda p, c: grad.at[p, c]

    def core(self, p):
        return remote(
            self.at(p, 1 - self.place.core), self.twin.at[p], self.send.at[p], self.recv.at[p],
            self.place.sibling(),
        )

    def plane(self, k):
        return remote(
            self.at(self.place.plane_at(k), self.place.core), self.across.at[k - 1],
            self.send.at[3 + k], self.recv.at[3 + k], self.place.in_plane(k),
        )

    def depth(self, k):
        return remote(
            self.at(self.place.plane, self.place.core).at[self.place.depth_at(k)],
            self.along.at[k - 1], self.send.at[6 + k], self.recv.at[6 + k], self.place.in_depth(k),
        )

    def first(self):
        for p in range(PLANE):
            self.core(p).start()

    def second(self):
        for p in range(PLANE):
            self.core(p).wait_recv()
        own = self.place.core

        def one(p, carry):
            mine = self.at(p, own)
            mine[...] = (mine[...].astype(f32) + self.twin[p].astype(f32)).astype(mine.dtype)
            return carry

        lax.fori_loop(0, PLANE, one, 0)
        for k in range(1, 4):
            self.plane(k).start()

    def third(self):
        for k in range(1, 4):
            self.plane(k).wait_recv()
        mine = self.at(self.place.plane, self.place.core)

        def one(q, carry):
            total = mine[q].astype(f32)
            for k in range(3):
                total = total + self.across[k, q].astype(f32)
            mine[q] = total.astype(mine.dtype)
            return carry

        lax.fori_loop(0, DEPTH, one, 0)
        for k in range(1, 4):
            self.depth(k).start()

    def total(self):
        for k in range(1, 4):
            self.depth(k).wait_recv()
        total = self.at(self.place.plane, self.place.core)[self.place.z].astype(f32)
        for k in range(3):
            total = total + self.along[k].astype(f32)
        return total

    def finish(self):
        for p in range(PLANE):
            self.core(p).wait_send()
        for k in range(1, 4):
            self.plane(k).wait_send()
            self.depth(k).wait_send()


def turned(ref, value):
    ref[...] = jnp.zeros_like(ref)
    ref[: value.shape[0], : value.shape[1]] = value
    return ref[...].T


def heads_of(block, h):
    return block[h * HEAD_DIM : (h + 1) * HEAD_DIM]


def only_head(block, h):
    zero = jnp.zeros((HEAD_DIM, block.shape[1]), block.dtype)
    mine = heads_of(block, h)
    return jnp.concatenate([mine, zero] if h % 2 == 0 else [zero, mine], 0)


def pair_of(block, h):
    at = h // 2 * 2 * HEAD_DIM
    return block[:, at : at + 2 * HEAD_DIM]


def mask_parts(tag, pair):
    query, key = tag_rows(tag, pair)
    width = tag.shape[1]
    zero = jnp.zeros((128 - AUG, width), bf16)
    return jnp.concatenate([key, zero], 0).T, jnp.concatenate([query, zero], 0)


class Slots:
    def __init__(self, tag_ref, seq, seq_count):
        self.tag_ref, self.seq, self.count = tag_ref, seq, 8 * seq_count
        self.last_pair = 8 * seq_count

    def tag(self, j):
        wide = self.tag_ref[:, pl.ds(pl.multiple_of(j * SLOT, 128), SLOT + 128)]
        offset = HALO - 8 * self.seq - j
        return pltpu.roll(wide, SLOT + 128 - offset, 1)[:1, :SLOT]

    def tail_tag(self):
        tag = self.tag_ref[:, 2048:2176]
        if self.count < TAIL:
            tag = pltpu.roll(tag, 128 - (TAIL - self.count), 1)
        place = lax.broadcasted_iota(jnp.int32, (1, TAIL), 1)
        return jnp.where(place < self.count, tag[:1, :TAIL], 2 * (2 * self.last_pair + 3))

    def tail(self, ref):
        return jnp.concatenate(
            [ref[t * TILE + 2 * SLOT : (t + 1) * TILE, :] for t in range(TILES)], 0
        )

    def set_tail(self, ref, value):
        for t in range(TILES):
            ref[t * TILE + 2 * SLOT : (t + 1) * TILE, :] = value[t * PIECE : (t + 1) * PIECE]


def forward_block(xb, tag, pair, lanes, wt_ref, biases, xt_ref, qt_ref, kt_ref, vt_ref, lse_ref, s_ref, a_ref):
    width = xb.shape[0]
    xt_ref[:D, lanes] = xb.T
    q = dot(wt_ref[:D, :], xb, 1, 1) + biases[0]
    q = (q.astype(bf16).astype(f32) * HEAD_DIM**-0.5).astype(bf16)
    k = dot(wt_ref[D : 2 * D, :], xb, 1, 1).astype(bf16)
    v = (dot(wt_ref[2 * D :, :], xb, 1, 1) + biases[1]).astype(bf16)
    qt_ref[:, lanes] = q
    kt_ref[:, lanes] = k
    vt_ref[:, lanes] = v
    key_mask, query_mask = mask_parts(tag, pair)
    kn = k.T
    for h in range(HEADS):
        left = jnp.concatenate([pair_of(kn, h), key_mask], 1)
        right = jnp.concatenate([only_head(q, h), query_mask], 0)
        s_ref[h, :width, :width] = dot(left, right, 1, 0)
    for h in range(HEADS):
        s = s_ref[h, :width, :width]
        top = jnp.max(s, axis=0, keepdims=True)
        ex = jnp.exp(s - top)
        total = jnp.sum(ex, axis=0, keepdims=True)
        lse_ref[h : h + 1, lanes] = top + jnp.log(total)
        a_ref[h, :width, :width] = (ex * (1.0 / total)).astype(bf16)
    context = [
        dot(heads_of(v, h), a_ref[h, :width, :width], 1, 0).astype(bf16) for h in range(HEADS)
    ]
    return jnp.concatenate(context, 0).T


def backward_block(dr, c, tag, pair, lanes, wo, qt_ref, kt_ref, vt_ref, lse_ref, dpt_ref, a_ref, ds_ref):
    width = dr.shape[0]
    dct32 = dot(wo, dr, 1, 1)
    dct = dct32.astype(bf16)
    product = c.T.astype(f32) * dct.astype(f32)
    q = qt_ref[:, lanes]
    k = kt_ref[:, lanes]
    kn = k.T
    vn = vt_ref[:, lanes].T
    key_mask, query_mask = mask_parts(tag, pair)
    for h in range(HEADS):
        left = jnp.concatenate([pair_of(kn, h), key_mask], 1)
        right = jnp.concatenate([only_head(q, h), query_mask], 0)
        delta = jnp.sum(heads_of(product, h), axis=0, keepdims=True)
        a = jnp.exp(dot(left, right, 1, 0) - lse_ref[h : h + 1, lanes])
        da = dot(pair_of(vn, h), only_head(dct, h), 1, 0)
        a_ref[h, :width, :width] = a.astype(bf16)
        ds_ref[h, :width, :width] = (a * (da - delta)).astype(bf16)
    for h in range(HEADS):
        rows = slice(h * HEAD_DIM, (h + 1) * HEAD_DIM)
        ds = ds_ref[h, :width, :width]
        dv = dot(dct[rows], a_ref[h, :width, :width], 1, 1)
        dk = dot(q[rows], ds, 1, 1)
        dq = dot(k[rows], ds, 1, 0) * HEAD_DIM**-0.5
        dpt_ref[rows, lanes] = dq.astype(bf16)
        dpt_ref[slice(D + h * HEAD_DIM, D + (h + 1) * HEAD_DIM), lanes] = dk.astype(bf16)
        dpt_ref[slice(2 * D + h * HEAD_DIM, 2 * D + (h + 1) * HEAD_DIM), lanes] = dv.astype(bf16)


def mean(v):
    return jnp.mean(v, axis=-1, keepdims=True)


def row_sum(v):
    return jnp.sum(v, axis=0, keepdims=True)


def flat(value):
    return value.reshape(-1, value.shape[-1])


def feed_tile(
    rows, xs_ref, c_ref, es_ref, wo_ref, w1_ref, w2_ref, vec_ref, dh_ref, gvec_ref,
    u_ref, g_ref, awo_ref, aw1_ref, aw2_ref,
):
    bo, b2, g1, c1, g2, c2 = (vec_ref[i : i + 1, :] for i in range(2, 8))
    c = c_ref[rows, :]
    h1 = xs_ref[rows, :].astype(f32) + (dot(c, flat(wo_ref[...]), 1, 0) + bo)
    mid = h1 - mean(h1)
    inv1 = lax.rsqrt(mean(mid * mid) + norm_epsilon)
    n1 = mid * inv1
    y = n1 * g1 + c1
    yb = y.astype(bf16)
    per = FF // D

    def cols_of(k):
        return pl.ds(pl.multiple_of(k * D, 128), D)

    def w2_part(k):
        return flat(w2_ref[pl.ds(8 // per * k, 8 // per)])

    def w1_part(k):
        return flat(w1_ref[:, :, :, cols_of(k)])

    def chunk(k):
        return pl.ds(pl.multiple_of(k * TILE, 16), TILE)

    def inner(k, carry):
        u = dot(yb, w1_part(k), 1, 0) + vec_ref[pl.ds(8 + k, 1), :]
        cdf = 0.5 * (1.0 + lax.erf(u * 0.7071067811865476))
        g_ref[chunk(k), :] = (u * cdf).astype(bf16)
        u_ref[chunk(k), :] = cdf + u * jnp.exp(u * u * -0.5) * 0.3989422804014327
        return carry

    lax.fori_loop(0, per, inner, 0)
    f = None
    for k in range(per):
        part = dot(g_ref[chunk(k), :], w2_part(k), 1, 0)
        f = part if f is None else f + part
    h2 = y + (f + b2)
    mid2 = h2 - mean(h2)
    inv2 = lax.rsqrt(mean(mid2 * mid2) + norm_epsilon)
    n2 = mid2 * inv2
    xs_ref[rows, :] = (n2 * g2 + c2).astype(bf16)
    e = es_ref[rows, :].astype(f32)
    gvec_ref[7:8, :] += row_sum(e)
    gvec_ref[6:7, :] += row_sum(e * n2)
    eg = e * g2
    dh2 = (eg - mean(eg) - n2 * mean(eg * n2)) * inv2
    df = dh2.astype(bf16)
    gvec_ref[3:4, :] += row_sum(df.astype(f32))
    dft = df.T
    ybt = yb.T

    def outer(k, carry):
        cols = cols_of(k)
        aw2_ref[:, cols] += dot(dft, g_ref[chunk(k), :], 1, 0)
        dg = dot(df, w2_part(k), 1, 1)
        du = (dg * u_ref[chunk(k), :]).astype(bf16)
        gvec_ref[pl.ds(8 + k, 1), :] += row_sum(du.astype(f32))
        aw1_ref[:, cols] += dot(ybt, du, 1, 0)
        g_ref[chunk(k), :] = du
        return carry

    lax.fori_loop(0, per, outer, 0)
    dy = dh2
    for k in range(per):
        dy = dy + dot(g_ref[chunk(k), :], w1_part(k), 1, 1)
    gvec_ref[5:6, :] += row_sum(dy)
    gvec_ref[4:5, :] += row_sum(dy * n1)
    eg = dy * g1
    dh1 = (eg - mean(eg) - n1 * mean(eg * n1)) * inv1
    dh_ref[rows, :] = dh1
    dr = dh1.astype(bf16)
    es_ref[rows, :] = dr
    gvec_ref[2:3, :] += row_sum(dr.astype(f32))
    awo_ref[...] += dot(c.T, dr, 1, 0)


def whole_kernel(*refs):
    refs = list(refs)

    def take(count):
        taken = refs[:count]
        del refs[:count]
        return taken

    state_in = take(15)
    tok_ref, cot_ref, seg_ref, keep_ref = take(4)
    out_ref, in_ref = take(2)
    state_out = take(15)
    copy_out = take(5)
    out_back, in_back = take(2)
    state = take(15)
    masters, firsts, seconds = state[:5], state[5:10], state[10:]
    weights = take(5)
    wa_ref, wo_ref, w1_ref, w2_ref, wv_ref = weights
    xs_ref, es_ref, xt_ref, qt_ref, kt_ref, vt_ref, c_ref, lse_ref, dh_ref, tag_ref = take(10)
    ext_x, ext_e, seg_halo, keep_halo = take(4)
    square, gvec_ref, gwa_ref, gwo_ref, grad_vec, halo_out, halo_in = take(7)
    twins, acrosses, alongs = take(5), take(5), take(5)
    parts, copies, whole_vec = take(4), take(5), take(1)[0]
    (
        state_sems, load_sems, gather_send, gather_recv, edge_send, edge_recv,
        sum_send, sum_recv, copy_send, copy_recv, store_sems,
    ) = refs
    place = Place()
    seq, seq_count = place.z, DEPTH
    is_last = seq == seq_count - 1
    slots = Slots(tag_ref, seq, seq_count)
    rows = tok_ref.shape[1]

    loads = [pltpu.make_async_copy(state_in[i], state[i], state_sems.at[i]) for i in range(15)]
    for load in loads:
        load.start()
    big_loads = [
        pltpu.make_async_copy(src.at[0], dst.at[pl.ds(HALO, rows)], load_sems.at[i])
        for i, (src, dst) in enumerate(((tok_ref, ext_x), (cot_ref, ext_e)))
    ]
    for load in big_loads:
        load.start()
    place.greet()
    edge = [
        remote(src, dst, edge_send.at[i], edge_recv.at[i], place.in_depth(1))
        for i, (src, dst) in enumerate((
            (tok_ref.at[0, pl.ds(rows - HALO, HALO)], ext_x.at[pl.ds(0, HALO)]),
            (cot_ref.at[0, pl.ds(rows - HALO, HALO)], ext_e.at[pl.ds(0, HALO)]),
            (seg_ref.at[:, pl.ds(rows - 128, 128)], seg_halo),
            (keep_ref.at[:, pl.ds(rows - 128, 128)], keep_halo),
        ))
    ]
    gathers = [Gather(place, weights[i], gather_send.at[i], gather_recv.at[i]) for i in range(5)]

    def put(i):
        shard = turned(square, masters[4][...])[: masters[4].shape[1]] if i == 4 else masters[i][...]
        weights[i][place.batch, place.z] = shard.astype(bf16)

    for i in (0, 4, 1, 2, 3):
        loads[i].wait()
    put(0)
    gathers[0].first()
    put(4)
    gathers[4].first()
    for copy in edge:
        copy.start()
    for i in (1, 2, 3):
        put(i)
    gathers[0].second()
    gathers[4].second()
    for i in (1, 2, 3):
        gathers[i].first()
    for load in big_loads:
        load.wait()
    for copy in edge:
        copy.wait()
    tag_ref[...] = jnp.zeros_like(tag_ref)
    rim = seg_halo[...] * 2 + keep_halo[...]
    tag_ref[:, :HALO] = jnp.broadcast_to(rim[:, 128 - HALO :], (8, HALO))
    tag_ref[:, HALO : HALO + rows] = jnp.broadcast_to(seg_ref[...] * 2 + keep_ref[...], (8, rows))

    def stage_one(j, carry):
        start = first_row(j, seq)
        row = slot_row(j)
        xs_ref[pl.ds(row, SLOT), :] = staged(ext_x, start)
        es_ref[pl.ds(row, SLOT), :] = staged(ext_e, start)
        return carry

    lax.fori_loop(0, 8, stage_one, 0)
    slots.set_tail(xs_ref, tail_rows(ext_x, slots.count, is_last))
    slots.set_tail(es_ref, tail_rows(ext_e, slots.count, is_last))
    gathers[0].third()
    gathers[4].third()
    xt_ref[:, 8 * SLOT :] = jnp.zeros((D + AUG, 128), bf16)
    ones = lax.broadcasted_iota(jnp.int32, (AUG, LANES), 0) == 0
    xt_ref[D:, :] = jnp.where(ones, 1.0, 0.0).astype(bf16)
    gathers[0].finish()
    gathers[4].finish()

    def forward(wt_ref, s_ref, a_ref):
        for part in range(3):
            wt_ref[part * D : (part + 1) * D, :] = flat(
                wa_ref[:, :, :, part * D : (part + 1) * D]
            ).T
        vec_t = flat(wv_ref[...])
        biases = (vec_t[:, 0:1].astype(f32), vec_t[:, 1:2].astype(f32))

        def block(xb, tag, pair, lanes):
            return forward_block(
                xb, tag, pair, lanes, wt_ref, biases, xt_ref, qt_ref, kt_ref, vt_ref, lse_ref,
                s_ref, a_ref,
            )

        def one(j, carry):
            for i, step in ((1, 1), (2, 2), (3, 3)):
                pl.when(j == step)(gathers[i].second)
            for i, step in ((1, 4), (2, 5), (3, 7)):
                pl.when(j == step)(gathers[i].third)
            row = slot_row(j)
            lanes = pl.ds(pl.multiple_of(j * SLOT, 128), SLOT)
            c_ref[pl.ds(row, SLOT), :] = block(
                xs_ref[pl.ds(row, SLOT), :], slots.tag(j), 8 * seq + j, lanes
            )
            return carry

        lax.fori_loop(0, 8, one, 0)
        slots.set_tail(
            c_ref,
            block(
                slots.tail(xs_ref), slots.tail_tag(), slots.last_pair, pl.ds(8 * SLOT, TAIL)
            ),
        )

    pl.run_scoped(
        forward,
        pltpu.VMEM((3 * D, D), bf16),
        pltpu.VMEM((HEADS, SLOT, SLOT), f32),
        pltpu.VMEM((HEADS, SLOT, SLOT), bf16),
    )
    for i in (1, 2, 3):
        gathers[i].finish()

    def feed_all(vec_ref, u_ref, awo_ref, aw1_ref, aw2_ref):
        g_ref = ext_x
        for ref in (awo_ref, aw1_ref, aw2_ref, gvec_ref):
            ref[...] = jnp.zeros_like(ref)
        vec_ref[...] = flat(wv_ref[...]).astype(f32).T

        def one(t, carry):
            feed_tile(
                pl.ds(pl.multiple_of(t * TILE, 16), TILE), xs_ref, c_ref, es_ref, wo_ref, w1_ref,
                w2_ref, vec_ref, dh_ref, gvec_ref, u_ref, g_ref, awo_ref, aw1_ref, aw2_ref,
            )
            return carry

        lax.fori_loop(0, TILES, one, 0)
        for k in range(FF // D):
            value = aw2_ref[:, k * D : (k + 1) * D].astype(bf16).T
            w2_ref[2 * k : 2 * k + 2] = value.reshape(2, DEPTH, -1, D)
        for k in range(FF // D):
            cols = slice(k * D, (k + 1) * D)
            w1_ref[:, :, :, cols] = aw1_ref[:, cols].astype(bf16).reshape(8, DEPTH, -1, D)
        gwo_ref[...] = awo_ref[...].astype(bf16).reshape(gwo_ref.shape)

    pl.run_scoped(
        feed_all,
        pltpu.VMEM((128, D), f32),
        pltpu.VMEM((FF // D * TILE, D), f32),
        pltpu.VMEM((D, D), f32),
        pltpu.VMEM((D, FF), f32),
        pltpu.VMEM((D, FF), f32),
    )
    grads = [gwa_ref, gwo_ref, w1_ref, w2_ref, grad_vec]
    scatters = [
        Scatter(place, grads[i], twins[i], acrosses[i], alongs[i], sum_send.at[i], sum_recv.at[i])
        for i in range(5)
    ]
    for i in (3, 2, 1):
        scatters[i].first()
    for load in loads[5:]:
        load.wait()
    copy_gathers = [
        Gather(place, copies[i], copy_send.at[i], copy_recv.at[i], parts[i]) for i in range(4)
    ]
    copy_gathers.append(Gather(place, whole_vec, copy_send.at[4], copy_recv.at[4]))
    stores = []

    def store(src, dst):
        stores.append(pltpu.make_async_copy(src, dst, store_sems.at[len(stores)]))
        stores[-1].start()

    def update(i):
        total = scatters[i].total()
        if i == 4:
            square[...] = jnp.zeros_like(square)
            square[: total.shape[0], :] = total
            here, cols = masters[4].shape
            total = square[...].T[:here, :cols]
        new = adam_update(masters[i][...], firsts[i][...], seconds[i][...], total, learn_rates[i])
        firsts[i][...], seconds[i][...], masters[i][...] = new
        if i == 4:
            shard = turned(square, new[2])[: new[2].shape[1]].astype(bf16)
            whole_vec[place.batch, place.z] = shard
        else:
            low = new[2].astype(bf16)
            width = low.shape[1] // DEPTH
            for q in range(DEPTH):
                parts[i][q] = low[:, q * width : (q + 1) * width]
            copies[i][place.batch, place.z] = parts[i][place.z]
        copy_gathers[i].first()

    def backward(dpt_ref, ext_ref, a_ref, ds_ref):
        low_ref = ext_e
        dpt_ref[:, 8 * SLOT :] = jnp.zeros((3 * D, 128), bf16)
        wo = flat(wo_ref[...])

        def block(dr, c, tag, pair, lanes):
            backward_block(
                dr, c, tag, pair, lanes, wo, qt_ref, kt_ref, vt_ref, lse_ref, dpt_ref, a_ref, ds_ref
            )

        def one(j, carry):
            for i, step in ((3, 0), (2, 1), (1, 1)):
                pl.when(j == step)(scatters[i].second)
            for i, step in ((3, 4), (2, 6), (1, 7)):
                pl.when(j == step)(scatters[i].third)
            row = slot_row(j)
            at = pl.ds(row, SLOT)
            lanes = pl.ds(pl.multiple_of(j * SLOT, 128), SLOT)
            block(es_ref[at, :], c_ref[at, :], slots.tag(j), 8 * seq + j, lanes)
            return carry

        lax.fori_loop(0, 8, one, 0)
        block(
            slots.tail(es_ref), slots.tail(c_ref), slots.tail_tag(), slots.last_pair,
            pl.ds(8 * SLOT, TAIL),
        )
        for part in range(3):
            cols = slice(part * D, (part + 1) * D)
            g = dot(xt_ref[...], dpt_ref[cols, :], 1, 1)
            gwa_ref[:, :, :, :, cols] = g[:D].astype(bf16).reshape(PLANE, 2, DEPTH, -1, D)
            if part != 1:
                gvec_ref[part // 2 : part // 2 + 1, :] = g[D : D + 1]
        grad_vec[...] = gvec_ref[...].T.reshape(grad_vec.shape)
        scatters[0].first()
        scatters[4].first()

        def output_one(j, carry):
            block = xs_ref[pl.ds(slot_row(j), SLOT), :].astype(f32)
            unstage(ext_ref, first_row(j, seq), block)
            return carry

        def close(value):
            @pl.when(is_last)
            def _():
                ext_ref[HALO + rows - slots.count : HALO + rows, :] = value[: slots.count]

        lax.fori_loop(0, 8, output_one, 0)
        close(slots.tail(xs_ref).astype(f32))
        scatters[0].second()
        scatters[4].second()
        low_ref[...] = ext_ref[: HALO + rows, :].astype(bf16)
        halo_out[...] = low_ref[:HALO, :]
        edge_back[0].start()
        store(low_ref.at[pl.ds(HALO, rows)], out_ref)
        wa = flat(wa_ref[...])

        def input_block(lanes):
            return dot(wa, dpt_ref[:, lanes], 1, 0).T

        def input_one(j, carry):
            for i, step in ((3, 1), (2, 3), (1, 5)):
                pl.when(j == step)(functools.partial(update, i))
            at = pl.ds(slot_row(j), SLOT)
            lanes = pl.ds(pl.multiple_of(j * SLOT, 128), SLOT)
            unstage(ext_ref, first_row(j, seq), input_block(lanes) + dh_ref[at, :])
            return carry

        lax.fori_loop(0, 8, input_one, 0)
        close(input_block(pl.ds(8 * SLOT, TAIL)) + slots.tail(dh_ref))
        halo_in[...] = ext_ref[:HALO, :]
        edge_back[1].start()
        store(ext_ref.at[pl.ds(HALO, rows)], in_ref)
        scatters[0].third()
        scatters[4].third()
        for i in (3, 2, 1):
            copy_gathers[i].second()
        update(4)
        update(0)
        for i in (3, 2, 1):
            copy_gathers[i].third()
        for i in (4, 0):
            copy_gathers[i].second()
        for i in range(5):
            for n, kind in enumerate((firsts, seconds, masters)):
                store(kind[i], state_out[5 * n + i])
        for i in (4, 0):
            copy_gathers[i].third()
        for i in (3, 2, 1, 4, 0):
            copy_gathers[i].finish()
            scatters[i].finish()
        here = masters[4].shape[0]
        mine = jnp.concatenate([whole_vec[seq * 2 + q // 4, q % 4] for q in range(8)], 0)
        copies[4][...] = mine.astype(f32).T[:here].astype(bf16)
        for i in range(5):
            store(copies[i], copy_out[i])
        for copy in stores:
            copy.wait()
        for copy in edge_back:
            copy.wait()

    edge_back = [
        remote(halo_out, out_back, edge_send.at[4], edge_recv.at[4], place.in_depth(3)),
        remote(halo_in, in_back, edge_send.at[5], edge_recv.at[5], place.in_depth(3)),
    ]
    pl.run_scoped(
        backward,
        pltpu.VMEM((3 * D, LANES), bf16),
        pltpu.VMEM((HALO + rows + 16, D), f32),
        pltpu.VMEM((HEADS, SLOT, SLOT), bf16),
        pltpu.VMEM((HEADS, SLOT, SLOT), bf16),
    )


def whole(masters, firsts, seconds, tokens, cotangent, segment, keep):
    shape = jax.ShapeDtypeStruct
    vmem = pl.BlockSpec(memory_space=pltpu.VMEM)
    hbm = pl.BlockSpec(memory_space=pl.ANY)
    state = (*masters, *firsts, *seconds)
    rows = tokens.shape[1]
    r = masters[0].shape[0]
    shapes = ((r, 3 * D), (r, D), (r, FF), (4 * r, D))
    copies = [((8, DEPTH, s[0], s[1] // DEPTH), bf16) for s in shapes]
    copies.append(((masters[4].shape[0], 128), bf16))
    halos = [((HALO, D), bf16), ((HALO, D), f32)]
    out_shape = [
        shape((rows, D), bf16),
        shape((rows, D), f32),
        *[shape(s.shape, f32) for i in range(3) for s in masters],
        *[shape(*c) for c in copies],
        *[shape(*h) for h in halos],
    ]
    five = [(s, bf16) for s in shapes] + [((r, 128), f32)]
    tall = ROWS
    scratch = [pltpu.VMEM(s.shape, f32) for s in state]
    scratch += [pltpu.VMEM((8, DEPTH) + s, bf16) for s in (*shapes, (r, 128))]
    scratch += [
        pltpu.VMEM((tall, D), bf16),
        pltpu.VMEM((tall, D), bf16),
        pltpu.VMEM((D + AUG, LANES), bf16),
        pltpu.VMEM((D, LANES), bf16),
        pltpu.VMEM((D, LANES), bf16),
        pltpu.VMEM((D, LANES), bf16),
        pltpu.VMEM((tall, D), bf16),
        pltpu.VMEM((HEADS, LANES), f32),
        pltpu.VMEM((tall, D), f32),
        pltpu.VMEM((8, LANES), jnp.int32),
        pltpu.VMEM((HALO + rows, D), bf16),
        pltpu.VMEM((HALO + rows, D), bf16),
        pltpu.VMEM((1, 128), jnp.int32),
        pltpu.VMEM((1, 128), jnp.int32),
        pltpu.VMEM((128, 128), f32),
        pltpu.VMEM((128, D), f32),
        pltpu.VMEM((PLANE, 2, DEPTH) + shapes[0], bf16),
        pltpu.VMEM((PLANE, 2, DEPTH) + shapes[1], bf16),
        pltpu.VMEM((PLANE, 2, DEPTH, r, 128), f32),
        *[pltpu.VMEM(*h) for h in halos],
    ]
    for lead in ((PLANE, DEPTH), (3, DEPTH), (3,)):
        scratch += [pltpu.VMEM(lead + s, t) for s, t in five]
    scratch += [pltpu.VMEM((DEPTH, s[0], s[1] // DEPTH), bf16) for s in shapes]
    scratch += [pltpu.VMEM(*c) for c in copies]
    scratch.append(pltpu.VMEM((8, DEPTH, r, 128), bf16))
    dma = pltpu.SemaphoreType.DMA
    scratch += [
        dma((15,)), dma((2,)), dma((5, 10)), dma((5, 10)), dma((6,)), dma((6,)),
        dma((5, 10)), dma((5, 10)), dma((5, 10)), dma((5, 10)), dma((22,)),
    ]
    return pl.pallas_call(
        whole_kernel,
        out_shape=out_shape,
        in_specs=[hbm] * 17 + [vmem] * 2,
        out_specs=[hbm] * 22 + [vmem] * 2,
        scratch_shapes=scratch,
        compiler_params=pltpu.CompilerParams(
            collective_id=0, has_side_effects=True, vmem_limit_bytes=63 * MIB
        ),
        name="whole",
    )(*state, tokens, cotangent, segment, keep)


def last_kernel(*refs):
    results, ends = refs[:22], refs[24:46]
    backs = refs[22:24]
    lows = refs[46:48]
    sems = refs[48]
    rows = results[0].shape[0]
    seq = lax.axis_index("seq")
    copies = []
    rims = []
    for i in range(22):
        src, dst = results[i], ends[i]
        if i < 2:
            rims.append(pltpu.make_async_copy(src.at[pl.ds(rows - HALO, HALO)], lows[i], sems.at[22 + i]))
            rims[-1].start()
            src, dst = src.at[pl.ds(0, rows - HALO)], dst.at[pl.ds(0, rows - HALO)]
        copies.append(pltpu.make_async_copy(src, dst, sems.at[i]))
        copies[-1].start()
    place = lax.broadcasted_iota(jnp.int32, (HALO, 1), 0)
    theirs = (place >= HALO - 8 * (seq + 1)) & (seq < lax.axis_size("seq") - 1)
    for i in range(2):
        rims[i].wait()
        low = lows[i]
        low[...] = jnp.where(theirs, backs[i][...].astype(f32), low[...].astype(f32)).astype(low.dtype)
        store = pltpu.make_async_copy(low, ends[i].at[pl.ds(rows - HALO, HALO)], sems.at[22 + i])
        store.start()
        store.wait()
    for copy in copies:
        copy.wait()


def last(results, out_back, in_back):
    shape = jax.ShapeDtypeStruct
    vmem = pl.BlockSpec(memory_space=pltpu.VMEM)
    hbm = pl.BlockSpec(memory_space=pl.ANY)
    return pl.pallas_call(
        last_kernel,
        out_shape=[shape(a.shape, a.dtype) for a in results],
        in_specs=[hbm] * 22 + [vmem, vmem],
        out_specs=[hbm] * 22,
        scratch_shapes=[
            pltpu.VMEM((HALO, D), bf16),
            pltpu.VMEM((HALO, D), f32),
            pltpu.SemaphoreType.DMA((24,)),
        ],
        compiler_params=pltpu.CompilerParams(vmem_limit_bytes=60 * MIB),
        name="last",
    )(*results, out_back, in_back)


def on_device(
    tokens,
    cotangent,
    segment,
    keep_mask,
    attn_master,
    out_master,
    in_master,
    back_master,
    vec_master,
    attn_first,
    out_first,
    in_first,
    back_first,
    vec_first,
    attn_second,
    out_second,
    in_second,
    back_second,
    vec_second,
):
    seq = lax.axis_index("seq")
    seq_count = lax.axis_size("seq")
    both = ("batch", "seq")
    rows = tokens.shape[1]
    masters = (attn_master, out_master, in_master, back_master, vec_master)
    firsts = (attn_first, out_first, in_first, back_first, vec_first)
    seconds = (attn_second, out_second, in_second, back_second, vec_second)
    direct = seq_count == DEPTH and lax.axis_size("batch") == 2 * PLANE
    forward = [(i, i + 1) for i in range(seq_count - 1)]
    backward = [(i + 1, i) for i in range(seq_count - 1)]
    if direct:
        *results, out_back, grad_back = whole(
            masters, firsts, seconds, tokens, cotangent, segment, keep_mask
        )
        for i in range(17, 21):
            results[i] = results[i].reshape(-1, results[i].shape[-1])
        ends = last(results, out_back, grad_back)
        return (ends[0][None], ends[1][None], *ends[2:])
    low = [w.astype(bf16) for w in masters]
    low[4] = jnp.pad(low[4].T, ((0, 0), (0, 128 - low[4].shape[0])))
    attn_w, out_w, in_w, back_w, vec_t = (
        lax.all_gather(w, both, axis=0, tiled=True) for w in low
    )
    x_halo, e_halo, seg_halo, keep_halo = (
        lax.ppermute(a, "seq", forward)
        for a in (
            tokens[0, rows - HALO :], cotangent[0, rows - HALO :],
            segment[:, rows - 128 :], keep_mask[:, rows - 128 :],
        )
    )
    xs, es, xt, qt, kt, vt, c, lse = attn_forward(
        seq_count, tokens, cotangent, x_halo, e_halo, segment, keep_mask, seg_halo, keep_halo,
        attn_w, vec_t,
    )
    z, dh, dr, gwo, gw1, gw2, gvec, gb1 = feed(xs, c, es, out_w, in_w, back_w, vec_t)
    out, out_halo, grad_in, grad_in_halo, gwa, gbias = attn_backward(
        seq_count, xt, qt, kt, vt, lse, dr, dh, z, attn_w, out_w
    )
    grads = (gwa, gwo, gw1, gw2)
    grad_vec = jnp.concatenate(
        [gbias[:1, :D], gbias[:1, 2 * D :], gvec[2:8], gb1[0].reshape(FF // D, D)], 0
    )
    sums = [lax.psum_scatter(g.astype(f32), both, scatter_dimension=0, tiled=True) for g in grads]
    sums.append(lax.psum_scatter(grad_vec, both, scatter_dimension=1, tiled=True))
    new = [
        adam_update(masters[i], firsts[i], seconds[i], sums[i], learn_rates[i]) for i in range(5)
    ]

    def own_columns(i):
        whole = lax.all_gather(new[i][2].astype(bf16), both, axis=1 if i == 4 else 0, tiled=True)
        count = whole.shape[1] // seq_count
        return lax.dynamic_slice_in_dim(whole, seq * count, count, 1)

    results = [out, grad_in] + [new[i][part] for part in range(3) for i in range(5)]
    results += [own_columns(i) for i in range(5)]
    out_back = lax.ppermute(out_halo, "seq", backward)
    grad_back = lax.ppermute(grad_in_halo, "seq", backward)
    ends = last(results, out_back, grad_back)
    return (ends[0][None], ends[1][None], *ends[2:])


def solution(mesh):
    stream = P("batch", "seq", None)
    rows = P(("batch", "seq"), None)
    vector = P(None, ("batch", "seq"))
    five = (rows, rows, rows, rows, vector)
    return jax.shard_map(
        on_device,
        mesh=mesh,
        in_specs=(stream, stream, P("batch", "seq"), P("batch", "seq")) + five * 3,
        out_specs=(stream, stream) + five * 3 + (P(None, "seq"),) * 5,
        check_vma=False,
    )
```

```python
import functools

import jax
import jax.numpy as jnp
from jax import lax
from jax.experimental import pallas as pl
from jax.experimental.pallas import tpu as pltpu
from jax.sharding import PartitionSpec as P

D = 512
HEADS = 8
HEAD_DIM = 64
FF = 2048
STEP = 10
PAIR = 255
SLOT = 256
HALO = 64
TILES = 4
TAIL = 64
PIECE = TAIL // TILES
TILE = 2 * SLOT + PIECE
ROWS = TILES * TILE
LANES = 8 * SLOT + 128
AUG = 16
MIB = 1 << 20

norm_epsilon = 1e-05
beta_first = 0.9
beta_second = 0.999
adam_epsilon = 1e-08
weight_decay = 0.01
learn_rates = (0.03, 0.2, 0.03, 0.02, 0.5)
big = 1e30

f32 = jnp.float32
bf16 = jnp.bfloat16


def dot(a, b, ca, cb):
    return lax.dot_general(a, b, (((ca,), (cb,)), ((), ())), preferred_element_type=f32)


def adam_update(master, first, second, gradient, rate):
    first_new = beta_first * first + (1.0 - beta_first) * gradient
    second_new = beta_second * second + (1.0 - beta_second) * gradient * gradient
    first_hat = first_new / (1.0 - beta_first**STEP)
    second_hat = second_new / (1.0 - beta_second**STEP)
    master_new = master - rate * (
        first_hat / (jnp.sqrt(second_hat) + adam_epsilon) + weight_decay * master
    )
    return (first_new, second_new, master_new)


def slot_row(j):
    return pl.multiple_of((j // 2) * TILE + (j % 2) * SLOT, 16)


def first_row(j, seq):
    return HALO + PAIR * j - 8 * seq


def staged(ref, start):
    base = pl.multiple_of((start // 16) * 16, 16)
    rest = start - base
    wide = ref[pl.ds(base, SLOT + 16), :].astype(f32)
    wide = jnp.where(rest >= 8, wide[8:], wide[:-8])
    shift = rest % 8
    groups = (SLOT + 8) // 8
    wide = wide.reshape(groups, 8, D)
    turned = pltpu.roll(wide, lax.rem(8 - shift, 8), 1)
    place = lax.broadcasted_iota(jnp.int32, (groups - 1, 8, D), 1)
    block = jnp.where(place < 8 - shift, turned[:-1], turned[1:]).reshape(SLOT, D)
    row = lax.broadcasted_iota(jnp.int32, (SLOT, D), 0)
    return jnp.where(row < PAIR, block, 0.0).astype(bf16)


def unstage(ref, start, block):
    base = pl.multiple_of((start // 8) * 8, 8)
    shift = start - base
    turned = pltpu.roll(block.reshape(SLOT // 8, 8, D), shift, 1)
    place = lax.broadcasted_iota(jnp.int32, (1, 8, D), 1)
    keep = ref[pl.ds(base, 8), :].reshape(1, 8, D)
    low = jnp.concatenate([keep, turned], 0)
    high = jnp.concatenate([turned, turned[-1:]], 0)
    place = lax.broadcasted_iota(jnp.int32, low.shape, 1)
    ref[pl.ds(base, SLOT + 8), :] = jnp.where(place < shift, low, high).reshape(SLOT + 8, D)


def tail_rows(ref, count, is_last):
    kept = ref[HALO + 2048 - count : HALO + 2048, :].astype(f32)
    if count < TAIL:
        kept = jnp.concatenate([kept, jnp.zeros((TAIL - count, D), f32)], 0)
    return jnp.where(is_last, kept, 0.0).astype(bf16)


def tag_rows(tag, pair):
    width = tag.shape[1]
    number = tag // 2 - 2 * pair
    kept = tag % 2
    row = lax.broadcasted_iota(jnp.int32, (AUG, width), 0)
    match = row == number
    query = jnp.where(match, 1.0, 0.0).astype(bf16)
    key = jnp.where(match & (kept == 1), 0.0, -big)
    key = jnp.where(row < 4, key, 0.0).astype(bf16)
    return query, key


def attn_forward_kernel(
    seq_count, tok_ref, cot_ref, tok_halo, cot_halo, seg_ref, keep_ref, seg_halo, keep_halo,
    w_ref, vec_ref,
    xs_ref, es_ref, xt_ref, qt_ref, kt_ref, vt_ref, c_ref, lse_ref,
    wt_ref, x_ref, e_ref, tag_ref, sems,
):
    seq = lax.axis_index("seq")
    is_last = seq == seq_count - 1
    rows = tok_ref.shape[1]
    loads = []
    for i, (whole, halo, ext) in enumerate(((tok_ref, tok_halo, x_ref), (cot_ref, cot_halo, e_ref))):
        loads.append(pltpu.make_async_copy(whole.at[0], ext.at[pl.ds(HALO, rows)], sems.at[2 * i]))
        loads.append(pltpu.make_async_copy(halo, ext.at[pl.ds(0, HALO)], sems.at[2 * i + 1]))
    for load in loads:
        load.start()
    for part in range(3):
        wt_ref[part * D : (part + 1) * D, :] = w_ref[:, part * D : (part + 1) * D].T
    tag_ref[...] = jnp.zeros_like(tag_ref)
    edge = seg_halo[...] * 2 + keep_halo[...]
    tag_ref[:, :HALO] = jnp.broadcast_to(edge[:, 128 - HALO :], (8, HALO))
    tag_ref[:, HALO : HALO + rows] = jnp.broadcast_to(seg_ref[...] * 2 + keep_ref[...], (8, rows))
    query_bias = vec_ref[:, 0:1].astype(f32)
    value_bias = vec_ref[:, 1:2].astype(f32)
    for load in loads:
        load.wait()

    def block(xb, tag, pair, lane, width):
        lanes = pl.ds(lane, width)
        xt_ref[:D, lanes] = xb.T
        q = dot(wt_ref[:D, :], xb, 1, 1) + query_bias
        q = (q.astype(bf16).astype(f32) * HEAD_DIM**-0.5).astype(bf16)
        k = dot(wt_ref[D : 2 * D, :], xb, 1, 1).astype(bf16)
        v = (dot(wt_ref[2 * D :, :], xb, 1, 1) + value_bias).astype(bf16)
        query_tag, key_tag = tag_rows(tag, pair)
        vt_ref[:, lanes] = v
        context = []
        for h in range(HEADS):
            rows = slice(h * HEAD_DIM, (h + 1) * HEAD_DIM)
            qh = jnp.concatenate([q[rows], query_tag], 0)
            kh = jnp.concatenate([k[rows], key_tag], 0)
            qt_ref[h, :, lanes] = qh
            kt_ref[h, :, lanes] = kh
            s = dot(kh, qh, 0, 0)
            top = jnp.max(s, axis=0, keepdims=True)
            ex = jnp.exp(s - top)
            total = jnp.sum(ex, axis=0, keepdims=True)
            lse_ref[h : h + 1, lanes] = top + jnp.log(total)
            a = (ex * (1.0 / total)).astype(bf16)
            context.append(dot(v[rows], a, 1, 0))
        return jnp.concatenate(context, 0).astype(bf16).T

    def one(j, carry):
        start = first_row(j, seq)
        row = slot_row(j)
        xb = staged(x_ref, start)
        xs_ref[pl.ds(row, SLOT), :] = xb
        es_ref[pl.ds(row, SLOT), :] = staged(e_ref, start)
        wide = tag_ref[:, pl.ds(pl.multiple_of(j * SLOT, 128), SLOT + 128)]
        width = SLOT + 128
        tag = pltpu.roll(wide, width - (start - j * SLOT), 1)[:1, :SLOT]
        c_ref[pl.ds(row, SLOT), :] = block(
            xb, tag, 8 * seq + j, pl.multiple_of(j * SLOT, 128), SLOT
        )
        return carry

    lax.fori_loop(0, 8, one, 0)
    count = 8 * seq_count
    xt_ref[:, 8 * SLOT :] = jnp.zeros((D + AUG, 128), bf16)
    xb = tail_rows(x_ref, count, is_last)
    eb = tail_rows(e_ref, count, is_last)
    tag = tag_ref[:1, 2048:2176]
    tag = pltpu.roll(tag_ref[:, 2048:2176], 128 - (64 - count), 1)[:1, :TAIL] if count < 64 else tag[:, :TAIL]
    place = lax.broadcasted_iota(jnp.int32, (1, TAIL), 1)
    tag = jnp.where(place < count, tag, (2 * 8 * seq_count + 3) * 2)
    cb = block(xb, tag, 8 * seq_count, 8 * SLOT, TAIL)
    for t in range(TILES):
        rows = slice(t * PIECE, (t + 1) * PIECE)
        at = slice(t * TILE + 2 * SLOT, (t + 1) * TILE)
        xs_ref[at, :] = xb[rows]
        es_ref[at, :] = eb[rows]
        c_ref[at, :] = cb[rows]
    ones = lax.broadcasted_iota(jnp.int32, (AUG, LANES), 0) == 0
    xt_ref[D:, :] = jnp.where(ones, 1.0, 0.0).astype(bf16)


def attn_forward(seq_count, tokens, cotangent, *others):
    shape = jax.ShapeDtypeStruct
    vmem = pl.BlockSpec(memory_space=pltpu.VMEM)
    hbm = pl.BlockSpec(memory_space=pl.ANY)
    return pl.pallas_call(
        functools.partial(attn_forward_kernel, seq_count),
        out_shape=(
            shape((ROWS, D), bf16),
            shape((ROWS, D), bf16),
            shape((D + AUG, LANES), bf16),
            shape((HEADS, HEAD_DIM + AUG, LANES), bf16),
            shape((HEADS, HEAD_DIM + AUG, LANES), bf16),
            shape((D, LANES), bf16),
            shape((ROWS, D), bf16),
            shape((HEADS, LANES), f32),
        ),
        in_specs=[hbm, hbm] + [vmem] * len(others),
        out_specs=[vmem] * 8,
        scratch_shapes=[
            pltpu.VMEM((3 * D, D), bf16),
            pltpu.VMEM((HALO + tokens.shape[1], D), bf16),
            pltpu.VMEM((HALO + tokens.shape[1], D), bf16),
            pltpu.VMEM((8, LANES), jnp.int32),
            pltpu.SemaphoreType.DMA((4,)),
        ],
        compiler_params=pltpu.CompilerParams(vmem_limit_bytes=56 * MIB),
        name="attn_forward",
    )(tokens, cotangent, *others)


def feed_kernel(
    xs_ref, c_ref, es_ref, wo_ref, w1_ref, w2_ref, vect_ref,
    z_ref, dh_ref, dr_ref, gwo_ref, gw1_ref, gw2_ref, gvec_ref, gb1_ref,
    u_ref, g_ref, awo_ref, aw1_ref, aw2_ref, vec_ref,
):
    step = pl.program_id(0)

    @pl.when(step == 0)
    def _():
        awo_ref[...] = jnp.zeros_like(awo_ref)
        aw1_ref[...] = jnp.zeros_like(aw1_ref)
        aw2_ref[...] = jnp.zeros_like(aw2_ref)
        gvec_ref[...] = jnp.zeros_like(gvec_ref)
        gb1_ref[...] = jnp.zeros_like(gb1_ref)
        vec_ref[...] = vect_ref[...].astype(f32).T

    def mean(v):
        return jnp.mean(v, axis=-1, keepdims=True)

    def row_sum(v):
        return jnp.sum(v, axis=0, keepdims=True)

    bo, b2, g1, c1, g2, c2 = (vec_ref[i : i + 1, :] for i in range(2, 8))
    h1 = xs_ref[...].astype(f32) + (dot(c_ref[...], wo_ref[...], 1, 0) + bo)
    mid = h1 - mean(h1)
    inv1 = lax.rsqrt(mean(mid * mid) + norm_epsilon)
    n1 = mid * inv1
    y = n1 * g1 + c1
    yb = y.astype(bf16)
    chunk = D
    f = None
    for k in range(FF // chunk):
        cols = slice(k * chunk, (k + 1) * chunk)
        u = dot(yb, w1_ref[:, cols], 1, 0) + vec_ref[8 + k : 9 + k, :]
        cdf = 0.5 * (1.0 + lax.erf(u * 0.7071067811865476))
        gk = (u * cdf).astype(bf16)
        u_ref[:, cols] = cdf + u * jnp.exp(u * u * -0.5) * 0.3989422804014327
        g_ref[:, cols] = gk
        part = dot(gk, w2_ref[cols, :], 1, 0)
        f = part if f is None else f + part
    h2 = y + (f + b2)
    mid2 = h2 - mean(h2)
    inv2 = lax.rsqrt(mean(mid2 * mid2) + norm_epsilon)
    n2 = mid2 * inv2
    z_ref[...] = (n2 * g2 + c2).astype(bf16)
    e = es_ref[...].astype(f32)
    gvec_ref[7:8, :] += row_sum(e)
    gvec_ref[6:7, :] += row_sum(e * n2)
    eg = e * g2
    dh2 = (eg - mean(eg) - n2 * mean(eg * n2)) * inv2
    df = dh2.astype(bf16)
    gvec_ref[3:4, :] += row_sum(df.astype(f32))
    dft = df.T
    ybt = yb.T
    dy = dh2
    for k in range(FF // chunk):
        cols = slice(k * chunk, (k + 1) * chunk)
        aw2_ref[:, cols] += dot(dft, g_ref[:, cols], 1, 0)
        dg = dot(df, w2_ref[cols, :], 1, 1)
        du = (dg * u_ref[:, cols]).astype(bf16)
        gb1_ref[:1, cols] += row_sum(du.astype(f32))
        aw1_ref[:, cols] += dot(ybt, du, 1, 0)
        dy = dy + dot(du, w1_ref[:, cols], 1, 1)
    gvec_ref[5:6, :] += row_sum(dy)
    gvec_ref[4:5, :] += row_sum(dy * n1)
    eg = dy * g1
    dh1 = (eg - mean(eg) - n1 * mean(eg * n1)) * inv1
    dh_ref[...] = dh1
    dr = dh1.astype(bf16)
    dr_ref[...] = dr
    gvec_ref[2:3, :] += row_sum(dr.astype(f32))
    awo_ref[...] += dot(c_ref[...].T, dr, 1, 0)

    @pl.when(step == TILES - 1)
    def _():
        gwo_ref[...] = awo_ref[...].astype(bf16)
        gw1_ref[...] = aw1_ref[...].astype(bf16)
        for k in range(FF // chunk):
            cols = slice(k * chunk, (k + 1) * chunk)
            gw2_ref[cols, :] = aw2_ref[:, cols].astype(bf16).T


def feed(xs, c, es, wo, w1, w2, vec_t):
    shape = jax.ShapeDtypeStruct
    tile = pl.BlockSpec((TILE, D), lambda i: (i, 0))

    def whole(*dims):
        return pl.BlockSpec(dims, lambda i: (0,) * len(dims), pipeline_mode=pl.Buffered(1))

    return pl.pallas_call(
        feed_kernel,
        grid=(TILES,),
        out_shape=(
            shape((ROWS, D), bf16),
            shape((ROWS, D), f32),
            shape((ROWS, D), bf16),
            shape((D, D), bf16),
            shape((D, FF), bf16),
            shape((FF, D), bf16),
            shape((8, D), f32),
            shape((8, FF), f32),
        ),
        in_specs=[tile, tile, tile, whole(D, D), whole(D, FF), whole(FF, D), whole(D, 128)],
        out_specs=[tile, tile, tile, whole(D, D), whole(D, FF), whole(FF, D), whole(8, D), whole(8, FF)],
        scratch_shapes=[
            pltpu.VMEM((TILE, FF), f32),
            pltpu.VMEM((TILE, FF), bf16),
            pltpu.VMEM((D, D), f32),
            pltpu.VMEM((D, FF), f32),
            pltpu.VMEM((D, FF), f32),
            pltpu.VMEM((128, D), f32),
        ],
        compiler_params=pltpu.CompilerParams(vmem_limit_bytes=60 * MIB),
        name="feed",
    )(xs, c, es, wo, w1, w2, vec_t)


def attn_backward_kernel(
    seq_count, xt_ref, qt_ref, kt_ref, vt_ref, lse_ref, dr_ref, dh_ref, z_ref, w_ref, wo_ref,
    out_ref, out_halo_ref, in_ref, in_halo_ref, gwa_ref, gbias_ref,
    dpt_ref, ext_ref,
):
    seq = lax.axis_index("seq")
    is_last = seq == seq_count - 1

    def block(dr, lane, width):
        lanes = pl.ds(lane, width)
        dct = dot(wo_ref[...], dr, 1, 1).astype(bf16)
        for h in range(HEADS):
            rows = slice(h * HEAD_DIM, (h + 1) * HEAD_DIM)
            qh = qt_ref[h, :, lanes]
            kh = kt_ref[h, :, lanes]
            vh = vt_ref[rows, lanes]
            dch = dct[rows]
            a = jnp.exp(dot(kh, qh, 0, 0) - lse_ref[h : h + 1, lanes])
            da = dot(vh, dch, 0, 0)
            ada = a * da
            ds = (ada - a * jnp.sum(ada, axis=0, keepdims=True)).astype(bf16)
            dv = dot(dch, a.astype(bf16), 1, 1)
            dk = dot(qh[:HEAD_DIM], ds, 1, 1)
            dq = dot(kh[:HEAD_DIM], ds, 1, 0) * HEAD_DIM**-0.5
            dpt_ref[rows, lanes] = dq.astype(bf16)
            dpt_ref[slice(D + h * HEAD_DIM, D + (h + 1) * HEAD_DIM), lanes] = dk.astype(bf16)
            dpt_ref[slice(2 * D + h * HEAD_DIM, 2 * D + (h + 1) * HEAD_DIM), lanes] = dv.astype(bf16)
        return dot(w_ref[...], dpt_ref[:, lanes], 1, 0).T

    dpt_ref[:, 8 * SLOT :] = jnp.zeros((3 * D, 128), bf16)

    def one(j, carry):
        row = slot_row(j)
        grad = block(dr_ref[pl.ds(row, SLOT), :], pl.multiple_of(j * SLOT, 128), SLOT)
        unstage(ext_ref, first_row(j, seq), grad + dh_ref[pl.ds(row, SLOT), :])
        return carry

    lax.fori_loop(0, 8, one, 0)
    count = 8 * seq_count

    def tail_of(ref):
        return jnp.concatenate(
            [ref[t * TILE + 2 * SLOT : (t + 1) * TILE, :] for t in range(TILES)], 0
        )

    grad = block(tail_of(dr_ref), 8 * SLOT, TAIL) + tail_of(dh_ref)

    @pl.when(is_last)
    def _():
        ext_ref[HALO + 2048 - count : HALO + 2048, :] = grad[:count]

    in_halo_ref[...] = ext_ref[:HALO, :]
    in_ref[...] = ext_ref[HALO : HALO + 2048, :]

    def two(j, carry):
        unstage(ext_ref, first_row(j, seq), z_ref[pl.ds(slot_row(j), SLOT), :].astype(f32))
        return carry

    lax.fori_loop(0, 8, two, 0)
    tail = tail_of(z_ref).astype(f32)

    @pl.when(is_last)
    def _():
        ext_ref[HALO + 2048 - count : HALO + 2048, :] = tail[:count]

    out_halo_ref[...] = ext_ref[:HALO, :].astype(bf16)
    out_ref[...] = ext_ref[HALO : HALO + 2048, :].astype(bf16)
    for part in range(3):
        cols = slice(part * D, (part + 1) * D)
        g = dot(xt_ref[...], dpt_ref[cols, :], 1, 1)
        gwa_ref[:, cols] = g[:D].astype(bf16)
        gbias_ref[:, cols] = g[D : D + 8]


def attn_backward(seq_count, *operands):
    shape = jax.ShapeDtypeStruct
    return pl.pallas_call(
        functools.partial(attn_backward_kernel, seq_count),
        out_shape=(
            shape((2048, D), bf16),
            shape((HALO, D), bf16),
            shape((2048, D), f32),
            shape((HALO, D), f32),
            shape((D, 3 * D), bf16),
            shape((8, 3 * D), f32),
        ),
        in_specs=[pl.BlockSpec(memory_space=pltpu.VMEM)] * len(operands),
        out_specs=[pl.BlockSpec(memory_space=pltpu.VMEM)] * 6,
        scratch_shapes=[
            pltpu.VMEM((3 * D, LANES), bf16),
            pltpu.VMEM((HALO + 2048 + 16, D), f32),
        ],
        compiler_params=pltpu.CompilerParams(vmem_limit_bytes=60 * MIB),
        name="attn_backward",
    )(*operands)


MESH = pl.DeviceIdType.MESH
PLANE = 4
DEPTH = 4


class Place:
    def __init__(self):
        self.batch = lax.axis_index("batch")
        self.z = lax.axis_index("seq")
        self.core = self.batch % 2
        self.plane = self.batch // 2

    def plane_at(self, k):
        x = (self.plane % 2 + k % 2) % 2
        y = (self.plane // 2 + k // 2) % 2
        return y * 2 + x

    def in_plane(self, k):
        return {"batch": self.plane_at(k) * 2 + self.core, "seq": self.z}

    def depth_at(self, k):
        return (self.z + k) % DEPTH

    def in_depth(self, k):
        return {"batch": self.batch, "seq": self.depth_at(k)}

    def sibling(self):
        return {"batch": self.plane * 2 + 1 - self.core, "seq": self.z}

    def greet(self):
        barrier = pltpu.get_barrier_semaphore()
        for k in range(1, 4):
            pl.semaphore_signal(barrier, inc=1, device_id=self.in_plane(k), device_id_type=MESH)
            pl.semaphore_signal(barrier, inc=1, device_id=self.in_depth(k), device_id_type=MESH)
        pl.semaphore_signal(barrier, inc=1, device_id=self.sibling(), device_id_type=MESH)
        pl.semaphore_wait(barrier, 7)


def remote(src, dst, send, recv, device):
    return pltpu.make_async_remote_copy(
        src_ref=src, dst_ref=dst, send_sem=send, recv_sem=recv, device_id=device, device_id_type=MESH
    )


class Gather:
    def __init__(self, place, whole, send, recv, parts=None):
        self.place, self.whole, self.send, self.recv, self.parts = place, whole, send, recv, parts

    def depth(self, k):
        at = self.place
        here = self.whole.at[at.batch, at.z]
        source = here if self.parts is None else self.parts.at[at.depth_at(k)]
        return remote(source, here, self.send.at[k - 1], self.recv.at[k - 1], at.in_depth(k))

    def plane(self, k):
        block = self.whole.at[self.place.batch]
        return remote(block, block, self.send.at[2 + k], self.recv.at[2 + k], self.place.in_plane(k))

    def core(self, k):
        block = self.whole.at[self.place.plane_at(k) * 2 + self.place.core]
        return remote(block, block, self.send.at[6 + k], self.recv.at[6 + k], self.place.sibling())

    def first(self):
        for k in range(1, 4):
            self.depth(k).start()

    def second(self):
        for k in range(1, 4):
            self.depth(k).wait_recv()
        for k in range(1, 4):
            self.plane(k).start()
        self.core(0).start()

    def third(self):
        for k in range(1, 4):
            self.plane(k).wait_recv()
            self.core(k).start()

    def finish(self):
        for k in range(4):
            self.core(k).wait_recv()
        for k in range(1, 4):
            self.depth(k).wait_send()
            self.plane(k).wait_send()
        for k in range(4):
            self.core(k).wait_send()


class Scatter:
    def __init__(self, place, grad, twin, across, along, send, recv):
        self.place, self.grad, self.twin = place, grad, twin
        self.across, self.along, self.send, self.recv = across, along, send, recv
        shape = grad.shape
        if len(shape) == 4:
            self.at = lambda p, c: grad.at[p * 2 + c]
        else:
            self.at = lambda p, c: grad.at[p, c]

    def core(self, p):
        return remote(
            self.at(p, 1 - self.place.core), self.twin.at[p], self.send.at[p], self.recv.at[p],
            self.place.sibling(),
        )

    def plane(self, k):
        return remote(
            self.at(self.place.plane_at(k), self.place.core), self.across.at[k - 1],
            self.send.at[3 + k], self.recv.at[3 + k], self.place.in_plane(k),
        )

    def depth(self, k):
        return remote(
            self.at(self.place.plane, self.place.core).at[self.place.depth_at(k)],
            self.along.at[k - 1], self.send.at[6 + k], self.recv.at[6 + k], self.place.in_depth(k),
        )

    def first(self):
        for p in range(PLANE):
            self.core(p).start()

    def second(self):
        for p in range(PLANE):
            self.core(p).wait_recv()
        own = self.place.core

        def one(p, carry):
            mine = self.at(p, own)
            mine[...] = (mine[...].astype(f32) + self.twin[p].astype(f32)).astype(mine.dtype)
            return carry

        lax.fori_loop(0, PLANE, one, 0)
        for k in range(1, 4):
            self.plane(k).start()

    def third(self):
        for k in range(1, 4):
            self.plane(k).wait_recv()
        mine = self.at(self.place.plane, self.place.core)

        def one(q, carry):
            total = mine[q].astype(f32)
            for k in range(3):
                total = total + self.across[k, q].astype(f32)
            mine[q] = total.astype(mine.dtype)
            return carry

        lax.fori_loop(0, DEPTH, one, 0)
        for k in range(1, 4):
            self.depth(k).start()

    def total(self):
        for k in range(1, 4):
            self.depth(k).wait_recv()
        total = self.at(self.place.plane, self.place.core)[self.place.z].astype(f32)
        for k in range(3):
            total = total + self.along[k].astype(f32)
        return total

    def finish(self):
        for p in range(PLANE):
            self.core(p).wait_send()
        for k in range(1, 4):
            self.plane(k).wait_send()
            self.depth(k).wait_send()


def turned(ref, value):
    ref[...] = jnp.zeros_like(ref)
    ref[: value.shape[0], : value.shape[1]] = value
    return ref[...].T


def heads_of(block, h):
    return block[h * HEAD_DIM : (h + 1) * HEAD_DIM]


def only_head(block, h):
    zero = jnp.zeros((HEAD_DIM, block.shape[1]), block.dtype)
    mine = heads_of(block, h)
    return jnp.concatenate([mine, zero] if h % 2 == 0 else [zero, mine], 0)


def pair_of(block, h):
    at = h // 2 * 2 * HEAD_DIM
    return block[:, at : at + 2 * HEAD_DIM]


def mask_parts(tag, pair):
    query, key = tag_rows(tag, pair)
    width = tag.shape[1]
    zero = jnp.zeros((128 - AUG, width), bf16)
    return jnp.concatenate([key, zero], 0).T, jnp.concatenate([query, zero], 0)


class Slots:
    def __init__(self, tag_ref, seq, seq_count):
        self.tag_ref, self.seq, self.count = tag_ref, seq, 8 * seq_count
        self.last_pair = 8 * seq_count

    def tag(self, j):
        wide = self.tag_ref[:, pl.ds(pl.multiple_of(j * SLOT, 128), SLOT + 128)]
        offset = HALO - 8 * self.seq - j
        return pltpu.roll(wide, SLOT + 128 - offset, 1)[:1, :SLOT]

    def tail_tag(self):
        tag = self.tag_ref[:, 2048:2176]
        if self.count < TAIL:
            tag = pltpu.roll(tag, 128 - (TAIL - self.count), 1)
        place = lax.broadcasted_iota(jnp.int32, (1, TAIL), 1)
        return jnp.where(place < self.count, tag[:1, :TAIL], 2 * (2 * self.last_pair + 3))

    def tail(self, ref):
        return jnp.concatenate(
            [ref[t * TILE + 2 * SLOT : (t + 1) * TILE, :] for t in range(TILES)], 0
        )

    def set_tail(self, ref, value):
        for t in range(TILES):
            ref[t * TILE + 2 * SLOT : (t + 1) * TILE, :] = value[t * PIECE : (t + 1) * PIECE]


def forward_block(xb, tag, pair, lanes, wt_ref, biases, xt_ref, qt_ref, kt_ref, vt_ref, lse_ref, s_ref, a_ref):
    width = xb.shape[0]
    xt_ref[:D, lanes] = xb.T
    q = dot(wt_ref[:D, :], xb, 1, 1) + biases[0]
    q = (q.astype(bf16).astype(f32) * HEAD_DIM**-0.5).astype(bf16)
    k = dot(wt_ref[D : 2 * D, :], xb, 1, 1).astype(bf16)
    v = (dot(wt_ref[2 * D :, :], xb, 1, 1) + biases[1]).astype(bf16)
    qt_ref[:, lanes] = q
    kt_ref[:, lanes] = k
    vt_ref[:, lanes] = v
    key_mask, query_mask = mask_parts(tag, pair)
    kn = k.T
    for h in range(HEADS):
        left = jnp.concatenate([pair_of(kn, h), key_mask], 1)
        right = jnp.concatenate([only_head(q, h), query_mask], 0)
        s_ref[h, :width, :width] = dot(left, right, 1, 0)
    for h in range(HEADS):
        s = s_ref[h, :width, :width]
        top = jnp.max(s, axis=0, keepdims=True)
        ex = jnp.exp(s - top)
        total = jnp.sum(ex, axis=0, keepdims=True)
        lse_ref[h : h + 1, lanes] = top + jnp.log(total)
        a_ref[h, :width, :width] = (ex * (1.0 / total)).astype(bf16)
    context = [
        dot(heads_of(v, h), a_ref[h, :width, :width], 1, 0).astype(bf16) for h in range(HEADS)
    ]
    return jnp.concatenate(context, 0).T


def backward_block(dr, c, tag, pair, lanes, wo, qt_ref, kt_ref, vt_ref, lse_ref, dpt_ref, a_ref, ds_ref):
    width = dr.shape[0]
    dct32 = dot(wo, dr, 1, 1)
    dct = dct32.astype(bf16)
    product = c.T.astype(f32) * dct.astype(f32)
    q = qt_ref[:, lanes]
    k = kt_ref[:, lanes]
    kn = k.T
    vn = vt_ref[:, lanes].T
    key_mask, query_mask = mask_parts(tag, pair)
    for h in range(HEADS):
        left = jnp.concatenate([pair_of(kn, h), key_mask], 1)
        right = jnp.concatenate([only_head(q, h), query_mask], 0)
        delta = jnp.sum(heads_of(product, h), axis=0, keepdims=True)
        a = jnp.exp(dot(left, right, 1, 0) - lse_ref[h : h + 1, lanes])
        da = dot(pair_of(vn, h), only_head(dct, h), 1, 0)
        a_ref[h, :width, :width] = a.astype(bf16)
        ds_ref[h, :width, :width] = (a * (da - delta)).astype(bf16)
    for h in range(HEADS):
        rows = slice(h * HEAD_DIM, (h + 1) * HEAD_DIM)
        ds = ds_ref[h, :width, :width]
        dv = dot(dct[rows], a_ref[h, :width, :width], 1, 1)
        dk = dot(q[rows], ds, 1, 1)
        dq = dot(k[rows], ds, 1, 0) * HEAD_DIM**-0.5
        dpt_ref[rows, lanes] = dq.astype(bf16)
        dpt_ref[slice(D + h * HEAD_DIM, D + (h + 1) * HEAD_DIM), lanes] = dk.astype(bf16)
        dpt_ref[slice(2 * D + h * HEAD_DIM, 2 * D + (h + 1) * HEAD_DIM), lanes] = dv.astype(bf16)


def mean(v):
    return jnp.mean(v, axis=-1, keepdims=True)


def row_sum(v):
    return jnp.sum(v, axis=0, keepdims=True)


def flat(value):
    return value.reshape(-1, value.shape[-1])


def gelu_pair(u):
    bell = jnp.exp(u * u * -0.5)
    t = pl.reciprocal(1.0 + jnp.abs(u) * (0.3275911 * 0.7071067811865476))
    tail = 0.5 * 1.061405429
    for term in (-1.453152027, 1.421413741, -0.284496736, 0.254829592):
        tail = tail * t + 0.5 * term
    tail = tail * t * bell
    cdf = jnp.where(u < 0.0, tail, 1.0 - tail)
    return u * cdf, cdf + u * bell * 0.3989422804014327


def feed_tile(
    rows, xs_ref, c_ref, es_ref, wo_ref, w1_ref, w2_ref, vec_ref, dh_ref, gvec_ref,
    u_ref, g_ref, awo_ref, aw1_ref, aw2_ref,
):
    bo, b2, g1, c1, g2, c2 = (vec_ref[i : i + 1, :] for i in range(2, 8))
    c = c_ref[rows, :]
    h1 = xs_ref[rows, :].astype(f32) + (dot(c, flat(wo_ref[...]), 1, 0) + bo)
    mid = h1 - mean(h1)
    inv1 = lax.rsqrt(mean(mid * mid) + norm_epsilon)
    n1 = mid * inv1
    y = n1 * g1 + c1
    yb = y.astype(bf16)
    per = FF // D

    def cols_of(k):
        return pl.ds(pl.multiple_of(k * D, 128), D)

    def w2_part(k):
        return flat(w2_ref[pl.ds(8 // per * k, 8 // per)])

    def w1_part(k):
        return flat(w1_ref[:, :, :, cols_of(k)])

    def chunk(k):
        return pl.ds(pl.multiple_of(k * TILE, 16), TILE)

    def inner(k, carry):
        u = dot(yb, w1_part(k), 1, 0) + vec_ref[pl.ds(8 + k, 1), :]
        active, slope = gelu_pair(u)
        g_ref[chunk(k), :] = active.astype(bf16)
        u_ref[chunk(k), :] = slope
        return carry

    lax.fori_loop(0, per, inner, 0)
    f = None
    for k in range(per):
        part = dot(g_ref[chunk(k), :], w2_part(k), 1, 0)
        f = part if f is None else f + part
    h2 = y + (f + b2)
    mid2 = h2 - mean(h2)
    inv2 = lax.rsqrt(mean(mid2 * mid2) + norm_epsilon)
    n2 = mid2 * inv2
    xs_ref[rows, :] = (n2 * g2 + c2).astype(bf16)
    e = es_ref[rows, :].astype(f32)
    gvec_ref[7:8, :] += row_sum(e)
    gvec_ref[6:7, :] += row_sum(e * n2)
    eg = e * g2
    dh2 = (eg - mean(eg) - n2 * mean(eg * n2)) * inv2
    df = dh2.astype(bf16)
    gvec_ref[3:4, :] += row_sum(df.astype(f32))
    dft = df.T
    ybt = yb.T

    def outer(k, carry):
        cols = cols_of(k)
        aw2_ref[:, cols] += dot(dft, g_ref[chunk(k), :], 1, 0)
        dg = dot(df, w2_part(k), 1, 1)
        du = (dg * u_ref[chunk(k), :]).astype(bf16)
        gvec_ref[pl.ds(8 + k, 1), :] += row_sum(du.astype(f32))
        aw1_ref[:, cols] += dot(ybt, du, 1, 0)
        g_ref[chunk(k), :] = du
        return carry

    lax.fori_loop(0, per, outer, 0)
    dy = dh2
    for k in range(per):
        dy = dy + dot(g_ref[chunk(k), :], w1_part(k), 1, 1)
    gvec_ref[5:6, :] += row_sum(dy)
    gvec_ref[4:5, :] += row_sum(dy * n1)
    eg = dy * g1
    dh1 = (eg - mean(eg) - n1 * mean(eg * n1)) * inv1
    dh_ref[rows, :] = dh1
    dr = dh1.astype(bf16)
    es_ref[rows, :] = dr
    gvec_ref[2:3, :] += row_sum(dr.astype(f32))
    awo_ref[...] += dot(c.T, dr, 1, 0)


def whole_kernel(*refs):
    refs = list(refs)

    def take(count):
        taken = refs[:count]
        del refs[:count]
        return taken

    state_in = take(15)
    tok_ref, cot_ref, seg_ref, keep_ref = take(4)
    out_ref, in_ref = take(2)
    state_out = take(15)
    copy_out = take(5)
    out_back, in_back = take(2)
    state = take(15)
    masters, firsts, seconds = state[:5], state[5:10], state[10:]
    weights = take(5)
    wa_ref, wo_ref, w1_ref, w2_ref, wv_ref = weights
    xs_ref, es_ref, xt_ref, qt_ref, kt_ref, vt_ref, c_ref, lse_ref, dh_ref, tag_ref = take(10)
    ext_x, ext_e, seg_halo, keep_halo = take(4)
    square, gvec_ref, gwa_ref, gwo_ref, grad_vec, halo_out, halo_in = take(7)
    twins, acrosses, alongs = take(5), take(5), take(5)
    parts, copies, whole_vec = take(4), take(5), take(1)[0]
    (
        state_sems, load_sems, gather_send, gather_recv, edge_send, edge_recv,
        sum_send, sum_recv, copy_send, copy_recv, store_sems,
    ) = refs
    place = Place()
    seq, seq_count = place.z, DEPTH
    is_last = seq == seq_count - 1
    slots = Slots(tag_ref, seq, seq_count)
    rows = tok_ref.shape[1]

    loads = [pltpu.make_async_copy(state_in[i], state[i], state_sems.at[i]) for i in range(15)]
    for load in loads:
        load.start()
    big_loads = [
        pltpu.make_async_copy(src.at[0], dst.at[pl.ds(HALO, rows)], load_sems.at[i])
        for i, (src, dst) in enumerate(((tok_ref, ext_x), (cot_ref, ext_e)))
    ]
    for load in big_loads:
        load.start()
    place.greet()
    edge = [
        remote(src, dst, edge_send.at[i], edge_recv.at[i], place.in_depth(1))
        for i, (src, dst) in enumerate((
            (tok_ref.at[0, pl.ds(rows - HALO, HALO)], ext_x.at[pl.ds(0, HALO)]),
            (cot_ref.at[0, pl.ds(rows - HALO, HALO)], ext_e.at[pl.ds(0, HALO)]),
            (seg_ref.at[:, pl.ds(rows - 128, 128)], seg_halo),
            (keep_ref.at[:, pl.ds(rows - 128, 128)], keep_halo),
        ))
    ]
    gathers = [Gather(place, weights[i], gather_send.at[i], gather_recv.at[i]) for i in range(5)]

    def put(i):
        shard = turned(square, masters[4][...])[: masters[4].shape[1]] if i == 4 else masters[i][...]
        weights[i][place.batch, place.z] = shard.astype(bf16)

    for i in (0, 4, 1, 2, 3):
        loads[i].wait()
    put(0)
    gathers[0].first()
    put(4)
    gathers[4].first()
    for copy in edge:
        copy.start()
    for i in (1, 2, 3):
        put(i)
    gathers[0].second()
    gathers[4].second()
    for i in (1, 2, 3):
        gathers[i].first()
    for load in big_loads:
        load.wait()
    for copy in edge:
        copy.wait()
    tag_ref[...] = jnp.zeros_like(tag_ref)
    rim = seg_halo[...] * 2 + keep_halo[...]
    tag_ref[:, :HALO] = jnp.broadcast_to(rim[:, 128 - HALO :], (8, HALO))
    tag_ref[:, HALO : HALO + rows] = jnp.broadcast_to(seg_ref[...] * 2 + keep_ref[...], (8, rows))

    def stage_one(j, carry):
        start = first_row(j, seq)
        row = slot_row(j)
        xs_ref[pl.ds(row, SLOT), :] = staged(ext_x, start)
        es_ref[pl.ds(row, SLOT), :] = staged(ext_e, start)
        return carry

    lax.fori_loop(0, 8, stage_one, 0)
    slots.set_tail(xs_ref, tail_rows(ext_x, slots.count, is_last))
    slots.set_tail(es_ref, tail_rows(ext_e, slots.count, is_last))
    gathers[0].third()
    gathers[4].third()
    xt_ref[:, 8 * SLOT :] = jnp.zeros((D + AUG, 128), bf16)
    ones = lax.broadcasted_iota(jnp.int32, (AUG, LANES), 0) == 0
    xt_ref[D:, :] = jnp.where(ones, 1.0, 0.0).astype(bf16)
    gathers[0].finish()
    gathers[4].finish()

    def forward(wt_ref, s_ref, a_ref):
        for part in range(3):
            wt_ref[part * D : (part + 1) * D, :] = flat(
                wa_ref[:, :, :, part * D : (part + 1) * D]
            ).T
        vec_t = flat(wv_ref[...])
        biases = (vec_t[:, 0:1].astype(f32), vec_t[:, 1:2].astype(f32))

        def block(xb, tag, pair, lanes):
            return forward_block(
                xb, tag, pair, lanes, wt_ref, biases, xt_ref, qt_ref, kt_ref, vt_ref, lse_ref,
                s_ref, a_ref,
            )

        def one(j, carry):
            for i, step in ((1, 1), (2, 2), (3, 3)):
                pl.when(j == step)(gathers[i].second)
            for i, step in ((1, 4), (2, 5), (3, 7)):
                pl.when(j == step)(gathers[i].third)
            row = slot_row(j)
            lanes = pl.ds(pl.multiple_of(j * SLOT, 128), SLOT)
            c_ref[pl.ds(row, SLOT), :] = block(
                xs_ref[pl.ds(row, SLOT), :], slots.tag(j), 8 * seq + j, lanes
            )
            return carry

        lax.fori_loop(0, 8, one, 0)
        slots.set_tail(
            c_ref,
            block(
                slots.tail(xs_ref), slots.tail_tag(), slots.last_pair, pl.ds(8 * SLOT, TAIL)
            ),
        )

    pl.run_scoped(
        forward,
        pltpu.VMEM((3 * D, D), bf16),
        pltpu.VMEM((HEADS, SLOT, SLOT), f32),
        pltpu.VMEM((HEADS, SLOT, SLOT), bf16),
    )
    for i in (1, 2, 3):
        gathers[i].finish()

    def feed_all(vec_ref, u_ref, awo_ref, aw1_ref, aw2_ref):
        g_ref = ext_x
        for ref in (awo_ref, aw1_ref, aw2_ref, gvec_ref):
            ref[...] = jnp.zeros_like(ref)
        vec_ref[...] = flat(wv_ref[...]).astype(f32).T

        def one(t, carry):
            feed_tile(
                pl.ds(pl.multiple_of(t * TILE, 16), TILE), xs_ref, c_ref, es_ref, wo_ref, w1_ref,
                w2_ref, vec_ref, dh_ref, gvec_ref, u_ref, g_ref, awo_ref, aw1_ref, aw2_ref,
            )
            return carry

        lax.fori_loop(0, TILES, one, 0)
        for k in range(FF // D):
            value = aw2_ref[:, k * D : (k + 1) * D].astype(bf16).T
            w2_ref[2 * k : 2 * k + 2] = value.reshape(2, DEPTH, -1, D)
        for k in range(FF // D):
            cols = slice(k * D, (k + 1) * D)
            w1_ref[:, :, :, cols] = aw1_ref[:, cols].astype(bf16).reshape(8, DEPTH, -1, D)
        gwo_ref[...] = awo_ref[...].astype(bf16).reshape(gwo_ref.shape)

    pl.run_scoped(
        feed_all,
        pltpu.VMEM((128, D), f32),
        pltpu.VMEM((FF // D * TILE, D), f32),
        pltpu.VMEM((D, D), f32),
        pltpu.VMEM((D, FF), f32),
        pltpu.VMEM((D, FF), f32),
    )
    grads = [gwa_ref, gwo_ref, w1_ref, w2_ref, grad_vec]
    scatters = [
        Scatter(place, grads[i], twins[i], acrosses[i], alongs[i], sum_send.at[i], sum_recv.at[i])
        for i in range(5)
    ]
    for i in (3, 2, 1):
        scatters[i].first()
    for load in loads[5:]:
        load.wait()
    copy_gathers = [
        Gather(place, copies[i], copy_send.at[i], copy_recv.at[i], parts[i]) for i in range(4)
    ]
    copy_gathers.append(Gather(place, whole_vec, copy_send.at[4], copy_recv.at[4]))
    stores = []

    def store(src, dst):
        stores.append(pltpu.make_async_copy(src, dst, store_sems.at[len(stores)]))
        stores[-1].start()

    def update(i):
        total = scatters[i].total()
        if i == 4:
            square[...] = jnp.zeros_like(square)
            square[: total.shape[0], :] = total
            here, cols = masters[4].shape
            total = square[...].T[:here, :cols]
        new = adam_update(masters[i][...], firsts[i][...], seconds[i][...], total, learn_rates[i])
        firsts[i][...], seconds[i][...], masters[i][...] = new
        if i == 4:
            shard = turned(square, new[2])[: new[2].shape[1]].astype(bf16)
            whole_vec[place.batch, place.z] = shard
        else:
            low = new[2].astype(bf16)
            width = low.shape[1] // DEPTH
            for q in range(DEPTH):
                parts[i][q] = low[:, q * width : (q + 1) * width]
            copies[i][place.batch, place.z] = parts[i][place.z]
        copy_gathers[i].first()

    def backward(dpt_ref, ext_ref, a_ref, ds_ref):
        low_ref = ext_e
        dpt_ref[:, 8 * SLOT :] = jnp.zeros((3 * D, 128), bf16)
        wo = flat(wo_ref[...])

        def block(dr, c, tag, pair, lanes):
            backward_block(
                dr, c, tag, pair, lanes, wo, qt_ref, kt_ref, vt_ref, lse_ref, dpt_ref, a_ref, ds_ref
            )

        def one(j, carry):
            for i, step in ((3, 0), (2, 1), (1, 1)):
                pl.when(j == step)(scatters[i].second)
            for i, step in ((3, 4), (2, 6), (1, 7)):
                pl.when(j == step)(scatters[i].third)
            row = slot_row(j)
            at = pl.ds(row, SLOT)
            lanes = pl.ds(pl.multiple_of(j * SLOT, 128), SLOT)
            block(es_ref[at, :], c_ref[at, :], slots.tag(j), 8 * seq + j, lanes)
            return carry

        lax.fori_loop(0, 8, one, 0)
        block(
            slots.tail(es_ref), slots.tail(c_ref), slots.tail_tag(), slots.last_pair,
            pl.ds(8 * SLOT, TAIL),
        )
        for part in range(3):
            cols = slice(part * D, (part + 1) * D)
            g = dot(xt_ref[...], dpt_ref[cols, :], 1, 1)
            gwa_ref[:, :, :, :, cols] = g[:D].astype(bf16).reshape(PLANE, 2, DEPTH, -1, D)
            if part != 1:
                gvec_ref[part // 2 : part // 2 + 1, :] = g[D : D + 1]
        grad_vec[...] = gvec_ref[...].T.reshape(grad_vec.shape)
        scatters[0].first()
        scatters[4].first()

        def output_one(j, carry):
            block = xs_ref[pl.ds(slot_row(j), SLOT), :].astype(f32)
            unstage(ext_ref, first_row(j, seq), block)
            return carry

        def close(value):
            @pl.when(is_last)
            def _():
                ext_ref[HALO + rows - slots.count : HALO + rows, :] = value[: slots.count]

        lax.fori_loop(0, 8, output_one, 0)
        close(slots.tail(xs_ref).astype(f32))
        scatters[0].second()
        scatters[4].second()
        low_ref[...] = ext_ref[: HALO + rows, :].astype(bf16)
        halo_out[...] = low_ref[:HALO, :]
        edge_back[0].start()
        store(low_ref.at[pl.ds(HALO, rows)], out_ref)
        wa = flat(wa_ref[...])

        def input_block(lanes):
            return dot(wa, dpt_ref[:, lanes], 1, 0).T

        def input_one(j, carry):
            for i, step in ((3, 1), (2, 3), (1, 5)):
                pl.when(j == step)(functools.partial(update, i))
            at = pl.ds(slot_row(j), SLOT)
            lanes = pl.ds(pl.multiple_of(j * SLOT, 128), SLOT)
            unstage(ext_ref, first_row(j, seq), input_block(lanes) + dh_ref[at, :])
            return carry

        lax.fori_loop(0, 8, input_one, 0)
        close(input_block(pl.ds(8 * SLOT, TAIL)) + slots.tail(dh_ref))
        halo_in[...] = ext_ref[:HALO, :]
        edge_back[1].start()
        store(ext_ref.at[pl.ds(HALO, rows)], in_ref)
        scatters[0].third()
        scatters[4].third()
        for i in (3, 2, 1):
            copy_gathers[i].second()
        update(4)
        update(0)
        for i in (3, 2, 1):
            copy_gathers[i].third()
        for i in (4, 0):
            copy_gathers[i].second()
        for i in range(5):
            for n, kind in enumerate((firsts, seconds, masters)):
                store(kind[i], state_out[5 * n + i])
        for i in (4, 0):
            copy_gathers[i].third()
        for i in (3, 2, 1, 4, 0):
            copy_gathers[i].finish()
            scatters[i].finish()
        here = masters[4].shape[0]
        mine = jnp.concatenate([whole_vec[seq * 2 + q // 4, q % 4] for q in range(8)], 0)
        copies[4][...] = mine.astype(f32).T[:here].astype(bf16)
        for i in range(5):
            store(copies[i], copy_out[i])
        for copy in stores:
            copy.wait()
        for copy in edge_back:
            copy.wait()

    edge_back = [
        remote(halo_out, out_back, edge_send.at[4], edge_recv.at[4], place.in_depth(3)),
        remote(halo_in, in_back, edge_send.at[5], edge_recv.at[5], place.in_depth(3)),
    ]
    pl.run_scoped(
        backward,
        pltpu.VMEM((3 * D, LANES), bf16),
        pltpu.VMEM((HALO + rows + 16, D), f32),
        pltpu.VMEM((HEADS, SLOT, SLOT), bf16),
        pltpu.VMEM((HEADS, SLOT, SLOT), bf16),
    )


def whole(masters, firsts, seconds, tokens, cotangent, segment, keep):
    shape = jax.ShapeDtypeStruct
    vmem = pl.BlockSpec(memory_space=pltpu.VMEM)
    hbm = pl.BlockSpec(memory_space=pl.ANY)
    state = (*masters, *firsts, *seconds)
    rows = tokens.shape[1]
    r = masters[0].shape[0]
    shapes = ((r, 3 * D), (r, D), (r, FF), (4 * r, D))
    copies = [((8, DEPTH, s[0], s[1] // DEPTH), bf16) for s in shapes]
    copies.append(((masters[4].shape[0], 128), bf16))
    halos = [((HALO, D), bf16), ((HALO, D), f32)]
    out_shape = [
        shape((rows, D), bf16),
        shape((rows, D), f32),
        *[shape(s.shape, f32) for i in range(3) for s in masters],
        *[shape(*c) for c in copies],
        *[shape(*h) for h in halos],
    ]
    five = [(s, bf16) for s in shapes] + [((r, 128), f32)]
    tall = ROWS
    scratch = [pltpu.VMEM(s.shape, f32) for s in state]
    scratch += [pltpu.VMEM((8, DEPTH) + s, bf16) for s in (*shapes, (r, 128))]
    scratch += [
        pltpu.VMEM((tall, D), bf16),
        pltpu.VMEM((tall, D), bf16),
        pltpu.VMEM((D + AUG, LANES), bf16),
        pltpu.VMEM((D, LANES), bf16),
        pltpu.VMEM((D, LANES), bf16),
        pltpu.VMEM((D, LANES), bf16),
        pltpu.VMEM((tall, D), bf16),
        pltpu.VMEM((HEADS, LANES), f32),
        pltpu.VMEM((tall, D), f32),
        pltpu.VMEM((8, LANES), jnp.int32),
        pltpu.VMEM((HALO + rows, D), bf16),
        pltpu.VMEM((HALO + rows, D), bf16),
        pltpu.VMEM((1, 128), jnp.int32),
        pltpu.VMEM((1, 128), jnp.int32),
        pltpu.VMEM((128, 128), f32),
        pltpu.VMEM((128, D), f32),
        pltpu.VMEM((PLANE, 2, DEPTH) + shapes[0], bf16),
        pltpu.VMEM((PLANE, 2, DEPTH) + shapes[1], bf16),
        pltpu.VMEM((PLANE, 2, DEPTH, r, 128), f32),
        *[pltpu.VMEM(*h) for h in halos],
    ]
    for lead in ((PLANE, DEPTH), (3, DEPTH), (3,)):
        scratch += [pltpu.VMEM(lead + s, t) for s, t in five]
    scratch += [pltpu.VMEM((DEPTH, s[0], s[1] // DEPTH), bf16) for s in shapes]
    scratch += [pltpu.VMEM(*c) for c in copies]
    scratch.append(pltpu.VMEM((8, DEPTH, r, 128), bf16))
    dma = pltpu.SemaphoreType.DMA
    scratch += [
        dma((15,)), dma((2,)), dma((5, 10)), dma((5, 10)), dma((6,)), dma((6,)),
        dma((5, 10)), dma((5, 10)), dma((5, 10)), dma((5, 10)), dma((22,)),
    ]
    return pl.pallas_call(
        whole_kernel,
        out_shape=out_shape,
        in_specs=[hbm] * 17 + [vmem] * 2,
        out_specs=[hbm] * 22 + [vmem] * 2,
        scratch_shapes=scratch,
        compiler_params=pltpu.CompilerParams(
            collective_id=0, has_side_effects=True, vmem_limit_bytes=63 * MIB
        ),
        name="whole",
    )(*state, tokens, cotangent, segment, keep)


LAST_PART = 496


def last_kernel(*refs):
    results, backs, ends = refs[:22], refs[22:24], refs[24:46]
    lows, (load_sems, store_sems) = refs[46:68], refs[68:]
    rows = results[0].shape[0]
    seq = lax.axis_index("seq")
    rim = pl.ds(rows - HALO, HALO)
    places = [(i, rim) for i in range(2)]
    places += [
        (i, pl.ds(first, LAST_PART))
        for i in range(2)
        for first in range(0, rows - HALO, LAST_PART)
    ]
    places += [(i, pl.ds(0, results[i].shape[0])) for i in range(2, 22)]
    loads = [
        pltpu.make_async_copy(results[i].at[at], lows[i].at[at], load_sems.at[n])
        for n, (i, at) in enumerate(places)
    ]
    stores = [
        pltpu.make_async_copy(lows[i].at[at], ends[i].at[at], store_sems.at[n])
        for n, (i, at) in enumerate(places)
    ]
    for load in loads:
        load.start()
    place = lax.broadcasted_iota(jnp.int32, (HALO, 1), 0)
    theirs = (place >= HALO - 8 * (seq + 1)) & (seq < lax.axis_size("seq") - 1)
    for n, (i, at) in enumerate(places):
        loads[n].wait()
        if n < 2:
            own = lows[i][rim, :].astype(f32)
            lows[i][rim, :] = jnp.where(theirs, backs[i][...].astype(f32), own).astype(lows[i].dtype)
        stores[n].start()
    for store in stores:
        store.wait()


def last(results, out_back, in_back):
    shape = jax.ShapeDtypeStruct
    vmem = pl.BlockSpec(memory_space=pltpu.VMEM)
    hbm = pl.BlockSpec(memory_space=pl.ANY)
    count = 22 + 2 * ((results[0].shape[0] - HALO) // LAST_PART)
    return pl.pallas_call(
        last_kernel,
        out_shape=[shape(a.shape, a.dtype) for a in results],
        in_specs=[hbm] * 22 + [vmem, vmem],
        out_specs=[hbm] * 22,
        scratch_shapes=[pltpu.VMEM(a.shape, a.dtype) for a in results]
        + [pltpu.SemaphoreType.DMA((count,)), pltpu.SemaphoreType.DMA((count,))],
        compiler_params=pltpu.CompilerParams(vmem_limit_bytes=60 * MIB),
        name="last",
    )(*results, out_back, in_back)


def on_device(
    tokens,
    cotangent,
    segment,
    keep_mask,
    attn_master,
    out_master,
    in_master,
    back_master,
    vec_master,
    attn_first,
    out_first,
    in_first,
    back_first,
    vec_first,
    attn_second,
    out_second,
    in_second,
    back_second,
    vec_second,
):
    seq = lax.axis_index("seq")
    seq_count = lax.axis_size("seq")
    both = ("batch", "seq")
    rows = tokens.shape[1]
    masters = (attn_master, out_master, in_master, back_master, vec_master)
    firsts = (attn_first, out_first, in_first, back_first, vec_first)
    seconds = (attn_second, out_second, in_second, back_second, vec_second)
    direct = seq_count == DEPTH and lax.axis_size("batch") == 2 * PLANE
    forward = [(i, i + 1) for i in range(seq_count - 1)]
    backward = [(i + 1, i) for i in range(seq_count - 1)]
    if direct:
        *results, out_back, grad_back = whole(
            masters, firsts, seconds, tokens, cotangent, segment, keep_mask
        )
        for i in range(17, 21):
            results[i] = results[i].reshape(-1, results[i].shape[-1])
        ends = last(results, out_back, grad_back)
        return (ends[0][None], ends[1][None], *ends[2:])
    low = [w.astype(bf16) for w in masters]
    low[4] = jnp.pad(low[4].T, ((0, 0), (0, 128 - low[4].shape[0])))
    attn_w, out_w, in_w, back_w, vec_t = (
        lax.all_gather(w, both, axis=0, tiled=True) for w in low
    )
    x_halo, e_halo, seg_halo, keep_halo = (
        lax.ppermute(a, "seq", forward)
        for a in (
            tokens[0, rows - HALO :], cotangent[0, rows - HALO :],
            segment[:, rows - 128 :], keep_mask[:, rows - 128 :],
        )
    )
    xs, es, xt, qt, kt, vt, c, lse = attn_forward(
        seq_count, tokens, cotangent, x_halo, e_halo, segment, keep_mask, seg_halo, keep_halo,
        attn_w, vec_t,
    )
    z, dh, dr, gwo, gw1, gw2, gvec, gb1 = feed(xs, c, es, out_w, in_w, back_w, vec_t)
    out, out_halo, grad_in, grad_in_halo, gwa, gbias = attn_backward(
        seq_count, xt, qt, kt, vt, lse, dr, dh, z, attn_w, out_w
    )
    grads = (gwa, gwo, gw1, gw2)
    grad_vec = jnp.concatenate(
        [gbias[:1, :D], gbias[:1, 2 * D :], gvec[2:8], gb1[0].reshape(FF // D, D)], 0
    )
    sums = [lax.psum_scatter(g.astype(f32), both, scatter_dimension=0, tiled=True) for g in grads]
    sums.append(lax.psum_scatter(grad_vec, both, scatter_dimension=1, tiled=True))
    new = [
        adam_update(masters[i], firsts[i], seconds[i], sums[i], learn_rates[i]) for i in range(5)
    ]

    def own_columns(i):
        whole = lax.all_gather(new[i][2].astype(bf16), both, axis=1 if i == 4 else 0, tiled=True)
        count = whole.shape[1] // seq_count
        return lax.dynamic_slice_in_dim(whole, seq * count, count, 1)

    results = [out, grad_in] + [new[i][part] for part in range(3) for i in range(5)]
    results += [own_columns(i) for i in range(5)]
    out_back = lax.ppermute(out_halo, "seq", backward)
    grad_back = lax.ppermute(grad_in_halo, "seq", backward)
    ends = last(results, out_back, grad_back)
    return (ends[0][None], ends[1][None], *ends[2:])


def solution(mesh):
    stream = P("batch", "seq", None)
    rows = P(("batch", "seq"), None)
    vector = P(None, ("batch", "seq"))
    five = (rows, rows, rows, rows, vector)
    return jax.shard_map(
        on_device,
        mesh=mesh,
        in_specs=(stream, stream, P("batch", "seq"), P("batch", "seq")) + five * 3,
        out_specs=(stream, stream) + five * 3 + (P(None, "seq"),) * 5,
        check_vma=False,
    )
```

```python
import functools

import jax
import jax.numpy as jnp
from jax import lax
from jax.experimental import pallas as pl
from jax.experimental.pallas import tpu as pltpu
from jax.sharding import PartitionSpec as P

D = 512
HEADS = 8
HEAD_DIM = 64
FF = 2048
STEP = 10
PAIR = 255
SLOT = 256
HALO = 64
TILES = 4
TAIL = 64
PIECE = TAIL // TILES
TILE = 2 * SLOT + PIECE
ROWS = TILES * TILE
LANES = 8 * SLOT + 128
AUG = 16
MIB = 1 << 20

norm_epsilon = 1e-05
beta_first = 0.9
beta_second = 0.999
adam_epsilon = 1e-08
weight_decay = 0.01
learn_rates = (0.03, 0.2, 0.03, 0.02, 0.5)
big = 1e30

f32 = jnp.float32
bf16 = jnp.bfloat16


def dot(a, b, ca, cb):
    return lax.dot_general(a, b, (((ca,), (cb,)), ((), ())), preferred_element_type=f32)


def adam_update(master, first, second, gradient, rate):
    first_new = beta_first * first + (1.0 - beta_first) * gradient
    second_new = beta_second * second + (1.0 - beta_second) * gradient * gradient
    first_hat = first_new / (1.0 - beta_first**STEP)
    second_hat = second_new / (1.0 - beta_second**STEP)
    master_new = master - rate * (
        first_hat / (jnp.sqrt(second_hat) + adam_epsilon) + weight_decay * master
    )
    return (first_new, second_new, master_new)


def slot_row(j):
    return pl.multiple_of((j // 2) * TILE + (j % 2) * SLOT, 16)


def first_row(j, seq):
    return HALO + PAIR * j - 8 * seq


def staged(ref, start):
    base = pl.multiple_of((start // 16) * 16, 16)
    rest = start - base
    wide = ref[pl.ds(base, SLOT + 16), :].astype(f32)
    wide = jnp.where(rest >= 8, wide[8:], wide[:-8])
    shift = rest % 8
    groups = (SLOT + 8) // 8
    wide = wide.reshape(groups, 8, D)
    turned = pltpu.roll(wide, lax.rem(8 - shift, 8), 1)
    place = lax.broadcasted_iota(jnp.int32, (groups - 1, 8, D), 1)
    block = jnp.where(place < 8 - shift, turned[:-1], turned[1:]).reshape(SLOT, D)
    row = lax.broadcasted_iota(jnp.int32, (SLOT, D), 0)
    return jnp.where(row < PAIR, block, 0.0).astype(bf16)


def unstage(ref, start, block):
    base = pl.multiple_of((start // 8) * 8, 8)
    shift = start - base
    turned = pltpu.roll(block.reshape(SLOT // 8, 8, D), shift, 1)
    place = lax.broadcasted_iota(jnp.int32, (1, 8, D), 1)
    keep = ref[pl.ds(base, 8), :].reshape(1, 8, D)
    low = jnp.concatenate([keep, turned], 0)
    high = jnp.concatenate([turned, turned[-1:]], 0)
    place = lax.broadcasted_iota(jnp.int32, low.shape, 1)
    ref[pl.ds(base, SLOT + 8), :] = jnp.where(place < shift, low, high).reshape(SLOT + 8, D)


def stage_slot(ref, start, out_ref, row):
    base = pl.multiple_of((start // 16) * 16, 16)
    rest = start - base
    shift = rest % 8
    groups = (SLOT + 8) // 8
    place = lax.broadcasted_iota(jnp.int32, (groups - 1, 8, 128), 1)
    number = lax.broadcasted_iota(jnp.int32, (groups - 1, 8, 128), 0) * 8 + place
    for g in range(D // 128):
        cols = slice(g * 128, (g + 1) * 128)
        wide = ref[pl.ds(base, SLOT + 16), cols].astype(f32)
        wide = jnp.where(rest >= 8, wide[8:], wide[:-8]).reshape(groups, 8, 128)
        turned = pltpu.roll(wide, lax.rem(8 - shift, 8), 1)
        block = jnp.where(place < 8 - shift, turned[:-1], turned[1:])
        block = jnp.where(number < PAIR, block, 0.0)
        out_ref[pl.ds(row, SLOT), cols] = block.reshape(SLOT, 128).astype(bf16)


def unstage_slot(ref, start, column):
    base = pl.multiple_of((start // 8) * 8, 8)
    shift = start - base
    for g in range(D // 128):
        cols = slice(g * 128, (g + 1) * 128)
        turned = pltpu.roll(column(g).reshape(SLOT // 8, 8, 128), shift, 1)
        keep = ref[pl.ds(base, 8), cols].reshape(1, 8, 128)
        low = jnp.concatenate([keep, turned], 0)
        high = jnp.concatenate([turned, turned[-1:]], 0)
        place = lax.broadcasted_iota(jnp.int32, low.shape, 1)
        ref[pl.ds(base, SLOT + 8), cols] = jnp.where(place < shift, low, high).reshape(SLOT + 8, 128)


def tail_rows(ref, count, is_last):
    kept = ref[HALO + 2048 - count : HALO + 2048, :].astype(f32)
    if count < TAIL:
        kept = jnp.concatenate([kept, jnp.zeros((TAIL - count, D), f32)], 0)
    return jnp.where(is_last, kept, 0.0).astype(bf16)


def tag_rows(tag, pair):
    width = tag.shape[1]
    number = tag // 2 - 2 * pair
    kept = tag % 2
    row = lax.broadcasted_iota(jnp.int32, (AUG, width), 0)
    match = row == number
    query = jnp.where(match, 1.0, 0.0).astype(bf16)
    key = jnp.where(match & (kept == 1), 0.0, -big)
    key = jnp.where(row < 4, key, 0.0).astype(bf16)
    return query, key


def attn_forward_kernel(
    seq_count, tok_ref, cot_ref, tok_halo, cot_halo, seg_ref, keep_ref, seg_halo, keep_halo,
    w_ref, vec_ref,
    xs_ref, es_ref, xt_ref, qt_ref, kt_ref, vt_ref, c_ref, lse_ref,
    wt_ref, x_ref, e_ref, tag_ref, sems,
):
    seq = lax.axis_index("seq")
    is_last = seq == seq_count - 1
    rows = tok_ref.shape[1]
    loads = []
    for i, (whole, halo, ext) in enumerate(((tok_ref, tok_halo, x_ref), (cot_ref, cot_halo, e_ref))):
        loads.append(pltpu.make_async_copy(whole.at[0], ext.at[pl.ds(HALO, rows)], sems.at[2 * i]))
        loads.append(pltpu.make_async_copy(halo, ext.at[pl.ds(0, HALO)], sems.at[2 * i + 1]))
    for load in loads:
        load.start()
    for part in range(3):
        wt_ref[part * D : (part + 1) * D, :] = w_ref[:, part * D : (part + 1) * D].T
    tag_ref[...] = jnp.zeros_like(tag_ref)
    edge = seg_halo[...] * 2 + keep_halo[...]
    tag_ref[:, :HALO] = jnp.broadcast_to(edge[:, 128 - HALO :], (8, HALO))
    tag_ref[:, HALO : HALO + rows] = jnp.broadcast_to(seg_ref[...] * 2 + keep_ref[...], (8, rows))
    query_bias = vec_ref[:, 0:1].astype(f32)
    value_bias = vec_ref[:, 1:2].astype(f32)
    for load in loads:
        load.wait()

    def block(xb, tag, pair, lane, width):
        lanes = pl.ds(lane, width)
        xt_ref[:D, lanes] = xb.T
        q = dot(wt_ref[:D, :], xb, 1, 1) + query_bias
        q = (q.astype(bf16).astype(f32) * HEAD_DIM**-0.5).astype(bf16)
        k = dot(wt_ref[D : 2 * D, :], xb, 1, 1).astype(bf16)
        v = (dot(wt_ref[2 * D :, :], xb, 1, 1) + value_bias).astype(bf16)
        query_tag, key_tag = tag_rows(tag, pair)
        vt_ref[:, lanes] = v
        context = []
        for h in range(HEADS):
            rows = slice(h * HEAD_DIM, (h + 1) * HEAD_DIM)
            qh = jnp.concatenate([q[rows], query_tag], 0)
            kh = jnp.concatenate([k[rows], key_tag], 0)
            qt_ref[h, :, lanes] = qh
            kt_ref[h, :, lanes] = kh
            s = dot(kh, qh, 0, 0)
            top = jnp.max(s, axis=0, keepdims=True)
            ex = jnp.exp(s - top)
            total = jnp.sum(ex, axis=0, keepdims=True)
            lse_ref[h : h + 1, lanes] = top + jnp.log(total)
            a = (ex * (1.0 / total)).astype(bf16)
            context.append(dot(v[rows], a, 1, 0))
        return jnp.concatenate(context, 0).astype(bf16).T

    def one(j, carry):
        start = first_row(j, seq)
        row = slot_row(j)
        xb = staged(x_ref, start)
        xs_ref[pl.ds(row, SLOT), :] = xb
        es_ref[pl.ds(row, SLOT), :] = staged(e_ref, start)
        wide = tag_ref[:, pl.ds(pl.multiple_of(j * SLOT, 128), SLOT + 128)]
        width = SLOT + 128
        tag = pltpu.roll(wide, width - (start - j * SLOT), 1)[:1, :SLOT]
        c_ref[pl.ds(row, SLOT), :] = block(
            xb, tag, 8 * seq + j, pl.multiple_of(j * SLOT, 128), SLOT
        )
        return carry

    lax.fori_loop(0, 8, one, 0)
    count = 8 * seq_count
    xt_ref[:, 8 * SLOT :] = jnp.zeros((D + AUG, 128), bf16)
    xb = tail_rows(x_ref, count, is_last)
    eb = tail_rows(e_ref, count, is_last)
    tag = tag_ref[:1, 2048:2176]
    tag = pltpu.roll(tag_ref[:, 2048:2176], 128 - (64 - count), 1)[:1, :TAIL] if count < 64 else tag[:, :TAIL]
    place = lax.broadcasted_iota(jnp.int32, (1, TAIL), 1)
    tag = jnp.where(place < count, tag, (2 * 8 * seq_count + 3) * 2)
    cb = block(xb, tag, 8 * seq_count, 8 * SLOT, TAIL)
    for t in range(TILES):
        rows = slice(t * PIECE, (t + 1) * PIECE)
        at = slice(t * TILE + 2 * SLOT, (t + 1) * TILE)
        xs_ref[at, :] = xb[rows]
        es_ref[at, :] = eb[rows]
        c_ref[at, :] = cb[rows]
    ones = lax.broadcasted_iota(jnp.int32, (AUG, LANES), 0) == 0
    xt_ref[D:, :] = jnp.where(ones, 1.0, 0.0).astype(bf16)


def attn_forward(seq_count, tokens, cotangent, *others):
    shape = jax.ShapeDtypeStruct
    vmem = pl.BlockSpec(memory_space=pltpu.VMEM)
    hbm = pl.BlockSpec(memory_space=pl.ANY)
    return pl.pallas_call(
        functools.partial(attn_forward_kernel, seq_count),
        out_shape=(
            shape((ROWS, D), bf16),
            shape((ROWS, D), bf16),
            shape((D + AUG, LANES), bf16),
            shape((HEADS, HEAD_DIM + AUG, LANES), bf16),
            shape((HEADS, HEAD_DIM + AUG, LANES), bf16),
            shape((D, LANES), bf16),
            shape((ROWS, D), bf16),
            shape((HEADS, LANES), f32),
        ),
        in_specs=[hbm, hbm] + [vmem] * len(others),
        out_specs=[vmem] * 8,
        scratch_shapes=[
            pltpu.VMEM((3 * D, D), bf16),
            pltpu.VMEM((HALO + tokens.shape[1], D), bf16),
            pltpu.VMEM((HALO + tokens.shape[1], D), bf16),
            pltpu.VMEM((8, LANES), jnp.int32),
            pltpu.SemaphoreType.DMA((4,)),
        ],
        compiler_params=pltpu.CompilerParams(vmem_limit_bytes=56 * MIB),
        name="attn_forward",
    )(tokens, cotangent, *others)


def feed_kernel(
    xs_ref, c_ref, es_ref, wo_ref, w1_ref, w2_ref, vect_ref,
    z_ref, dh_ref, dr_ref, gwo_ref, gw1_ref, gw2_ref, gvec_ref, gb1_ref,
    u_ref, g_ref, awo_ref, aw1_ref, aw2_ref, vec_ref,
):
    step = pl.program_id(0)

    @pl.when(step == 0)
    def _():
        awo_ref[...] = jnp.zeros_like(awo_ref)
        aw1_ref[...] = jnp.zeros_like(aw1_ref)
        aw2_ref[...] = jnp.zeros_like(aw2_ref)
        gvec_ref[...] = jnp.zeros_like(gvec_ref)
        gb1_ref[...] = jnp.zeros_like(gb1_ref)
        vec_ref[...] = vect_ref[...].astype(f32).T

    def mean(v):
        return jnp.mean(v, axis=-1, keepdims=True)

    def row_sum(v):
        return jnp.sum(v, axis=0, keepdims=True)

    bo, b2, g1, c1, g2, c2 = (vec_ref[i : i + 1, :] for i in range(2, 8))
    h1 = xs_ref[...].astype(f32) + (dot(c_ref[...], wo_ref[...], 1, 0) + bo)
    mid = h1 - mean(h1)
    inv1 = lax.rsqrt(mean(mid * mid) + norm_epsilon)
    n1 = mid * inv1
    y = n1 * g1 + c1
    yb = y.astype(bf16)
    chunk = D
    f = None
    for k in range(FF // chunk):
        cols = slice(k * chunk, (k + 1) * chunk)
        u = dot(yb, w1_ref[:, cols], 1, 0) + vec_ref[8 + k : 9 + k, :]
        cdf = 0.5 * (1.0 + lax.erf(u * 0.7071067811865476))
        gk = (u * cdf).astype(bf16)
        u_ref[:, cols] = cdf + u * jnp.exp(u * u * -0.5) * 0.3989422804014327
        g_ref[:, cols] = gk
        part = dot(gk, w2_ref[cols, :], 1, 0)
        f = part if f is None else f + part
    h2 = y + (f + b2)
    mid2 = h2 - mean(h2)
    inv2 = lax.rsqrt(mean(mid2 * mid2) + norm_epsilon)
    n2 = mid2 * inv2
    z_ref[...] = (n2 * g2 + c2).astype(bf16)
    e = es_ref[...].astype(f32)
    gvec_ref[7:8, :] += row_sum(e)
    gvec_ref[6:7, :] += row_sum(e * n2)
    eg = e * g2
    dh2 = (eg - mean(eg) - n2 * mean(eg * n2)) * inv2
    df = dh2.astype(bf16)
    gvec_ref[3:4, :] += row_sum(df.astype(f32))
    dft = df.T
    ybt = yb.T
    dy = dh2
    for k in range(FF // chunk):
        cols = slice(k * chunk, (k + 1) * chunk)
        aw2_ref[:, cols] += dot(dft, g_ref[:, cols], 1, 0)
        dg = dot(df, w2_ref[cols, :], 1, 1)
        du = (dg * u_ref[:, cols]).astype(bf16)
        gb1_ref[:1, cols] += row_sum(du.astype(f32))
        aw1_ref[:, cols] += dot(ybt, du, 1, 0)
        dy = dy + dot(du, w1_ref[:, cols], 1, 1)
    gvec_ref[5:6, :] += row_sum(dy)
    gvec_ref[4:5, :] += row_sum(dy * n1)
    eg = dy * g1
    dh1 = (eg - mean(eg) - n1 * mean(eg * n1)) * inv1
    dh_ref[...] = dh1
    dr = dh1.astype(bf16)
    dr_ref[...] = dr
    gvec_ref[2:3, :] += row_sum(dr.astype(f32))
    awo_ref[...] += dot(c_ref[...].T, dr, 1, 0)

    @pl.when(step == TILES - 1)
    def _():
        gwo_ref[...] = awo_ref[...].astype(bf16)
        gw1_ref[...] = aw1_ref[...].astype(bf16)
        for k in range(FF // chunk):
            cols = slice(k * chunk, (k + 1) * chunk)
            gw2_ref[cols, :] = aw2_ref[:, cols].astype(bf16).T


def feed(xs, c, es, wo, w1, w2, vec_t):
    shape = jax.ShapeDtypeStruct
    tile = pl.BlockSpec((TILE, D), lambda i: (i, 0))

    def whole(*dims):
        return pl.BlockSpec(dims, lambda i: (0,) * len(dims), pipeline_mode=pl.Buffered(1))

    return pl.pallas_call(
        feed_kernel,
        grid=(TILES,),
        out_shape=(
            shape((ROWS, D), bf16),
            shape((ROWS, D), f32),
            shape((ROWS, D), bf16),
            shape((D, D), bf16),
            shape((D, FF), bf16),
            shape((FF, D), bf16),
            shape((8, D), f32),
            shape((8, FF), f32),
        ),
        in_specs=[tile, tile, tile, whole(D, D), whole(D, FF), whole(FF, D), whole(D, 128)],
        out_specs=[tile, tile, tile, whole(D, D), whole(D, FF), whole(FF, D), whole(8, D), whole(8, FF)],
        scratch_shapes=[
            pltpu.VMEM((TILE, FF), f32),
            pltpu.VMEM((TILE, FF), bf16),
            pltpu.VMEM((D, D), f32),
            pltpu.VMEM((D, FF), f32),
            pltpu.VMEM((D, FF), f32),
            pltpu.VMEM((128, D), f32),
        ],
        compiler_params=pltpu.CompilerParams(vmem_limit_bytes=60 * MIB),
        name="feed",
    )(xs, c, es, wo, w1, w2, vec_t)


def attn_backward_kernel(
    seq_count, xt_ref, qt_ref, kt_ref, vt_ref, lse_ref, dr_ref, dh_ref, z_ref, w_ref, wo_ref,
    out_ref, out_halo_ref, in_ref, in_halo_ref, gwa_ref, gbias_ref,
    dpt_ref, ext_ref,
):
    seq = lax.axis_index("seq")
    is_last = seq == seq_count - 1

    def block(dr, lane, width):
        lanes = pl.ds(lane, width)
        dct = dot(wo_ref[...], dr, 1, 1).astype(bf16)
        for h in range(HEADS):
            rows = slice(h * HEAD_DIM, (h + 1) * HEAD_DIM)
            qh = qt_ref[h, :, lanes]
            kh = kt_ref[h, :, lanes]
            vh = vt_ref[rows, lanes]
            dch = dct[rows]
            a = jnp.exp(dot(kh, qh, 0, 0) - lse_ref[h : h + 1, lanes])
            da = dot(vh, dch, 0, 0)
            ada = a * da
            ds = (ada - a * jnp.sum(ada, axis=0, keepdims=True)).astype(bf16)
            dv = dot(dch, a.astype(bf16), 1, 1)
            dk = dot(qh[:HEAD_DIM], ds, 1, 1)
            dq = dot(kh[:HEAD_DIM], ds, 1, 0) * HEAD_DIM**-0.5
            dpt_ref[rows, lanes] = dq.astype(bf16)
            dpt_ref[slice(D + h * HEAD_DIM, D + (h + 1) * HEAD_DIM), lanes] = dk.astype(bf16)
            dpt_ref[slice(2 * D + h * HEAD_DIM, 2 * D + (h + 1) * HEAD_DIM), lanes] = dv.astype(bf16)
        return dot(w_ref[...], dpt_ref[:, lanes], 1, 0).T

    dpt_ref[:, 8 * SLOT :] = jnp.zeros((3 * D, 128), bf16)

    def one(j, carry):
        row = slot_row(j)
        grad = block(dr_ref[pl.ds(row, SLOT), :], pl.multiple_of(j * SLOT, 128), SLOT)
        unstage(ext_ref, first_row(j, seq), grad + dh_ref[pl.ds(row, SLOT), :])
        return carry

    lax.fori_loop(0, 8, one, 0)
    count = 8 * seq_count

    def tail_of(ref):
        return jnp.concatenate(
            [ref[t * TILE + 2 * SLOT : (t + 1) * TILE, :] for t in range(TILES)], 0
        )

    grad = block(tail_of(dr_ref), 8 * SLOT, TAIL) + tail_of(dh_ref)

    @pl.when(is_last)
    def _():
        ext_ref[HALO + 2048 - count : HALO + 2048, :] = grad[:count]

    in_halo_ref[...] = ext_ref[:HALO, :]
    in_ref[...] = ext_ref[HALO : HALO + 2048, :]

    def two(j, carry):
        unstage(ext_ref, first_row(j, seq), z_ref[pl.ds(slot_row(j), SLOT), :].astype(f32))
        return carry

    lax.fori_loop(0, 8, two, 0)
    tail = tail_of(z_ref).astype(f32)

    @pl.when(is_last)
    def _():
        ext_ref[HALO + 2048 - count : HALO + 2048, :] = tail[:count]

    out_halo_ref[...] = ext_ref[:HALO, :].astype(bf16)
    out_ref[...] = ext_ref[HALO : HALO + 2048, :].astype(bf16)
    for part in range(3):
        cols = slice(part * D, (part + 1) * D)
        g = dot(xt_ref[...], dpt_ref[cols, :], 1, 1)
        gwa_ref[:, cols] = g[:D].astype(bf16)
        gbias_ref[:, cols] = g[D : D + 8]


def attn_backward(seq_count, *operands):
    shape = jax.ShapeDtypeStruct
    return pl.pallas_call(
        functools.partial(attn_backward_kernel, seq_count),
        out_shape=(
            shape((2048, D), bf16),
            shape((HALO, D), bf16),
            shape((2048, D), f32),
            shape((HALO, D), f32),
            shape((D, 3 * D), bf16),
            shape((8, 3 * D), f32),
        ),
        in_specs=[pl.BlockSpec(memory_space=pltpu.VMEM)] * len(operands),
        out_specs=[pl.BlockSpec(memory_space=pltpu.VMEM)] * 6,
        scratch_shapes=[
            pltpu.VMEM((3 * D, LANES), bf16),
            pltpu.VMEM((HALO + 2048 + 16, D), f32),
        ],
        compiler_params=pltpu.CompilerParams(vmem_limit_bytes=60 * MIB),
        name="attn_backward",
    )(*operands)


MESH = pl.DeviceIdType.MESH
PLANE = 4
DEPTH = 4


class Place:
    def __init__(self):
        self.batch = lax.axis_index("batch")
        self.z = lax.axis_index("seq")
        self.core = self.batch % 2
        self.plane = self.batch // 2

    def plane_at(self, k):
        x = (self.plane % 2 + k % 2) % 2
        y = (self.plane // 2 + k // 2) % 2
        return y * 2 + x

    def in_plane(self, k):
        return {"batch": self.plane_at(k) * 2 + self.core, "seq": self.z}

    def depth_at(self, k):
        return (self.z + k) % DEPTH

    def in_depth(self, k):
        return {"batch": self.batch, "seq": self.depth_at(k)}

    def sibling(self):
        return {"batch": self.plane * 2 + 1 - self.core, "seq": self.z}

    def greet(self):
        barrier = pltpu.get_barrier_semaphore()
        for k in range(1, 4):
            pl.semaphore_signal(barrier, inc=1, device_id=self.in_plane(k), device_id_type=MESH)
            pl.semaphore_signal(barrier, inc=1, device_id=self.in_depth(k), device_id_type=MESH)
        pl.semaphore_signal(barrier, inc=1, device_id=self.sibling(), device_id_type=MESH)
        pl.semaphore_wait(barrier, 7)


def remote(src, dst, send, recv, device):
    return pltpu.make_async_remote_copy(
        src_ref=src, dst_ref=dst, send_sem=send, recv_sem=recv, device_id=device, device_id_type=MESH
    )


class Gather:
    def __init__(self, place, whole, send, recv, parts=None):
        self.place, self.whole, self.send, self.recv, self.parts = place, whole, send, recv, parts

    def depth(self, k):
        at = self.place
        here = self.whole.at[at.batch, at.z]
        source = here if self.parts is None else self.parts.at[at.depth_at(k)]
        return remote(source, here, self.send.at[k - 1], self.recv.at[k - 1], at.in_depth(k))

    def plane(self, k):
        block = self.whole.at[self.place.batch]
        return remote(block, block, self.send.at[2 + k], self.recv.at[2 + k], self.place.in_plane(k))

    def core(self, k):
        block = self.whole.at[self.place.plane_at(k) * 2 + self.place.core]
        return remote(block, block, self.send.at[6 + k], self.recv.at[6 + k], self.place.sibling())

    def first(self):
        for k in range(1, 4):
            self.depth(k).start()

    def second(self):
        for k in range(1, 4):
            self.depth(k).wait_recv()
        for k in range(1, 4):
            self.plane(k).start()
        self.core(0).start()

    def third(self):
        for k in range(1, 4):
            self.plane(k).wait_recv()
            self.core(k).start()

    def finish(self):
        for k in range(4):
            self.core(k).wait_recv()
        for k in range(1, 4):
            self.depth(k).wait_send()
            self.plane(k).wait_send()
        for k in range(4):
            self.core(k).wait_send()


class Scatter:
    def __init__(self, place, grad, twin, across, along, send, recv):
        self.place, self.grad, self.twin = place, grad, twin
        self.across, self.along, self.send, self.recv = across, along, send, recv
        shape = grad.shape
        if len(shape) == 4:
            self.at = lambda p, c: grad.at[p * 2 + c]
        else:
            self.at = lambda p, c: grad.at[p, c]

    def core(self, p):
        return remote(
            self.at(p, 1 - self.place.core), self.twin.at[p], self.send.at[p], self.recv.at[p],
            self.place.sibling(),
        )

    def plane(self, k):
        return remote(
            self.at(self.place.plane_at(k), self.place.core), self.across.at[k - 1],
            self.send.at[3 + k], self.recv.at[3 + k], self.place.in_plane(k),
        )

    def depth(self, k):
        return remote(
            self.at(self.place.plane, self.place.core).at[self.place.depth_at(k)],
            self.along.at[k - 1], self.send.at[6 + k], self.recv.at[6 + k], self.place.in_depth(k),
        )

    def first(self):
        for p in range(PLANE):
            self.core(p).start()

    def second(self):
        for p in range(PLANE):
            self.core(p).wait_recv()
        own = self.place.core

        def one(p, carry):
            mine = self.at(p, own)
            mine[...] = (mine[...].astype(f32) + self.twin[p].astype(f32)).astype(mine.dtype)
            return carry

        lax.fori_loop(0, PLANE, one, 0)
        for k in range(1, 4):
            self.plane(k).start()

    def third(self):
        for k in range(1, 4):
            self.plane(k).wait_recv()
        mine = self.at(self.place.plane, self.place.core)

        def one(q, carry):
            total = mine[q].astype(f32)
            for k in range(3):
                total = total + self.across[k, q].astype(f32)
            mine[q] = total.astype(mine.dtype)
            return carry

        lax.fori_loop(0, DEPTH, one, 0)
        for k in range(1, 4):
            self.depth(k).start()

    def total(self):
        for k in range(1, 4):
            self.depth(k).wait_recv()
        total = self.at(self.place.plane, self.place.core)[self.place.z].astype(f32)
        for k in range(3):
            total = total + self.along[k].astype(f32)
        return total

    def finish(self):
        for p in range(PLANE):
            self.core(p).wait_send()
        for k in range(1, 4):
            self.plane(k).wait_send()
            self.depth(k).wait_send()


def turned(ref, value):
    ref[...] = jnp.zeros_like(ref)
    ref[: value.shape[0], : value.shape[1]] = value
    return ref[...].T


def heads_of(block, h):
    return block[h * HEAD_DIM : (h + 1) * HEAD_DIM]


def only_head(block, h):
    zero = jnp.zeros((HEAD_DIM, block.shape[1]), block.dtype)
    mine = heads_of(block, h)
    return jnp.concatenate([mine, zero] if h % 2 == 0 else [zero, mine], 0)


def pair_of(block, h):
    at = h // 2 * 2 * HEAD_DIM
    return block[:, at : at + 2 * HEAD_DIM]


def mask_parts(tag, pair):
    query, key = tag_rows(tag, pair)
    width = tag.shape[1]
    zero = jnp.zeros((128 - AUG, width), bf16)
    return jnp.concatenate([key, zero], 0).T, jnp.concatenate([query, zero], 0)


class Slots:
    def __init__(self, tag_ref, seq, seq_count):
        self.tag_ref, self.seq, self.count = tag_ref, seq, 8 * seq_count
        self.last_pair = 8 * seq_count

    def tag(self, j):
        wide = self.tag_ref[:, pl.ds(pl.multiple_of(j * SLOT, 128), SLOT + 128)]
        offset = HALO - 8 * self.seq - j
        return pltpu.roll(wide, SLOT + 128 - offset, 1)[:1, :SLOT]

    def tail_tag(self):
        tag = self.tag_ref[:, 2048:2176]
        if self.count < TAIL:
            tag = pltpu.roll(tag, 128 - (TAIL - self.count), 1)
        place = lax.broadcasted_iota(jnp.int32, (1, TAIL), 1)
        return jnp.where(place < self.count, tag[:1, :TAIL], 2 * (2 * self.last_pair + 3))

    def tail(self, ref):
        return jnp.concatenate(
            [ref[t * TILE + 2 * SLOT : (t + 1) * TILE, :] for t in range(TILES)], 0
        )

    def set_tail(self, ref, value):
        for t in range(TILES):
            ref[t * TILE + 2 * SLOT : (t + 1) * TILE, :] = value[t * PIECE : (t + 1) * PIECE]


def halves_of(width):
    step = min(width, 128)
    return [slice(i, i + step) for i in range(0, width, step)]


def forward_block(
    xb, tag, pair, lanes, wt_ref, biases, xt_ref, qt_ref, kt_ref, vt_ref, lse_ref, s_ref, a_ref, kn_ref
):
    width = xb.shape[0]
    xt_ref[:D, lanes] = xb.T
    for part, (out_ref, bias) in enumerate(((qt_ref, biases[0]), (kt_ref, None), (vt_ref, biases[1]))):
        p = dot(wt_ref[part * D : (part + 1) * D, :], xb, 1, 1)
        s_ref[2 * (part % 2), :, :width] = p[:SLOT]
        s_ref[2 * (part % 2) + 1, :, :width] = p[SLOT:]
        for h in range(HEADS):
            at = h % 4 * HEAD_DIM
            value = s_ref[2 * (part % 2) + h // 4, at : at + HEAD_DIM, :width]
            rows = slice(h * HEAD_DIM, (h + 1) * HEAD_DIM)
            if bias is not None:
                value = value + bias[rows]
            value = value.astype(bf16)
            if part == 0:
                value = (value.astype(f32) * HEAD_DIM**-0.5).astype(bf16)
            out_ref[rows, lanes] = value
    key_mask, query_mask = mask_parts(tag, pair)
    kn_ref[:width, :] = kt_ref[:, lanes].T
    zero = jnp.zeros((HEAD_DIM, width), bf16)
    for h in range(HEADS):
        pair_at = slice(h // 2 * 128, h // 2 * 128 + 128)
        left = jnp.concatenate([kn_ref[:width, pair_at], key_mask], 1)
        q = qt_ref[h * HEAD_DIM : (h + 1) * HEAD_DIM, lanes]
        right = jnp.concatenate([q, zero, query_mask] if h % 2 == 0 else [zero, q, query_mask], 0)
        s_ref[h, :width, :width] = dot(left, right, 1, 0)
    for h in range(HEADS):
        for half in halves_of(width):
            s = s_ref[h, :width, half]
            top = jnp.max(s, axis=0, keepdims=True)
            ex = jnp.exp(s - top)
            total = jnp.sum(ex, axis=0, keepdims=True)
            a_ref[h, :width, half] = (ex * (1.0 / total)).astype(bf16)
            at = pl.ds(pl.multiple_of(lanes.start + half.start, 128), half.stop - half.start)
            lse_ref[h : h + 1, at] = top + jnp.log(total)
    context = [
        dot(vt_ref[h * HEAD_DIM : (h + 1) * HEAD_DIM, lanes], a_ref[h, :width, :width], 1, 0).astype(bf16)
        for h in range(HEADS)
    ]
    return jnp.concatenate(context, 0).T


def backward_block(
    dr, c, tag, pair, lanes, wo, qt_ref, kt_ref, vt_ref, lse_ref, dpt_ref, s_ref, da_ref, a_ref,
    ds_ref, kn_ref, vn_ref, dct_ref, ct_ref,
):
    width = dr.shape[0]
    dct_ref[:, :width] = dot(wo, dr, 1, 1).astype(bf16)
    ct_ref[:, :width] = c.T
    kn_ref[:width, :] = kt_ref[:, lanes].T
    vn_ref[:width, :] = vt_ref[:, lanes].T
    key_mask, query_mask = mask_parts(tag, pair)
    zero = jnp.zeros((HEAD_DIM, width), bf16)

    def stack(value, h, *rest):
        return jnp.concatenate([value, zero, *rest] if h % 2 == 0 else [zero, value, *rest], 0)

    for h in range(HEADS):
        rows = slice(h * HEAD_DIM, (h + 1) * HEAD_DIM)
        pair_at = slice(h // 2 * 128, h // 2 * 128 + 128)
        left = jnp.concatenate([kn_ref[:width, pair_at], key_mask], 1)
        s_ref[h, :width, :width] = dot(left, stack(qt_ref[rows, lanes], h, query_mask), 1, 0)
        da_ref[h, :width, :width] = dot(vn_ref[:width, pair_at], stack(dct_ref[rows, :width], h), 1, 0)
    for h in range(HEADS):
        rows = slice(h * HEAD_DIM, (h + 1) * HEAD_DIM)
        for half in halves_of(width):
            at = pl.ds(pl.multiple_of(lanes.start + half.start, 128), half.stop - half.start)
            product = ct_ref[rows, half].astype(f32) * dct_ref[rows, half].astype(f32)
            delta = jnp.sum(product, axis=0, keepdims=True)
            lse = lse_ref[h : h + 1, at]
            for first in range(0, width, 64):
                keys = slice(first, first + 64)
                a = jnp.exp(s_ref[h, keys, half] - lse)
                a_ref[h, keys, half] = a.astype(bf16)
                ds_ref[h, keys, half] = (a * (da_ref[h, keys, half] - delta)).astype(bf16)
    for h in range(HEADS):
        rows = slice(h * HEAD_DIM, (h + 1) * HEAD_DIM)
        ds = ds_ref[h, :width, :width]
        dv = dot(dct_ref[rows, :width], a_ref[h, :width, :width], 1, 1)
        dk = dot(qt_ref[rows, lanes], ds, 1, 1)
        dq = dot(kt_ref[rows, lanes], ds, 1, 0) * HEAD_DIM**-0.5
        dpt_ref[rows, lanes] = dq.astype(bf16)
        dpt_ref[slice(D + h * HEAD_DIM, D + (h + 1) * HEAD_DIM), lanes] = dk.astype(bf16)
        dpt_ref[slice(2 * D + h * HEAD_DIM, 2 * D + (h + 1) * HEAD_DIM), lanes] = dv.astype(bf16)


def mean(v):
    return jnp.mean(v, axis=-1, keepdims=True)


def row_sum(v):
    return jnp.sum(v, axis=0, keepdims=True)


def flat(value):
    return value.reshape(-1, value.shape[-1])


BLOCK = 48
MAIN = 2 * SLOT


def eights(v):
    return jnp.sum(v.reshape(-1, 8, v.shape[-1]), axis=0)


def feed_tile(
    t, xs_ref, c_ref, es_ref, wo_ref, w1_ref, w2_ref, vec_ref, dh_ref, gvec_ref,
    acc_ref, n1_ref, inv_ref, yb_ref, df_ref, u_ref, g_ref, tails, awo_ref, aw1_ref, aw2_ref,
):
    first = pl.multiple_of(t * TILE, 16)
    rows = pl.ds(first, TILE)
    piece = pl.ds(pl.multiple_of(t * PIECE, 16), PIECE)
    g_tail, du_tail, df_tail, yb_tail = tails
    bo, b2, g1, c1, g2, c2 = (vec_ref[i : i + 1, :] for i in range(2, 8))
    per = FF // D
    blocks = [slice(i, i + BLOCK) for i in range(0, TILE, BLOCK)]

    def at(block):
        return pl.ds(pl.multiple_of(first + block.start, 16), BLOCK)

    def cols_of(k):
        return pl.ds(pl.multiple_of(k * D, 128), D)

    def chunk(k, start, count):
        return pl.ds(pl.multiple_of(k * TILE + start, 16), count)

    def all_chunks():
        return jnp.concatenate([g_ref[k * TILE : (k + 1) * TILE, :] for k in range(per)], 1)

    acc_ref[...] = dot(c_ref[rows, :], flat(wo_ref[...]), 1, 0)
    for block in blocks:
        h1 = xs_ref[at(block), :].astype(f32) + (acc_ref[block, :] + bo)
        mid = h1 - mean(h1)
        inv1 = lax.rsqrt(mean(mid * mid) + norm_epsilon)
        n1 = mid * inv1
        n1_ref[block, :] = n1
        inv_ref[block, :] = jnp.broadcast_to(inv1, (BLOCK, 128))
        yb_ref[block, :] = (n1 * g1 + c1).astype(bf16)

    def inner(k, carry):
        cols = cols_of(k)
        acc_ref[...] = dot(yb_ref[...], flat(w1_ref[:, :, :, cols]), 1, 0)
        b1 = vec_ref[pl.ds(8 + k, 1), :]
        for block in blocks:
            u = acc_ref[block, :] + b1
            cdf = 0.5 * (1.0 + lax.erf(u * 0.7071067811865476))
            g_ref[chunk(k, block.start, BLOCK), :] = (u * cdf).astype(bf16)
            u_ref[block, cols] = cdf + u * jnp.exp(u * u * -0.5) * 0.3989422804014327
        return carry

    lax.fori_loop(0, per, inner, 0)
    acc_ref[...] = dot(all_chunks(), flat(w2_ref[...]), 1, 0)
    sums = [jnp.zeros((8, D), f32)] * 3
    for block in blocks:
        h2 = (n1_ref[block, :] * g1 + c1) + (acc_ref[block, :] + b2)
        mid2 = h2 - mean(h2)
        inv2 = lax.rsqrt(mean(mid2 * mid2) + norm_epsilon)
        n2 = mid2 * inv2
        xs_ref[at(block), :] = (n2 * g2 + c2).astype(bf16)
        e = es_ref[at(block), :].astype(f32)
        en = e * n2
        eg = e * g2
        dh2 = (eg - mean(eg) - n2 * mean(eg * n2)) * inv2
        dh_ref[at(block), :] = dh2
        df = dh2.astype(bf16)
        df_ref[block, :] = df
        sums = [sums[0] + eights(e), sums[1] + eights(en), sums[2] + eights(df.astype(f32))]
    for i, value in zip((7, 6, 3), sums):
        gvec_ref[i : i + 1, :] += row_sum(value)
    dft = df_ref[:MAIN, :].T
    ybt = yb_ref[:MAIN, :].T
    df_tail[piece, :] = df_ref[MAIN:, :]
    yb_tail[piece, :] = yb_ref[MAIN:, :]

    def outer(k, carry):
        cols = cols_of(k)
        aw2_ref[:, cols] += dot(dft, g_ref[chunk(k, 0, MAIN), :], 1, 0)
        acc_ref[...] = dot(df_ref[...], flat(w2_ref[pl.ds(8 // per * k, 8 // per)]), 1, 1)
        at_tail = pl.ds(pl.multiple_of(k * TAIL + t * PIECE, 16), PIECE)
        g_tail[at_tail, :] = g_ref[chunk(k, MAIN, PIECE), :]
        total = jnp.zeros((8, D), f32)
        for block in blocks:
            du = (acc_ref[block, :] * u_ref[block, cols]).astype(bf16)
            g_ref[chunk(k, block.start, BLOCK), :] = du
            total = total + eights(du.astype(f32))
        gvec_ref[pl.ds(8 + k, 1), :] += row_sum(total)
        aw1_ref[:, cols] += dot(ybt, g_ref[chunk(k, 0, MAIN), :], 1, 0)
        du_tail[at_tail, :] = g_ref[chunk(k, MAIN, PIECE), :]
        return carry

    lax.fori_loop(0, per, outer, 0)
    acc_ref[...] = dot(all_chunks(), flat(w1_ref[...]), 1, 1)
    sums = [jnp.zeros((8, D), f32)] * 3
    for block in blocks:
        dy = dh_ref[at(block), :] + acc_ref[block, :]
        n1 = n1_ref[block, :]
        eg = dy * g1
        dh1 = (eg - mean(eg) - n1 * mean(eg * n1)) * inv_ref[block, :1]
        dh_ref[at(block), :] = dh1
        dr = dh1.astype(bf16)
        es_ref[at(block), :] = dr
        sums = [sums[0] + eights(dy), sums[1] + eights(dy * n1), sums[2] + eights(dr.astype(f32))]
    for i, value in zip((5, 4, 2), sums):
        gvec_ref[i : i + 1, :] += row_sum(value)
    main = pl.ds(first, MAIN)
    awo_ref[...] += dot(c_ref[main, :].T, es_ref[main, :], 1, 0)


def whole_kernel(*refs):
    refs = list(refs)

    def take(count):
        taken = refs[:count]
        del refs[:count]
        return taken

    state_in = take(15)
    tok_ref, cot_ref, seg_ref, keep_ref = take(4)
    out_ref, in_ref = take(2)
    state_out = take(15)
    copy_out = take(5)
    out_back, in_back = take(2)
    state = take(15)
    masters, firsts, seconds = state[:5], state[5:10], state[10:]
    weights = take(5)
    wa_ref, wo_ref, w1_ref, w2_ref, wv_ref = weights
    xs_ref, es_ref, xt_ref, qt_ref, kt_ref, vt_ref, c_ref, lse_ref, dh_ref, tag_ref = take(10)
    ext_ref, seg_halo, keep_halo = take(3)
    square, gvec_ref, gwa_ref, gwo_ref, grad_vec, halo_out, halo_in = take(7)
    twins, acrosses, alongs = take(5), take(5), take(5)
    parts, copies, whole_vec = take(4), take(5), take(1)[0]
    (
        state_sems, load_sems, gather_send, gather_recv, edge_send, edge_recv,
        sum_send, sum_recv, copy_send, copy_recv, store_sems,
    ) = refs
    place = Place()
    seq, seq_count = place.z, DEPTH
    is_last = seq == seq_count - 1
    slots = Slots(tag_ref, seq, seq_count)
    rows = tok_ref.shape[1]
    ext_x, ext_e = ext_ref.at[pl.ds(0, HALO + rows)], ext_ref.at[pl.ds(HALO + rows, HALO + rows)]

    loads = [pltpu.make_async_copy(state_in[i], state[i], state_sems.at[i]) for i in range(15)]
    for load in loads:
        load.start()
    big_loads = [
        pltpu.make_async_copy(src.at[0], dst.at[pl.ds(HALO, rows)], load_sems.at[i])
        for i, (src, dst) in enumerate(((tok_ref, ext_x), (cot_ref, ext_e)))
    ]
    for load in big_loads:
        load.start()
    place.greet()
    edge = [
        remote(src, dst, edge_send.at[i], edge_recv.at[i], place.in_depth(1))
        for i, (src, dst) in enumerate((
            (tok_ref.at[0, pl.ds(rows - HALO, HALO)], ext_x.at[pl.ds(0, HALO)]),
            (cot_ref.at[0, pl.ds(rows - HALO, HALO)], ext_e.at[pl.ds(0, HALO)]),
            (seg_ref.at[:, pl.ds(rows - 128, 128)], seg_halo),
            (keep_ref.at[:, pl.ds(rows - 128, 128)], keep_halo),
        ))
    ]
    gathers = [Gather(place, weights[i], gather_send.at[i], gather_recv.at[i]) for i in range(5)]

    def put(i):
        shard = turned(square, masters[4][...])[: masters[4].shape[1]] if i == 4 else masters[i][...]
        weights[i][place.batch, place.z] = shard.astype(bf16)

    for i in (0, 4, 1, 2, 3):
        loads[i].wait()
    put(0)
    gathers[0].first()
    put(4)
    gathers[4].first()
    for copy in edge:
        copy.start()
    for i in (1, 2, 3):
        put(i)
    gathers[0].second()
    gathers[4].second()
    for i in (1, 2, 3):
        gathers[i].first()
    for load in big_loads:
        load.wait()
    for copy in edge:
        copy.wait()
    tag_ref[...] = jnp.zeros_like(tag_ref)
    rim = seg_halo[...] * 2 + keep_halo[...]
    tag_ref[:, :HALO] = jnp.broadcast_to(rim[:, 128 - HALO :], (8, HALO))
    tag_ref[:, HALO : HALO + rows] = jnp.broadcast_to(seg_ref[...] * 2 + keep_ref[...], (8, rows))

    def stage_one(j, carry):
        start = first_row(j, seq)
        row = slot_row(j)
        stage_slot(ext_x, start, xs_ref, row)
        stage_slot(ext_e, start, es_ref, row)
        return carry

    lax.fori_loop(0, 8, stage_one, 0)
    slots.set_tail(xs_ref, tail_rows(ext_x, slots.count, is_last))
    slots.set_tail(es_ref, tail_rows(ext_e, slots.count, is_last))
    gathers[0].third()
    gathers[4].third()
    xt_ref[:, 8 * SLOT :] = jnp.zeros((D + AUG, 128), bf16)
    ones = lax.broadcasted_iota(jnp.int32, (AUG, LANES), 0) == 0
    xt_ref[D:, :] = jnp.where(ones, 1.0, 0.0).astype(bf16)
    gathers[0].finish()
    gathers[4].finish()

    def forward(wt_ref, s_ref, a_ref, kn_ref):
        for part in range(3):
            wt_ref[part * D : (part + 1) * D, :] = flat(
                wa_ref[:, :, :, part * D : (part + 1) * D]
            ).T
        vec_t = flat(wv_ref[...])
        biases = (vec_t[:, 0:1].astype(f32), vec_t[:, 1:2].astype(f32))

        def block(xb, tag, pair, lanes):
            return forward_block(
                xb, tag, pair, lanes, wt_ref, biases, xt_ref, qt_ref, kt_ref, vt_ref, lse_ref,
                s_ref, a_ref, kn_ref,
            )

        def one(j, carry):
            for i, step in ((1, 1), (2, 2), (3, 3)):
                pl.when(j == step)(gathers[i].second)
            for i, step in ((1, 4), (2, 5), (3, 7)):
                pl.when(j == step)(gathers[i].third)
            row = slot_row(j)
            lanes = pl.ds(pl.multiple_of(j * SLOT, 128), SLOT)
            c_ref[pl.ds(row, SLOT), :] = block(
                xs_ref[pl.ds(row, SLOT), :], slots.tag(j), 8 * seq + j, lanes
            )
            return carry

        lax.fori_loop(0, 8, one, 0)
        slots.set_tail(
            c_ref,
            block(
                slots.tail(xs_ref), slots.tail_tag(), slots.last_pair, pl.ds(8 * SLOT, TAIL)
            ),
        )

    pl.run_scoped(
        forward,
        pltpu.VMEM((3 * D, D), bf16),
        pltpu.VMEM((HEADS, SLOT, SLOT), f32),
        pltpu.VMEM((HEADS, SLOT, SLOT), bf16),
        pltpu.VMEM((SLOT, D), bf16),
    )
    for i in (1, 2, 3):
        gathers[i].finish()

    def feed_all(
        vec_ref, acc_ref, n1_ref, inv_ref, u_ref, awo_ref, aw1_ref, aw2_ref
    ):
        used = 0
        views = []
        for count in (4 * TILE, TILE, TILE, TAIL, TAIL, 4 * TAIL, 4 * TAIL):
            views.append(ext_ref.at[pl.ds(used, count)])
            used += count
        g_ref, yb_ref, df_ref, yb_tail, df_tail, g_tail, du_tail = views
        for ref in (awo_ref, aw1_ref, aw2_ref, gvec_ref):
            ref[...] = jnp.zeros_like(ref)
        vec_ref[...] = flat(wv_ref[...]).astype(f32).T[:16]

        def one(t, carry):
            feed_tile(
                t, xs_ref, c_ref, es_ref, wo_ref, w1_ref, w2_ref, vec_ref, dh_ref, gvec_ref, acc_ref,
                n1_ref, inv_ref, yb_ref, df_ref, u_ref, g_ref, (g_tail, du_tail, df_tail, yb_tail),
                awo_ref, aw1_ref, aw2_ref,
            )
            return carry

        lax.fori_loop(0, TILES, one, 0)
        for k in range(FF // D):
            cols = slice(k * D, (k + 1) * D)
            at = slice(k * TAIL, (k + 1) * TAIL)
            aw2_ref[:, cols] += dot(df_tail[...].T, g_tail[at, :], 1, 0)
            aw1_ref[:, cols] += dot(yb_tail[...].T, du_tail[at, :], 1, 0)
        awo_ref[...] += dot(slots.tail(c_ref).T, slots.tail(es_ref), 1, 0)
        def convert(i, carry):
            value = aw2_ref[:, pl.ds(pl.multiple_of(i * 128, 128), 128)].astype(bf16).T
            w2_ref[i // 2, pl.ds(i % 2 * 2, 2)] = value.reshape(2, -1, D)
            return carry

        def convert_rows(i, carry):
            value = aw1_ref[pl.ds(pl.multiple_of(i * 64, 64), 64), :].astype(bf16)
            w1_ref[i] = value.reshape(DEPTH, -1, FF)
            gwo_ref[i // 2, i % 2] = (
                awo_ref[pl.ds(pl.multiple_of(i * 64, 64), 64), :].astype(bf16).reshape(DEPTH, -1, D)
            )
            return carry

        lax.fori_loop(0, FF // 128, convert, 0)
        lax.fori_loop(0, 8, convert_rows, 0)

    pl.run_scoped(
        feed_all,
        pltpu.VMEM((16, D), f32),
        pltpu.VMEM((TILE, D), f32),
        pltpu.VMEM((TILE, D), f32),
        pltpu.VMEM((TILE, 128), f32),
        pltpu.VMEM((TILE, FF), f32),
        pltpu.VMEM((D, D), f32),
        pltpu.VMEM((D, FF), f32),
        pltpu.VMEM((D, FF), f32),
    )
    grads = [gwa_ref, gwo_ref, w1_ref, w2_ref, grad_vec]
    scatters = [
        Scatter(place, grads[i], twins[i], acrosses[i], alongs[i], sum_send.at[i], sum_recv.at[i])
        for i in range(5)
    ]
    for i in (3, 2, 1):
        scatters[i].first()
    for load in loads[5:]:
        load.wait()
    copy_gathers = [
        Gather(place, copies[i], copy_send.at[i], copy_recv.at[i], parts[i]) for i in range(4)
    ]
    copy_gathers.append(Gather(place, whole_vec, copy_send.at[4], copy_recv.at[4]))
    stores = []

    def store(src, dst):
        stores.append(pltpu.make_async_copy(src, dst, store_sems.at[len(stores)]))
        stores[-1].start()

    def update(i):
        total = scatters[i].total()
        if i == 4:
            square[...] = jnp.zeros_like(square)
            square[: total.shape[0], :] = total
            here, cols = masters[4].shape
            total = square[...].T[:here, :cols]
        new = adam_update(masters[i][...], firsts[i][...], seconds[i][...], total, learn_rates[i])
        firsts[i][...], seconds[i][...], masters[i][...] = new
        if i == 4:
            shard = turned(square, new[2])[: new[2].shape[1]].astype(bf16)
            whole_vec[place.batch, place.z] = shard
        else:
            low = new[2].astype(bf16)
            width = low.shape[1] // DEPTH
            for q in range(DEPTH):
                parts[i][q] = low[:, q * width : (q + 1) * width]
            copies[i][place.batch, place.z] = parts[i][place.z]
        copy_gathers[i].first()

    def backward(
        dpt_ref, ext_ref, s_ref, da_ref, a_ref, ds_ref, kn_ref, vn_ref, dct_ref, ct_ref
    ):
        low_ref = ext_e
        dpt_ref[:, 8 * SLOT :] = jnp.zeros((3 * D, 128), bf16)
        wo = flat(wo_ref[...])

        def block(dr, c, tag, pair, lanes):
            backward_block(
                dr, c, tag, pair, lanes, wo, qt_ref, kt_ref, vt_ref, lse_ref, dpt_ref,
                s_ref, da_ref, a_ref, ds_ref, kn_ref, vn_ref, dct_ref, ct_ref,
            )

        def one(j, carry):
            for i, step in ((3, 0), (2, 1), (1, 1)):
                pl.when(j == step)(scatters[i].second)
            for i, step in ((3, 4), (2, 6), (1, 7)):
                pl.when(j == step)(scatters[i].third)
            row = slot_row(j)
            at = pl.ds(row, SLOT)
            lanes = pl.ds(pl.multiple_of(j * SLOT, 128), SLOT)
            block(es_ref[at, :], c_ref[at, :], slots.tag(j), 8 * seq + j, lanes)
            return carry

        lax.fori_loop(0, 8, one, 0)
        block(
            slots.tail(es_ref), slots.tail(c_ref), slots.tail_tag(), slots.last_pair,
            pl.ds(8 * SLOT, TAIL),
        )
        for part in range(3):
            cols = slice(part * D, (part + 1) * D)
            g = dot(xt_ref[...], dpt_ref[cols, :], 1, 1)
            gwa_ref[:, :, :, :, cols] = g[:D].astype(bf16).reshape(PLANE, 2, DEPTH, -1, D)
            if part != 1:
                gvec_ref[part // 2 : part // 2 + 1, :] = g[D : D + 1]
        grad_vec[...] = gvec_ref[...].T.reshape(grad_vec.shape)
        scatters[0].first()
        scatters[4].first()

        def output_one(j, carry):
            at = pl.ds(slot_row(j), SLOT)
            unstage_slot(
                ext_ref, first_row(j, seq),
                lambda g: xs_ref[at, g * 128 : (g + 1) * 128].astype(f32),
            )
            return carry

        def close(value):
            @pl.when(is_last)
            def _():
                ext_ref[HALO + rows - slots.count : HALO + rows, :] = value[: slots.count]

        lax.fori_loop(0, 8, output_one, 0)
        close(slots.tail(xs_ref).astype(f32))
        scatters[0].second()
        scatters[4].second()
        low_ref[...] = ext_ref[: HALO + rows, :].astype(bf16)
        halo_out[...] = low_ref[:HALO, :]
        edge_back[0].start()
        store(low_ref.at[pl.ds(HALO, rows)], out_ref)
        wa = flat(wa_ref[...])

        def input_block(lanes):
            return dot(wa, dpt_ref[:, lanes], 1, 0).T

        def input_one(j, carry):
            for i, step in ((3, 1), (2, 3), (1, 5)):
                pl.when(j == step)(functools.partial(update, i))
            at = pl.ds(slot_row(j), SLOT)
            lanes = pl.ds(pl.multiple_of(j * SLOT, 128), SLOT)
            grad = dot(wa, dpt_ref[:, lanes], 1, 0)
            s_ref[0], s_ref[1] = grad[:SLOT], grad[SLOT:]

            def column(g):
                part = s_ref[g // 2, g % 2 * 128 : g % 2 * 128 + 128, :].T
                return part + dh_ref[at, g * 128 : (g + 1) * 128]

            unstage_slot(ext_ref, first_row(j, seq), column)
            return carry

        lax.fori_loop(0, 8, input_one, 0)
        close(input_block(pl.ds(8 * SLOT, TAIL)) + slots.tail(dh_ref))
        halo_in[...] = ext_ref[:HALO, :]
        edge_back[1].start()
        store(ext_ref.at[pl.ds(HALO, rows)], in_ref)
        scatters[0].third()
        scatters[4].third()
        for i in (3, 2, 1):
            copy_gathers[i].second()
        update(4)
        update(0)
        for i in (3, 2, 1):
            copy_gathers[i].third()
        for i in (4, 0):
            copy_gathers[i].second()
        for i in range(5):
            for n, kind in enumerate((firsts, seconds, masters)):
                store(kind[i], state_out[5 * n + i])
        for i in (4, 0):
            copy_gathers[i].third()
        for i in (3, 2, 1, 4, 0):
            copy_gathers[i].finish()
            scatters[i].finish()
        here = masters[4].shape[0]
        mine = jnp.concatenate([whole_vec[seq * 2 + q // 4, q % 4] for q in range(8)], 0)
        copies[4][...] = mine.astype(f32).T[:here].astype(bf16)
        for i in range(5):
            store(copies[i], copy_out[i])
        for copy in stores:
            copy.wait()
        for copy in edge_back:
            copy.wait()

    edge_back = [
        remote(halo_out, out_back, edge_send.at[4], edge_recv.at[4], place.in_depth(3)),
        remote(halo_in, in_back, edge_send.at[5], edge_recv.at[5], place.in_depth(3)),
    ]
    pl.run_scoped(
        backward,
        pltpu.VMEM((3 * D, LANES), bf16),
        pltpu.VMEM((HALO + rows + 16, D), f32),
        pltpu.VMEM((HEADS, SLOT, SLOT), f32),
        pltpu.VMEM((HEADS, SLOT, SLOT), f32),
        pltpu.VMEM((HEADS, SLOT, SLOT), bf16),
        pltpu.VMEM((HEADS, SLOT, SLOT), bf16),
        pltpu.VMEM((SLOT, D), bf16),
        pltpu.VMEM((SLOT, D), bf16),
        pltpu.VMEM((D, SLOT), bf16),
        pltpu.VMEM((D, SLOT), bf16),
    )


def whole(masters, firsts, seconds, tokens, cotangent, segment, keep):
    shape = jax.ShapeDtypeStruct
    vmem = pl.BlockSpec(memory_space=pltpu.VMEM)
    hbm = pl.BlockSpec(memory_space=pl.ANY)
    state = (*masters, *firsts, *seconds)
    rows = tokens.shape[1]
    r = masters[0].shape[0]
    shapes = ((r, 3 * D), (r, D), (r, FF), (4 * r, D))
    copies = [((8, DEPTH, s[0], s[1] // DEPTH), bf16) for s in shapes]
    copies.append(((masters[4].shape[0], 128), bf16))
    halos = [((HALO, D), bf16), ((HALO, D), f32)]
    out_shape = [
        shape((rows, D), bf16),
        shape((rows, D), f32),
        *[shape(s.shape, f32) for i in range(3) for s in masters],
        *[shape(*c) for c in copies],
        *[shape(*h) for h in halos],
    ]
    five = [(s, bf16) for s in shapes] + [((r, 128), f32)]
    tall = ROWS
    scratch = [pltpu.VMEM(s.shape, f32) for s in state]
    scratch += [pltpu.VMEM((8, DEPTH) + s, bf16) for s in (*shapes, (r, 128))]
    scratch += [
        pltpu.VMEM((tall, D), bf16),
        pltpu.VMEM((tall, D), bf16),
        pltpu.VMEM((D + AUG, LANES), bf16),
        pltpu.VMEM((D, LANES), bf16),
        pltpu.VMEM((D, LANES), bf16),
        pltpu.VMEM((D, LANES), bf16),
        pltpu.VMEM((tall, D), bf16),
        pltpu.VMEM((HEADS, LANES), f32),
        pltpu.VMEM((tall, D), f32),
        pltpu.VMEM((8, LANES), jnp.int32),
        pltpu.VMEM((2 * (HALO + rows), D), bf16),
        pltpu.VMEM((1, 128), jnp.int32),
        pltpu.VMEM((1, 128), jnp.int32),
        pltpu.VMEM((128, 128), f32),
        pltpu.VMEM((128, D), f32),
        pltpu.VMEM((PLANE, 2, DEPTH) + shapes[0], bf16),
        pltpu.VMEM((PLANE, 2, DEPTH) + shapes[1], bf16),
        pltpu.VMEM((PLANE, 2, DEPTH, r, 128), f32),
        *[pltpu.VMEM(*h) for h in halos],
    ]
    for lead in ((PLANE, DEPTH), (3, DEPTH), (3,)):
        scratch += [pltpu.VMEM(lead + s, t) for s, t in five]
    scratch += [pltpu.VMEM((DEPTH, s[0], s[1] // DEPTH), bf16) for s in shapes]
    scratch += [pltpu.VMEM(*c) for c in copies]
    scratch.append(pltpu.VMEM((8, DEPTH, r, 128), bf16))
    dma = pltpu.SemaphoreType.DMA
    scratch += [
        dma((15,)), dma((2,)), dma((5, 10)), dma((5, 10)), dma((6,)), dma((6,)),
        dma((5, 10)), dma((5, 10)), dma((5, 10)), dma((5, 10)), dma((22,)),
    ]
    return pl.pallas_call(
        whole_kernel,
        out_shape=out_shape,
        in_specs=[hbm] * 17 + [vmem] * 2,
        out_specs=[hbm] * 22 + [vmem] * 2,
        scratch_shapes=scratch,
        compiler_params=pltpu.CompilerParams(
            collective_id=0, has_side_effects=True, vmem_limit_bytes=63 * MIB
        ),
        name="whole",
    )(*state, tokens, cotangent, segment, keep)


LAST_PART = 496


def last_kernel(*refs):
    results, backs, ends = refs[:22], refs[22:24], refs[24:46]
    lows, (load_sems, store_sems) = refs[46:68], refs[68:]
    rows = results[0].shape[0]
    seq = lax.axis_index("seq")
    rim = pl.ds(rows - HALO, HALO)
    places = [(i, rim) for i in range(2)]
    places += [
        (i, pl.ds(first, LAST_PART))
        for i in range(2)
        for first in range(0, rows - HALO, LAST_PART)
    ]
    places += [(i, pl.ds(0, results[i].shape[0])) for i in range(2, 22)]
    loads = [
        pltpu.make_async_copy(results[i].at[at], lows[i].at[at], load_sems.at[n])
        for n, (i, at) in enumerate(places)
    ]
    stores = [
        pltpu.make_async_copy(lows[i].at[at], ends[i].at[at], store_sems.at[n])
        for n, (i, at) in enumerate(places)
    ]
    for load in loads:
        load.start()
    place = lax.broadcasted_iota(jnp.int32, (HALO, 1), 0)
    theirs = (place >= HALO - 8 * (seq + 1)) & (seq < lax.axis_size("seq") - 1)
    for n, (i, at) in enumerate(places):
        loads[n].wait()
        if n < 2:
            own = lows[i][rim, :].astype(f32)
            lows[i][rim, :] = jnp.where(theirs, backs[i][...].astype(f32), own).astype(lows[i].dtype)
        stores[n].start()
    for store in stores:
        store.wait()


def last(results, out_back, in_back):
    shape = jax.ShapeDtypeStruct
    vmem = pl.BlockSpec(memory_space=pltpu.VMEM)
    hbm = pl.BlockSpec(memory_space=pl.ANY)
    count = 22 + 2 * ((results[0].shape[0] - HALO) // LAST_PART)
    return pl.pallas_call(
        last_kernel,
        out_shape=[shape(a.shape, a.dtype) for a in results],
        in_specs=[hbm] * 22 + [vmem, vmem],
        out_specs=[hbm] * 22,
        scratch_shapes=[pltpu.VMEM(a.shape, a.dtype) for a in results]
        + [pltpu.SemaphoreType.DMA((count,)), pltpu.SemaphoreType.DMA((count,))],
        compiler_params=pltpu.CompilerParams(vmem_limit_bytes=60 * MIB),
        name="last",
    )(*results, out_back, in_back)


def on_device(
    tokens,
    cotangent,
    segment,
    keep_mask,
    attn_master,
    out_master,
    in_master,
    back_master,
    vec_master,
    attn_first,
    out_first,
    in_first,
    back_first,
    vec_first,
    attn_second,
    out_second,
    in_second,
    back_second,
    vec_second,
):
    seq = lax.axis_index("seq")
    seq_count = lax.axis_size("seq")
    both = ("batch", "seq")
    rows = tokens.shape[1]
    masters = (attn_master, out_master, in_master, back_master, vec_master)
    firsts = (attn_first, out_first, in_first, back_first, vec_first)
    seconds = (attn_second, out_second, in_second, back_second, vec_second)
    direct = seq_count == DEPTH and lax.axis_size("batch") == 2 * PLANE
    forward = [(i, i + 1) for i in range(seq_count - 1)]
    backward = [(i + 1, i) for i in range(seq_count - 1)]
    if direct:
        *results, out_back, grad_back = whole(
            masters, firsts, seconds, tokens, cotangent, segment, keep_mask
        )
        for i in range(17, 21):
            results[i] = results[i].reshape(-1, results[i].shape[-1])
        ends = last(results, out_back, grad_back)
        return (ends[0][None], ends[1][None], *ends[2:])
    low = [w.astype(bf16) for w in masters]
    low[4] = jnp.pad(low[4].T, ((0, 0), (0, 128 - low[4].shape[0])))
    attn_w, out_w, in_w, back_w, vec_t = (
        lax.all_gather(w, both, axis=0, tiled=True) for w in low
    )
    x_halo, e_halo, seg_halo, keep_halo = (
        lax.ppermute(a, "seq", forward)
        for a in (
            tokens[0, rows - HALO :], cotangent[0, rows - HALO :],
            segment[:, rows - 128 :], keep_mask[:, rows - 128 :],
        )
    )
    xs, es, xt, qt, kt, vt, c, lse = attn_forward(
        seq_count, tokens, cotangent, x_halo, e_halo, segment, keep_mask, seg_halo, keep_halo,
        attn_w, vec_t,
    )
    z, dh, dr, gwo, gw1, gw2, gvec, gb1 = feed(xs, c, es, out_w, in_w, back_w, vec_t)
    out, out_halo, grad_in, grad_in_halo, gwa, gbias = attn_backward(
        seq_count, xt, qt, kt, vt, lse, dr, dh, z, attn_w, out_w
    )
    grads = (gwa, gwo, gw1, gw2)
    grad_vec = jnp.concatenate(
        [gbias[:1, :D], gbias[:1, 2 * D :], gvec[2:8], gb1[0].reshape(FF // D, D)], 0
    )
    sums = [lax.psum_scatter(g.astype(f32), both, scatter_dimension=0, tiled=True) for g in grads]
    sums.append(lax.psum_scatter(grad_vec, both, scatter_dimension=1, tiled=True))
    new = [
        adam_update(masters[i], firsts[i], seconds[i], sums[i], learn_rates[i]) for i in range(5)
    ]

    def own_columns(i):
        whole = lax.all_gather(new[i][2].astype(bf16), both, axis=1 if i == 4 else 0, tiled=True)
        count = whole.shape[1] // seq_count
        return lax.dynamic_slice_in_dim(whole, seq * count, count, 1)

    results = [out, grad_in] + [new[i][part] for part in range(3) for i in range(5)]
    results += [own_columns(i) for i in range(5)]
    out_back = lax.ppermute(out_halo, "seq", backward)
    grad_back = lax.ppermute(grad_in_halo, "seq", backward)
    ends = last(results, out_back, grad_back)
    return (ends[0][None], ends[1][None], *ends[2:])


def solution(mesh):
    stream = P("batch", "seq", None)
    rows = P(("batch", "seq"), None)
    vector = P(None, ("batch", "seq"))
    five = (rows, rows, rows, rows, vector)
    return jax.shard_map(
        on_device,
        mesh=mesh,
        in_specs=(stream, stream, P("batch", "seq"), P("batch", "seq")) + five * 3,
        out_specs=(stream, stream) + five * 3 + (P(None, "seq"),) * 5,
        check_vma=False,
    )
```

```python
import functools

import jax
import jax.numpy as jnp
from jax import lax
from jax.experimental import pallas as pl
from jax.experimental.pallas import tpu as pltpu
from jax.sharding import PartitionSpec as P

D = 512
HEADS = 8
HEAD_DIM = 64
FF = 2048
STEP = 10
PAIR = 255
SLOT = 256
HALO = 64
TILES = 4
TAIL = 64
PIECE = TAIL // TILES
TILE = 2 * SLOT + PIECE
ROWS = TILES * TILE
LANES = 8 * SLOT + 128
AUG = 16
MIB = 1 << 20

norm_epsilon = 1e-05
beta_first = 0.9
beta_second = 0.999
adam_epsilon = 1e-08
weight_decay = 0.01
learn_rates = (0.03, 0.2, 0.03, 0.02, 0.5)
big = 1e30

f32 = jnp.float32
bf16 = jnp.bfloat16


def dot(a, b, ca, cb):
    return lax.dot_general(a, b, (((ca,), (cb,)), ((), ())), preferred_element_type=f32)


def adam_update(master, first, second, gradient, rate):
    first_new = beta_first * first + (1.0 - beta_first) * gradient
    second_new = beta_second * second + (1.0 - beta_second) * gradient * gradient
    first_hat = first_new / (1.0 - beta_first**STEP)
    second_hat = second_new / (1.0 - beta_second**STEP)
    master_new = master - rate * (
        first_hat / (jnp.sqrt(second_hat) + adam_epsilon) + weight_decay * master
    )
    return (first_new, second_new, master_new)


def slot_row(j):
    return pl.multiple_of((j // 2) * TILE + (j % 2) * SLOT, 16)


def first_row(j, seq):
    return HALO + PAIR * j - 8 * seq


def staged(ref, start):
    base = pl.multiple_of((start // 16) * 16, 16)
    rest = start - base
    wide = ref[pl.ds(base, SLOT + 16), :].astype(f32)
    wide = jnp.where(rest >= 8, wide[8:], wide[:-8])
    shift = rest % 8
    groups = (SLOT + 8) // 8
    wide = wide.reshape(groups, 8, D)
    turned = pltpu.roll(wide, lax.rem(8 - shift, 8), 1)
    place = lax.broadcasted_iota(jnp.int32, (groups - 1, 8, D), 1)
    block = jnp.where(place < 8 - shift, turned[:-1], turned[1:]).reshape(SLOT, D)
    row = lax.broadcasted_iota(jnp.int32, (SLOT, D), 0)
    return jnp.where(row < PAIR, block, 0.0).astype(bf16)


def unstage(ref, start, block):
    base = pl.multiple_of((start // 8) * 8, 8)
    shift = start - base
    turned = pltpu.roll(block.reshape(SLOT // 8, 8, D), shift, 1)
    place = lax.broadcasted_iota(jnp.int32, (1, 8, D), 1)
    keep = ref[pl.ds(base, 8), :].reshape(1, 8, D)
    low = jnp.concatenate([keep, turned], 0)
    high = jnp.concatenate([turned, turned[-1:]], 0)
    place = lax.broadcasted_iota(jnp.int32, low.shape, 1)
    ref[pl.ds(base, SLOT + 8), :] = jnp.where(place < shift, low, high).reshape(SLOT + 8, D)


def stage_slot(ref, start, out_ref, row):
    base = pl.multiple_of((start // 16) * 16, 16)
    rest = start - base
    shift = rest % 8
    groups = (SLOT + 8) // 8
    place = lax.broadcasted_iota(jnp.int32, (groups - 1, 8, 128), 1)
    number = lax.broadcasted_iota(jnp.int32, (groups - 1, 8, 128), 0) * 8 + place
    for g in range(D // 128):
        cols = slice(g * 128, (g + 1) * 128)
        wide = ref[pl.ds(base, SLOT + 16), cols].astype(f32)
        wide = jnp.where(rest >= 8, wide[8:], wide[:-8]).reshape(groups, 8, 128)
        turned = pltpu.roll(wide, lax.rem(8 - shift, 8), 1)
        block = jnp.where(place < 8 - shift, turned[:-1], turned[1:])
        block = jnp.where(number < PAIR, block, 0.0)
        out_ref[pl.ds(row, SLOT), cols] = block.reshape(SLOT, 128).astype(bf16)


def unstage_slot(ref, start, column):
    base = pl.multiple_of((start // 8) * 8, 8)
    shift = start - base
    for g in range(D // 128):
        cols = slice(g * 128, (g + 1) * 128)
        turned = pltpu.roll(column(g).reshape(SLOT // 8, 8, 128), shift, 1)
        keep = ref[pl.ds(base, 8), cols].reshape(1, 8, 128)
        low = jnp.concatenate([keep, turned], 0)
        high = jnp.concatenate([turned, turned[-1:]], 0)
        place = lax.broadcasted_iota(jnp.int32, low.shape, 1)
        ref[pl.ds(base, SLOT + 8), cols] = jnp.where(place < shift, low, high).reshape(SLOT + 8, 128)


def tail_rows(ref, count, is_last):
    kept = ref[HALO + 2048 - count : HALO + 2048, :].astype(f32)
    if count < TAIL:
        kept = jnp.concatenate([kept, jnp.zeros((TAIL - count, D), f32)], 0)
    return jnp.where(is_last, kept, 0.0).astype(bf16)


def tag_rows(tag, pair):
    width = tag.shape[1]
    number = tag // 2 - 2 * pair
    kept = tag % 2
    row = lax.broadcasted_iota(jnp.int32, (AUG, width), 0)
    match = row == number
    query = jnp.where(match, 1.0, 0.0).astype(bf16)
    key = jnp.where(match & (kept == 1), 0.0, -big)
    key = jnp.where(row < 4, key, 0.0).astype(bf16)
    return query, key


def attn_forward_kernel(
    seq_count, tok_ref, cot_ref, tok_halo, cot_halo, seg_ref, keep_ref, seg_halo, keep_halo,
    w_ref, vec_ref,
    xs_ref, es_ref, xt_ref, qt_ref, kt_ref, vt_ref, c_ref, lse_ref,
    wt_ref, x_ref, e_ref, tag_ref, sems,
):
    seq = lax.axis_index("seq")
    is_last = seq == seq_count - 1
    rows = tok_ref.shape[1]
    loads = []
    for i, (whole, halo, ext) in enumerate(((tok_ref, tok_halo, x_ref), (cot_ref, cot_halo, e_ref))):
        loads.append(pltpu.make_async_copy(whole.at[0], ext.at[pl.ds(HALO, rows)], sems.at[2 * i]))
        loads.append(pltpu.make_async_copy(halo, ext.at[pl.ds(0, HALO)], sems.at[2 * i + 1]))
    for load in loads:
        load.start()
    for part in range(3):
        wt_ref[part * D : (part + 1) * D, :] = w_ref[:, part * D : (part + 1) * D].T
    tag_ref[...] = jnp.zeros_like(tag_ref)
    edge = seg_halo[...] * 2 + keep_halo[...]
    tag_ref[:, :HALO] = jnp.broadcast_to(edge[:, 128 - HALO :], (8, HALO))
    tag_ref[:, HALO : HALO + rows] = jnp.broadcast_to(seg_ref[...] * 2 + keep_ref[...], (8, rows))
    query_bias = vec_ref[:, 0:1].astype(f32)
    value_bias = vec_ref[:, 1:2].astype(f32)
    for load in loads:
        load.wait()

    def block(xb, tag, pair, lane, width):
        lanes = pl.ds(lane, width)
        xt_ref[:D, lanes] = xb.T
        q = dot(wt_ref[:D, :], xb, 1, 1) + query_bias
        q = (q.astype(bf16).astype(f32) * HEAD_DIM**-0.5).astype(bf16)
        k = dot(wt_ref[D : 2 * D, :], xb, 1, 1).astype(bf16)
        v = (dot(wt_ref[2 * D :, :], xb, 1, 1) + value_bias).astype(bf16)
        query_tag, key_tag = tag_rows(tag, pair)
        vt_ref[:, lanes] = v
        context = []
        for h in range(HEADS):
            rows = slice(h * HEAD_DIM, (h + 1) * HEAD_DIM)
            qh = jnp.concatenate([q[rows], query_tag], 0)
            kh = jnp.concatenate([k[rows], key_tag], 0)
            qt_ref[h, :, lanes] = qh
            kt_ref[h, :, lanes] = kh
            s = dot(kh, qh, 0, 0)
            top = jnp.max(s, axis=0, keepdims=True)
            ex = jnp.exp(s - top)
            total = jnp.sum(ex, axis=0, keepdims=True)
            lse_ref[h : h + 1, lanes] = top + jnp.log(total)
            a = (ex * (1.0 / total)).astype(bf16)
            context.append(dot(v[rows], a, 1, 0))
        return jnp.concatenate(context, 0).astype(bf16).T

    def one(j, carry):
        start = first_row(j, seq)
        row = slot_row(j)
        xb = staged(x_ref, start)
        xs_ref[pl.ds(row, SLOT), :] = xb
        es_ref[pl.ds(row, SLOT), :] = staged(e_ref, start)
        wide = tag_ref[:, pl.ds(pl.multiple_of(j * SLOT, 128), SLOT + 128)]
        width = SLOT + 128
        tag = pltpu.roll(wide, width - (start - j * SLOT), 1)[:1, :SLOT]
        c_ref[pl.ds(row, SLOT), :] = block(
            xb, tag, 8 * seq + j, pl.multiple_of(j * SLOT, 128), SLOT
        )
        return carry

    lax.fori_loop(0, 8, one, 0)
    count = 8 * seq_count
    xt_ref[:, 8 * SLOT :] = jnp.zeros((D + AUG, 128), bf16)
    xb = tail_rows(x_ref, count, is_last)
    eb = tail_rows(e_ref, count, is_last)
    tag = tag_ref[:1, 2048:2176]
    tag = pltpu.roll(tag_ref[:, 2048:2176], 128 - (64 - count), 1)[:1, :TAIL] if count < 64 else tag[:, :TAIL]
    place = lax.broadcasted_iota(jnp.int32, (1, TAIL), 1)
    tag = jnp.where(place < count, tag, (2 * 8 * seq_count + 3) * 2)
    cb = block(xb, tag, 8 * seq_count, 8 * SLOT, TAIL)
    for t in range(TILES):
        rows = slice(t * PIECE, (t + 1) * PIECE)
        at = slice(t * TILE + 2 * SLOT, (t + 1) * TILE)
        xs_ref[at, :] = xb[rows]
        es_ref[at, :] = eb[rows]
        c_ref[at, :] = cb[rows]
    ones = lax.broadcasted_iota(jnp.int32, (AUG, LANES), 0) == 0
    xt_ref[D:, :] = jnp.where(ones, 1.0, 0.0).astype(bf16)


def attn_forward(seq_count, tokens, cotangent, *others):
    shape = jax.ShapeDtypeStruct
    vmem = pl.BlockSpec(memory_space=pltpu.VMEM)
    hbm = pl.BlockSpec(memory_space=pl.ANY)
    return pl.pallas_call(
        functools.partial(attn_forward_kernel, seq_count),
        out_shape=(
            shape((ROWS, D), bf16),
            shape((ROWS, D), bf16),
            shape((D + AUG, LANES), bf16),
            shape((HEADS, HEAD_DIM + AUG, LANES), bf16),
            shape((HEADS, HEAD_DIM + AUG, LANES), bf16),
            shape((D, LANES), bf16),
            shape((ROWS, D), bf16),
            shape((HEADS, LANES), f32),
        ),
        in_specs=[hbm, hbm] + [vmem] * len(others),
        out_specs=[vmem] * 8,
        scratch_shapes=[
            pltpu.VMEM((3 * D, D), bf16),
            pltpu.VMEM((HALO + tokens.shape[1], D), bf16),
            pltpu.VMEM((HALO + tokens.shape[1], D), bf16),
            pltpu.VMEM((8, LANES), jnp.int32),
            pltpu.SemaphoreType.DMA((4,)),
        ],
        compiler_params=pltpu.CompilerParams(vmem_limit_bytes=56 * MIB),
        name="attn_forward",
    )(tokens, cotangent, *others)


def feed_kernel(
    xs_ref, c_ref, es_ref, wo_ref, w1_ref, w2_ref, vect_ref,
    z_ref, dh_ref, dr_ref, gwo_ref, gw1_ref, gw2_ref, gvec_ref, gb1_ref,
    u_ref, g_ref, awo_ref, aw1_ref, aw2_ref, vec_ref,
):
    step = pl.program_id(0)

    @pl.when(step == 0)
    def _():
        awo_ref[...] = jnp.zeros_like(awo_ref)
        aw1_ref[...] = jnp.zeros_like(aw1_ref)
        aw2_ref[...] = jnp.zeros_like(aw2_ref)
        gvec_ref[...] = jnp.zeros_like(gvec_ref)
        gb1_ref[...] = jnp.zeros_like(gb1_ref)
        vec_ref[...] = vect_ref[...].astype(f32).T

    def mean(v):
        return jnp.mean(v, axis=-1, keepdims=True)

    def row_sum(v):
        return jnp.sum(v, axis=0, keepdims=True)

    bo, b2, g1, c1, g2, c2 = (vec_ref[i : i + 1, :] for i in range(2, 8))
    h1 = xs_ref[...].astype(f32) + (dot(c_ref[...], wo_ref[...], 1, 0) + bo)
    mid = h1 - mean(h1)
    inv1 = lax.rsqrt(mean(mid * mid) + norm_epsilon)
    n1 = mid * inv1
    y = n1 * g1 + c1
    yb = y.astype(bf16)
    chunk = D
    f = None
    for k in range(FF // chunk):
        cols = slice(k * chunk, (k + 1) * chunk)
        u = dot(yb, w1_ref[:, cols], 1, 0) + vec_ref[8 + k : 9 + k, :]
        cdf = 0.5 * (1.0 + lax.erf(u * 0.7071067811865476))
        gk = (u * cdf).astype(bf16)
        u_ref[:, cols] = cdf + u * jnp.exp(u * u * -0.5) * 0.3989422804014327
        g_ref[:, cols] = gk
        part = dot(gk, w2_ref[cols, :], 1, 0)
        f = part if f is None else f + part
    h2 = y + (f + b2)
    mid2 = h2 - mean(h2)
    inv2 = lax.rsqrt(mean(mid2 * mid2) + norm_epsilon)
    n2 = mid2 * inv2
    z_ref[...] = (n2 * g2 + c2).astype(bf16)
    e = es_ref[...].astype(f32)
    gvec_ref[7:8, :] += row_sum(e)
    gvec_ref[6:7, :] += row_sum(e * n2)
    eg = e * g2
    dh2 = (eg - mean(eg) - n2 * mean(eg * n2)) * inv2
    df = dh2.astype(bf16)
    gvec_ref[3:4, :] += row_sum(df.astype(f32))
    dft = df.T
    ybt = yb.T
    dy = dh2
    for k in range(FF // chunk):
        cols = slice(k * chunk, (k + 1) * chunk)
        aw2_ref[:, cols] += dot(dft, g_ref[:, cols], 1, 0)
        dg = dot(df, w2_ref[cols, :], 1, 1)
        du = (dg * u_ref[:, cols]).astype(bf16)
        gb1_ref[:1, cols] += row_sum(du.astype(f32))
        aw1_ref[:, cols] += dot(ybt, du, 1, 0)
        dy = dy + dot(du, w1_ref[:, cols], 1, 1)
    gvec_ref[5:6, :] += row_sum(dy)
    gvec_ref[4:5, :] += row_sum(dy * n1)
    eg = dy * g1
    dh1 = (eg - mean(eg) - n1 * mean(eg * n1)) * inv1
    dh_ref[...] = dh1
    dr = dh1.astype(bf16)
    dr_ref[...] = dr
    gvec_ref[2:3, :] += row_sum(dr.astype(f32))
    awo_ref[...] += dot(c_ref[...].T, dr, 1, 0)

    @pl.when(step == TILES - 1)
    def _():
        gwo_ref[...] = awo_ref[...].astype(bf16)
        gw1_ref[...] = aw1_ref[...].astype(bf16)
        for k in range(FF // chunk):
            cols = slice(k * chunk, (k + 1) * chunk)
            gw2_ref[cols, :] = aw2_ref[:, cols].astype(bf16).T


def feed(xs, c, es, wo, w1, w2, vec_t):
    shape = jax.ShapeDtypeStruct
    tile = pl.BlockSpec((TILE, D), lambda i: (i, 0))

    def whole(*dims):
        return pl.BlockSpec(dims, lambda i: (0,) * len(dims), pipeline_mode=pl.Buffered(1))

    return pl.pallas_call(
        feed_kernel,
        grid=(TILES,),
        out_shape=(
            shape((ROWS, D), bf16),
            shape((ROWS, D), f32),
            shape((ROWS, D), bf16),
            shape((D, D), bf16),
            shape((D, FF), bf16),
            shape((FF, D), bf16),
            shape((8, D), f32),
            shape((8, FF), f32),
        ),
        in_specs=[tile, tile, tile, whole(D, D), whole(D, FF), whole(FF, D), whole(D, 128)],
        out_specs=[tile, tile, tile, whole(D, D), whole(D, FF), whole(FF, D), whole(8, D), whole(8, FF)],
        scratch_shapes=[
            pltpu.VMEM((TILE, FF), f32),
            pltpu.VMEM((TILE, FF), bf16),
            pltpu.VMEM((D, D), f32),
            pltpu.VMEM((D, FF), f32),
            pltpu.VMEM((D, FF), f32),
            pltpu.VMEM((128, D), f32),
        ],
        compiler_params=pltpu.CompilerParams(vmem_limit_bytes=60 * MIB),
        name="feed",
    )(xs, c, es, wo, w1, w2, vec_t)


def attn_backward_kernel(
    seq_count, xt_ref, qt_ref, kt_ref, vt_ref, lse_ref, dr_ref, dh_ref, z_ref, w_ref, wo_ref,
    out_ref, out_halo_ref, in_ref, in_halo_ref, gwa_ref, gbias_ref,
    dpt_ref, ext_ref,
):
    seq = lax.axis_index("seq")
    is_last = seq == seq_count - 1

    def block(dr, lane, width):
        lanes = pl.ds(lane, width)
        dct = dot(wo_ref[...], dr, 1, 1).astype(bf16)
        for h in range(HEADS):
            rows = slice(h * HEAD_DIM, (h + 1) * HEAD_DIM)
            qh = qt_ref[h, :, lanes]
            kh = kt_ref[h, :, lanes]
            vh = vt_ref[rows, lanes]
            dch = dct[rows]
            a = jnp.exp(dot(kh, qh, 0, 0) - lse_ref[h : h + 1, lanes])
            da = dot(vh, dch, 0, 0)
            ada = a * da
            ds = (ada - a * jnp.sum(ada, axis=0, keepdims=True)).astype(bf16)
            dv = dot(dch, a.astype(bf16), 1, 1)
            dk = dot(qh[:HEAD_DIM], ds, 1, 1)
            dq = dot(kh[:HEAD_DIM], ds, 1, 0) * HEAD_DIM**-0.5
            dpt_ref[rows, lanes] = dq.astype(bf16)
            dpt_ref[slice(D + h * HEAD_DIM, D + (h + 1) * HEAD_DIM), lanes] = dk.astype(bf16)
            dpt_ref[slice(2 * D + h * HEAD_DIM, 2 * D + (h + 1) * HEAD_DIM), lanes] = dv.astype(bf16)
        return dot(w_ref[...], dpt_ref[:, lanes], 1, 0).T

    dpt_ref[:, 8 * SLOT :] = jnp.zeros((3 * D, 128), bf16)

    def one(j, carry):
        row = slot_row(j)
        grad = block(dr_ref[pl.ds(row, SLOT), :], pl.multiple_of(j * SLOT, 128), SLOT)
        unstage(ext_ref, first_row(j, seq), grad + dh_ref[pl.ds(row, SLOT), :])
        return carry

    lax.fori_loop(0, 8, one, 0)
    count = 8 * seq_count

    def tail_of(ref):
        return jnp.concatenate(
            [ref[t * TILE + 2 * SLOT : (t + 1) * TILE, :] for t in range(TILES)], 0
        )

    grad = block(tail_of(dr_ref), 8 * SLOT, TAIL) + tail_of(dh_ref)

    @pl.when(is_last)
    def _():
        ext_ref[HALO + 2048 - count : HALO + 2048, :] = grad[:count]

    in_halo_ref[...] = ext_ref[:HALO, :]
    in_ref[...] = ext_ref[HALO : HALO + 2048, :]

    def two(j, carry):
        unstage(ext_ref, first_row(j, seq), z_ref[pl.ds(slot_row(j), SLOT), :].astype(f32))
        return carry

    lax.fori_loop(0, 8, two, 0)
    tail = tail_of(z_ref).astype(f32)

    @pl.when(is_last)
    def _():
        ext_ref[HALO + 2048 - count : HALO + 2048, :] = tail[:count]

    out_halo_ref[...] = ext_ref[:HALO, :].astype(bf16)
    out_ref[...] = ext_ref[HALO : HALO + 2048, :].astype(bf16)
    for part in range(3):
        cols = slice(part * D, (part + 1) * D)
        g = dot(xt_ref[...], dpt_ref[cols, :], 1, 1)
        gwa_ref[:, cols] = g[:D].astype(bf16)
        gbias_ref[:, cols] = g[D : D + 8]


def attn_backward(seq_count, *operands):
    shape = jax.ShapeDtypeStruct
    return pl.pallas_call(
        functools.partial(attn_backward_kernel, seq_count),
        out_shape=(
            shape((2048, D), bf16),
            shape((HALO, D), bf16),
            shape((2048, D), f32),
            shape((HALO, D), f32),
            shape((D, 3 * D), bf16),
            shape((8, 3 * D), f32),
        ),
        in_specs=[pl.BlockSpec(memory_space=pltpu.VMEM)] * len(operands),
        out_specs=[pl.BlockSpec(memory_space=pltpu.VMEM)] * 6,
        scratch_shapes=[
            pltpu.VMEM((3 * D, LANES), bf16),
            pltpu.VMEM((HALO + 2048 + 16, D), f32),
        ],
        compiler_params=pltpu.CompilerParams(vmem_limit_bytes=60 * MIB),
        name="attn_backward",
    )(*operands)


MESH = pl.DeviceIdType.MESH
PLANE = 4
DEPTH = 4


class Place:
    def __init__(self):
        self.batch = lax.axis_index("batch")
        self.z = lax.axis_index("seq")
        self.core = self.batch % 2
        self.plane = self.batch // 2

    def plane_at(self, k):
        x = (self.plane % 2 + k % 2) % 2
        y = (self.plane // 2 + k // 2) % 2
        return y * 2 + x

    def in_plane(self, k):
        return {"batch": self.plane_at(k) * 2 + self.core, "seq": self.z}

    def depth_at(self, k):
        return (self.z + k) % DEPTH

    def in_depth(self, k):
        return {"batch": self.batch, "seq": self.depth_at(k)}

    def sibling(self):
        return {"batch": self.plane * 2 + 1 - self.core, "seq": self.z}

    def greet(self):
        barrier = pltpu.get_barrier_semaphore()
        for k in range(1, 4):
            pl.semaphore_signal(barrier, inc=1, device_id=self.in_plane(k), device_id_type=MESH)
            pl.semaphore_signal(barrier, inc=1, device_id=self.in_depth(k), device_id_type=MESH)
        pl.semaphore_signal(barrier, inc=1, device_id=self.sibling(), device_id_type=MESH)
        pl.semaphore_wait(barrier, 7)


def remote(src, dst, send, recv, device):
    return pltpu.make_async_remote_copy(
        src_ref=src, dst_ref=dst, send_sem=send, recv_sem=recv, device_id=device, device_id_type=MESH
    )


LOW, HIGH = pl.ds(0, DEPTH // 2), pl.ds(DEPTH // 2, DEPTH // 2)


class Gather:
    def __init__(self, place, whole, send, recv, parts=None):
        self.place, self.whole, self.send, self.recv, self.parts = place, whole, send, recv, parts

    def block(self, k):
        return self.whole.at[self.place.plane_at(k) * 2 + self.place.core]

    def copy(self, n, source, target, device):
        return remote(source, target, self.send.at[n], self.recv.at[n], device)

    def depth(self, k):
        at = self.place
        here = self.whole.at[at.batch, at.z]
        source = here if self.parts is None else self.parts.at[at.depth_at(k)]
        return self.copy(k - 1, source, here, at.in_depth(k))

    def plane(self, k):
        return self.copy(2 + k, self.block(0), self.block(0), self.place.in_plane(k))

    def across(self, k):
        half = self.block(k).at[LOW if k == 1 else HIGH]
        return self.copy(4 + k, half, half, self.place.in_plane(3 - k))

    def core(self, k):
        return self.copy(7 + k, self.block(k), self.block(k), self.place.sibling())

    def first(self):
        for k in range(1, 4):
            self.depth(k).start()

    def second(self):
        for k in range(1, 4):
            self.depth(k).wait_recv()
        for k in (1, 2):
            self.plane(k).start()
        self.core(0).start()

    def third(self):
        for k in (1, 2):
            self.plane(k).wait_recv()
            self.across(k).start()
            self.core(k).start()

    def fourth(self):
        for k in (1, 2):
            self.across(k).wait_recv()
        self.core(3).start()

    def finish(self):
        for k in range(4):
            self.core(k).wait_recv()
        for k in range(1, 4):
            self.depth(k).wait_send()
        for k in (1, 2):
            self.plane(k).wait_send()
            self.across(k).wait_send()
        for k in range(4):
            self.core(k).wait_send()


class Scatter:
    def __init__(self, place, grad, twin, near, far, along, send, recv):
        self.place, self.grad, self.twin = place, grad, twin
        self.near, self.far, self.along, self.send, self.recv = near, far, along, send, recv
        shape = grad.shape
        if len(shape) == 4:
            self.at = lambda p, c: grad.at[p * 2 + c]
        else:
            self.at = lambda p, c: grad.at[p, c]

    def block(self, k):
        return self.at(self.place.plane_at(k), self.place.core)

    def copy(self, n, source, target, device):
        return remote(source, target, self.send.at[n], self.recv.at[n], device)

    def core(self, p):
        source = self.at(p, 1 - self.place.core)
        return self.copy(p, source, self.twin.at[p], self.place.sibling())

    def plane(self, n):
        k, half = ((1, LOW), (3, LOW), (2, HIGH), (3, HIGH))[n]
        target = self.near.at[n]
        return self.copy(4 + n, self.block(k).at[half], target, self.place.in_plane(1 + n // 2))

    def across(self, n):
        k, half = ((2, LOW), (1, HIGH))[n]
        return self.copy(8 + n, self.block(k).at[half], self.far.at[n], self.place.in_plane(2 - n))

    def depth(self, k):
        source = self.block(0).at[self.place.depth_at(k)]
        return self.copy(9 + k, source, self.along.at[k - 1], self.place.in_depth(k))

    def first(self):
        for p in range(PLANE):
            self.core(p).start()

    def second(self):
        for p in range(PLANE):
            self.core(p).wait_recv()
        own = self.place.core

        def one(p, carry):
            mine = self.at(p, own)
            mine[...] = (mine[...].astype(f32) + self.twin[p].astype(f32)).astype(mine.dtype)
            return carry

        lax.fori_loop(0, PLANE, one, 0)
        for n in range(4):
            self.plane(n).start()

    def third(self):
        for n in range(4):
            self.plane(n).wait_recv()
        for n, (k, base) in enumerate(((2, 0), (1, 2))):
            mine = self.block(k)

            def one(q, carry):
                total = mine[base + q].astype(f32) + self.near[2 * n + 1, q].astype(f32)
                mine[base + q] = total.astype(mine.dtype)
                return carry

            lax.fori_loop(0, 2, one, 0)
            self.across(n).start()

    def fourth(self):
        for n in range(2):
            self.across(n).wait_recv()
        mine = self.block(0)

        def one(i, carry):
            n, q = i // 2, i % 2
            total = mine[i].astype(f32) + self.near[2 * n, q].astype(f32) + self.far[n, q].astype(f32)
            mine[i] = total.astype(mine.dtype)
            return carry

        lax.fori_loop(0, DEPTH, one, 0)
        for k in range(1, 4):
            self.depth(k).start()

    def total(self):
        for k in range(1, 4):
            self.depth(k).wait_recv()
        total = self.block(0)[self.place.z].astype(f32)
        for k in range(3):
            total = total + self.along[k].astype(f32)
        return total

    def finish(self):
        for p in range(PLANE):
            self.core(p).wait_send()
        for n in range(4):
            self.plane(n).wait_send()
        for n in range(2):
            self.across(n).wait_send()
        for k in range(1, 4):
            self.depth(k).wait_send()


def turned(ref, value):
    ref[...] = jnp.zeros_like(ref)
    ref[: value.shape[0], : value.shape[1]] = value
    return ref[...].T


def heads_of(block, h):
    return block[h * HEAD_DIM : (h + 1) * HEAD_DIM]


def only_head(block, h):
    zero = jnp.zeros((HEAD_DIM, block.shape[1]), block.dtype)
    mine = heads_of(block, h)
    return jnp.concatenate([mine, zero] if h % 2 == 0 else [zero, mine], 0)


def pair_of(block, h):
    at = h // 2 * 2 * HEAD_DIM
    return block[:, at : at + 2 * HEAD_DIM]


def mask_parts(tag, pair):
    query, key = tag_rows(tag, pair)
    width = tag.shape[1]
    zero = jnp.zeros((128 - AUG, width), bf16)
    return jnp.concatenate([key, zero], 0).T, jnp.concatenate([query, zero], 0)


class Slots:
    def __init__(self, tag_ref, seq, seq_count):
        self.tag_ref, self.seq, self.count = tag_ref, seq, 8 * seq_count
        self.last_pair = 8 * seq_count

    def tag(self, j):
        wide = self.tag_ref[:, pl.ds(pl.multiple_of(j * SLOT, 128), SLOT + 128)]
        offset = HALO - 8 * self.seq - j
        return pltpu.roll(wide, SLOT + 128 - offset, 1)[:1, :SLOT]

    def tail_tag(self):
        tag = self.tag_ref[:, 2048:2176]
        if self.count < TAIL:
            tag = pltpu.roll(tag, 128 - (TAIL - self.count), 1)
        place = lax.broadcasted_iota(jnp.int32, (1, TAIL), 1)
        return jnp.where(place < self.count, tag[:1, :TAIL], 2 * (2 * self.last_pair + 3))

    def tail(self, ref):
        return jnp.concatenate(
            [ref[t * TILE + 2 * SLOT : (t + 1) * TILE, :] for t in range(TILES)], 0
        )

    def set_tail(self, ref, value):
        for t in range(TILES):
            ref[t * TILE + 2 * SLOT : (t + 1) * TILE, :] = value[t * PIECE : (t + 1) * PIECE]


def halves_of(width):
    step = min(width, 128)
    return [slice(i, i + step) for i in range(0, width, step)]


def forward_block(
    xb, tag, pair, lanes, wt_ref, biases, xt_ref, qt_ref, kt_ref, vt_ref, lse_ref, s_ref, a_ref, kn_ref
):
    width = xb.shape[0]
    xt_ref[:D, lanes] = xb.T
    for part, (out_ref, bias) in enumerate(((qt_ref, biases[0]), (kt_ref, None), (vt_ref, biases[1]))):
        p = dot(wt_ref[part * D : (part + 1) * D, :], xb, 1, 1)
        s_ref[2 * (part % 2), :, :width] = p[:SLOT]
        s_ref[2 * (part % 2) + 1, :, :width] = p[SLOT:]
        for h in range(HEADS):
            at = h % 4 * HEAD_DIM
            value = s_ref[2 * (part % 2) + h // 4, at : at + HEAD_DIM, :width]
            rows = slice(h * HEAD_DIM, (h + 1) * HEAD_DIM)
            if bias is not None:
                value = value + bias[rows]
            value = value.astype(bf16)
            if part == 0:
                value = (value.astype(f32) * HEAD_DIM**-0.5).astype(bf16)
            out_ref[rows, lanes] = value
    key_mask, query_mask = mask_parts(tag, pair)
    kn_ref[:width, :] = kt_ref[:, lanes].T
    zero = jnp.zeros((HEAD_DIM, width), bf16)
    for h in range(HEADS):
        pair_at = slice(h // 2 * 128, h // 2 * 128 + 128)
        left = jnp.concatenate([kn_ref[:width, pair_at], key_mask], 1)
        q = qt_ref[h * HEAD_DIM : (h + 1) * HEAD_DIM, lanes]
        right = jnp.concatenate([q, zero, query_mask] if h % 2 == 0 else [zero, q, query_mask], 0)
        s_ref[h, :width, :width] = dot(left, right, 1, 0)
    for h in range(HEADS):
        for half in halves_of(width):
            s = s_ref[h, :width, half]
            top = jnp.max(s, axis=0, keepdims=True)
            ex = jnp.exp(s - top)
            total = jnp.sum(ex, axis=0, keepdims=True)
            a_ref[h, :width, half] = (ex * (1.0 / total)).astype(bf16)
            at = pl.ds(pl.multiple_of(lanes.start + half.start, 128), half.stop - half.start)
            lse_ref[h : h + 1, at] = top + jnp.log(total)
    context = [
        dot(vt_ref[h * HEAD_DIM : (h + 1) * HEAD_DIM, lanes], a_ref[h, :width, :width], 1, 0).astype(bf16)
        for h in range(HEADS)
    ]
    return jnp.concatenate(context, 0).T


def backward_block(
    dr, c, tag, pair, lanes, wo, qt_ref, kt_ref, vt_ref, lse_ref, dpt_ref, s_ref, da_ref, a_ref,
    ds_ref, kn_ref, vn_ref, dct_ref, ct_ref,
):
    width = dr.shape[0]
    dct_ref[:, :width] = dot(wo, dr, 1, 1).astype(bf16)
    ct_ref[:, :width] = c.T
    kn_ref[:width, :] = kt_ref[:, lanes].T
    vn_ref[:width, :] = vt_ref[:, lanes].T
    key_mask, query_mask = mask_parts(tag, pair)
    zero = jnp.zeros((HEAD_DIM, width), bf16)

    def stack(value, h, *rest):
        return jnp.concatenate([value, zero, *rest] if h % 2 == 0 else [zero, value, *rest], 0)

    for h in range(HEADS):
        rows = slice(h * HEAD_DIM, (h + 1) * HEAD_DIM)
        pair_at = slice(h // 2 * 128, h // 2 * 128 + 128)
        left = jnp.concatenate([kn_ref[:width, pair_at], key_mask], 1)
        s_ref[h, :width, :width] = dot(left, stack(qt_ref[rows, lanes], h, query_mask), 1, 0)
        da_ref[h, :width, :width] = dot(vn_ref[:width, pair_at], stack(dct_ref[rows, :width], h), 1, 0)
    for h in range(HEADS):
        rows = slice(h * HEAD_DIM, (h + 1) * HEAD_DIM)
        for half in halves_of(width):
            at = pl.ds(pl.multiple_of(lanes.start + half.start, 128), half.stop - half.start)
            product = ct_ref[rows, half].astype(f32) * dct_ref[rows, half].astype(f32)
            delta = jnp.sum(product, axis=0, keepdims=True)
            lse = lse_ref[h : h + 1, at]
            for first in range(0, width, 64):
                keys = slice(first, first + 64)
                a = jnp.exp(s_ref[h, keys, half] - lse)
                a_ref[h, keys, half] = a.astype(bf16)
                ds_ref[h, keys, half] = (a * (da_ref[h, keys, half] - delta)).astype(bf16)
    for h in range(HEADS):
        rows = slice(h * HEAD_DIM, (h + 1) * HEAD_DIM)
        ds = ds_ref[h, :width, :width]
        dv = dot(dct_ref[rows, :width], a_ref[h, :width, :width], 1, 1)
        dk = dot(qt_ref[rows, lanes], ds, 1, 1)
        dq = dot(kt_ref[rows, lanes], ds, 1, 0) * HEAD_DIM**-0.5
        dpt_ref[rows, lanes] = dq.astype(bf16)
        dpt_ref[slice(D + h * HEAD_DIM, D + (h + 1) * HEAD_DIM), lanes] = dk.astype(bf16)
        dpt_ref[slice(2 * D + h * HEAD_DIM, 2 * D + (h + 1) * HEAD_DIM), lanes] = dv.astype(bf16)


def mean(v):
    return jnp.mean(v, axis=-1, keepdims=True)


def row_sum(v):
    return jnp.sum(v, axis=0, keepdims=True)


def flat(value):
    return value.reshape(-1, value.shape[-1])


BLOCK = 48
MAIN = 2 * SLOT


def eights(v):
    return jnp.sum(v.reshape(-1, 8, v.shape[-1]), axis=0)


def feed_tile(
    t, xs_ref, c_ref, es_ref, wo_ref, w1_ref, w2_ref, vec_ref, dh_ref, gvec_ref,
    acc_ref, n1_ref, inv_ref, yb_ref, df_ref, u_ref, g_ref, tails, awo_ref, aw1_ref, aw2_ref,
):
    first = pl.multiple_of(t * TILE, 16)
    rows = pl.ds(first, TILE)
    piece = pl.ds(pl.multiple_of(t * PIECE, 16), PIECE)
    g_tail, du_tail, df_tail, yb_tail = tails
    bo, b2, g1, c1, g2, c2 = (vec_ref[i : i + 1, :] for i in range(2, 8))
    per = FF // D
    blocks = [slice(i, i + BLOCK) for i in range(0, TILE, BLOCK)]

    def at(block):
        return pl.ds(pl.multiple_of(first + block.start, 16), BLOCK)

    def cols_of(k):
        return pl.ds(pl.multiple_of(k * D, 128), D)

    def chunk(k, start, count):
        return pl.ds(pl.multiple_of(k * TILE + start, 16), count)

    def all_chunks():
        return jnp.concatenate([g_ref[k * TILE : (k + 1) * TILE, :] for k in range(per)], 1)

    acc_ref[...] = dot(c_ref[rows, :], flat(wo_ref[...]), 1, 0)
    for block in blocks:
        h1 = xs_ref[at(block), :].astype(f32) + (acc_ref[block, :] + bo)
        mid = h1 - mean(h1)
        inv1 = lax.rsqrt(mean(mid * mid) + norm_epsilon)
        n1 = mid * inv1
        n1_ref[block, :] = n1
        inv_ref[block, :] = jnp.broadcast_to(inv1, (BLOCK, 128))
        yb_ref[block, :] = (n1 * g1 + c1).astype(bf16)

    def inner(k, carry):
        cols = cols_of(k)
        acc_ref[...] = dot(yb_ref[...], flat(w1_ref[:, :, :, cols]), 1, 0)
        b1 = vec_ref[pl.ds(8 + k, 1), :]
        for block in blocks:
            u = acc_ref[block, :] + b1
            cdf = 0.5 * (1.0 + lax.erf(u * 0.7071067811865476))
            g_ref[chunk(k, block.start, BLOCK), :] = (u * cdf).astype(bf16)
            u_ref[block, cols] = cdf + u * jnp.exp(u * u * -0.5) * 0.3989422804014327
        return carry

    lax.fori_loop(0, per, inner, 0)
    acc_ref[...] = dot(all_chunks(), flat(w2_ref[...]), 1, 0)
    sums = [jnp.zeros((8, D), f32)] * 3
    for block in blocks:
        h2 = (n1_ref[block, :] * g1 + c1) + (acc_ref[block, :] + b2)
        mid2 = h2 - mean(h2)
        inv2 = lax.rsqrt(mean(mid2 * mid2) + norm_epsilon)
        n2 = mid2 * inv2
        xs_ref[at(block), :] = (n2 * g2 + c2).astype(bf16)
        e = es_ref[at(block), :].astype(f32)
        en = e * n2
        eg = e * g2
        dh2 = (eg - mean(eg) - n2 * mean(eg * n2)) * inv2
        dh_ref[at(block), :] = dh2
        df = dh2.astype(bf16)
        df_ref[block, :] = df
        sums = [sums[0] + eights(e), sums[1] + eights(en), sums[2] + eights(df.astype(f32))]
    for i, value in zip((7, 6, 3), sums):
        gvec_ref[i : i + 1, :] += row_sum(value)
    dft = df_ref[:MAIN, :].T
    ybt = yb_ref[:MAIN, :].T
    df_tail[piece, :] = df_ref[MAIN:, :]
    yb_tail[piece, :] = yb_ref[MAIN:, :]

    def outer(k, carry):
        cols = cols_of(k)
        aw2_ref[:, cols] += dot(dft, g_ref[chunk(k, 0, MAIN), :], 1, 0)
        acc_ref[...] = dot(df_ref[...], flat(w2_ref[pl.ds(8 // per * k, 8 // per)]), 1, 1)
        at_tail = pl.ds(pl.multiple_of(k * TAIL + t * PIECE, 16), PIECE)
        g_tail[at_tail, :] = g_ref[chunk(k, MAIN, PIECE), :]
        total = jnp.zeros((8, D), f32)
        for block in blocks:
            du = (acc_ref[block, :] * u_ref[block, cols]).astype(bf16)
            g_ref[chunk(k, block.start, BLOCK), :] = du
            total = total + eights(du.astype(f32))
        gvec_ref[pl.ds(8 + k, 1), :] += row_sum(total)
        aw1_ref[:, cols] += dot(ybt, g_ref[chunk(k, 0, MAIN), :], 1, 0)
        du_tail[at_tail, :] = g_ref[chunk(k, MAIN, PIECE), :]
        return carry

    lax.fori_loop(0, per, outer, 0)
    acc_ref[...] = dot(all_chunks(), flat(w1_ref[...]), 1, 1)
    sums = [jnp.zeros((8, D), f32)] * 3
    for block in blocks:
        dy = dh_ref[at(block), :] + acc_ref[block, :]
        n1 = n1_ref[block, :]
        eg = dy * g1
        dh1 = (eg - mean(eg) - n1 * mean(eg * n1)) * inv_ref[block, :1]
        dh_ref[at(block), :] = dh1
        dr = dh1.astype(bf16)
        es_ref[at(block), :] = dr
        sums = [sums[0] + eights(dy), sums[1] + eights(dy * n1), sums[2] + eights(dr.astype(f32))]
    for i, value in zip((5, 4, 2), sums):
        gvec_ref[i : i + 1, :] += row_sum(value)
    main = pl.ds(first, MAIN)
    awo_ref[...] += dot(c_ref[main, :].T, es_ref[main, :], 1, 0)


def whole_kernel(*refs):
    refs = list(refs)

    def take(count):
        taken = refs[:count]
        del refs[:count]
        return taken

    state_in = take(15)
    tok_ref, cot_ref, seg_ref, keep_ref = take(4)
    out_ref, in_ref = take(2)
    state_out = take(15)
    copy_out = take(5)
    out_back, in_back = take(2)
    state = take(15)
    masters, firsts, seconds = state[:5], state[5:10], state[10:]
    weights = take(5)
    wa_ref, wo_ref, w1_ref, w2_ref, wv_ref = weights
    xs_ref, es_ref, xt_ref, qt_ref, kt_ref, vt_ref, c_ref, lse_ref, dh_ref, tag_ref = take(10)
    ext_ref, seg_halo, keep_halo = take(3)
    square, gvec_ref, gwa_ref, gwo_ref, grad_vec, halo_out, halo_in = take(7)
    twins, nears, fars, alongs = take(5), take(5), take(5), take(5)
    parts, copies, whole_vec = take(4), take(5), take(1)[0]
    (
        state_sems, load_sems, gather_send, gather_recv, edge_send, edge_recv,
        sum_send, sum_recv, copy_send, copy_recv, store_sems,
    ) = refs
    place = Place()
    seq, seq_count = place.z, DEPTH
    is_last = seq == seq_count - 1
    slots = Slots(tag_ref, seq, seq_count)
    rows = tok_ref.shape[1]
    ext_x, ext_e = ext_ref.at[pl.ds(0, HALO + rows)], ext_ref.at[pl.ds(HALO + rows, HALO + rows)]

    loads = [pltpu.make_async_copy(state_in[i], state[i], state_sems.at[i]) for i in range(15)]
    for load in loads:
        load.start()
    big_loads = [
        pltpu.make_async_copy(src.at[0], dst.at[pl.ds(HALO, rows)], load_sems.at[i])
        for i, (src, dst) in enumerate(((tok_ref, ext_x), (cot_ref, ext_e)))
    ]
    for load in big_loads:
        load.start()
    place.greet()
    edge = [
        remote(src, dst, edge_send.at[i], edge_recv.at[i], place.in_depth(1))
        for i, (src, dst) in enumerate((
            (tok_ref.at[0, pl.ds(rows - HALO, HALO)], ext_x.at[pl.ds(0, HALO)]),
            (cot_ref.at[0, pl.ds(rows - HALO, HALO)], ext_e.at[pl.ds(0, HALO)]),
            (seg_ref.at[:, pl.ds(rows - 128, 128)], seg_halo),
            (keep_ref.at[:, pl.ds(rows - 128, 128)], keep_halo),
        ))
    ]
    gathers = [Gather(place, weights[i], gather_send.at[i], gather_recv.at[i]) for i in range(5)]

    def put(i):
        shard = turned(square, masters[4][...])[: masters[4].shape[1]] if i == 4 else masters[i][...]
        weights[i][place.batch, place.z] = shard.astype(bf16)

    for i in (0, 4, 1, 2, 3):
        loads[i].wait()
    put(0)
    gathers[0].first()
    put(4)
    gathers[4].first()
    for copy in edge:
        copy.start()
    for i in (1, 2, 3):
        put(i)
    gathers[0].second()
    gathers[4].second()
    for i in (1, 2):
        gathers[i].first()
    for load in big_loads:
        load.wait()
    for copy in edge:
        copy.wait()
    tag_ref[...] = jnp.zeros_like(tag_ref)
    rim = seg_halo[...] * 2 + keep_halo[...]
    tag_ref[:, :HALO] = jnp.broadcast_to(rim[:, 128 - HALO :], (8, HALO))
    tag_ref[:, HALO : HALO + rows] = jnp.broadcast_to(seg_ref[...] * 2 + keep_ref[...], (8, rows))

    def stage_one(j, carry):
        start = first_row(j, seq)
        row = slot_row(j)
        stage_slot(ext_x, start, xs_ref, row)
        stage_slot(ext_e, start, es_ref, row)
        return carry

    lax.fori_loop(0, 8, stage_one, 0)
    slots.set_tail(xs_ref, tail_rows(ext_x, slots.count, is_last))
    slots.set_tail(es_ref, tail_rows(ext_e, slots.count, is_last))
    gathers[0].third()
    gathers[4].third()
    gathers[3].first()
    xt_ref[:, 8 * SLOT :] = jnp.zeros((D + AUG, 128), bf16)
    ones = lax.broadcasted_iota(jnp.int32, (AUG, LANES), 0) == 0
    xt_ref[D:, :] = jnp.where(ones, 1.0, 0.0).astype(bf16)
    gathers[0].fourth()
    gathers[4].fourth()
    for i in (1, 2):
        gathers[i].second()
    gathers[0].finish()
    gathers[4].finish()

    def forward(wt_ref, s_ref, a_ref, kn_ref):
        for part in range(3):
            wt_ref[part * D : (part + 1) * D, :] = flat(
                wa_ref[:, :, :, part * D : (part + 1) * D]
            ).T
        vec_t = flat(wv_ref[...])
        biases = (vec_t[:, 0:1].astype(f32), vec_t[:, 1:2].astype(f32))

        def block(xb, tag, pair, lanes):
            return forward_block(
                xb, tag, pair, lanes, wt_ref, biases, xt_ref, qt_ref, kt_ref, vt_ref, lse_ref,
                s_ref, a_ref, kn_ref,
            )

        def one(j, carry):
            for step, event in (
                (1, gathers[1].third), (1, gathers[3].second), (2, gathers[2].third),
                (3, gathers[1].fourth), (4, gathers[2].fourth), (5, gathers[3].third),
                (7, gathers[3].fourth),
            ):
                pl.when(j == step)(event)
            row = slot_row(j)
            lanes = pl.ds(pl.multiple_of(j * SLOT, 128), SLOT)
            c_ref[pl.ds(row, SLOT), :] = block(
                xs_ref[pl.ds(row, SLOT), :], slots.tag(j), 8 * seq + j, lanes
            )
            return carry

        lax.fori_loop(0, 8, one, 0)
        slots.set_tail(
            c_ref,
            block(
                slots.tail(xs_ref), slots.tail_tag(), slots.last_pair, pl.ds(8 * SLOT, TAIL)
            ),
        )

    pl.run_scoped(
        forward,
        pltpu.VMEM((3 * D, D), bf16),
        pltpu.VMEM((HEADS, SLOT, SLOT), f32),
        pltpu.VMEM((HEADS, SLOT, SLOT), bf16),
        pltpu.VMEM((SLOT, D), bf16),
    )
    for i in (1, 2, 3):
        gathers[i].finish()

    def feed_all(
        vec_ref, acc_ref, n1_ref, inv_ref, u_ref, awo_ref, aw1_ref, aw2_ref
    ):
        used = 0
        views = []
        for count in (4 * TILE, TILE, TILE, TAIL, TAIL, 4 * TAIL, 4 * TAIL):
            views.append(ext_ref.at[pl.ds(used, count)])
            used += count
        g_ref, yb_ref, df_ref, yb_tail, df_tail, g_tail, du_tail = views
        for ref in (awo_ref, aw1_ref, aw2_ref, gvec_ref):
            ref[...] = jnp.zeros_like(ref)
        vec_ref[...] = flat(wv_ref[...]).astype(f32).T[:16]

        def one(t, carry):
            feed_tile(
                t, xs_ref, c_ref, es_ref, wo_ref, w1_ref, w2_ref, vec_ref, dh_ref, gvec_ref, acc_ref,
                n1_ref, inv_ref, yb_ref, df_ref, u_ref, g_ref, (g_tail, du_tail, df_tail, yb_tail),
                awo_ref, aw1_ref, aw2_ref,
            )
            return carry

        lax.fori_loop(0, TILES, one, 0)
        for k in range(FF // D):
            cols = slice(k * D, (k + 1) * D)
            at = slice(k * TAIL, (k + 1) * TAIL)
            aw2_ref[:, cols] += dot(df_tail[...].T, g_tail[at, :], 1, 0)
            aw1_ref[:, cols] += dot(yb_tail[...].T, du_tail[at, :], 1, 0)
        awo_ref[...] += dot(slots.tail(c_ref).T, slots.tail(es_ref), 1, 0)
        def convert(i, carry):
            value = aw2_ref[:, pl.ds(pl.multiple_of(i * 128, 128), 128)].astype(bf16).T
            w2_ref[i // 2, pl.ds(i % 2 * 2, 2)] = value.reshape(2, -1, D)
            return carry

        def convert_rows(i, carry):
            value = aw1_ref[pl.ds(pl.multiple_of(i * 64, 64), 64), :].astype(bf16)
            w1_ref[i] = value.reshape(DEPTH, -1, FF)
            gwo_ref[i // 2, i % 2] = (
                awo_ref[pl.ds(pl.multiple_of(i * 64, 64), 64), :].astype(bf16).reshape(DEPTH, -1, D)
            )
            return carry

        lax.fori_loop(0, FF // 128, convert, 0)
        lax.fori_loop(0, 8, convert_rows, 0)

    pl.run_scoped(
        feed_all,
        pltpu.VMEM((16, D), f32),
        pltpu.VMEM((TILE, D), f32),
        pltpu.VMEM((TILE, D), f32),
        pltpu.VMEM((TILE, 128), f32),
        pltpu.VMEM((TILE, FF), f32),
        pltpu.VMEM((D, D), f32),
        pltpu.VMEM((D, FF), f32),
        pltpu.VMEM((D, FF), f32),
    )
    grads = [gwa_ref, gwo_ref, w1_ref, w2_ref, grad_vec]
    scatters = [
        Scatter(
            place, grads[i], twins[i], nears[i], fars[i], alongs[i], sum_send.at[i], sum_recv.at[i]
        )
        for i in range(5)
    ]
    for i in (3, 2, 1):
        scatters[i].first()
    for load in loads[5:]:
        load.wait()
    copy_gathers = [
        Gather(place, copies[i], copy_send.at[i], copy_recv.at[i], parts[i]) for i in range(4)
    ]
    copy_gathers.append(Gather(place, whole_vec, copy_send.at[4], copy_recv.at[4]))
    stores = []

    def store(src, dst):
        stores.append(pltpu.make_async_copy(src, dst, store_sems.at[len(stores)]))
        stores[-1].start()

    def update(i):
        total = scatters[i].total()
        if i == 4:
            square[...] = jnp.zeros_like(square)
            square[: total.shape[0], :] = total
            here, cols = masters[4].shape
            total = square[...].T[:here, :cols]
        new = adam_update(masters[i][...], firsts[i][...], seconds[i][...], total, learn_rates[i])
        firsts[i][...], seconds[i][...], masters[i][...] = new
        if i == 4:
            shard = turned(square, new[2])[: new[2].shape[1]].astype(bf16)
            whole_vec[place.batch, place.z] = shard
        else:
            low = new[2].astype(bf16)
            width = low.shape[1] // DEPTH
            for q in range(DEPTH):
                parts[i][q] = low[:, q * width : (q + 1) * width]
            copies[i][place.batch, place.z] = parts[i][place.z]
        copy_gathers[i].first()

    def backward(
        dpt_ref, ext_ref, s_ref, da_ref, a_ref, ds_ref, kn_ref, vn_ref, dct_ref, ct_ref
    ):
        low_ref = ext_e
        dpt_ref[:, 8 * SLOT :] = jnp.zeros((3 * D, 128), bf16)
        wo = flat(wo_ref[...])

        def block(dr, c, tag, pair, lanes):
            backward_block(
                dr, c, tag, pair, lanes, wo, qt_ref, kt_ref, vt_ref, lse_ref, dpt_ref,
                s_ref, da_ref, a_ref, ds_ref, kn_ref, vn_ref, dct_ref, ct_ref,
            )

        def one(j, carry):
            for step, event in (
                (0, scatters[3].second), (1, scatters[2].second), (2, scatters[3].third),
                (3, scatters[3].fourth), (3, scatters[1].second), (4, scatters[2].third),
                (5, scatters[2].fourth), (5, scatters[1].third), (6, scatters[1].fourth),
                (6, functools.partial(update, 3)), (7, functools.partial(update, 2)),
            ):
                pl.when(j == step)(event)
            row = slot_row(j)
            at = pl.ds(row, SLOT)
            lanes = pl.ds(pl.multiple_of(j * SLOT, 128), SLOT)
            block(es_ref[at, :], c_ref[at, :], slots.tag(j), 8 * seq + j, lanes)
            return carry

        lax.fori_loop(0, 8, one, 0)
        block(
            slots.tail(es_ref), slots.tail(c_ref), slots.tail_tag(), slots.last_pair,
            pl.ds(8 * SLOT, TAIL),
        )
        for part in range(3):
            cols = slice(part * D, (part + 1) * D)
            g = dot(xt_ref[...], dpt_ref[cols, :], 1, 1)
            gwa_ref[:, :, :, :, cols] = g[:D].astype(bf16).reshape(PLANE, 2, DEPTH, -1, D)
            if part != 1:
                gvec_ref[part // 2 : part // 2 + 1, :] = g[D : D + 1]
        grad_vec[...] = gvec_ref[...].T.reshape(grad_vec.shape)
        scatters[0].first()
        scatters[4].first()

        def output_one(j, carry):
            at = pl.ds(slot_row(j), SLOT)
            unstage_slot(
                ext_ref, first_row(j, seq),
                lambda g: xs_ref[at, g * 128 : (g + 1) * 128].astype(f32),
            )
            return carry

        def close(value):
            @pl.when(is_last)
            def _():
                ext_ref[HALO + rows - slots.count : HALO + rows, :] = value[: slots.count]

        lax.fori_loop(0, 8, output_one, 0)
        close(slots.tail(xs_ref).astype(f32))
        scatters[0].second()
        scatters[4].second()
        copy_gathers[3].second()
        copy_gathers[2].second()
        update(1)
        low_ref[...] = ext_ref[: HALO + rows, :].astype(bf16)
        halo_out[...] = low_ref[:HALO, :]
        edge_back[0].start()
        store(low_ref.at[pl.ds(HALO, rows)], out_ref)
        wa = flat(wa_ref[...])

        def input_block(lanes):
            return dot(wa, dpt_ref[:, lanes], 1, 0).T

        def input_one(j, carry):
            for step, event in (
                (1, copy_gathers[3].third), (2, copy_gathers[2].third), (2, copy_gathers[1].second),
                (3, copy_gathers[3].fourth), (3, scatters[0].third), (3, scatters[4].third),
                (4, copy_gathers[2].fourth), (5, copy_gathers[1].third), (6, scatters[0].fourth),
                (6, scatters[4].fourth), (7, copy_gathers[1].fourth),
            ):
                pl.when(j == step)(event)
            at = pl.ds(slot_row(j), SLOT)
            lanes = pl.ds(pl.multiple_of(j * SLOT, 128), SLOT)
            grad = dot(wa, dpt_ref[:, lanes], 1, 0)
            s_ref[0], s_ref[1] = grad[:SLOT], grad[SLOT:]

            def column(g):
                part = s_ref[g // 2, g % 2 * 128 : g % 2 * 128 + 128, :].T
                return part + dh_ref[at, g * 128 : (g + 1) * 128]

            unstage_slot(ext_ref, first_row(j, seq), column)
            return carry

        lax.fori_loop(0, 8, input_one, 0)
        close(input_block(pl.ds(8 * SLOT, TAIL)) + slots.tail(dh_ref))
        halo_in[...] = ext_ref[:HALO, :]
        edge_back[1].start()
        store(ext_ref.at[pl.ds(HALO, rows)], in_ref)
        update(4)
        update(0)
        for i in range(5):
            for n, kind in enumerate((firsts, seconds, masters)):
                store(kind[i], state_out[5 * n + i])
        for i in (4, 0):
            copy_gathers[i].second()
        for i in (4, 0):
            copy_gathers[i].third()
        for i in (4, 0):
            copy_gathers[i].fourth()
        for i in (3, 2, 1, 4, 0):
            copy_gathers[i].finish()
            scatters[i].finish()
        here = masters[4].shape[0]
        mine = jnp.concatenate([whole_vec[seq * 2 + q // 4, q % 4] for q in range(8)], 0)
        copies[4][...] = mine.astype(f32).T[:here].astype(bf16)
        for i in range(5):
            store(copies[i], copy_out[i])
        for copy in stores:
            copy.wait()
        for copy in edge_back:
            copy.wait()

    edge_back = [
        remote(halo_out, out_back, edge_send.at[4], edge_recv.at[4], place.in_depth(3)),
        remote(halo_in, in_back, edge_send.at[5], edge_recv.at[5], place.in_depth(3)),
    ]
    pl.run_scoped(
        backward,
        pltpu.VMEM((3 * D, LANES), bf16),
        pltpu.VMEM((HALO + rows + 16, D), f32),
        pltpu.VMEM((HEADS, SLOT, SLOT), f32),
        pltpu.VMEM((HEADS, SLOT, SLOT), f32),
        pltpu.VMEM((HEADS, SLOT, SLOT), bf16),
        pltpu.VMEM((HEADS, SLOT, SLOT), bf16),
        pltpu.VMEM((SLOT, D), bf16),
        pltpu.VMEM((SLOT, D), bf16),
        pltpu.VMEM((D, SLOT), bf16),
        pltpu.VMEM((D, SLOT), bf16),
    )


def whole(masters, firsts, seconds, tokens, cotangent, segment, keep):
    shape = jax.ShapeDtypeStruct
    vmem = pl.BlockSpec(memory_space=pltpu.VMEM)
    hbm = pl.BlockSpec(memory_space=pl.ANY)
    state = (*masters, *firsts, *seconds)
    rows = tokens.shape[1]
    r = masters[0].shape[0]
    shapes = ((r, 3 * D), (r, D), (r, FF), (4 * r, D))
    copies = [((8, DEPTH, s[0], s[1] // DEPTH), bf16) for s in shapes]
    copies.append(((masters[4].shape[0], 128), bf16))
    halos = [((HALO, D), bf16), ((HALO, D), f32)]
    out_shape = [
        shape((rows, D), bf16),
        shape((rows, D), f32),
        *[shape(s.shape, f32) for i in range(3) for s in masters],
        *[shape(*c) for c in copies],
        *[shape(*h) for h in halos],
    ]
    five = [(s, bf16) for s in shapes] + [((r, 128), f32)]
    tall = ROWS
    scratch = [pltpu.VMEM(s.shape, f32) for s in state]
    scratch += [pltpu.VMEM((8, DEPTH) + s, bf16) for s in (*shapes, (r, 128))]
    scratch += [
        pltpu.VMEM((tall, D), bf16),
        pltpu.VMEM((tall, D), bf16),
        pltpu.VMEM((D + AUG, LANES), bf16),
        pltpu.VMEM((D, LANES), bf16),
        pltpu.VMEM((D, LANES), bf16),
        pltpu.VMEM((D, LANES), bf16),
        pltpu.VMEM((tall, D), bf16),
        pltpu.VMEM((HEADS, LANES), f32),
        pltpu.VMEM((tall, D), f32),
        pltpu.VMEM((8, LANES), jnp.int32),
        pltpu.VMEM((2 * (HALO + rows), D), bf16),
        pltpu.VMEM((1, 128), jnp.int32),
        pltpu.VMEM((1, 128), jnp.int32),
        pltpu.VMEM((128, 128), f32),
        pltpu.VMEM((128, D), f32),
        pltpu.VMEM((PLANE, 2, DEPTH) + shapes[0], bf16),
        pltpu.VMEM((PLANE, 2, DEPTH) + shapes[1], bf16),
        pltpu.VMEM((PLANE, 2, DEPTH, r, 128), f32),
        *[pltpu.VMEM(*h) for h in halos],
    ]
    for lead in ((PLANE, DEPTH), (4, DEPTH // 2), (2, DEPTH // 2), (3,)):
        scratch += [pltpu.VMEM(lead + s, t) for s, t in five]
    scratch += [pltpu.VMEM((DEPTH, s[0], s[1] // DEPTH), bf16) for s in shapes]
    scratch += [pltpu.VMEM(*c) for c in copies]
    scratch.append(pltpu.VMEM((8, DEPTH, r, 128), bf16))
    dma = pltpu.SemaphoreType.DMA
    scratch += [
        dma((15,)), dma((2,)), dma((5, 11)), dma((5, 11)), dma((6,)), dma((6,)),
        dma((5, 13)), dma((5, 13)), dma((5, 11)), dma((5, 11)), dma((22,)),
    ]
    return pl.pallas_call(
        whole_kernel,
        out_shape=out_shape,
        in_specs=[hbm] * 17 + [vmem] * 2,
        out_specs=[hbm] * 22 + [vmem] * 2,
        scratch_shapes=scratch,
        compiler_params=pltpu.CompilerParams(
            collective_id=0, has_side_effects=True, vmem_limit_bytes=63 * MIB
        ),
        name="whole",
    )(*state, tokens, cotangent, segment, keep)


LAST_PART = 496


def last_kernel(*refs):
    results, backs, ends = refs[:22], refs[22:24], refs[24:46]
    lows, (load_sems, store_sems) = refs[46:68], refs[68:]
    rows = results[0].shape[0]
    seq = lax.axis_index("seq")
    rim = pl.ds(rows - HALO, HALO)
    places = [(i, rim) for i in range(2)]
    places += [
        (i, pl.ds(first, LAST_PART))
        for i in range(2)
        for first in range(0, rows - HALO, LAST_PART)
    ]
    places += [(i, pl.ds(0, results[i].shape[0])) for i in range(2, 22)]
    loads = [
        pltpu.make_async_copy(results[i].at[at], lows[i].at[at], load_sems.at[n])
        for n, (i, at) in enumerate(places)
    ]
    stores = [
        pltpu.make_async_copy(lows[i].at[at], ends[i].at[at], store_sems.at[n])
        for n, (i, at) in enumerate(places)
    ]
    for load in loads:
        load.start()
    place = lax.broadcasted_iota(jnp.int32, (HALO, 1), 0)
    theirs = (place >= HALO - 8 * (seq + 1)) & (seq < lax.axis_size("seq") - 1)
    for n, (i, at) in enumerate(places):
        loads[n].wait()
        if n < 2:
            own = lows[i][rim, :].astype(f32)
            lows[i][rim, :] = jnp.where(theirs, backs[i][...].astype(f32), own).astype(lows[i].dtype)
        stores[n].start()
    for store in stores:
        store.wait()


def last(results, out_back, in_back):
    shape = jax.ShapeDtypeStruct
    vmem = pl.BlockSpec(memory_space=pltpu.VMEM)
    hbm = pl.BlockSpec(memory_space=pl.ANY)
    count = 22 + 2 * ((results[0].shape[0] - HALO) // LAST_PART)
    return pl.pallas_call(
        last_kernel,
        out_shape=[shape(a.shape, a.dtype) for a in results],
        in_specs=[hbm] * 22 + [vmem, vmem],
        out_specs=[hbm] * 22,
        scratch_shapes=[pltpu.VMEM(a.shape, a.dtype) for a in results]
        + [pltpu.SemaphoreType.DMA((count,)), pltpu.SemaphoreType.DMA((count,))],
        compiler_params=pltpu.CompilerParams(vmem_limit_bytes=60 * MIB),
        name="last",
    )(*results, out_back, in_back)


def on_device(
    tokens,
    cotangent,
    segment,
    keep_mask,
    attn_master,
    out_master,
    in_master,
    back_master,
    vec_master,
    attn_first,
    out_first,
    in_first,
    back_first,
    vec_first,
    attn_second,
    out_second,
    in_second,
    back_second,
    vec_second,
):
    seq = lax.axis_index("seq")
    seq_count = lax.axis_size("seq")
    both = ("batch", "seq")
    rows = tokens.shape[1]
    masters = (attn_master, out_master, in_master, back_master, vec_master)
    firsts = (attn_first, out_first, in_first, back_first, vec_first)
    seconds = (attn_second, out_second, in_second, back_second, vec_second)
    direct = seq_count == DEPTH and lax.axis_size("batch") == 2 * PLANE
    forward = [(i, i + 1) for i in range(seq_count - 1)]
    backward = [(i + 1, i) for i in range(seq_count - 1)]
    if direct:
        *results, out_back, grad_back = whole(
            masters, firsts, seconds, tokens, cotangent, segment, keep_mask
        )
        for i in range(17, 21):
            results[i] = results[i].reshape(-1, results[i].shape[-1])
        ends = last(results, out_back, grad_back)
        return (ends[0][None], ends[1][None], *ends[2:])
    low = [w.astype(bf16) for w in masters]
    low[4] = jnp.pad(low[4].T, ((0, 0), (0, 128 - low[4].shape[0])))
    attn_w, out_w, in_w, back_w, vec_t = (
        lax.all_gather(w, both, axis=0, tiled=True) for w in low
    )
    x_halo, e_halo, seg_halo, keep_halo = (
        lax.ppermute(a, "seq", forward)
        for a in (
            tokens[0, rows - HALO :], cotangent[0, rows - HALO :],
            segment[:, rows - 128 :], keep_mask[:, rows - 128 :],
        )
    )
    xs, es, xt, qt, kt, vt, c, lse = attn_forward(
        seq_count, tokens, cotangent, x_halo, e_halo, segment, keep_mask, seg_halo, keep_halo,
        attn_w, vec_t,
    )
    z, dh, dr, gwo, gw1, gw2, gvec, gb1 = feed(xs, c, es, out_w, in_w, back_w, vec_t)
    out, out_halo, grad_in, grad_in_halo, gwa, gbias = attn_backward(
        seq_count, xt, qt, kt, vt, lse, dr, dh, z, attn_w, out_w
    )
    grads = (gwa, gwo, gw1, gw2)
    grad_vec = jnp.concatenate(
        [gbias[:1, :D], gbias[:1, 2 * D :], gvec[2:8], gb1[0].reshape(FF // D, D)], 0
    )
    sums = [lax.psum_scatter(g.astype(f32), both, scatter_dimension=0, tiled=True) for g in grads]
    sums.append(lax.psum_scatter(grad_vec, both, scatter_dimension=1, tiled=True))
    new = [
        adam_update(masters[i], firsts[i], seconds[i], sums[i], learn_rates[i]) for i in range(5)
    ]

    def own_columns(i):
        whole = lax.all_gather(new[i][2].astype(bf16), both, axis=1 if i == 4 else 0, tiled=True)
        count = whole.shape[1] // seq_count
        return lax.dynamic_slice_in_dim(whole, seq * count, count, 1)

    results = [out, grad_in] + [new[i][part] for part in range(3) for i in range(5)]
    results += [own_columns(i) for i in range(5)]
    out_back = lax.ppermute(out_halo, "seq", backward)
    grad_back = lax.ppermute(grad_in_halo, "seq", backward)
    ends = last(results, out_back, grad_back)
    return (ends[0][None], ends[1][None], *ends[2:])


def solution(mesh):
    stream = P("batch", "seq", None)
    rows = P(("batch", "seq"), None)
    vector = P(None, ("batch", "seq"))
    five = (rows, rows, rows, rows, vector)
    return jax.shard_map(
        on_device,
        mesh=mesh,
        in_specs=(stream, stream, P("batch", "seq"), P("batch", "seq")) + five * 3,
        out_specs=(stream, stream) + five * 3 + (P(None, "seq"),) * 5,
        check_vma=False,
    )
```

```python
import functools

import jax
import jax.numpy as jnp
from jax import lax
from jax.experimental import pallas as pl
from jax.experimental.pallas import tpu as pltpu
from jax.sharding import PartitionSpec as P

D = 512
HEADS = 8
HEAD_DIM = 64
FF = 2048
STEP = 10
PAIR = 255
SLOT = 256
HALO = 64
TILES = 4
TAIL = 64
PIECE = TAIL // TILES
TILE = 2 * SLOT + PIECE
ROWS = TILES * TILE
LANES = 8 * SLOT + 128
AUG = 16
MIB = 1 << 20

norm_epsilon = 1e-05
beta_first = 0.9
beta_second = 0.999
adam_epsilon = 1e-08
weight_decay = 0.01
learn_rates = (0.03, 0.2, 0.03, 0.02, 0.5)
big = 1e30

f32 = jnp.float32
bf16 = jnp.bfloat16


def dot(a, b, ca, cb):
    return lax.dot_general(a, b, (((ca,), (cb,)), ((), ())), preferred_element_type=f32)


def adam_update(master, first, second, gradient, rate):
    first_new = beta_first * first + (1.0 - beta_first) * gradient
    second_new = beta_second * second + (1.0 - beta_second) * gradient * gradient
    first_hat = first_new / (1.0 - beta_first**STEP)
    second_hat = second_new / (1.0 - beta_second**STEP)
    master_new = master - rate * (
        first_hat / (jnp.sqrt(second_hat) + adam_epsilon) + weight_decay * master
    )
    return (first_new, second_new, master_new)


def slot_row(j):
    return pl.multiple_of((j // 2) * TILE + (j % 2) * SLOT, 16)


def first_row(j, seq):
    return HALO + PAIR * j - 8 * seq


def staged(ref, start):
    base = pl.multiple_of((start // 16) * 16, 16)
    rest = start - base
    wide = ref[pl.ds(base, SLOT + 16), :].astype(f32)
    wide = jnp.where(rest >= 8, wide[8:], wide[:-8])
    shift = rest % 8
    groups = (SLOT + 8) // 8
    wide = wide.reshape(groups, 8, D)
    turned = pltpu.roll(wide, lax.rem(8 - shift, 8), 1)
    place = lax.broadcasted_iota(jnp.int32, (groups - 1, 8, D), 1)
    block = jnp.where(place < 8 - shift, turned[:-1], turned[1:]).reshape(SLOT, D)
    row = lax.broadcasted_iota(jnp.int32, (SLOT, D), 0)
    return jnp.where(row < PAIR, block, 0.0).astype(bf16)


def unstage(ref, start, block):
    base = pl.multiple_of((start // 8) * 8, 8)
    shift = start - base
    turned = pltpu.roll(block.reshape(SLOT // 8, 8, D), shift, 1)
    place = lax.broadcasted_iota(jnp.int32, (1, 8, D), 1)
    keep = ref[pl.ds(base, 8), :].reshape(1, 8, D)
    low = jnp.concatenate([keep, turned], 0)
    high = jnp.concatenate([turned, turned[-1:]], 0)
    place = lax.broadcasted_iota(jnp.int32, low.shape, 1)
    ref[pl.ds(base, SLOT + 8), :] = jnp.where(place < shift, low, high).reshape(SLOT + 8, D)


def stage_slot(ref, start, out_ref, row):
    base = pl.multiple_of((start // 16) * 16, 16)
    rest = start - base
    shift = rest % 8
    groups = (SLOT + 8) // 8
    place = lax.broadcasted_iota(jnp.int32, (groups - 1, 8, 128), 1)
    number = lax.broadcasted_iota(jnp.int32, (groups - 1, 8, 128), 0) * 8 + place
    for g in range(D // 128):
        cols = slice(g * 128, (g + 1) * 128)
        wide = ref[pl.ds(base, SLOT + 16), cols].astype(f32)
        wide = jnp.where(rest >= 8, wide[8:], wide[:-8]).reshape(groups, 8, 128)
        turned = pltpu.roll(wide, lax.rem(8 - shift, 8), 1)
        block = jnp.where(place < 8 - shift, turned[:-1], turned[1:])
        block = jnp.where(number < PAIR, block, 0.0)
        out_ref[pl.ds(row, SLOT), cols] = block.reshape(SLOT, 128).astype(bf16)


def unstage_slot(ref, start, column):
    base = pl.multiple_of((start // 8) * 8, 8)
    shift = start - base
    for g in range(D // 128):
        cols = slice(g * 128, (g + 1) * 128)
        turned = pltpu.roll(column(g).reshape(SLOT // 8, 8, 128), shift, 1)
        keep = ref[pl.ds(base, 8), cols].reshape(1, 8, 128)
        low = jnp.concatenate([keep, turned], 0)
        high = jnp.concatenate([turned, turned[-1:]], 0)
        place = lax.broadcasted_iota(jnp.int32, low.shape, 1)
        ref[pl.ds(base, SLOT + 8), cols] = jnp.where(place < shift, low, high).reshape(SLOT + 8, 128)


def tail_rows(ref, count, is_last):
    kept = ref[HALO + 2048 - count : HALO + 2048, :].astype(f32)
    if count < TAIL:
        kept = jnp.concatenate([kept, jnp.zeros((TAIL - count, D), f32)], 0)
    return jnp.where(is_last, kept, 0.0).astype(bf16)


def tag_rows(tag, pair):
    width = tag.shape[1]
    number = tag // 2 - 2 * pair
    kept = tag % 2
    row = lax.broadcasted_iota(jnp.int32, (AUG, width), 0)
    match = row == number
    query = jnp.where(match, 1.0, 0.0).astype(bf16)
    key = jnp.where(match & (kept == 1), 0.0, -big)
    key = jnp.where(row < 4, key, 0.0).astype(bf16)
    return query, key


def attn_forward_kernel(
    seq_count, tok_ref, cot_ref, tok_halo, cot_halo, seg_ref, keep_ref, seg_halo, keep_halo,
    w_ref, vec_ref,
    xs_ref, es_ref, xt_ref, qt_ref, kt_ref, vt_ref, c_ref, lse_ref,
    wt_ref, x_ref, e_ref, tag_ref, sems,
):
    seq = lax.axis_index("seq")
    is_last = seq == seq_count - 1
    rows = tok_ref.shape[1]
    loads = []
    for i, (whole, halo, ext) in enumerate(((tok_ref, tok_halo, x_ref), (cot_ref, cot_halo, e_ref))):
        loads.append(pltpu.make_async_copy(whole.at[0], ext.at[pl.ds(HALO, rows)], sems.at[2 * i]))
        loads.append(pltpu.make_async_copy(halo, ext.at[pl.ds(0, HALO)], sems.at[2 * i + 1]))
    for load in loads:
        load.start()
    for part in range(3):
        wt_ref[part * D : (part + 1) * D, :] = w_ref[:, part * D : (part + 1) * D].T
    tag_ref[...] = jnp.zeros_like(tag_ref)
    edge = seg_halo[...] * 2 + keep_halo[...]
    tag_ref[:, :HALO] = jnp.broadcast_to(edge[:, 128 - HALO :], (8, HALO))
    tag_ref[:, HALO : HALO + rows] = jnp.broadcast_to(seg_ref[...] * 2 + keep_ref[...], (8, rows))
    query_bias = vec_ref[:, 0:1].astype(f32)
    value_bias = vec_ref[:, 1:2].astype(f32)
    for load in loads:
        load.wait()

    def block(xb, tag, pair, lane, width):
        lanes = pl.ds(lane, width)
        xt_ref[:D, lanes] = xb.T
        q = dot(wt_ref[:D, :], xb, 1, 1) + query_bias
        q = (q.astype(bf16).astype(f32) * HEAD_DIM**-0.5).astype(bf16)
        k = dot(wt_ref[D : 2 * D, :], xb, 1, 1).astype(bf16)
        v = (dot(wt_ref[2 * D :, :], xb, 1, 1) + value_bias).astype(bf16)
        query_tag, key_tag = tag_rows(tag, pair)
        vt_ref[:, lanes] = v
        context = []
        for h in range(HEADS):
            rows = slice(h * HEAD_DIM, (h + 1) * HEAD_DIM)
            qh = jnp.concatenate([q[rows], query_tag], 0)
            kh = jnp.concatenate([k[rows], key_tag], 0)
            qt_ref[h, :, lanes] = qh
            kt_ref[h, :, lanes] = kh
            s = dot(kh, qh, 0, 0)
            top = jnp.max(s, axis=0, keepdims=True)
            ex = jnp.exp(s - top)
            total = jnp.sum(ex, axis=0, keepdims=True)
            lse_ref[h : h + 1, lanes] = top + jnp.log(total)
            a = (ex * (1.0 / total)).astype(bf16)
            context.append(dot(v[rows], a, 1, 0))
        return jnp.concatenate(context, 0).astype(bf16).T

    def one(j, carry):
        start = first_row(j, seq)
        row = slot_row(j)
        xb = staged(x_ref, start)
        xs_ref[pl.ds(row, SLOT), :] = xb
        es_ref[pl.ds(row, SLOT), :] = staged(e_ref, start)
        wide = tag_ref[:, pl.ds(pl.multiple_of(j * SLOT, 128), SLOT + 128)]
        width = SLOT + 128
        tag = pltpu.roll(wide, width - (start - j * SLOT), 1)[:1, :SLOT]
        c_ref[pl.ds(row, SLOT), :] = block(
            xb, tag, 8 * seq + j, pl.multiple_of(j * SLOT, 128), SLOT
        )
        return carry

    lax.fori_loop(0, 8, one, 0)
    count = 8 * seq_count
    xt_ref[:, 8 * SLOT :] = jnp.zeros((D + AUG, 128), bf16)
    xb = tail_rows(x_ref, count, is_last)
    eb = tail_rows(e_ref, count, is_last)
    tag = tag_ref[:1, 2048:2176]
    tag = pltpu.roll(tag_ref[:, 2048:2176], 128 - (64 - count), 1)[:1, :TAIL] if count < 64 else tag[:, :TAIL]
    place = lax.broadcasted_iota(jnp.int32, (1, TAIL), 1)
    tag = jnp.where(place < count, tag, (2 * 8 * seq_count + 3) * 2)
    cb = block(xb, tag, 8 * seq_count, 8 * SLOT, TAIL)
    for t in range(TILES):
        rows = slice(t * PIECE, (t + 1) * PIECE)
        at = slice(t * TILE + 2 * SLOT, (t + 1) * TILE)
        xs_ref[at, :] = xb[rows]
        es_ref[at, :] = eb[rows]
        c_ref[at, :] = cb[rows]
    ones = lax.broadcasted_iota(jnp.int32, (AUG, LANES), 0) == 0
    xt_ref[D:, :] = jnp.where(ones, 1.0, 0.0).astype(bf16)


def attn_forward(seq_count, tokens, cotangent, *others):
    shape = jax.ShapeDtypeStruct
    vmem = pl.BlockSpec(memory_space=pltpu.VMEM)
    hbm = pl.BlockSpec(memory_space=pl.ANY)
    return pl.pallas_call(
        functools.partial(attn_forward_kernel, seq_count),
        out_shape=(
            shape((ROWS, D), bf16),
            shape((ROWS, D), bf16),
            shape((D + AUG, LANES), bf16),
            shape((HEADS, HEAD_DIM + AUG, LANES), bf16),
            shape((HEADS, HEAD_DIM + AUG, LANES), bf16),
            shape((D, LANES), bf16),
            shape((ROWS, D), bf16),
            shape((HEADS, LANES), f32),
        ),
        in_specs=[hbm, hbm] + [vmem] * len(others),
        out_specs=[vmem] * 8,
        scratch_shapes=[
            pltpu.VMEM((3 * D, D), bf16),
            pltpu.VMEM((HALO + tokens.shape[1], D), bf16),
            pltpu.VMEM((HALO + tokens.shape[1], D), bf16),
            pltpu.VMEM((8, LANES), jnp.int32),
            pltpu.SemaphoreType.DMA((4,)),
        ],
        compiler_params=pltpu.CompilerParams(vmem_limit_bytes=56 * MIB),
        name="attn_forward",
    )(tokens, cotangent, *others)


def feed_kernel(
    xs_ref, c_ref, es_ref, wo_ref, w1_ref, w2_ref, vect_ref,
    z_ref, dh_ref, dr_ref, gwo_ref, gw1_ref, gw2_ref, gvec_ref, gb1_ref,
    u_ref, g_ref, awo_ref, aw1_ref, aw2_ref, vec_ref,
):
    step = pl.program_id(0)

    @pl.when(step == 0)
    def _():
        awo_ref[...] = jnp.zeros_like(awo_ref)
        aw1_ref[...] = jnp.zeros_like(aw1_ref)
        aw2_ref[...] = jnp.zeros_like(aw2_ref)
        gvec_ref[...] = jnp.zeros_like(gvec_ref)
        gb1_ref[...] = jnp.zeros_like(gb1_ref)
        vec_ref[...] = vect_ref[...].astype(f32).T

    def mean(v):
        return jnp.mean(v, axis=-1, keepdims=True)

    def row_sum(v):
        return jnp.sum(v, axis=0, keepdims=True)

    bo, b2, g1, c1, g2, c2 = (vec_ref[i : i + 1, :] for i in range(2, 8))
    h1 = xs_ref[...].astype(f32) + (dot(c_ref[...], wo_ref[...], 1, 0) + bo)
    mid = h1 - mean(h1)
    inv1 = lax.rsqrt(mean(mid * mid) + norm_epsilon)
    n1 = mid * inv1
    y = n1 * g1 + c1
    yb = y.astype(bf16)
    chunk = D
    f = None
    for k in range(FF // chunk):
        cols = slice(k * chunk, (k + 1) * chunk)
        u = dot(yb, w1_ref[:, cols], 1, 0) + vec_ref[8 + k : 9 + k, :]
        cdf = 0.5 * (1.0 + lax.erf(u * 0.7071067811865476))
        gk = (u * cdf).astype(bf16)
        u_ref[:, cols] = cdf + u * jnp.exp(u * u * -0.5) * 0.3989422804014327
        g_ref[:, cols] = gk
        part = dot(gk, w2_ref[cols, :], 1, 0)
        f = part if f is None else f + part
    h2 = y + (f + b2)
    mid2 = h2 - mean(h2)
    inv2 = lax.rsqrt(mean(mid2 * mid2) + norm_epsilon)
    n2 = mid2 * inv2
    z_ref[...] = (n2 * g2 + c2).astype(bf16)
    e = es_ref[...].astype(f32)
    gvec_ref[7:8, :] += row_sum(e)
    gvec_ref[6:7, :] += row_sum(e * n2)
    eg = e * g2
    dh2 = (eg - mean(eg) - n2 * mean(eg * n2)) * inv2
    df = dh2.astype(bf16)
    gvec_ref[3:4, :] += row_sum(df.astype(f32))
    dft = df.T
    ybt = yb.T
    dy = dh2
    for k in range(FF // chunk):
        cols = slice(k * chunk, (k + 1) * chunk)
        aw2_ref[:, cols] += dot(dft, g_ref[:, cols], 1, 0)
        dg = dot(df, w2_ref[cols, :], 1, 1)
        du = (dg * u_ref[:, cols]).astype(bf16)
        gb1_ref[:1, cols] += row_sum(du.astype(f32))
        aw1_ref[:, cols] += dot(ybt, du, 1, 0)
        dy = dy + dot(du, w1_ref[:, cols], 1, 1)
    gvec_ref[5:6, :] += row_sum(dy)
    gvec_ref[4:5, :] += row_sum(dy * n1)
    eg = dy * g1
    dh1 = (eg - mean(eg) - n1 * mean(eg * n1)) * inv1
    dh_ref[...] = dh1
    dr = dh1.astype(bf16)
    dr_ref[...] = dr
    gvec_ref[2:3, :] += row_sum(dr.astype(f32))
    awo_ref[...] += dot(c_ref[...].T, dr, 1, 0)

    @pl.when(step == TILES - 1)
    def _():
        gwo_ref[...] = awo_ref[...].astype(bf16)
        gw1_ref[...] = aw1_ref[...].astype(bf16)
        for k in range(FF // chunk):
            cols = slice(k * chunk, (k + 1) * chunk)
            gw2_ref[cols, :] = aw2_ref[:, cols].astype(bf16).T


def feed(xs, c, es, wo, w1, w2, vec_t):
    shape = jax.ShapeDtypeStruct
    tile = pl.BlockSpec((TILE, D), lambda i: (i, 0))

    def whole(*dims):
        return pl.BlockSpec(dims, lambda i: (0,) * len(dims), pipeline_mode=pl.Buffered(1))

    return pl.pallas_call(
        feed_kernel,
        grid=(TILES,),
        out_shape=(
            shape((ROWS, D), bf16),
            shape((ROWS, D), f32),
            shape((ROWS, D), bf16),
            shape((D, D), bf16),
            shape((D, FF), bf16),
            shape((FF, D), bf16),
            shape((8, D), f32),
            shape((8, FF), f32),
        ),
        in_specs=[tile, tile, tile, whole(D, D), whole(D, FF), whole(FF, D), whole(D, 128)],
        out_specs=[tile, tile, tile, whole(D, D), whole(D, FF), whole(FF, D), whole(8, D), whole(8, FF)],
        scratch_shapes=[
            pltpu.VMEM((TILE, FF), f32),
            pltpu.VMEM((TILE, FF), bf16),
            pltpu.VMEM((D, D), f32),
            pltpu.VMEM((D, FF), f32),
            pltpu.VMEM((D, FF), f32),
            pltpu.VMEM((128, D), f32),
        ],
        compiler_params=pltpu.CompilerParams(vmem_limit_bytes=60 * MIB),
        name="feed",
    )(xs, c, es, wo, w1, w2, vec_t)


def attn_backward_kernel(
    seq_count, xt_ref, qt_ref, kt_ref, vt_ref, lse_ref, dr_ref, dh_ref, z_ref, w_ref, wo_ref,
    out_ref, out_halo_ref, in_ref, in_halo_ref, gwa_ref, gbias_ref,
    dpt_ref, ext_ref,
):
    seq = lax.axis_index("seq")
    is_last = seq == seq_count - 1

    def block(dr, lane, width):
        lanes = pl.ds(lane, width)
        dct = dot(wo_ref[...], dr, 1, 1).astype(bf16)
        for h in range(HEADS):
            rows = slice(h * HEAD_DIM, (h + 1) * HEAD_DIM)
            qh = qt_ref[h, :, lanes]
            kh = kt_ref[h, :, lanes]
            vh = vt_ref[rows, lanes]
            dch = dct[rows]
            a = jnp.exp(dot(kh, qh, 0, 0) - lse_ref[h : h + 1, lanes])
            da = dot(vh, dch, 0, 0)
            ada = a * da
            ds = (ada - a * jnp.sum(ada, axis=0, keepdims=True)).astype(bf16)
            dv = dot(dch, a.astype(bf16), 1, 1)
            dk = dot(qh[:HEAD_DIM], ds, 1, 1)
            dq = dot(kh[:HEAD_DIM], ds, 1, 0) * HEAD_DIM**-0.5
            dpt_ref[rows, lanes] = dq.astype(bf16)
            dpt_ref[slice(D + h * HEAD_DIM, D + (h + 1) * HEAD_DIM), lanes] = dk.astype(bf16)
            dpt_ref[slice(2 * D + h * HEAD_DIM, 2 * D + (h + 1) * HEAD_DIM), lanes] = dv.astype(bf16)
        return dot(w_ref[...], dpt_ref[:, lanes], 1, 0).T

    dpt_ref[:, 8 * SLOT :] = jnp.zeros((3 * D, 128), bf16)

    def one(j, carry):
        row = slot_row(j)
        grad = block(dr_ref[pl.ds(row, SLOT), :], pl.multiple_of(j * SLOT, 128), SLOT)
        unstage(ext_ref, first_row(j, seq), grad + dh_ref[pl.ds(row, SLOT), :])
        return carry

    lax.fori_loop(0, 8, one, 0)
    count = 8 * seq_count

    def tail_of(ref):
        return jnp.concatenate(
            [ref[t * TILE + 2 * SLOT : (t + 1) * TILE, :] for t in range(TILES)], 0
        )

    grad = block(tail_of(dr_ref), 8 * SLOT, TAIL) + tail_of(dh_ref)

    @pl.when(is_last)
    def _():
        ext_ref[HALO + 2048 - count : HALO + 2048, :] = grad[:count]

    in_halo_ref[...] = ext_ref[:HALO, :]
    in_ref[...] = ext_ref[HALO : HALO + 2048, :]

    def two(j, carry):
        unstage(ext_ref, first_row(j, seq), z_ref[pl.ds(slot_row(j), SLOT), :].astype(f32))
        return carry

    lax.fori_loop(0, 8, two, 0)
    tail = tail_of(z_ref).astype(f32)

    @pl.when(is_last)
    def _():
        ext_ref[HALO + 2048 - count : HALO + 2048, :] = tail[:count]

    out_halo_ref[...] = ext_ref[:HALO, :].astype(bf16)
    out_ref[...] = ext_ref[HALO : HALO + 2048, :].astype(bf16)
    for part in range(3):
        cols = slice(part * D, (part + 1) * D)
        g = dot(xt_ref[...], dpt_ref[cols, :], 1, 1)
        gwa_ref[:, cols] = g[:D].astype(bf16)
        gbias_ref[:, cols] = g[D : D + 8]


def attn_backward(seq_count, *operands):
    shape = jax.ShapeDtypeStruct
    return pl.pallas_call(
        functools.partial(attn_backward_kernel, seq_count),
        out_shape=(
            shape((2048, D), bf16),
            shape((HALO, D), bf16),
            shape((2048, D), f32),
            shape((HALO, D), f32),
            shape((D, 3 * D), bf16),
            shape((8, 3 * D), f32),
        ),
        in_specs=[pl.BlockSpec(memory_space=pltpu.VMEM)] * len(operands),
        out_specs=[pl.BlockSpec(memory_space=pltpu.VMEM)] * 6,
        scratch_shapes=[
            pltpu.VMEM((3 * D, LANES), bf16),
            pltpu.VMEM((HALO + 2048 + 16, D), f32),
        ],
        compiler_params=pltpu.CompilerParams(vmem_limit_bytes=60 * MIB),
        name="attn_backward",
    )(*operands)


MESH = pl.DeviceIdType.MESH
PLANE = 4
DEPTH = 4


class Place:
    def __init__(self):
        self.batch = lax.axis_index("batch")
        self.z = lax.axis_index("seq")
        self.core = self.batch % 2
        self.plane = self.batch // 2

    def plane_at(self, k):
        x = (self.plane % 2 + k % 2) % 2
        y = (self.plane // 2 + k // 2) % 2
        return y * 2 + x

    def in_plane(self, k):
        return {"batch": self.plane_at(k) * 2 + self.core, "seq": self.z}

    def depth_at(self, k):
        return (self.z + k) % DEPTH

    def in_depth(self, k):
        return {"batch": self.batch, "seq": self.depth_at(k)}

    def sibling(self):
        return {"batch": self.plane * 2 + 1 - self.core, "seq": self.z}

    def greet(self):
        barrier = pltpu.get_barrier_semaphore()
        for k in range(1, 4):
            pl.semaphore_signal(barrier, inc=1, device_id=self.in_plane(k), device_id_type=MESH)
            pl.semaphore_signal(barrier, inc=1, device_id=self.in_depth(k), device_id_type=MESH)
        pl.semaphore_signal(barrier, inc=1, device_id=self.sibling(), device_id_type=MESH)
        pl.semaphore_wait(barrier, 7)


def remote(src, dst, send, recv, device):
    return pltpu.make_async_remote_copy(
        src_ref=src, dst_ref=dst, send_sem=send, recv_sem=recv, device_id=device, device_id_type=MESH
    )


LOW, HIGH = pl.ds(0, DEPTH // 2), pl.ds(DEPTH // 2, DEPTH // 2)


class Gather:
    def __init__(self, place, whole, send, recv, parts=None):
        self.place, self.whole, self.send, self.recv, self.parts = place, whole, send, recv, parts

    def block(self, k):
        return self.whole.at[self.place.plane_at(k) * 2 + self.place.core]

    def copy(self, n, source, target, device):
        return remote(source, target, self.send.at[n], self.recv.at[n], device)

    def depth(self, k):
        at = self.place
        here = self.whole.at[at.batch, at.z]
        source = here if self.parts is None else self.parts.at[at.depth_at(k)]
        return self.copy(k - 1, source, here, at.in_depth(k))

    def plane(self, k):
        return self.copy(2 + k, self.block(0), self.block(0), self.place.in_plane(k))

    def across(self, k):
        half = self.block(k).at[LOW if k == 1 else HIGH]
        return self.copy(4 + k, half, half, self.place.in_plane(3 - k))

    def core(self, k):
        return self.copy(7 + k, self.block(k), self.block(k), self.place.sibling())

    def first(self):
        for k in range(1, 4):
            self.depth(k).start()

    def second(self):
        for k in range(1, 4):
            self.depth(k).wait_recv()
        for k in (1, 2):
            self.plane(k).start()
        self.core(0).start()

    def third(self):
        for k in (1, 2):
            self.plane(k).wait_recv()
            self.across(k).start()
            self.core(k).start()

    def fourth(self):
        for k in (1, 2):
            self.across(k).wait_recv()
        self.core(3).start()

    def finish(self):
        for k in range(4):
            self.core(k).wait_recv()
        for k in range(1, 4):
            self.depth(k).wait_send()
        for k in (1, 2):
            self.plane(k).wait_send()
            self.across(k).wait_send()
        for k in range(4):
            self.core(k).wait_send()


class Scatter:
    def __init__(self, place, grad, twin, near, far, along, send, recv):
        self.place, self.grad, self.twin = place, grad, twin
        self.near, self.far, self.along, self.send, self.recv = near, far, along, send, recv
        shape = grad.shape
        if len(shape) == 4:
            self.at = lambda p, c: grad.at[p * 2 + c]
        else:
            self.at = lambda p, c: grad.at[p, c]

    def block(self, k):
        return self.at(self.place.plane_at(k), self.place.core)

    def copy(self, n, source, target, device):
        return remote(source, target, self.send.at[n], self.recv.at[n], device)

    def core(self, p):
        source = self.at(p, 1 - self.place.core)
        return self.copy(p, source, self.twin.at[p], self.place.sibling())

    def plane(self, n):
        k, half = ((1, LOW), (3, LOW), (2, HIGH), (3, HIGH))[n]
        target = self.near.at[n]
        return self.copy(4 + n, self.block(k).at[half], target, self.place.in_plane(1 + n // 2))

    def across(self, n):
        k, half = ((2, LOW), (1, HIGH))[n]
        return self.copy(8 + n, self.block(k).at[half], self.far.at[n], self.place.in_plane(2 - n))

    def depth(self, k):
        source = self.block(0).at[self.place.depth_at(k)]
        return self.copy(9 + k, source, self.along.at[k - 1], self.place.in_depth(k))

    def first(self):
        for p in range(PLANE):
            self.core(p).start()

    def second(self):
        for p in range(PLANE):
            self.core(p).wait_recv()
        own = self.place.core

        def one(p, carry):
            mine = self.at(p, own)
            mine[...] = (mine[...].astype(f32) + self.twin[p].astype(f32)).astype(mine.dtype)
            return carry

        lax.fori_loop(0, PLANE, one, 0)
        for n in range(4):
            self.plane(n).start()

    def third(self):
        for n in range(4):
            self.plane(n).wait_recv()
        for n, (k, base) in enumerate(((2, 0), (1, 2))):
            mine = self.block(k)

            def one(q, carry):
                total = mine[base + q].astype(f32) + self.near[2 * n + 1, q].astype(f32)
                mine[base + q] = total.astype(mine.dtype)
                return carry

            lax.fori_loop(0, 2, one, 0)
            self.across(n).start()

    def fourth(self):
        for n in range(2):
            self.across(n).wait_recv()
        mine = self.block(0)

        def one(i, carry):
            n, q = i // 2, i % 2
            total = mine[i].astype(f32) + self.near[2 * n, q].astype(f32) + self.far[n, q].astype(f32)
            mine[i] = total.astype(mine.dtype)
            return carry

        lax.fori_loop(0, DEPTH, one, 0)
        for k in range(1, 4):
            self.depth(k).start()

    def total(self):
        for k in range(1, 4):
            self.depth(k).wait_recv()
        total = self.block(0)[self.place.z].astype(f32)
        for k in range(3):
            total = total + self.along[k].astype(f32)
        return total

    def finish(self):
        for p in range(PLANE):
            self.core(p).wait_send()
        for n in range(4):
            self.plane(n).wait_send()
        for n in range(2):
            self.across(n).wait_send()
        for k in range(1, 4):
            self.depth(k).wait_send()


def turned(ref, value):
    ref[...] = jnp.zeros_like(ref)
    ref[: value.shape[0], : value.shape[1]] = value
    return ref[...].T


def heads_of(block, h):
    return block[h * HEAD_DIM : (h + 1) * HEAD_DIM]


def only_head(block, h):
    zero = jnp.zeros((HEAD_DIM, block.shape[1]), block.dtype)
    mine = heads_of(block, h)
    return jnp.concatenate([mine, zero] if h % 2 == 0 else [zero, mine], 0)


def pair_of(block, h):
    at = h // 2 * 2 * HEAD_DIM
    return block[:, at : at + 2 * HEAD_DIM]


def mask_parts(tag, pair):
    query, key = tag_rows(tag, pair)
    width = tag.shape[1]
    zero = jnp.zeros((128 - AUG, width), bf16)
    return jnp.concatenate([key, zero], 0).T, jnp.concatenate([query, zero], 0)


class Slots:
    def __init__(self, tag_ref, seq, seq_count):
        self.tag_ref, self.seq, self.count = tag_ref, seq, 8 * seq_count
        self.last_pair = 8 * seq_count

    def tag(self, j):
        wide = self.tag_ref[:, pl.ds(pl.multiple_of(j * SLOT, 128), SLOT + 128)]
        offset = HALO - 8 * self.seq - j
        return pltpu.roll(wide, SLOT + 128 - offset, 1)[:1, :SLOT]

    def tail_tag(self):
        tag = self.tag_ref[:, 2048:2176]
        if self.count < TAIL:
            tag = pltpu.roll(tag, 128 - (TAIL - self.count), 1)
        place = lax.broadcasted_iota(jnp.int32, (1, TAIL), 1)
        return jnp.where(place < self.count, tag[:1, :TAIL], 2 * (2 * self.last_pair + 3))

    def tail(self, ref):
        return jnp.concatenate(
            [ref[t * TILE + 2 * SLOT : (t + 1) * TILE, :] for t in range(TILES)], 0
        )

    def set_tail(self, ref, value):
        for t in range(TILES):
            ref[t * TILE + 2 * SLOT : (t + 1) * TILE, :] = value[t * PIECE : (t + 1) * PIECE]


def halves_of(width):
    step = min(width, 128)
    return [slice(i, i + step) for i in range(0, width, step)]


def pair_stack(values, *rest):
    zero = jnp.zeros_like(values[0])
    left = jnp.concatenate([values[0], zero, *rest], 0)
    right = jnp.concatenate([zero, values[1], *rest], 0)
    return left, right


def forward_block(
    xb, tag, pair, lanes, wt_ref, biases, xt_ref, qt_ref, kt_ref, vt_ref, lse_ref, s_ref, a_ref, kn_ref, ct_ref
):
    width = xb.shape[0]
    xt_ref[:D, lanes] = xb.T
    parts = ((kt_ref, None), (qt_ref, biases[0]), (vt_ref, biases[1]))

    def project(n):
        at = (1, 0, 2)[n]
        p = dot(wt_ref[at * D : (at + 1) * D, :], xb, 1, 1)
        s_ref[2 * n, :, :width] = p[:SLOT]
        s_ref[2 * n + 1, :, :width] = p[SLOT:]

    def keep(n):
        out_ref, bias = parts[n]
        for h in range(HEADS):
            at = h % 4 * HEAD_DIM
            value = s_ref[2 * n + h // 4, at : at + HEAD_DIM, :width]
            rows = slice(h * HEAD_DIM, (h + 1) * HEAD_DIM)
            if bias is not None:
                value = value + bias[rows]
            value = value.astype(bf16)
            if n == 1:
                value = (value.astype(f32) * HEAD_DIM**-0.5).astype(bf16)
            out_ref[rows, lanes] = value

    project(0)
    project(1)
    keep(0)
    kn_ref[:width, :] = kt_ref[:, lanes].T
    project(2)
    keep(1)
    key_mask, query_mask = mask_parts(tag, pair)
    keep(2)

    def rows_of(h):
        return slice(h * HEAD_DIM, (h + 1) * HEAD_DIM)

    def scores(p):
        left = jnp.concatenate([kn_ref[:width, p * 128 : (p + 1) * 128], key_mask], 1)
        both = pair_stack([qt_ref[rows_of(2 * p + i), lanes] for i in range(2)], query_mask)
        if width % 128 == 0:
            s = dot(left, jnp.concatenate(both, 1), 1, 0)
            s_ref[2 * p], s_ref[2 * p + 1] = s[:, :width], s[:, width:]
        else:
            for i in range(2):
                s_ref[2 * p + i, :width, :width] = dot(left, both[i], 1, 0)

    def weigh(p):
        for h in (2 * p, 2 * p + 1):
            for half in halves_of(width):
                s = s_ref[h, :width, half]
                top = jnp.max(s, axis=0, keepdims=True)
                ex = jnp.exp(s - top)
                total = jnp.sum(ex, axis=0, keepdims=True)
                a_ref[h, :width, half] = (ex * (1.0 / total)).astype(bf16)
                at = pl.ds(pl.multiple_of(lanes.start + half.start, 128), half.stop - half.start)
                lse_ref[h : h + 1, at] = top + jnp.log(total)

    def collect(p):
        for h in (2 * p, 2 * p + 1):
            c = dot(vt_ref[rows_of(h), lanes], a_ref[h, :width, :width], 1, 0)
            ct_ref[rows_of(h), :width] = c.astype(bf16)

    skewed(HEADS // 2, scores, weigh, collect)
    return ct_ref[:, :width].T


def skewed(count, *stages):
    for i in range(count + len(stages) - 1):
        for n, stage in enumerate(stages):
            if 0 <= i - n < count:
                stage(i - n)


def backward_block(
    dr, c, tag, pair, lanes, wo, qt_ref, kt_ref, vt_ref, lse_ref, dpt_ref, s_ref, da_ref, a_ref,
    ds_ref, kn_ref, vn_ref, dct_ref, ct_ref,
):
    width = dr.shape[0]
    kn_ref[:width, :] = kt_ref[:, lanes].T
    vn_ref[:width, :] = vt_ref[:, lanes].T
    dct_ref[:, :width] = dot(wo, dr, 1, 1).astype(bf16)
    ct_ref[:, :width] = c.T
    key_mask, query_mask = mask_parts(tag, pair)

    def rows_of(h):
        return slice(h * HEAD_DIM, (h + 1) * HEAD_DIM)

    def scores(p):
        at = slice(p * 128, (p + 1) * 128)
        left = jnp.concatenate([kn_ref[:width, at], key_mask], 1)
        both = pair_stack([qt_ref[rows_of(2 * p + i), lanes] for i in range(2)], query_mask)
        both_d = pair_stack([dct_ref[rows_of(2 * p + i), :width] for i in range(2)])
        right = vn_ref[:width, at]
        if width % 128 == 0:
            s = dot(left, jnp.concatenate(both, 1), 1, 0)
            u = 2 * (p % 2)
            s_ref[u], s_ref[u + 1] = s[:, :width], s[:, width:]
            da = dot(right, jnp.concatenate(both_d, 1), 1, 0)
            da_ref[u], da_ref[u + 1] = da[:, :width], da[:, width:]
        else:
            for i in range(2):
                s_ref[2 * (p % 2) + i, :width, :width] = dot(left, both[i], 1, 0)
                da_ref[2 * (p % 2) + i, :width, :width] = dot(right, both_d[i], 1, 0)

    def weigh(p):
        for h in (2 * p, 2 * p + 1):
            rows = rows_of(h)
            for half in halves_of(width):
                at = pl.ds(pl.multiple_of(lanes.start + half.start, 128), half.stop - half.start)
                product = ct_ref[rows, half].astype(f32) * dct_ref[rows, half].astype(f32)
                delta = jnp.sum(product, axis=0, keepdims=True)
                lse = lse_ref[h : h + 1, at]
                for first in range(0, width, 64):
                    keys = slice(first, first + 64)
                    a = jnp.exp(s_ref[h % 4, keys, half] - lse)
                    a_ref[h % 4, keys, half] = a.astype(bf16)
                    ds_ref[h % 4, keys, half] = (a * (da_ref[h % 4, keys, half] - delta)).astype(bf16)

    def collect(p):
        for h in (2 * p, 2 * p + 1):
            rows = rows_of(h)
            ds = ds_ref[h % 4, :width, :width]
            dv = dot(dct_ref[rows, :width], a_ref[h % 4, :width, :width], 1, 1)
            dk = dot(qt_ref[rows, lanes], ds, 1, 1)
            dq = dot(kt_ref[rows, lanes], ds, 1, 0) * HEAD_DIM**-0.5
            dpt_ref[rows, lanes] = dq.astype(bf16)
            dpt_ref[slice(D + rows.start, D + rows.stop), lanes] = dk.astype(bf16)
            dpt_ref[slice(2 * D + rows.start, 2 * D + rows.stop), lanes] = dv.astype(bf16)

    skewed(HEADS // 2, scores, weigh, collect)


def mean(v):
    return jnp.mean(v, axis=-1, keepdims=True)


def row_sum(v):
    return jnp.sum(v, axis=0, keepdims=True)


def flat(value):
    return value.reshape(-1, value.shape[-1])


BLOCK = 48
MAIN = 2 * SLOT


def eights(v):
    return jnp.sum(v.reshape(-1, 8, v.shape[-1]), axis=0)


def feed_tile(
    t, xs_ref, c_ref, es_ref, wo_ref, w1_ref, w2_ref, vec_ref, dh_ref, gvec_ref,
    acc_ref, other_ref, n1_ref, inv_ref, yb_ref, df_ref, u_ref, g_ref, tails,
    awo_ref, aw1_ref, aw2_ref,
):
    first = pl.multiple_of(t * TILE, 16)
    rows = pl.ds(first, TILE)
    piece = pl.ds(pl.multiple_of(t * PIECE, 16), PIECE)
    g_tail, du_tail, df_tail, yb_tail = tails
    bo, b2, g1, c1, g2, c2 = (vec_ref[i : i + 1, :] for i in range(2, 8))
    per = FF // D
    blocks = [slice(i, i + BLOCK) for i in range(0, TILE, BLOCK)]

    def at(block):
        return pl.ds(pl.multiple_of(first + block.start, 16), BLOCK)

    acc_ref[...] = dot(c_ref[rows, :], flat(wo_ref[...]), 1, 0)
    for block in blocks:
        h1 = xs_ref[at(block), :].astype(f32) + (acc_ref[block, :] + bo)
        mid = h1 - mean(h1)
        inv1 = lax.rsqrt(mean(mid * mid) + norm_epsilon)
        n1 = mid * inv1
        n1_ref[block, :] = n1
        inv_ref[block, :] = jnp.broadcast_to(inv1, (BLOCK, 128))
        yb_ref[block, :] = (n1 * g1 + c1).astype(bf16)

    pads = (acc_ref, other_ref)

    def w2_part(k):
        return flat(w2_ref[8 // per * k : 8 // per * (k + 1)])

    def w1_part(k):
        return flat(w1_ref[:, :, :, k * D : (k + 1) * D])

    def up(k):
        pads[k % 2][...] = dot(yb_ref[...], w1_part(k), 1, 0)

    def activate(k):
        cols = slice(k * D, (k + 1) * D)
        b1 = vec_ref[8 + k : 9 + k, :]
        for block in blocks:
            u = pads[k % 2][block, :] + b1
            cdf = 0.5 * (1.0 + lax.erf(u * 0.7071067811865476))
            g_ref[k * TILE + block.start : k * TILE + block.stop, :] = (u * cdf).astype(bf16)
            u_ref[block, cols] = cdf + u * jnp.exp(u * u * -0.5) * 0.3989422804014327

    def down(k):
        part = dot(g_ref[k * TILE : (k + 1) * TILE, :], w2_part(k), 1, 0)
        if k == 0:
            dh_ref[rows, :] = part
        else:
            dh_ref[rows, :] += part

    skewed(per, up, activate, down)
    sums = [jnp.zeros((8, D), f32)] * 3
    for block in blocks:
        h2 = (n1_ref[block, :] * g1 + c1) + (dh_ref[at(block), :] + b2)
        mid2 = h2 - mean(h2)
        inv2 = lax.rsqrt(mean(mid2 * mid2) + norm_epsilon)
        n2 = mid2 * inv2
        xs_ref[at(block), :] = (n2 * g2 + c2).astype(bf16)
        e = es_ref[at(block), :].astype(f32)
        en = e * n2
        eg = e * g2
        dh2 = (eg - mean(eg) - n2 * mean(eg * n2)) * inv2
        dh_ref[at(block), :] = dh2
        df = dh2.astype(bf16)
        df_ref[block, :] = df
        sums = [sums[0] + eights(e), sums[1] + eights(en), sums[2] + eights(df.astype(f32))]
    for i, value in zip((7, 6, 3), sums):
        gvec_ref[i : i + 1, :] += row_sum(value)
    dft = df_ref[:MAIN, :].T
    ybt = yb_ref[:MAIN, :].T
    df_tail[piece, :] = df_ref[MAIN:, :]
    yb_tail[piece, :] = yb_ref[MAIN:, :]

    def up_back(k):
        pads[k % 2][...] = dot(df_ref[...], w2_part(k), 1, 1)

    def activate_back(k):
        cols = slice(k * D, (k + 1) * D)
        here = slice(k * TILE, k * TILE + MAIN)
        at_tail = pl.ds(pl.multiple_of(k * TAIL + t * PIECE, 16), PIECE)
        aw2_ref[:, cols] += dot(dft, g_ref[here, :], 1, 0)
        g_tail[at_tail, :] = g_ref[here.stop : here.stop + PIECE, :]
        total = jnp.zeros((8, D), f32)
        for block in blocks:
            du = (pads[k % 2][block, :] * u_ref[block, cols]).astype(bf16)
            g_ref[k * TILE + block.start : k * TILE + block.stop, :] = du
            total = total + eights(du.astype(f32))
        gvec_ref[8 + k : 9 + k, :] += row_sum(total)

    def down_back(k):
        cols = slice(k * D, (k + 1) * D)
        here = slice(k * TILE, k * TILE + MAIN)
        at_tail = pl.ds(pl.multiple_of(k * TAIL + t * PIECE, 16), PIECE)
        aw1_ref[:, cols] += dot(ybt, g_ref[here, :], 1, 0)
        du_tail[at_tail, :] = g_ref[here.stop : here.stop + PIECE, :]
        part = dot(g_ref[k * TILE : (k + 1) * TILE, :], w1_part(k), 1, 1)
        dh_ref[rows, :] += part

    skewed(per, up_back, activate_back, down_back)
    sums = [jnp.zeros((8, D), f32)] * 3
    for block in blocks:
        dy = dh_ref[at(block), :]
        n1 = n1_ref[block, :]
        eg = dy * g1
        dh1 = (eg - mean(eg) - n1 * mean(eg * n1)) * inv_ref[block, :1]
        dh_ref[at(block), :] = dh1
        dr = dh1.astype(bf16)
        es_ref[at(block), :] = dr
        sums = [sums[0] + eights(dy), sums[1] + eights(dy * n1), sums[2] + eights(dr.astype(f32))]
    for i, value in zip((5, 4, 2), sums):
        gvec_ref[i : i + 1, :] += row_sum(value)
    main = pl.ds(first, MAIN)
    awo_ref[...] += dot(c_ref[main, :].T, es_ref[main, :], 1, 0)


def whole_kernel(*refs):
    refs = list(refs)

    def take(count):
        taken = refs[:count]
        del refs[:count]
        return taken

    state_in = take(15)
    tok_ref, cot_ref, seg_ref, keep_ref = take(4)
    out_ref, in_ref = take(2)
    state_out = take(15)
    copy_out = take(5)
    out_back, in_back = take(2)
    state = take(15)
    masters, firsts, seconds = state[:5], state[5:10], state[10:]
    weights = take(5)
    wa_ref, wo_ref, w1_ref, w2_ref, wv_ref = weights
    xs_ref, es_ref, xt_ref, qt_ref, kt_ref, vt_ref, c_ref, lse_ref, dh_ref, tag_ref = take(10)
    ext_ref, seg_halo, keep_halo = take(3)
    square, gvec_ref, gwa_ref, gwo_ref, grad_vec, halo_out, halo_in = take(7)
    twins, nears, fars, alongs = take(5), take(5), take(5), take(5)
    parts, copies, whole_vec = take(4), take(5), take(1)[0]
    (
        state_sems, load_sems, gather_send, gather_recv, edge_send, edge_recv,
        sum_send, sum_recv, copy_send, copy_recv, store_sems,
    ) = refs
    place = Place()
    seq, seq_count = place.z, DEPTH
    is_last = seq == seq_count - 1
    slots = Slots(tag_ref, seq, seq_count)
    rows = tok_ref.shape[1]
    ext_x, ext_e = ext_ref.at[pl.ds(0, HALO + rows)], ext_ref.at[pl.ds(HALO + rows, HALO + rows)]

    loads = [pltpu.make_async_copy(state_in[i], state[i], state_sems.at[i]) for i in range(15)]
    for load in loads:
        load.start()
    big_loads = [
        pltpu.make_async_copy(src.at[0], dst.at[pl.ds(HALO, rows)], load_sems.at[i])
        for i, (src, dst) in enumerate(((tok_ref, ext_x), (cot_ref, ext_e)))
    ]
    for load in big_loads:
        load.start()
    place.greet()
    edge = [
        remote(src, dst, edge_send.at[i], edge_recv.at[i], place.in_depth(1))
        for i, (src, dst) in enumerate((
            (tok_ref.at[0, pl.ds(rows - HALO, HALO)], ext_x.at[pl.ds(0, HALO)]),
            (cot_ref.at[0, pl.ds(rows - HALO, HALO)], ext_e.at[pl.ds(0, HALO)]),
            (seg_ref.at[:, pl.ds(rows - 128, 128)], seg_halo),
            (keep_ref.at[:, pl.ds(rows - 128, 128)], keep_halo),
        ))
    ]
    gathers = [Gather(place, weights[i], gather_send.at[i], gather_recv.at[i]) for i in range(5)]

    def put(i):
        shard = turned(square, masters[4][...])[: masters[4].shape[1]] if i == 4 else masters[i][...]
        weights[i][place.batch, place.z] = shard.astype(bf16)

    for i in (0, 4, 1, 2, 3):
        loads[i].wait()
    put(0)
    gathers[0].first()
    put(4)
    gathers[4].first()
    for copy in edge:
        copy.start()
    for i in (1, 2, 3):
        put(i)
    gathers[0].second()
    gathers[4].second()
    for i in (1, 2):
        gathers[i].first()
    for load in big_loads:
        load.wait()
    for copy in edge:
        copy.wait()
    tag_ref[...] = jnp.zeros_like(tag_ref)
    rim = seg_halo[...] * 2 + keep_halo[...]
    tag_ref[:, :HALO] = jnp.broadcast_to(rim[:, 128 - HALO :], (8, HALO))
    tag_ref[:, HALO : HALO + rows] = jnp.broadcast_to(seg_ref[...] * 2 + keep_ref[...], (8, rows))

    def stage_one(j, carry):
        start = first_row(j, seq)
        row = slot_row(j)
        stage_slot(ext_x, start, xs_ref, row)
        stage_slot(ext_e, start, es_ref, row)
        return carry

    lax.fori_loop(0, 8, stage_one, 0)
    slots.set_tail(xs_ref, tail_rows(ext_x, slots.count, is_last))
    slots.set_tail(es_ref, tail_rows(ext_e, slots.count, is_last))
    gathers[0].third()
    gathers[4].third()
    gathers[3].first()
    xt_ref[:, 8 * SLOT :] = jnp.zeros((D + AUG, 128), bf16)
    ones = lax.broadcasted_iota(jnp.int32, (AUG, LANES), 0) == 0
    xt_ref[D:, :] = jnp.where(ones, 1.0, 0.0).astype(bf16)
    gathers[0].fourth()
    gathers[4].fourth()
    for i in (1, 2):
        gathers[i].second()
    gathers[0].finish()
    gathers[4].finish()

    def forward(wt_ref, s_ref, a_ref, kn_ref, ct_ref):
        for part in range(3):
            wt_ref[part * D : (part + 1) * D, :] = flat(
                wa_ref[:, :, :, part * D : (part + 1) * D]
            ).T
        vec_t = flat(wv_ref[...])
        biases = (vec_t[:, 0:1].astype(f32), vec_t[:, 1:2].astype(f32))

        def block(xb, tag, pair, lanes):
            return forward_block(
                xb, tag, pair, lanes, wt_ref, biases, xt_ref, qt_ref, kt_ref, vt_ref, lse_ref,
                s_ref, a_ref, kn_ref, ct_ref,
            )

        def one(j, carry):
            for step, event in (
                (1, gathers[1].third), (1, gathers[3].second), (2, gathers[2].third),
                (3, gathers[1].fourth), (4, gathers[2].fourth), (5, gathers[3].third),
                (7, gathers[3].fourth),
            ):
                pl.when(j == step)(event)
            row = slot_row(j)
            lanes = pl.ds(pl.multiple_of(j * SLOT, 128), SLOT)
            c_ref[pl.ds(row, SLOT), :] = block(
                xs_ref[pl.ds(row, SLOT), :], slots.tag(j), 8 * seq + j, lanes
            )
            return carry

        lax.fori_loop(0, 8, one, 0)
        slots.set_tail(
            c_ref,
            block(
                slots.tail(xs_ref), slots.tail_tag(), slots.last_pair, pl.ds(8 * SLOT, TAIL)
            ),
        )

    pl.run_scoped(
        forward,
        pltpu.VMEM((3 * D, D), bf16),
        pltpu.VMEM((HEADS, SLOT, SLOT), f32),
        pltpu.VMEM((HEADS, SLOT, SLOT), bf16),
        pltpu.VMEM((SLOT, D), bf16),
        pltpu.VMEM((D, SLOT), bf16),
    )
    for i in (1, 2, 3):
        gathers[i].finish()

    def feed_all(
        vec_ref, acc_ref, other_ref, n1_ref, inv_ref, u_ref, awo_ref, aw1_ref, aw2_ref
    ):
        used = 0
        views = []
        for count in (4 * TILE, TILE, TILE, TAIL, TAIL, 4 * TAIL, 4 * TAIL):
            views.append(ext_ref.at[pl.ds(used, count)])
            used += count
        g_ref, yb_ref, df_ref, yb_tail, df_tail, g_tail, du_tail = views
        for ref in (awo_ref, aw1_ref, aw2_ref, gvec_ref):
            ref[...] = jnp.zeros_like(ref)
        vec_ref[...] = flat(wv_ref[...]).astype(f32).T[:16]

        def one(t, carry):
            feed_tile(
                t, xs_ref, c_ref, es_ref, wo_ref, w1_ref, w2_ref, vec_ref, dh_ref, gvec_ref, acc_ref,
                other_ref, n1_ref, inv_ref, yb_ref, df_ref, u_ref, g_ref, (g_tail, du_tail, df_tail, yb_tail),
                awo_ref, aw1_ref, aw2_ref,
            )
            return carry

        lax.fori_loop(0, TILES, one, 0)
        for k in range(FF // D):
            cols = slice(k * D, (k + 1) * D)
            at = slice(k * TAIL, (k + 1) * TAIL)
            aw2_ref[:, cols] += dot(df_tail[...].T, g_tail[at, :], 1, 0)
            aw1_ref[:, cols] += dot(yb_tail[...].T, du_tail[at, :], 1, 0)
        awo_ref[...] += dot(slots.tail(c_ref).T, slots.tail(es_ref), 1, 0)
        def convert(i, carry):
            value = aw2_ref[:, pl.ds(pl.multiple_of(i * 128, 128), 128)].astype(bf16).T
            w2_ref[i // 2, pl.ds(i % 2 * 2, 2)] = value.reshape(2, -1, D)
            return carry

        def convert_rows(i, carry):
            value = aw1_ref[pl.ds(pl.multiple_of(i * 64, 64), 64), :].astype(bf16)
            w1_ref[i] = value.reshape(DEPTH, -1, FF)
            gwo_ref[i // 2, i % 2] = (
                awo_ref[pl.ds(pl.multiple_of(i * 64, 64), 64), :].astype(bf16).reshape(DEPTH, -1, D)
            )
            return carry

        lax.fori_loop(0, FF // 128, convert, 0)
        lax.fori_loop(0, 8, convert_rows, 0)

    pl.run_scoped(
        feed_all,
        pltpu.VMEM((16, D), f32),
        pltpu.VMEM((TILE, D), f32),
        pltpu.VMEM((TILE, D), f32),
        pltpu.VMEM((TILE, D), f32),
        pltpu.VMEM((TILE, 128), f32),
        pltpu.VMEM((TILE, FF), f32),
        pltpu.VMEM((D, D), f32),
        pltpu.VMEM((D, FF), f32),
        pltpu.VMEM((D, FF), f32),
    )
    grads = [gwa_ref, gwo_ref, w1_ref, w2_ref, grad_vec]
    scatters = [
        Scatter(
            place, grads[i], twins[i], nears[i], fars[i], alongs[i], sum_send.at[i], sum_recv.at[i]
        )
        for i in range(5)
    ]
    for i in (3, 2, 1):
        scatters[i].first()
    for load in loads[5:]:
        load.wait()
    copy_gathers = [
        Gather(place, copies[i], copy_send.at[i], copy_recv.at[i], parts[i]) for i in range(4)
    ]
    copy_gathers.append(Gather(place, whole_vec, copy_send.at[4], copy_recv.at[4]))
    stores = []

    def store(src, dst):
        stores.append(pltpu.make_async_copy(src, dst, store_sems.at[len(stores)]))
        stores[-1].start()

    def update(i):
        total = scatters[i].total()
        if i == 4:
            square[...] = jnp.zeros_like(square)
            square[: total.shape[0], :] = total
            here, cols = masters[4].shape
            total = square[...].T[:here, :cols]
        new = adam_update(masters[i][...], firsts[i][...], seconds[i][...], total, learn_rates[i])
        firsts[i][...], seconds[i][...], masters[i][...] = new
        if i == 4:
            shard = turned(square, new[2])[: new[2].shape[1]].astype(bf16)
            whole_vec[place.batch, place.z] = shard
        else:
            low = new[2].astype(bf16)
            width = low.shape[1] // DEPTH
            for q in range(DEPTH):
                parts[i][q] = low[:, q * width : (q + 1) * width]
            copies[i][place.batch, place.z] = parts[i][place.z]
        copy_gathers[i].first()

    def backward(
        dpt_ref, ext_ref, s_ref, da_ref, a_ref, ds_ref, kn_ref, vn_ref, dct_ref, ct_ref
    ):
        low_ref = ext_e
        dpt_ref[:, 8 * SLOT :] = jnp.zeros((3 * D, 128), bf16)
        wo = flat(wo_ref[...])

        def block(dr, c, tag, pair, lanes):
            backward_block(
                dr, c, tag, pair, lanes, wo, qt_ref, kt_ref, vt_ref, lse_ref, dpt_ref,
                s_ref, da_ref, a_ref, ds_ref, kn_ref, vn_ref, dct_ref, ct_ref,
            )

        def one(j, carry):
            for step, event in (
                (0, scatters[3].second), (1, scatters[2].second), (2, scatters[3].third),
                (3, scatters[3].fourth), (3, scatters[1].second), (4, scatters[2].third),
                (5, scatters[2].fourth), (5, scatters[1].third), (6, scatters[1].fourth),
                (6, functools.partial(update, 3)), (7, functools.partial(update, 2)),
            ):
                pl.when(j == step)(event)
            row = slot_row(j)
            at = pl.ds(row, SLOT)
            lanes = pl.ds(pl.multiple_of(j * SLOT, 128), SLOT)
            block(es_ref[at, :], c_ref[at, :], slots.tag(j), 8 * seq + j, lanes)
            return carry

        lax.fori_loop(0, 8, one, 0)
        block(
            slots.tail(es_ref), slots.tail(c_ref), slots.tail_tag(), slots.last_pair,
            pl.ds(8 * SLOT, TAIL),
        )
        for part in range(3):
            cols = slice(part * D, (part + 1) * D)
            g = dot(xt_ref[...], dpt_ref[cols, :], 1, 1)
            gwa_ref[:, :, :, :, cols] = g[:D].astype(bf16).reshape(PLANE, 2, DEPTH, -1, D)
            if part != 1:
                gvec_ref[part // 2 : part // 2 + 1, :] = g[D : D + 1]
        grad_vec[...] = gvec_ref[...].T.reshape(grad_vec.shape)
        scatters[0].first()
        scatters[4].first()

        def output_one(j, carry):
            at = pl.ds(slot_row(j), SLOT)
            unstage_slot(
                ext_ref, first_row(j, seq),
                lambda g: xs_ref[at, g * 128 : (g + 1) * 128].astype(f32),
            )
            return carry

        def close(value):
            @pl.when(is_last)
            def _():
                ext_ref[HALO + rows - slots.count : HALO + rows, :] = value[: slots.count]

        lax.fori_loop(0, 8, output_one, 0)
        close(slots.tail(xs_ref).astype(f32))
        scatters[0].second()
        scatters[4].second()
        copy_gathers[3].second()
        copy_gathers[2].second()
        update(1)
        low_ref[...] = ext_ref[: HALO + rows, :].astype(bf16)
        halo_out[...] = low_ref[:HALO, :]
        edge_back[0].start()
        store(low_ref.at[pl.ds(HALO, rows)], out_ref)
        wa = flat(wa_ref[...])

        def input_block(lanes):
            return dot(wa, dpt_ref[:, lanes], 1, 0).T

        def input_two(i, carry):
            for step, event in (
                (0, copy_gathers[3].third), (1, copy_gathers[2].third), (1, copy_gathers[1].second),
                (1, copy_gathers[3].fourth), (1, scatters[0].third), (1, scatters[4].third),
                (2, copy_gathers[2].fourth), (2, copy_gathers[1].third), (3, scatters[0].fourth),
                (3, scatters[4].fourth), (3, copy_gathers[1].fourth),
            ):
                pl.when(i == step)(event)

            def product(n):
                lanes = pl.ds(pl.multiple_of((2 * i + n) * SLOT, 128), SLOT)
                grad = dot(wa, dpt_ref[:, lanes], 1, 0)
                s_ref[2 * n], s_ref[2 * n + 1] = grad[:SLOT], grad[SLOT:]

            def put_back(n):
                j = 2 * i + n
                at = pl.ds(slot_row(j), SLOT)

                def column(g):
                    part = s_ref[2 * n + g // 2, g % 2 * 128 : g % 2 * 128 + 128, :].T
                    return part + dh_ref[at, g * 128 : (g + 1) * 128]

                unstage_slot(ext_ref, first_row(j, seq), column)

            skewed(2, product, put_back)
            return carry

        lax.fori_loop(0, 4, input_two, 0)
        close(input_block(pl.ds(8 * SLOT, TAIL)) + slots.tail(dh_ref))
        halo_in[...] = ext_ref[:HALO, :]
        edge_back[1].start()
        store(ext_ref.at[pl.ds(HALO, rows)], in_ref)
        update(4)
        update(0)
        for i in range(5):
            for n, kind in enumerate((firsts, seconds, masters)):
                store(kind[i], state_out[5 * n + i])
        for i in (4, 0):
            copy_gathers[i].second()
        for i in (4, 0):
            copy_gathers[i].third()
        for i in (4, 0):
            copy_gathers[i].fourth()
        for i in (3, 2, 1, 4, 0):
            copy_gathers[i].finish()
            scatters[i].finish()
        here = masters[4].shape[0]
        mine = jnp.concatenate([whole_vec[seq * 2 + q // 4, q % 4] for q in range(8)], 0)
        copies[4][...] = mine.astype(f32).T[:here].astype(bf16)
        for i in range(5):
            store(copies[i], copy_out[i])
        for copy in stores:
            copy.wait()
        for copy in edge_back:
            copy.wait()

    edge_back = [
        remote(halo_out, out_back, edge_send.at[4], edge_recv.at[4], place.in_depth(3)),
        remote(halo_in, in_back, edge_send.at[5], edge_recv.at[5], place.in_depth(3)),
    ]
    pl.run_scoped(
        backward,
        pltpu.VMEM((3 * D, LANES), bf16),
        pltpu.VMEM((HALO + rows + 16, D), f32),
        pltpu.VMEM((4, SLOT, SLOT), f32),
        pltpu.VMEM((4, SLOT, SLOT), f32),
        pltpu.VMEM((4, SLOT, SLOT), bf16),
        pltpu.VMEM((4, SLOT, SLOT), bf16),
        pltpu.VMEM((SLOT, D), bf16),
        pltpu.VMEM((SLOT, D), bf16),
        pltpu.VMEM((D, SLOT), bf16),
        pltpu.VMEM((D, SLOT), bf16),
    )


def whole(masters, firsts, seconds, tokens, cotangent, segment, keep):
    shape = jax.ShapeDtypeStruct
    vmem = pl.BlockSpec(memory_space=pltpu.VMEM)
    hbm = pl.BlockSpec(memory_space=pl.ANY)
    state = (*masters, *firsts, *seconds)
    rows = tokens.shape[1]
    r = masters[0].shape[0]
    shapes = ((r, 3 * D), (r, D), (r, FF), (4 * r, D))
    copies = [((8, DEPTH, s[0], s[1] // DEPTH), bf16) for s in shapes]
    copies.append(((masters[4].shape[0], 128), bf16))
    halos = [((HALO, D), bf16), ((HALO, D), f32)]
    out_shape = [
        shape((rows, D), bf16),
        shape((rows, D), f32),
        *[shape(s.shape, f32) for i in range(3) for s in masters],
        *[shape(*c) for c in copies],
        *[shape(*h) for h in halos],
    ]
    five = [(s, bf16) for s in shapes] + [((r, 128), f32)]
    tall = ROWS
    scratch = [pltpu.VMEM(s.shape, f32) for s in state]
    scratch += [pltpu.VMEM((8, DEPTH) + s, bf16) for s in (*shapes, (r, 128))]
    scratch += [
        pltpu.VMEM((tall, D), bf16),
        pltpu.VMEM((tall, D), bf16),
        pltpu.VMEM((D + AUG, LANES), bf16),
        pltpu.VMEM((D, LANES), bf16),
        pltpu.VMEM((D, LANES), bf16),
        pltpu.VMEM((D, LANES), bf16),
        pltpu.VMEM((tall, D), bf16),
        pltpu.VMEM((HEADS, LANES), f32),
        pltpu.VMEM((tall, D), f32),
        pltpu.VMEM((8, LANES), jnp.int32),
        pltpu.VMEM((2 * (HALO + rows), D), bf16),
        pltpu.VMEM((1, 128), jnp.int32),
        pltpu.VMEM((1, 128), jnp.int32),
        pltpu.VMEM((128, 128), f32),
        pltpu.VMEM((128, D), f32),
        pltpu.VMEM((PLANE, 2, DEPTH) + shapes[0], bf16),
        pltpu.VMEM((PLANE, 2, DEPTH) + shapes[1], bf16),
        pltpu.VMEM((PLANE, 2, DEPTH, r, 128), f32),
        *[pltpu.VMEM(*h) for h in halos],
    ]
    for lead in ((PLANE, DEPTH), (4, DEPTH // 2), (2, DEPTH // 2), (3,)):
        scratch += [pltpu.VMEM(lead + s, t) for s, t in five]
    scratch += [pltpu.VMEM((DEPTH, s[0], s[1] // DEPTH), bf16) for s in shapes]
    scratch += [pltpu.VMEM(*c) for c in copies]
    scratch.append(pltpu.VMEM((8, DEPTH, r, 128), bf16))
    dma = pltpu.SemaphoreType.DMA
    scratch += [
        dma((15,)), dma((2,)), dma((5, 11)), dma((5, 11)), dma((6,)), dma((6,)),
        dma((5, 13)), dma((5, 13)), dma((5, 11)), dma((5, 11)), dma((22,)),
    ]
    return pl.pallas_call(
        whole_kernel,
        out_shape=out_shape,
        in_specs=[hbm] * 17 + [vmem] * 2,
        out_specs=[hbm] * 22 + [vmem] * 2,
        scratch_shapes=scratch,
        compiler_params=pltpu.CompilerParams(
            collective_id=0, has_side_effects=True, vmem_limit_bytes=63 * MIB
        ),
        name="whole",
    )(*state, tokens, cotangent, segment, keep)


LAST_PART = 496


def last_kernel(*refs):
    results, backs, ends = refs[:22], refs[22:24], refs[24:46]
    lows, (load_sems, store_sems) = refs[46:68], refs[68:]
    rows = results[0].shape[0]
    seq = lax.axis_index("seq")
    rim = pl.ds(rows - HALO, HALO)
    places = [(i, rim) for i in range(2)]
    places += [
        (i, pl.ds(first, LAST_PART))
        for i in range(2)
        for first in range(0, rows - HALO, LAST_PART)
    ]
    places += [(i, pl.ds(0, results[i].shape[0])) for i in range(2, 22)]
    loads = [
        pltpu.make_async_copy(results[i].at[at], lows[i].at[at], load_sems.at[n])
        for n, (i, at) in enumerate(places)
    ]
    stores = [
        pltpu.make_async_copy(lows[i].at[at], ends[i].at[at], store_sems.at[n])
        for n, (i, at) in enumerate(places)
    ]
    for load in loads:
        load.start()
    place = lax.broadcasted_iota(jnp.int32, (HALO, 1), 0)
    theirs = (place >= HALO - 8 * (seq + 1)) & (seq < lax.axis_size("seq") - 1)
    for n, (i, at) in enumerate(places):
        loads[n].wait()
        if n < 2:
            own = lows[i][rim, :].astype(f32)
            lows[i][rim, :] = jnp.where(theirs, backs[i][...].astype(f32), own).astype(lows[i].dtype)
        stores[n].start()
    for store in stores:
        store.wait()


def last(results, out_back, in_back):
    shape = jax.ShapeDtypeStruct
    vmem = pl.BlockSpec(memory_space=pltpu.VMEM)
    hbm = pl.BlockSpec(memory_space=pl.ANY)
    count = 22 + 2 * ((results[0].shape[0] - HALO) // LAST_PART)
    return pl.pallas_call(
        last_kernel,
        out_shape=[shape(a.shape, a.dtype) for a in results],
        in_specs=[hbm] * 22 + [vmem, vmem],
        out_specs=[hbm] * 22,
        scratch_shapes=[pltpu.VMEM(a.shape, a.dtype) for a in results]
        + [pltpu.SemaphoreType.DMA((count,)), pltpu.SemaphoreType.DMA((count,))],
        compiler_params=pltpu.CompilerParams(vmem_limit_bytes=60 * MIB),
        name="last",
    )(*results, out_back, in_back)


def on_device(
    tokens,
    cotangent,
    segment,
    keep_mask,
    attn_master,
    out_master,
    in_master,
    back_master,
    vec_master,
    attn_first,
    out_first,
    in_first,
    back_first,
    vec_first,
    attn_second,
    out_second,
    in_second,
    back_second,
    vec_second,
):
    seq = lax.axis_index("seq")
    seq_count = lax.axis_size("seq")
    both = ("batch", "seq")
    rows = tokens.shape[1]
    masters = (attn_master, out_master, in_master, back_master, vec_master)
    firsts = (attn_first, out_first, in_first, back_first, vec_first)
    seconds = (attn_second, out_second, in_second, back_second, vec_second)
    direct = seq_count == DEPTH and lax.axis_size("batch") == 2 * PLANE
    forward = [(i, i + 1) for i in range(seq_count - 1)]
    backward = [(i + 1, i) for i in range(seq_count - 1)]
    if direct:
        *results, out_back, grad_back = whole(
            masters, firsts, seconds, tokens, cotangent, segment, keep_mask
        )
        for i in range(17, 21):
            results[i] = results[i].reshape(-1, results[i].shape[-1])
        ends = last(results, out_back, grad_back)
        return (ends[0][None], ends[1][None], *ends[2:])
    low = [w.astype(bf16) for w in masters]
    low[4] = jnp.pad(low[4].T, ((0, 0), (0, 128 - low[4].shape[0])))
    attn_w, out_w, in_w, back_w, vec_t = (
        lax.all_gather(w, both, axis=0, tiled=True) for w in low
    )
    x_halo, e_halo, seg_halo, keep_halo = (
        lax.ppermute(a, "seq", forward)
        for a in (
            tokens[0, rows - HALO :], cotangent[0, rows - HALO :],
            segment[:, rows - 128 :], keep_mask[:, rows - 128 :],
        )
    )
    xs, es, xt, qt, kt, vt, c, lse = attn_forward(
        seq_count, tokens, cotangent, x_halo, e_halo, segment, keep_mask, seg_halo, keep_halo,
        attn_w, vec_t,
    )
    z, dh, dr, gwo, gw1, gw2, gvec, gb1 = feed(xs, c, es, out_w, in_w, back_w, vec_t)
    out, out_halo, grad_in, grad_in_halo, gwa, gbias = attn_backward(
        seq_count, xt, qt, kt, vt, lse, dr, dh, z, attn_w, out_w
    )
    grads = (gwa, gwo, gw1, gw2)
    grad_vec = jnp.concatenate(
        [gbias[:1, :D], gbias[:1, 2 * D :], gvec[2:8], gb1[0].reshape(FF // D, D)], 0
    )
    sums = [lax.psum_scatter(g.astype(f32), both, scatter_dimension=0, tiled=True) for g in grads]
    sums.append(lax.psum_scatter(grad_vec, both, scatter_dimension=1, tiled=True))
    new = [
        adam_update(masters[i], firsts[i], seconds[i], sums[i], learn_rates[i]) for i in range(5)
    ]

    def own_columns(i):
        whole = lax.all_gather(new[i][2].astype(bf16), both, axis=1 if i == 4 else 0, tiled=True)
        count = whole.shape[1] // seq_count
        return lax.dynamic_slice_in_dim(whole, seq * count, count, 1)

    results = [out, grad_in] + [new[i][part] for part in range(3) for i in range(5)]
    results += [own_columns(i) for i in range(5)]
    out_back = lax.ppermute(out_halo, "seq", backward)
    grad_back = lax.ppermute(grad_in_halo, "seq", backward)
    ends = last(results, out_back, grad_back)
    return (ends[0][None], ends[1][None], *ends[2:])


def solution(mesh):
    stream = P("batch", "seq", None)
    rows = P(("batch", "seq"), None)
    vector = P(None, ("batch", "seq"))
    five = (rows, rows, rows, rows, vector)
    return jax.shard_map(
        on_device,
        mesh=mesh,
        in_specs=(stream, stream, P("batch", "seq"), P("batch", "seq")) + five * 3,
        out_specs=(stream, stream) + five * 3 + (P(None, "seq"),) * 5,
        check_vma=False,
    )
```

```python
import functools

import jax
import jax.numpy as jnp
from jax import lax
from jax.experimental import pallas as pl
from jax.experimental.pallas import tpu as pltpu
from jax.sharding import PartitionSpec as P

D = 512
HEADS = 8
HEAD_DIM = 64
FF = 2048
STEP = 10
PAIR = 255
SLOT = 256
HALO = 64
TILES = 4
TAIL = 64
PIECE = TAIL // TILES
TILE = 2 * SLOT + PIECE
ROWS = TILES * TILE
LANES = 8 * SLOT + 128
AUG = 16
MIB = 1 << 20

norm_epsilon = 1e-05
beta_first = 0.9
beta_second = 0.999
adam_epsilon = 1e-08
weight_decay = 0.01
learn_rates = (0.03, 0.2, 0.03, 0.02, 0.5)
big = 1e30

f32 = jnp.float32
bf16 = jnp.bfloat16


def dot(a, b, ca, cb):
    return lax.dot_general(a, b, (((ca,), (cb,)), ((), ())), preferred_element_type=f32)


def adam_update(master, first, second, gradient, rate):
    first_new = beta_first * first + (1.0 - beta_first) * gradient
    second_new = beta_second * second + (1.0 - beta_second) * gradient * gradient
    first_hat = first_new / (1.0 - beta_first**STEP)
    second_hat = second_new / (1.0 - beta_second**STEP)
    master_new = master - rate * (
        first_hat / (jnp.sqrt(second_hat) + adam_epsilon) + weight_decay * master
    )
    return (first_new, second_new, master_new)


def slot_row(j):
    return pl.multiple_of((j // 2) * TILE + (j % 2) * SLOT, 16)


def first_row(j, seq):
    return HALO + PAIR * j - 8 * seq


def staged(ref, start):
    base = pl.multiple_of((start // 16) * 16, 16)
    rest = start - base
    wide = ref[pl.ds(base, SLOT + 16), :].astype(f32)
    wide = jnp.where(rest >= 8, wide[8:], wide[:-8])
    shift = rest % 8
    groups = (SLOT + 8) // 8
    wide = wide.reshape(groups, 8, D)
    turned = pltpu.roll(wide, lax.rem(8 - shift, 8), 1)
    place = lax.broadcasted_iota(jnp.int32, (groups - 1, 8, D), 1)
    block = jnp.where(place < 8 - shift, turned[:-1], turned[1:]).reshape(SLOT, D)
    row = lax.broadcasted_iota(jnp.int32, (SLOT, D), 0)
    return jnp.where(row < PAIR, block, 0.0).astype(bf16)


def unstage(ref, start, block):
    base = pl.multiple_of((start // 8) * 8, 8)
    shift = start - base
    turned = pltpu.roll(block.reshape(SLOT // 8, 8, D), shift, 1)
    place = lax.broadcasted_iota(jnp.int32, (1, 8, D), 1)
    keep = ref[pl.ds(base, 8), :].reshape(1, 8, D)
    low = jnp.concatenate([keep, turned], 0)
    high = jnp.concatenate([turned, turned[-1:]], 0)
    place = lax.broadcasted_iota(jnp.int32, low.shape, 1)
    ref[pl.ds(base, SLOT + 8), :] = jnp.where(place < shift, low, high).reshape(SLOT + 8, D)


def stage_slot(ref, start, out_ref, row):
    base = pl.multiple_of((start // 16) * 16, 16)
    rest = start - base
    shift = rest % 8
    groups = (SLOT + 8) // 8
    place = lax.broadcasted_iota(jnp.int32, (groups - 1, 8, 128), 1)
    number = lax.broadcasted_iota(jnp.int32, (groups - 1, 8, 128), 0) * 8 + place
    for g in range(D // 128):
        cols = slice(g * 128, (g + 1) * 128)
        wide = ref[pl.ds(base, SLOT + 16), cols].astype(f32)
        wide = jnp.where(rest >= 8, wide[8:], wide[:-8]).reshape(groups, 8, 128)
        turned = pltpu.roll(wide, lax.rem(8 - shift, 8), 1)
        block = jnp.where(place < 8 - shift, turned[:-1], turned[1:])
        block = jnp.where(number < PAIR, block, 0.0)
        out_ref[pl.ds(row, SLOT), cols] = block.reshape(SLOT, 128).astype(bf16)


def unstage_slot(ref, start, column):
    base = pl.multiple_of((start // 8) * 8, 8)
    shift = start - base
    for g in range(D // 128):
        cols = slice(g * 128, (g + 1) * 128)
        turned = pltpu.roll(column(g).reshape(SLOT // 8, 8, 128), shift, 1)
        keep = ref[pl.ds(base, 8), cols].reshape(1, 8, 128)
        low = jnp.concatenate([keep, turned], 0)
        high = jnp.concatenate([turned, turned[-1:]], 0)
        place = lax.broadcasted_iota(jnp.int32, low.shape, 1)
        ref[pl.ds(base, SLOT + 8), cols] = jnp.where(place < shift, low, high).reshape(SLOT + 8, 128)


def tail_rows(ref, count, is_last):
    kept = ref[HALO + 2048 - count : HALO + 2048, :].astype(f32)
    if count < TAIL:
        kept = jnp.concatenate([kept, jnp.zeros((TAIL - count, D), f32)], 0)
    return jnp.where(is_last, kept, 0.0).astype(bf16)


def tag_rows(tag, pair):
    width = tag.shape[1]
    number = tag // 2 - 2 * pair
    kept = tag % 2
    row = lax.broadcasted_iota(jnp.int32, (AUG, width), 0)
    match = row == number
    query = jnp.where(match, 1.0, 0.0).astype(bf16)
    key = jnp.where(match & (kept == 1), 0.0, -big)
    key = jnp.where(row < 4, key, 0.0).astype(bf16)
    return query, key


def attn_forward_kernel(
    seq_count, tok_ref, cot_ref, tok_halo, cot_halo, seg_ref, keep_ref, seg_halo, keep_halo,
    w_ref, vec_ref,
    xs_ref, es_ref, xt_ref, qt_ref, kt_ref, vt_ref, c_ref, lse_ref,
    wt_ref, x_ref, e_ref, tag_ref, sems,
):
    seq = lax.axis_index("seq")
    is_last = seq == seq_count - 1
    rows = tok_ref.shape[1]
    loads = []
    for i, (whole, halo, ext) in enumerate(((tok_ref, tok_halo, x_ref), (cot_ref, cot_halo, e_ref))):
        loads.append(pltpu.make_async_copy(whole.at[0], ext.at[pl.ds(HALO, rows)], sems.at[2 * i]))
        loads.append(pltpu.make_async_copy(halo, ext.at[pl.ds(0, HALO)], sems.at[2 * i + 1]))
    for load in loads:
        load.start()
    for part in range(3):
        wt_ref[part * D : (part + 1) * D, :] = w_ref[:, part * D : (part + 1) * D].T
    tag_ref[...] = jnp.zeros_like(tag_ref)
    edge = seg_halo[...] * 2 + keep_halo[...]
    tag_ref[:, :HALO] = jnp.broadcast_to(edge[:, 128 - HALO :], (8, HALO))
    tag_ref[:, HALO : HALO + rows] = jnp.broadcast_to(seg_ref[...] * 2 + keep_ref[...], (8, rows))
    query_bias = vec_ref[:, 0:1].astype(f32)
    value_bias = vec_ref[:, 1:2].astype(f32)
    for load in loads:
        load.wait()

    def block(xb, tag, pair, lane, width):
        lanes = pl.ds(lane, width)
        xt_ref[:D, lanes] = xb.T
        q = dot(wt_ref[:D, :], xb, 1, 1) + query_bias
        q = (q.astype(bf16).astype(f32) * HEAD_DIM**-0.5).astype(bf16)
        k = dot(wt_ref[D : 2 * D, :], xb, 1, 1).astype(bf16)
        v = (dot(wt_ref[2 * D :, :], xb, 1, 1) + value_bias).astype(bf16)
        query_tag, key_tag = tag_rows(tag, pair)
        vt_ref[:, lanes] = v
        context = []
        for h in range(HEADS):
            rows = slice(h * HEAD_DIM, (h + 1) * HEAD_DIM)
            qh = jnp.concatenate([q[rows], query_tag], 0)
            kh = jnp.concatenate([k[rows], key_tag], 0)
            qt_ref[h, :, lanes] = qh
            kt_ref[h, :, lanes] = kh
            s = dot(kh, qh, 0, 0)
            top = jnp.max(s, axis=0, keepdims=True)
            ex = jnp.exp(s - top)
            total = jnp.sum(ex, axis=0, keepdims=True)
            lse_ref[h : h + 1, lanes] = top + jnp.log(total)
            a = (ex * (1.0 / total)).astype(bf16)
            context.append(dot(v[rows], a, 1, 0))
        return jnp.concatenate(context, 0).astype(bf16).T

    def one(j, carry):
        start = first_row(j, seq)
        row = slot_row(j)
        xb = staged(x_ref, start)
        xs_ref[pl.ds(row, SLOT), :] = xb
        es_ref[pl.ds(row, SLOT), :] = staged(e_ref, start)
        wide = tag_ref[:, pl.ds(pl.multiple_of(j * SLOT, 128), SLOT + 128)]
        width = SLOT + 128
        tag = pltpu.roll(wide, width - (start - j * SLOT), 1)[:1, :SLOT]
        c_ref[pl.ds(row, SLOT), :] = block(
            xb, tag, 8 * seq + j, pl.multiple_of(j * SLOT, 128), SLOT
        )
        return carry

    lax.fori_loop(0, 8, one, 0)
    count = 8 * seq_count
    xt_ref[:, 8 * SLOT :] = jnp.zeros((D + AUG, 128), bf16)
    xb = tail_rows(x_ref, count, is_last)
    eb = tail_rows(e_ref, count, is_last)
    tag = tag_ref[:1, 2048:2176]
    tag = pltpu.roll(tag_ref[:, 2048:2176], 128 - (64 - count), 1)[:1, :TAIL] if count < 64 else tag[:, :TAIL]
    place = lax.broadcasted_iota(jnp.int32, (1, TAIL), 1)
    tag = jnp.where(place < count, tag, (2 * 8 * seq_count + 3) * 2)
    cb = block(xb, tag, 8 * seq_count, 8 * SLOT, TAIL)
    for t in range(TILES):
        rows = slice(t * PIECE, (t + 1) * PIECE)
        at = slice(t * TILE + 2 * SLOT, (t + 1) * TILE)
        xs_ref[at, :] = xb[rows]
        es_ref[at, :] = eb[rows]
        c_ref[at, :] = cb[rows]
    ones = lax.broadcasted_iota(jnp.int32, (AUG, LANES), 0) == 0
    xt_ref[D:, :] = jnp.where(ones, 1.0, 0.0).astype(bf16)


def attn_forward(seq_count, tokens, cotangent, *others):
    shape = jax.ShapeDtypeStruct
    vmem = pl.BlockSpec(memory_space=pltpu.VMEM)
    hbm = pl.BlockSpec(memory_space=pl.ANY)
    return pl.pallas_call(
        functools.partial(attn_forward_kernel, seq_count),
        out_shape=(
            shape((ROWS, D), bf16),
            shape((ROWS, D), bf16),
            shape((D + AUG, LANES), bf16),
            shape((HEADS, HEAD_DIM + AUG, LANES), bf16),
            shape((HEADS, HEAD_DIM + AUG, LANES), bf16),
            shape((D, LANES), bf16),
            shape((ROWS, D), bf16),
            shape((HEADS, LANES), f32),
        ),
        in_specs=[hbm, hbm] + [vmem] * len(others),
        out_specs=[vmem] * 8,
        scratch_shapes=[
            pltpu.VMEM((3 * D, D), bf16),
            pltpu.VMEM((HALO + tokens.shape[1], D), bf16),
            pltpu.VMEM((HALO + tokens.shape[1], D), bf16),
            pltpu.VMEM((8, LANES), jnp.int32),
            pltpu.SemaphoreType.DMA((4,)),
        ],
        compiler_params=pltpu.CompilerParams(vmem_limit_bytes=56 * MIB),
        name="attn_forward",
    )(tokens, cotangent, *others)


def feed_kernel(
    xs_ref, c_ref, es_ref, wo_ref, w1_ref, w2_ref, vect_ref,
    z_ref, dh_ref, dr_ref, gwo_ref, gw1_ref, gw2_ref, gvec_ref, gb1_ref,
    u_ref, g_ref, awo_ref, aw1_ref, aw2_ref, vec_ref,
):
    step = pl.program_id(0)

    @pl.when(step == 0)
    def _():
        awo_ref[...] = jnp.zeros_like(awo_ref)
        aw1_ref[...] = jnp.zeros_like(aw1_ref)
        aw2_ref[...] = jnp.zeros_like(aw2_ref)
        gvec_ref[...] = jnp.zeros_like(gvec_ref)
        gb1_ref[...] = jnp.zeros_like(gb1_ref)
        vec_ref[...] = vect_ref[...].astype(f32).T

    def mean(v):
        return jnp.mean(v, axis=-1, keepdims=True)

    def row_sum(v):
        return jnp.sum(v, axis=0, keepdims=True)

    bo, b2, g1, c1, g2, c2 = (vec_ref[i : i + 1, :] for i in range(2, 8))
    h1 = xs_ref[...].astype(f32) + (dot(c_ref[...], wo_ref[...], 1, 0) + bo)
    mid = h1 - mean(h1)
    inv1 = lax.rsqrt(mean(mid * mid) + norm_epsilon)
    n1 = mid * inv1
    y = n1 * g1 + c1
    yb = y.astype(bf16)
    chunk = D
    f = None
    for k in range(FF // chunk):
        cols = slice(k * chunk, (k + 1) * chunk)
        u = dot(yb, w1_ref[:, cols], 1, 0) + vec_ref[8 + k : 9 + k, :]
        cdf = 0.5 * (1.0 + lax.erf(u * 0.7071067811865476))
        gk = (u * cdf).astype(bf16)
        u_ref[:, cols] = cdf + u * jnp.exp(u * u * -0.5) * 0.3989422804014327
        g_ref[:, cols] = gk
        part = dot(gk, w2_ref[cols, :], 1, 0)
        f = part if f is None else f + part
    h2 = y + (f + b2)
    mid2 = h2 - mean(h2)
    inv2 = lax.rsqrt(mean(mid2 * mid2) + norm_epsilon)
    n2 = mid2 * inv2
    z_ref[...] = (n2 * g2 + c2).astype(bf16)
    e = es_ref[...].astype(f32)
    gvec_ref[7:8, :] += row_sum(e)
    gvec_ref[6:7, :] += row_sum(e * n2)
    eg = e * g2
    dh2 = (eg - mean(eg) - n2 * mean(eg * n2)) * inv2
    df = dh2.astype(bf16)
    gvec_ref[3:4, :] += row_sum(df.astype(f32))
    dft = df.T
    ybt = yb.T
    dy = dh2
    for k in range(FF // chunk):
        cols = slice(k * chunk, (k + 1) * chunk)
        aw2_ref[:, cols] += dot(dft, g_ref[:, cols], 1, 0)
        dg = dot(df, w2_ref[cols, :], 1, 1)
        du = (dg * u_ref[:, cols]).astype(bf16)
        gb1_ref[:1, cols] += row_sum(du.astype(f32))
        aw1_ref[:, cols] += dot(ybt, du, 1, 0)
        dy = dy + dot(du, w1_ref[:, cols], 1, 1)
    gvec_ref[5:6, :] += row_sum(dy)
    gvec_ref[4:5, :] += row_sum(dy * n1)
    eg = dy * g1
    dh1 = (eg - mean(eg) - n1 * mean(eg * n1)) * inv1
    dh_ref[...] = dh1
    dr = dh1.astype(bf16)
    dr_ref[...] = dr
    gvec_ref[2:3, :] += row_sum(dr.astype(f32))
    awo_ref[...] += dot(c_ref[...].T, dr, 1, 0)

    @pl.when(step == TILES - 1)
    def _():
        gwo_ref[...] = awo_ref[...].astype(bf16)
        gw1_ref[...] = aw1_ref[...].astype(bf16)
        for k in range(FF // chunk):
            cols = slice(k * chunk, (k + 1) * chunk)
            gw2_ref[cols, :] = aw2_ref[:, cols].astype(bf16).T


def feed(xs, c, es, wo, w1, w2, vec_t):
    shape = jax.ShapeDtypeStruct
    tile = pl.BlockSpec((TILE, D), lambda i: (i, 0))

    def whole(*dims):
        return pl.BlockSpec(dims, lambda i: (0,) * len(dims), pipeline_mode=pl.Buffered(1))

    return pl.pallas_call(
        feed_kernel,
        grid=(TILES,),
        out_shape=(
            shape((ROWS, D), bf16),
            shape((ROWS, D), f32),
            shape((ROWS, D), bf16),
            shape((D, D), bf16),
            shape((D, FF), bf16),
            shape((FF, D), bf16),
            shape((8, D), f32),
            shape((8, FF), f32),
        ),
        in_specs=[tile, tile, tile, whole(D, D), whole(D, FF), whole(FF, D), whole(D, 128)],
        out_specs=[tile, tile, tile, whole(D, D), whole(D, FF), whole(FF, D), whole(8, D), whole(8, FF)],
        scratch_shapes=[
            pltpu.VMEM((TILE, FF), f32),
            pltpu.VMEM((TILE, FF), bf16),
            pltpu.VMEM((D, D), f32),
            pltpu.VMEM((D, FF), f32),
            pltpu.VMEM((D, FF), f32),
            pltpu.VMEM((128, D), f32),
        ],
        compiler_params=pltpu.CompilerParams(vmem_limit_bytes=60 * MIB),
        name="feed",
    )(xs, c, es, wo, w1, w2, vec_t)


def attn_backward_kernel(
    seq_count, xt_ref, qt_ref, kt_ref, vt_ref, lse_ref, dr_ref, dh_ref, z_ref, w_ref, wo_ref,
    out_ref, out_halo_ref, in_ref, in_halo_ref, gwa_ref, gbias_ref,
    dpt_ref, ext_ref,
):
    seq = lax.axis_index("seq")
    is_last = seq == seq_count - 1

    def block(dr, lane, width):
        lanes = pl.ds(lane, width)
        dct = dot(wo_ref[...], dr, 1, 1).astype(bf16)
        for h in range(HEADS):
            rows = slice(h * HEAD_DIM, (h + 1) * HEAD_DIM)
            qh = qt_ref[h, :, lanes]
            kh = kt_ref[h, :, lanes]
            vh = vt_ref[rows, lanes]
            dch = dct[rows]
            a = jnp.exp(dot(kh, qh, 0, 0) - lse_ref[h : h + 1, lanes])
            da = dot(vh, dch, 0, 0)
            ada = a * da
            ds = (ada - a * jnp.sum(ada, axis=0, keepdims=True)).astype(bf16)
            dv = dot(dch, a.astype(bf16), 1, 1)
            dk = dot(qh[:HEAD_DIM], ds, 1, 1)
            dq = dot(kh[:HEAD_DIM], ds, 1, 0) * HEAD_DIM**-0.5
            dpt_ref[rows, lanes] = dq.astype(bf16)
            dpt_ref[slice(D + h * HEAD_DIM, D + (h + 1) * HEAD_DIM), lanes] = dk.astype(bf16)
            dpt_ref[slice(2 * D + h * HEAD_DIM, 2 * D + (h + 1) * HEAD_DIM), lanes] = dv.astype(bf16)
        return dot(w_ref[...], dpt_ref[:, lanes], 1, 0).T

    dpt_ref[:, 8 * SLOT :] = jnp.zeros((3 * D, 128), bf16)

    def one(j, carry):
        row = slot_row(j)
        grad = block(dr_ref[pl.ds(row, SLOT), :], pl.multiple_of(j * SLOT, 128), SLOT)
        unstage(ext_ref, first_row(j, seq), grad + dh_ref[pl.ds(row, SLOT), :])
        return carry

    lax.fori_loop(0, 8, one, 0)
    count = 8 * seq_count

    def tail_of(ref):
        return jnp.concatenate(
            [ref[t * TILE + 2 * SLOT : (t + 1) * TILE, :] for t in range(TILES)], 0
        )

    grad = block(tail_of(dr_ref), 8 * SLOT, TAIL) + tail_of(dh_ref)

    @pl.when(is_last)
    def _():
        ext_ref[HALO + 2048 - count : HALO + 2048, :] = grad[:count]

    in_halo_ref[...] = ext_ref[:HALO, :]
    in_ref[...] = ext_ref[HALO : HALO + 2048, :]

    def two(j, carry):
        unstage(ext_ref, first_row(j, seq), z_ref[pl.ds(slot_row(j), SLOT), :].astype(f32))
        return carry

    lax.fori_loop(0, 8, two, 0)
    tail = tail_of(z_ref).astype(f32)

    @pl.when(is_last)
    def _():
        ext_ref[HALO + 2048 - count : HALO + 2048, :] = tail[:count]

    out_halo_ref[...] = ext_ref[:HALO, :].astype(bf16)
    out_ref[...] = ext_ref[HALO : HALO + 2048, :].astype(bf16)
    for part in range(3):
        cols = slice(part * D, (part + 1) * D)
        g = dot(xt_ref[...], dpt_ref[cols, :], 1, 1)
        gwa_ref[:, cols] = g[:D].astype(bf16)
        gbias_ref[:, cols] = g[D : D + 8]


def attn_backward(seq_count, *operands):
    shape = jax.ShapeDtypeStruct
    return pl.pallas_call(
        functools.partial(attn_backward_kernel, seq_count),
        out_shape=(
            shape((2048, D), bf16),
            shape((HALO, D), bf16),
            shape((2048, D), f32),
            shape((HALO, D), f32),
            shape((D, 3 * D), bf16),
            shape((8, 3 * D), f32),
        ),
        in_specs=[pl.BlockSpec(memory_space=pltpu.VMEM)] * len(operands),
        out_specs=[pl.BlockSpec(memory_space=pltpu.VMEM)] * 6,
        scratch_shapes=[
            pltpu.VMEM((3 * D, LANES), bf16),
            pltpu.VMEM((HALO + 2048 + 16, D), f32),
        ],
        compiler_params=pltpu.CompilerParams(vmem_limit_bytes=60 * MIB),
        name="attn_backward",
    )(*operands)


MESH = pl.DeviceIdType.MESH
PLANE = 4
DEPTH = 4


class Place:
    def __init__(self):
        self.batch = lax.axis_index("batch")
        self.z = lax.axis_index("seq")
        self.core = self.batch % 2
        self.plane = self.batch // 2

    def plane_at(self, k):
        x = (self.plane % 2 + k % 2) % 2
        y = (self.plane // 2 + k // 2) % 2
        return y * 2 + x

    def in_plane(self, k, other=0):
        core = self.core if other == 0 else 1 - self.core
        return {"batch": self.plane_at(k) * 2 + core, "seq": self.z}

    def depth_at(self, k):
        return (self.z + k) % DEPTH

    def in_depth(self, k):
        return {"batch": self.batch, "seq": self.depth_at(k)}

    def sibling(self):
        return {"batch": self.plane * 2 + 1 - self.core, "seq": self.z}

    def greet(self):
        barrier = pltpu.get_barrier_semaphore()
        for k in range(1, 4):
            pl.semaphore_signal(barrier, inc=1, device_id=self.in_plane(k), device_id_type=MESH)
            pl.semaphore_signal(barrier, inc=1, device_id=self.in_depth(k), device_id_type=MESH)
            pl.semaphore_signal(barrier, inc=1, device_id=self.in_plane(k, 1), device_id_type=MESH)
        pl.semaphore_signal(barrier, inc=1, device_id=self.sibling(), device_id_type=MESH)
        pl.semaphore_wait(barrier, 10)


def remote(src, dst, send, recv, device):
    return pltpu.make_async_remote_copy(
        src_ref=src, dst_ref=dst, send_sem=send, recv_sem=recv, device_id=device, device_id_type=MESH
    )


LOW, HIGH = pl.ds(0, DEPTH // 2), pl.ds(DEPTH // 2, DEPTH // 2)


class Gather:
    def __init__(self, place, whole, send, recv, parts=None):
        self.place, self.whole, self.send, self.recv, self.parts = place, whole, send, recv, parts

    def block(self, k):
        return self.whole.at[self.place.plane_at(k) * 2 + self.place.core]

    def copy(self, n, source, target, device):
        return remote(source, target, self.send.at[n], self.recv.at[n], device)

    def depth(self, k):
        at = self.place
        here = self.whole.at[at.batch, at.z]
        source = here if self.parts is None else self.parts.at[at.depth_at(k)]
        return self.copy(k - 1, source, here, at.in_depth(k))

    def plane(self, k):
        return self.copy(2 + k, self.block(0), self.block(0), self.place.in_plane(k))

    def across(self, k):
        half = self.block(k).at[LOW if k == 1 else HIGH]
        return self.copy(4 + k, half, half, self.place.in_plane(3 - k))

    def core(self, k):
        return self.copy(7 + k, self.block(k), self.block(k), self.place.sibling())

    def first(self):
        for k in range(1, 4):
            self.depth(k).start()

    def second(self):
        for k in range(1, 4):
            self.depth(k).wait_recv()
        for k in (1, 2):
            self.plane(k).start()
        self.core(0).start()

    def third(self):
        for k in (1, 2):
            self.plane(k).wait_recv()
            self.across(k).start()
            self.core(k).start()

    def fourth(self):
        for k in (1, 2):
            self.across(k).wait_recv()
        self.core(3).start()

    def finish(self):
        for k in range(4):
            self.core(k).wait_recv()
        for k in range(1, 4):
            self.depth(k).wait_send()
        for k in (1, 2):
            self.plane(k).wait_send()
            self.across(k).wait_send()
        for k in range(4):
            self.core(k).wait_send()


class Spread(Gather):
    def step(self, k, other):
        device = self.place.in_plane(k, other) if k else self.place.sibling()
        return self.copy(2 * k + other + 3 if k else 3, self.block(0), self.block(0), device)

    def steps(self):
        return [self.step(0, 0)] + [self.step(k, other) for k in range(1, 4) for other in range(2)]

    def second(self):
        for k in range(1, 4):
            self.depth(k).wait_recv()
        for copy in self.steps():
            copy.start()

    def finish(self):
        for copy in self.steps():
            copy.wait_recv()
        for k in range(1, 4):
            self.depth(k).wait_send()
        for copy in self.steps():
            copy.wait_send()


class Scatter:
    def __init__(self, place, grad, twin, near, far, along, send, recv):
        self.place, self.grad, self.twin = place, grad, twin
        self.near, self.far, self.along, self.send, self.recv = near, far, along, send, recv
        shape = grad.shape
        if len(shape) == 4:
            self.at = lambda p, c: grad.at[p * 2 + c]
        else:
            self.at = lambda p, c: grad.at[p, c]

    def block(self, k):
        return self.at(self.place.plane_at(k), self.place.core)

    def copy(self, n, source, target, device):
        return remote(source, target, self.send.at[n], self.recv.at[n], device)

    def core(self, p):
        source = self.at(p, 1 - self.place.core)
        return self.copy(p, source, self.twin.at[p], self.place.sibling())

    def plane(self, n):
        k, half = ((1, LOW), (3, LOW), (2, HIGH), (3, HIGH))[n]
        target = self.near.at[n]
        return self.copy(4 + n, self.block(k).at[half], target, self.place.in_plane(1 + n // 2))

    def across(self, n):
        k, half = ((2, LOW), (1, HIGH))[n]
        return self.copy(8 + n, self.block(k).at[half], self.far.at[n], self.place.in_plane(2 - n))

    def depth(self, k):
        source = self.block(0).at[self.place.depth_at(k)]
        return self.copy(9 + k, source, self.along.at[k - 1], self.place.in_depth(k))

    def first(self):
        for p in range(PLANE):
            self.core(p).start()

    def second(self):
        for p in range(PLANE):
            self.core(p).wait_recv()
        own = self.place.core

        def one(p, carry):
            mine = self.at(p, own)
            mine[...] = (mine[...].astype(f32) + self.twin[p].astype(f32)).astype(mine.dtype)
            return carry

        lax.fori_loop(0, PLANE, one, 0)
        for n in range(4):
            self.plane(n).start()

    def third(self):
        for n in range(4):
            self.plane(n).wait_recv()
        for n, (k, base) in enumerate(((2, 0), (1, 2))):
            mine = self.block(k)

            def one(q, carry):
                total = mine[base + q].astype(f32) + self.near[2 * n + 1, q].astype(f32)
                mine[base + q] = total.astype(mine.dtype)
                return carry

            lax.fori_loop(0, 2, one, 0)
            self.across(n).start()

    def fourth(self):
        for n in range(2):
            self.across(n).wait_recv()
        mine = self.block(0)

        def one(i, carry):
            n, q = i // 2, i % 2
            total = mine[i].astype(f32) + self.near[2 * n, q].astype(f32) + self.far[n, q].astype(f32)
            mine[i] = total.astype(mine.dtype)
            return carry

        lax.fori_loop(0, DEPTH, one, 0)
        for k in range(1, 4):
            self.depth(k).start()

    def total(self):
        for k in range(1, 4):
            self.depth(k).wait_recv()
        total = self.block(0)[self.place.z].astype(f32)
        for k in range(3):
            total = total + self.along[k].astype(f32)
        return total

    def finish(self):
        for p in range(PLANE):
            self.core(p).wait_send()
        for n in range(4):
            self.plane(n).wait_send()
        for n in range(2):
            self.across(n).wait_send()
        for k in range(1, 4):
            self.depth(k).wait_send()


def turned(ref, value):
    ref[...] = jnp.zeros_like(ref)
    ref[: value.shape[0], : value.shape[1]] = value
    return ref[...].T


def heads_of(block, h):
    return block[h * HEAD_DIM : (h + 1) * HEAD_DIM]


def only_head(block, h):
    zero = jnp.zeros((HEAD_DIM, block.shape[1]), block.dtype)
    mine = heads_of(block, h)
    return jnp.concatenate([mine, zero] if h % 2 == 0 else [zero, mine], 0)


def pair_of(block, h):
    at = h // 2 * 2 * HEAD_DIM
    return block[:, at : at + 2 * HEAD_DIM]


def mask_parts(tag, pair):
    query, key = tag_rows(tag, pair)
    width = tag.shape[1]
    zero = jnp.zeros((128 - AUG, width), bf16)
    return jnp.concatenate([key, zero], 0).T, jnp.concatenate([query, zero], 0)


class Slots:
    def __init__(self, tag_ref, seq, seq_count):
        self.tag_ref, self.seq, self.count = tag_ref, seq, 8 * seq_count
        self.last_pair = 8 * seq_count

    def tag(self, j):
        wide = self.tag_ref[:, pl.ds(pl.multiple_of(j * SLOT, 128), SLOT + 128)]
        offset = HALO - 8 * self.seq - j
        return pltpu.roll(wide, SLOT + 128 - offset, 1)[:1, :SLOT]

    def tail_tag(self):
        tag = self.tag_ref[:, 2048:2176]
        if self.count < TAIL:
            tag = pltpu.roll(tag, 128 - (TAIL - self.count), 1)
        place = lax.broadcasted_iota(jnp.int32, (1, TAIL), 1)
        return jnp.where(place < self.count, tag[:1, :TAIL], 2 * (2 * self.last_pair + 3))

    def tail(self, ref):
        return jnp.concatenate(
            [ref[t * TILE + 2 * SLOT : (t + 1) * TILE, :] for t in range(TILES)], 0
        )

    def set_tail(self, ref, value):
        for t in range(TILES):
            ref[t * TILE + 2 * SLOT : (t + 1) * TILE, :] = value[t * PIECE : (t + 1) * PIECE]


def halves_of(width):
    step = min(width, 128)
    return [slice(i, i + step) for i in range(0, width, step)]


def pair_stack(values, *rest):
    zero = jnp.zeros_like(values[0])
    left = jnp.concatenate([values[0], zero, *rest], 0)
    right = jnp.concatenate([zero, values[1], *rest], 0)
    return left, right


def forward_block(
    xb, tag, pair, lanes, wt_ref, biases, xt_ref, qt_ref, kt_ref, vt_ref, lse_ref, s_ref, a_ref, kn_ref, ct_ref
):
    width = xb.shape[0]
    xt_ref[:D, lanes] = xb.T
    parts = ((kt_ref, None), (qt_ref, biases[0]), (vt_ref, biases[1]))

    def project(n):
        at = (1, 0, 2)[n]
        p = dot(wt_ref[at * D : (at + 1) * D, :], xb, 1, 1)
        s_ref[2 * n, :, :width] = p[:SLOT]
        s_ref[2 * n + 1, :, :width] = p[SLOT:]

    def keep(n):
        out_ref, bias = parts[n]
        for h in range(HEADS):
            at = h % 4 * HEAD_DIM
            value = s_ref[2 * n + h // 4, at : at + HEAD_DIM, :width]
            rows = slice(h * HEAD_DIM, (h + 1) * HEAD_DIM)
            if bias is not None:
                value = value + bias[rows]
            value = value.astype(bf16)
            if n == 1:
                value = (value.astype(f32) * HEAD_DIM**-0.5).astype(bf16)
            out_ref[rows, lanes] = value

    project(0)
    project(1)
    keep(0)
    kn_ref[:width, :] = kt_ref[:, lanes].T
    project(2)
    keep(1)
    key_mask, query_mask = mask_parts(tag, pair)
    keep(2)

    def rows_of(h):
        return slice(h * HEAD_DIM, (h + 1) * HEAD_DIM)

    def scores(p):
        left = jnp.concatenate([kn_ref[:width, p * 128 : (p + 1) * 128], key_mask], 1)
        both = pair_stack([qt_ref[rows_of(2 * p + i), lanes] for i in range(2)], query_mask)
        if width % 128 == 0:
            s = dot(left, jnp.concatenate(both, 1), 1, 0)
            s_ref[2 * p], s_ref[2 * p + 1] = s[:, :width], s[:, width:]
        else:
            for i in range(2):
                s_ref[2 * p + i, :width, :width] = dot(left, both[i], 1, 0)

    def weigh(p):
        for h in (2 * p, 2 * p + 1):
            for half in halves_of(width):
                s = s_ref[h, :width, half]
                top = jnp.max(s, axis=0, keepdims=True)
                ex = jnp.exp(s - top)
                total = jnp.sum(ex, axis=0, keepdims=True)
                a_ref[h, :width, half] = (ex * (1.0 / total)).astype(bf16)
                at = pl.ds(pl.multiple_of(lanes.start + half.start, 128), half.stop - half.start)
                lse_ref[h : h + 1, at] = top + jnp.log(total)

    def collect(p):
        for h in (2 * p, 2 * p + 1):
            c = dot(vt_ref[rows_of(h), lanes], a_ref[h, :width, :width], 1, 0)
            ct_ref[rows_of(h), :width] = c.astype(bf16)

    skewed(HEADS // 2, scores, weigh, collect)
    return ct_ref[:, :width].T


def skewed(count, *stages):
    for i in range(count + len(stages) - 1):
        for n, stage in enumerate(stages):
            if 0 <= i - n < count:
                stage(i - n)


def backward_block(
    dr, c, tag, pair, lanes, wo, qt_ref, kt_ref, vt_ref, lse_ref, dpt_ref, s_ref, da_ref, a_ref,
    ds_ref, kn_ref, vn_ref, dct_ref, ct_ref,
):
    width = dr.shape[0]
    kn_ref[:width, :] = kt_ref[:, lanes].T
    vn_ref[:width, :] = vt_ref[:, lanes].T
    dct_ref[:, :width] = dot(wo, dr, 1, 1).astype(bf16)
    ct_ref[:, :width] = c.T
    key_mask, query_mask = mask_parts(tag, pair)

    def rows_of(h):
        return slice(h * HEAD_DIM, (h + 1) * HEAD_DIM)

    def scores(p):
        at = slice(p * 128, (p + 1) * 128)
        left = jnp.concatenate([kn_ref[:width, at], key_mask], 1)
        both = pair_stack([qt_ref[rows_of(2 * p + i), lanes] for i in range(2)], query_mask)
        both_d = pair_stack([dct_ref[rows_of(2 * p + i), :width] for i in range(2)])
        right = vn_ref[:width, at]
        if width % 128 == 0:
            s = dot(left, jnp.concatenate(both, 1), 1, 0)
            u = 2 * (p % 2)
            s_ref[u], s_ref[u + 1] = s[:, :width], s[:, width:]
            da = dot(right, jnp.concatenate(both_d, 1), 1, 0)
            da_ref[u], da_ref[u + 1] = da[:, :width], da[:, width:]
        else:
            for i in range(2):
                s_ref[2 * (p % 2) + i, :width, :width] = dot(left, both[i], 1, 0)
                da_ref[2 * (p % 2) + i, :width, :width] = dot(right, both_d[i], 1, 0)

    def weigh(p):
        for h in (2 * p, 2 * p + 1):
            rows = rows_of(h)
            for half in halves_of(width):
                at = pl.ds(pl.multiple_of(lanes.start + half.start, 128), half.stop - half.start)
                product = ct_ref[rows, half].astype(f32) * dct_ref[rows, half].astype(f32)
                delta = jnp.sum(product, axis=0, keepdims=True)
                lse = lse_ref[h : h + 1, at]
                for first in range(0, width, 64):
                    keys = slice(first, first + 64)
                    a = jnp.exp(s_ref[h % 4, keys, half] - lse)
                    a_ref[h % 4, keys, half] = a.astype(bf16)
                    ds_ref[h % 4, keys, half] = (a * (da_ref[h % 4, keys, half] - delta)).astype(bf16)

    def collect(p):
        for h in (2 * p, 2 * p + 1):
            rows = rows_of(h)
            ds = ds_ref[h % 4, :width, :width]
            dv = dot(dct_ref[rows, :width], a_ref[h % 4, :width, :width], 1, 1)
            dk = dot(qt_ref[rows, lanes], ds, 1, 1)
            dq = dot(kt_ref[rows, lanes], ds, 1, 0) * HEAD_DIM**-0.5
            dpt_ref[rows, lanes] = dq.astype(bf16)
            dpt_ref[slice(D + rows.start, D + rows.stop), lanes] = dk.astype(bf16)
            dpt_ref[slice(2 * D + rows.start, 2 * D + rows.stop), lanes] = dv.astype(bf16)

    skewed(HEADS // 2, scores, weigh, collect)


def mean(v):
    return jnp.mean(v, axis=-1, keepdims=True)


def row_sum(v):
    return jnp.sum(v, axis=0, keepdims=True)


def flat(value):
    return value.reshape(-1, value.shape[-1])


BLOCK = 48
MAIN = 2 * SLOT


def eights(v):
    return jnp.sum(v.reshape(-1, 8, v.shape[-1]), axis=0)


def feed_tile(
    t, xs_ref, c_ref, es_ref, wo_ref, w1_ref, w2_ref, vec_ref, dh_ref, gvec_ref,
    acc_ref, other_ref, n1_ref, inv_ref, yb_ref, df_ref, u_ref, g_ref, back_ready, tails,
    awo_ref, aw1_ref, aw2_ref,
):
    first = pl.multiple_of(t * TILE, 16)
    rows = pl.ds(first, TILE)
    piece = pl.ds(pl.multiple_of(t * PIECE, 16), PIECE)
    g_tail, du_tail, df_tail, yb_tail = tails
    bo, b2, g1, c1, g2, c2 = (vec_ref[i : i + 1, :] for i in range(2, 8))
    per = FF // D
    blocks = [slice(i, i + BLOCK) for i in range(0, TILE, BLOCK)]

    def at(block):
        return pl.ds(pl.multiple_of(first + block.start, 16), BLOCK)

    acc_ref[...] = dot(c_ref[rows, :], flat(wo_ref[...]), 1, 0)
    for block in blocks:
        h1 = xs_ref[at(block), :].astype(f32) + (acc_ref[block, :] + bo)
        mid = h1 - mean(h1)
        inv1 = lax.rsqrt(mean(mid * mid) + norm_epsilon)
        n1 = mid * inv1
        n1_ref[block, :] = n1
        inv_ref[block, :] = jnp.broadcast_to(inv1, (BLOCK, 128))
        yb_ref[block, :] = (n1 * g1 + c1).astype(bf16)

    pads = (acc_ref, other_ref)

    def w2_part(k):
        return flat(w2_ref[8 // per * k : 8 // per * (k + 1)])

    def w1_part(k):
        return flat(w1_ref[:, :, :, k * D : (k + 1) * D])

    def up(k):
        pads[k % 2][...] = dot(yb_ref[...], w1_part(k), 1, 0)

    def activate(k):
        cols = slice(k * D, (k + 1) * D)
        b1 = vec_ref[8 + k : 9 + k, :]
        for block in blocks:
            u = pads[k % 2][block, :] + b1
            cdf = 0.5 * (1.0 + lax.erf(u * 0.7071067811865476))
            g_ref[k * TILE + block.start : k * TILE + block.stop, :] = (u * cdf).astype(bf16)
            u_ref[block, cols] = cdf + u * jnp.exp(u * u * -0.5) * 0.3989422804014327

    def down(k):
        part = dot(g_ref[k * TILE : (k + 1) * TILE, :], w2_part(k), 1, 0)
        if k == 0:
            dh_ref[rows, :] = part
        else:
            dh_ref[rows, :] += part

    up(0)
    up(1)
    activate(0)
    pl.when(t == 0)(back_ready)
    for k in range(per):
        if k + 2 < per:
            up(k + 2)
        down(k)
        if k + 1 < per:
            activate(k + 1)
    sums = [jnp.zeros((8, D), f32)] * 3
    for block in blocks:
        h2 = (n1_ref[block, :] * g1 + c1) + (dh_ref[at(block), :] + b2)
        mid2 = h2 - mean(h2)
        inv2 = lax.rsqrt(mean(mid2 * mid2) + norm_epsilon)
        n2 = mid2 * inv2
        xs_ref[at(block), :] = (n2 * g2 + c2).astype(bf16)
        e = es_ref[at(block), :].astype(f32)
        en = e * n2
        eg = e * g2
        dh2 = (eg - mean(eg) - n2 * mean(eg * n2)) * inv2
        dh_ref[at(block), :] = dh2
        df = dh2.astype(bf16)
        df_ref[block, :] = df
        sums = [sums[0] + eights(e), sums[1] + eights(en), sums[2] + eights(df.astype(f32))]
    for i, value in zip((7, 6, 3), sums):
        gvec_ref[i : i + 1, :] += row_sum(value)
    dft = df_ref[:MAIN, :].T
    ybt = yb_ref[:MAIN, :].T
    df_tail[piece, :] = df_ref[MAIN:, :]
    yb_tail[piece, :] = yb_ref[MAIN:, :]

    def up_back(k):
        pads[k % 2][...] = dot(df_ref[...], w2_part(k), 1, 1)

    def activate_back(k):
        cols = slice(k * D, (k + 1) * D)
        here = slice(k * TILE, k * TILE + MAIN)
        at_tail = pl.ds(pl.multiple_of(k * TAIL + t * PIECE, 16), PIECE)
        aw2_ref[:, cols] += dot(dft, g_ref[here, :], 1, 0)
        g_tail[at_tail, :] = g_ref[here.stop : here.stop + PIECE, :]
        total = jnp.zeros((8, D), f32)
        for block in blocks:
            du = (pads[k % 2][block, :] * u_ref[block, cols]).astype(bf16)
            g_ref[k * TILE + block.start : k * TILE + block.stop, :] = du
            total = total + eights(du.astype(f32))
        gvec_ref[8 + k : 9 + k, :] += row_sum(total)

    def down_back(k):
        cols = slice(k * D, (k + 1) * D)
        here = slice(k * TILE, k * TILE + MAIN)
        at_tail = pl.ds(pl.multiple_of(k * TAIL + t * PIECE, 16), PIECE)
        aw1_ref[:, cols] += dot(ybt, g_ref[here, :], 1, 0)
        du_tail[at_tail, :] = g_ref[here.stop : here.stop + PIECE, :]
        part = dot(g_ref[k * TILE : (k + 1) * TILE, :], w1_part(k), 1, 1)
        dh_ref[rows, :] += part

    skewed(per, up_back, activate_back, down_back)
    sums = [jnp.zeros((8, D), f32)] * 3
    for block in blocks:
        dy = dh_ref[at(block), :]
        n1 = n1_ref[block, :]
        eg = dy * g1
        dh1 = (eg - mean(eg) - n1 * mean(eg * n1)) * inv_ref[block, :1]
        dh_ref[at(block), :] = dh1
        dr = dh1.astype(bf16)
        es_ref[at(block), :] = dr
        sums = [sums[0] + eights(dy), sums[1] + eights(dy * n1), sums[2] + eights(dr.astype(f32))]
    for i, value in zip((5, 4, 2), sums):
        gvec_ref[i : i + 1, :] += row_sum(value)
    main = pl.ds(first, MAIN)
    awo_ref[...] += dot(c_ref[main, :].T, es_ref[main, :], 1, 0)


def whole_kernel(*refs):
    refs = list(refs)

    def take(count):
        taken = refs[:count]
        del refs[:count]
        return taken

    state_in = take(15)
    tok_ref, cot_ref, seg_ref, keep_ref = take(4)
    out_ref, in_ref = take(2)
    state_out = take(15)
    copy_out = take(5)
    out_back, in_back = take(2)
    state = take(15)
    masters, firsts, seconds = state[:5], state[5:10], state[10:]
    weights = take(5)
    wa_ref, wo_ref, w1_ref, w2_ref, wv_ref = weights
    xs_ref, es_ref, xt_ref, qt_ref, kt_ref, vt_ref, c_ref, lse_ref, dh_ref, tag_ref = take(10)
    ext_ref, seg_halo, keep_halo = take(3)
    square, gvec_ref, gwa_ref, gwo_ref, grad_vec, halo_out, halo_in = take(7)
    twins, nears, fars, alongs = take(5), take(5), take(5), take(5)
    parts, copies, whole_vec = take(4), take(5), take(1)[0]
    (
        state_sems, load_sems, gather_send, gather_recv, edge_send, edge_recv,
        sum_send, sum_recv, copy_send, copy_recv, store_sems,
    ) = refs
    place = Place()
    seq, seq_count = place.z, DEPTH
    is_last = seq == seq_count - 1
    slots = Slots(tag_ref, seq, seq_count)
    rows = tok_ref.shape[1]
    ext_x, ext_e = ext_ref.at[pl.ds(0, HALO + rows)], ext_ref.at[pl.ds(HALO + rows, HALO + rows)]

    loads = [pltpu.make_async_copy(state_in[i], state[i], state_sems.at[i]) for i in range(15)]
    for load in loads:
        load.start()
    big_loads = [
        pltpu.make_async_copy(src.at[0], dst.at[pl.ds(HALO, rows)], load_sems.at[i])
        for i, (src, dst) in enumerate(((tok_ref, ext_x), (cot_ref, ext_e)))
    ]
    for load in big_loads:
        load.start()
    place.greet()
    edge = [
        remote(src, dst, edge_send.at[i], edge_recv.at[i], place.in_depth(1))
        for i, (src, dst) in enumerate((
            (tok_ref.at[0, pl.ds(rows - HALO, HALO)], ext_x.at[pl.ds(0, HALO)]),
            (cot_ref.at[0, pl.ds(rows - HALO, HALO)], ext_e.at[pl.ds(0, HALO)]),
            (seg_ref.at[:, pl.ds(rows - 128, 128)], seg_halo),
            (keep_ref.at[:, pl.ds(rows - 128, 128)], keep_halo),
        ))
    ]
    gathers = [Gather(place, weights[i], gather_send.at[i], gather_recv.at[i]) for i in range(5)]

    def put(i):
        shard = turned(square, masters[4][...])[: masters[4].shape[1]] if i == 4 else masters[i][...]
        weights[i][place.batch, place.z] = shard.astype(bf16)

    for i in (0, 4):
        loads[i].wait()
        put(i)
        gathers[i].first()
    for copy in edge:
        copy.start()
    for i in (1, 2, 3):
        loads[i].wait()
        put(i)
    gathers[1].first()
    for load in big_loads:
        load.wait()
    for copy in edge:
        copy.wait()
    tag_ref[...] = jnp.zeros_like(tag_ref)
    rim = seg_halo[...] * 2 + keep_halo[...]
    tag_ref[:, :HALO] = jnp.broadcast_to(rim[:, 128 - HALO :], (8, HALO))
    tag_ref[:, HALO : HALO + rows] = jnp.broadcast_to(seg_ref[...] * 2 + keep_ref[...], (8, rows))

    def stage_one(j, carry):
        start = first_row(j, seq)
        row = slot_row(j)
        stage_slot(ext_x, start, xs_ref, row)
        stage_slot(ext_e, start, es_ref, row)
        return carry

    gathers[0].second()
    gathers[2].first()
    gathers[4].second()
    gathers[1].second()
    lax.fori_loop(0, 8, stage_one, 0)
    slots.set_tail(xs_ref, tail_rows(ext_x, slots.count, is_last))
    slots.set_tail(es_ref, tail_rows(ext_e, slots.count, is_last))
    gathers[0].third()
    gathers[4].third()
    xt_ref[:, 8 * SLOT :] = jnp.zeros((D + AUG, 128), bf16)
    ones = lax.broadcasted_iota(jnp.int32, (AUG, LANES), 0) == 0
    xt_ref[D:, :] = jnp.where(ones, 1.0, 0.0).astype(bf16)
    gathers[2].second()
    gathers[3].first()
    gathers[0].fourth()
    gathers[4].fourth()
    gathers[1].third()
    gathers[0].finish()
    gathers[4].finish()

    def forward(wt_ref, s_ref, a_ref, kn_ref, ct_ref):
        for part in range(3):
            wt_ref[part * D : (part + 1) * D, :] = flat(
                wa_ref[:, :, :, part * D : (part + 1) * D]
            ).T
        vec_t = flat(wv_ref[...])
        biases = (vec_t[:, 0:1].astype(f32), vec_t[:, 1:2].astype(f32))

        def block(xb, tag, pair, lanes):
            return forward_block(
                xb, tag, pair, lanes, wt_ref, biases, xt_ref, qt_ref, kt_ref, vt_ref, lse_ref,
                s_ref, a_ref, kn_ref, ct_ref,
            )

        def one(j, carry):
            for step, event in (
                (1, gathers[1].fourth), (3, gathers[2].third), (4, gathers[3].second),
                (6, gathers[2].fourth),
            ):
                pl.when(j == step)(event)
            row = slot_row(j)
            lanes = pl.ds(pl.multiple_of(j * SLOT, 128), SLOT)
            c_ref[pl.ds(row, SLOT), :] = block(
                xs_ref[pl.ds(row, SLOT), :], slots.tag(j), 8 * seq + j, lanes
            )
            return carry

        lax.fori_loop(0, 8, one, 0)
        slots.set_tail(
            c_ref,
            block(
                slots.tail(xs_ref), slots.tail_tag(), slots.last_pair, pl.ds(8 * SLOT, TAIL)
            ),
        )

    pl.run_scoped(
        forward,
        pltpu.VMEM((3 * D, D), bf16),
        pltpu.VMEM((HEADS, SLOT, SLOT), f32),
        pltpu.VMEM((HEADS, SLOT, SLOT), bf16),
        pltpu.VMEM((SLOT, D), bf16),
        pltpu.VMEM((D, SLOT), bf16),
    )
    for i in (1, 2):
        gathers[i].finish()
    gathers[3].third()

    def back_ready():
        gathers[3].fourth()
        gathers[3].finish()

    grads = [gwa_ref, gwo_ref, w1_ref, w2_ref, grad_vec]
    scatters = [
        Scatter(
            place, grads[i], twins[i], nears[i], fars[i], alongs[i], sum_send.at[i], sum_recv.at[i]
        )
        for i in range(5)
    ]

    def feed_all(
        vec_ref, acc_ref, other_ref, n1_ref, inv_ref, u_ref, awo_ref, aw1_ref, aw2_ref
    ):
        used = 0
        views = []
        for count in (4 * TILE, TILE, TILE, TAIL, TAIL, 4 * TAIL, 4 * TAIL):
            views.append(ext_ref.at[pl.ds(used, count)])
            used += count
        g_ref, yb_ref, df_ref, yb_tail, df_tail, g_tail, du_tail = views
        for ref in (awo_ref, aw1_ref, aw2_ref, gvec_ref):
            ref[...] = jnp.zeros_like(ref)
        vec_ref[...] = flat(wv_ref[...]).astype(f32).T[:16]

        def one(t, carry):
            feed_tile(
                t, xs_ref, c_ref, es_ref, wo_ref, w1_ref, w2_ref, vec_ref, dh_ref, gvec_ref, acc_ref,
                other_ref, n1_ref, inv_ref, yb_ref, df_ref, u_ref, g_ref, back_ready,
                (g_tail, du_tail, df_tail, yb_tail),
                awo_ref, aw1_ref, aw2_ref,
            )
            return carry

        lax.fori_loop(0, TILES, one, 0)
        for k in range(FF // D):
            cols = slice(k * D, (k + 1) * D)
            at = slice(k * TAIL, (k + 1) * TAIL)
            aw2_ref[:, cols] += dot(df_tail[...].T, g_tail[at, :], 1, 0)
            aw1_ref[:, cols] += dot(yb_tail[...].T, du_tail[at, :], 1, 0)
        awo_ref[...] += dot(slots.tail(c_ref).T, slots.tail(es_ref), 1, 0)
        def convert(i, carry):
            value = aw2_ref[:, pl.ds(pl.multiple_of(i * 128, 128), 128)].astype(bf16).T
            w2_ref[i // 2, pl.ds(i % 2 * 2, 2)] = value.reshape(2, -1, D)
            return carry

        def convert_rows(i, carry):
            value = aw1_ref[pl.ds(pl.multiple_of(i * 64, 64), 64), :].astype(bf16)
            w1_ref[i] = value.reshape(DEPTH, -1, FF)
            gwo_ref[i // 2, i % 2] = (
                awo_ref[pl.ds(pl.multiple_of(i * 64, 64), 64), :].astype(bf16).reshape(DEPTH, -1, D)
            )
            return carry

        lax.fori_loop(0, FF // 128, convert, 0)
        scatters[3].first()
        lax.fori_loop(0, 8, convert_rows, 0)
        scatters[2].first()
        scatters[1].first()

    pl.run_scoped(
        feed_all,
        pltpu.VMEM((16, D), f32),
        pltpu.VMEM((TILE, D), f32),
        pltpu.VMEM((TILE, D), f32),
        pltpu.VMEM((TILE, D), f32),
        pltpu.VMEM((TILE, 128), f32),
        pltpu.VMEM((TILE, FF), f32),
        pltpu.VMEM((D, D), f32),
        pltpu.VMEM((D, FF), f32),
        pltpu.VMEM((D, FF), f32),
    )
    for load in loads[5:]:
        load.wait()
    copy_gathers = [
        kind(place, copies[i], copy_send.at[i], copy_recv.at[i], parts[i])
        for i, kind in enumerate((Spread, Spread, Gather, Gather))
    ]
    copy_gathers.append(Spread(place, whole_vec, copy_send.at[4], copy_recv.at[4]))
    stores = []

    def store(src, dst):
        stores.append(pltpu.make_async_copy(src, dst, store_sems.at[len(stores)]))
        stores[-1].start()

    def update(i):
        total = scatters[i].total()
        if i == 4:
            square[...] = jnp.zeros_like(square)
            square[: total.shape[0], :] = total
            here, cols = masters[4].shape
            total = square[...].T[:here, :cols]
        new = adam_update(masters[i][...], firsts[i][...], seconds[i][...], total, learn_rates[i])
        firsts[i][...], seconds[i][...], masters[i][...] = new
        if i == 4:
            shard = turned(square, new[2])[: new[2].shape[1]].astype(bf16)
            whole_vec[place.batch, place.z] = shard
        else:
            low = new[2].astype(bf16)
            width = low.shape[1] // DEPTH
            for q in range(DEPTH):
                parts[i][q] = low[:, q * width : (q + 1) * width]
            copies[i][place.batch, place.z] = parts[i][place.z]
        copy_gathers[i].first()

    def backward(
        dpt_ref, ext_ref, s_ref, da_ref, a_ref, ds_ref, kn_ref, vn_ref, dct_ref, ct_ref
    ):
        low_ref = ext_e
        dpt_ref[:, 8 * SLOT :] = jnp.zeros((3 * D, 128), bf16)
        wo = flat(wo_ref[...])

        def block(dr, c, tag, pair, lanes):
            backward_block(
                dr, c, tag, pair, lanes, wo, qt_ref, kt_ref, vt_ref, lse_ref, dpt_ref,
                s_ref, da_ref, a_ref, ds_ref, kn_ref, vn_ref, dct_ref, ct_ref,
            )

        def one(j, carry):
            for step, event in (
                (0, scatters[3].second), (2, scatters[2].second), (5, scatters[3].third),
                (7, scatters[1].second),
            ):
                pl.when(j == step)(event)
            row = slot_row(j)
            at = pl.ds(row, SLOT)
            lanes = pl.ds(pl.multiple_of(j * SLOT, 128), SLOT)
            block(es_ref[at, :], c_ref[at, :], slots.tag(j), 8 * seq + j, lanes)
            return carry

        lax.fori_loop(0, 8, one, 0)
        block(
            slots.tail(es_ref), slots.tail(c_ref), slots.tail_tag(), slots.last_pair,
            pl.ds(8 * SLOT, TAIL),
        )
        for part in range(3):
            cols = slice(part * D, (part + 1) * D)
            g = dot(xt_ref[...], dpt_ref[cols, :], 1, 1)
            gwa_ref[:, :, :, :, cols] = g[:D].astype(bf16).reshape(PLANE, 2, DEPTH, -1, D)
            if part != 1:
                gvec_ref[part // 2 : part // 2 + 1, :] = g[D : D + 1]
        grad_vec[...] = gvec_ref[...].T.reshape(grad_vec.shape)
        scatters[0].first()
        scatters[4].first()
        scatters[2].third()

        def output_one(j, carry):
            at = pl.ds(slot_row(j), SLOT)
            unstage_slot(
                ext_ref, first_row(j, seq),
                lambda g: xs_ref[at, g * 128 : (g + 1) * 128].astype(f32),
            )
            return carry

        def close(value):
            @pl.when(is_last)
            def _():
                ext_ref[HALO + rows - slots.count : HALO + rows, :] = value[: slots.count]

        lax.fori_loop(0, 8, output_one, 0)
        close(slots.tail(xs_ref).astype(f32))
        scatters[0].second()
        scatters[4].second()
        scatters[3].fourth()
        scatters[1].third()
        low_ref[...] = ext_ref[: HALO + rows, :].astype(bf16)
        halo_out[...] = low_ref[:HALO, :]
        edge_back[0].start()
        store(low_ref.at[pl.ds(HALO, rows)], out_ref)
        wa = flat(wa_ref[...])

        def input_block(lanes):
            return dot(wa, dpt_ref[:, lanes], 1, 0).T

        def input_two(i, carry):
            for step, event in (
                (0, scatters[2].fourth), (1, scatters[0].third), (1, scatters[4].third),
                (2, scatters[1].fourth), (2, functools.partial(update, 3)),
                (3, scatters[0].fourth), (3, scatters[4].fourth),
            ):
                pl.when(i == step)(event)

            def product(n):
                lanes = pl.ds(pl.multiple_of((2 * i + n) * SLOT, 128), SLOT)
                grad = dot(wa, dpt_ref[:, lanes], 1, 0)
                s_ref[2 * n], s_ref[2 * n + 1] = grad[:SLOT], grad[SLOT:]

            def put_back(n):
                j = 2 * i + n
                at = pl.ds(slot_row(j), SLOT)

                def column(g):
                    part = s_ref[2 * n + g // 2, g % 2 * 128 : g % 2 * 128 + 128, :].T
                    return part + dh_ref[at, g * 128 : (g + 1) * 128]

                unstage_slot(ext_ref, first_row(j, seq), column)

            skewed(2, product, put_back)
            return carry

        lax.fori_loop(0, 4, input_two, 0)
        close(input_block(pl.ds(8 * SLOT, TAIL)) + slots.tail(dh_ref))
        halo_in[...] = ext_ref[:HALO, :]
        edge_back[1].start()
        store(ext_ref.at[pl.ds(HALO, rows)], in_ref)
        copy_gathers[3].second()
        update(2)
        update(1)
        copy_gathers[2].second()
        update(4)
        update(0)
        copy_gathers[3].third()
        copy_gathers[2].third()
        copy_gathers[1].second()
        copy_gathers[4].second()
        copy_gathers[0].second()
        copy_gathers[3].fourth()
        copy_gathers[2].fourth()
        for i in range(5):
            for n, kind in enumerate((firsts, seconds, masters)):
                store(kind[i], state_out[5 * n + i])
        for i in (3, 2, 1, 4, 0):
            copy_gathers[i].finish()
            scatters[i].finish()
        here = masters[4].shape[0]
        mine = jnp.concatenate([whole_vec[seq * 2 + q // 4, q % 4] for q in range(8)], 0)
        copies[4][...] = mine.astype(f32).T[:here].astype(bf16)
        for i in range(5):
            store(copies[i], copy_out[i])
        for copy in stores:
            copy.wait()
        for copy in edge_back:
            copy.wait()

    edge_back = [
        remote(halo_out, out_back, edge_send.at[4], edge_recv.at[4], place.in_depth(3)),
        remote(halo_in, in_back, edge_send.at[5], edge_recv.at[5], place.in_depth(3)),
    ]
    pl.run_scoped(
        backward,
        pltpu.VMEM((3 * D, LANES), bf16),
        pltpu.VMEM((HALO + rows + 16, D), f32),
        pltpu.VMEM((4, SLOT, SLOT), f32),
        pltpu.VMEM((4, SLOT, SLOT), f32),
        pltpu.VMEM((4, SLOT, SLOT), bf16),
        pltpu.VMEM((4, SLOT, SLOT), bf16),
        pltpu.VMEM((SLOT, D), bf16),
        pltpu.VMEM((SLOT, D), bf16),
        pltpu.VMEM((D, SLOT), bf16),
        pltpu.VMEM((D, SLOT), bf16),
    )


def whole(masters, firsts, seconds, tokens, cotangent, segment, keep):
    shape = jax.ShapeDtypeStruct
    vmem = pl.BlockSpec(memory_space=pltpu.VMEM)
    hbm = pl.BlockSpec(memory_space=pl.ANY)
    state = (*masters, *firsts, *seconds)
    rows = tokens.shape[1]
    r = masters[0].shape[0]
    shapes = ((r, 3 * D), (r, D), (r, FF), (4 * r, D))
    copies = [((8, DEPTH, s[0], s[1] // DEPTH), bf16) for s in shapes]
    copies.append(((masters[4].shape[0], 128), bf16))
    halos = [((HALO, D), bf16), ((HALO, D), f32)]
    out_shape = [
        shape((rows, D), bf16),
        shape((rows, D), f32),
        *[shape(s.shape, f32) for i in range(3) for s in masters],
        *[shape(*c) for c in copies],
        *[shape(*h) for h in halos],
    ]
    five = [(s, bf16) for s in shapes] + [((r, 128), f32)]
    tall = ROWS
    scratch = [pltpu.VMEM(s.shape, f32) for s in state]
    scratch += [pltpu.VMEM((8, DEPTH) + s, bf16) for s in (*shapes, (r, 128))]
    scratch += [
        pltpu.VMEM((tall, D), bf16),
        pltpu.VMEM((tall, D), bf16),
        pltpu.VMEM((D + AUG, LANES), bf16),
        pltpu.VMEM((D, LANES), bf16),
        pltpu.VMEM((D, LANES), bf16),
        pltpu.VMEM((D, LANES), bf16),
        pltpu.VMEM((tall, D), bf16),
        pltpu.VMEM((HEADS, LANES), f32),
        pltpu.VMEM((tall, D), f32),
        pltpu.VMEM((8, LANES), jnp.int32),
        pltpu.VMEM((2 * (HALO + rows), D), bf16),
        pltpu.VMEM((1, 128), jnp.int32),
        pltpu.VMEM((1, 128), jnp.int32),
        pltpu.VMEM((128, 128), f32),
        pltpu.VMEM((128, D), f32),
        pltpu.VMEM((PLANE, 2, DEPTH) + shapes[0], bf16),
        pltpu.VMEM((PLANE, 2, DEPTH) + shapes[1], bf16),
        pltpu.VMEM((PLANE, 2, DEPTH, r, 128), f32),
        *[pltpu.VMEM(*h) for h in halos],
    ]
    for lead in ((PLANE, DEPTH), (4, DEPTH // 2), (2, DEPTH // 2), (3,)):
        scratch += [pltpu.VMEM(lead + s, t) for s, t in five]
    scratch += [pltpu.VMEM((DEPTH, s[0], s[1] // DEPTH), bf16) for s in shapes]
    scratch += [pltpu.VMEM(*c) for c in copies]
    scratch.append(pltpu.VMEM((8, DEPTH, r, 128), bf16))
    dma = pltpu.SemaphoreType.DMA
    scratch += [
        dma((15,)), dma((2,)), dma((5, 11)), dma((5, 11)), dma((6,)), dma((6,)),
        dma((5, 13)), dma((5, 13)), dma((5, 11)), dma((5, 11)), dma((22,)),
    ]
    return pl.pallas_call(
        whole_kernel,
        out_shape=out_shape,
        in_specs=[hbm] * 17 + [vmem] * 2,
        out_specs=[hbm] * 22 + [vmem] * 2,
        scratch_shapes=scratch,
        compiler_params=pltpu.CompilerParams(
            collective_id=0, has_side_effects=True, vmem_limit_bytes=63 * MIB
        ),
        name="whole",
    )(*state, tokens, cotangent, segment, keep)


LAST_PART = 496


def last_kernel(*refs):
    results, backs, ends = refs[:22], refs[22:24], refs[24:46]
    lows, (load_sems, store_sems) = refs[46:68], refs[68:]
    rows = results[0].shape[0]
    seq = lax.axis_index("seq")
    rim = pl.ds(rows - HALO, HALO)
    places = [(i, rim) for i in range(2)]
    places += [
        (i, pl.ds(first, LAST_PART))
        for i in range(2)
        for first in range(0, rows - HALO, LAST_PART)
    ]
    places += [(i, pl.ds(0, results[i].shape[0])) for i in range(2, 22)]
    loads = [
        pltpu.make_async_copy(results[i].at[at], lows[i].at[at], load_sems.at[n])
        for n, (i, at) in enumerate(places)
    ]
    stores = [
        pltpu.make_async_copy(lows[i].at[at], ends[i].at[at], store_sems.at[n])
        for n, (i, at) in enumerate(places)
    ]
    for load in loads:
        load.start()
    place = lax.broadcasted_iota(jnp.int32, (HALO, 1), 0)
    theirs = (place >= HALO - 8 * (seq + 1)) & (seq < lax.axis_size("seq") - 1)
    for n, (i, at) in enumerate(places):
        loads[n].wait()
        if n < 2:
            own = lows[i][rim, :].astype(f32)
            lows[i][rim, :] = jnp.where(theirs, backs[i][...].astype(f32), own).astype(lows[i].dtype)
        stores[n].start()
    for store in stores:
        store.wait()


def last(results, out_back, in_back):
    shape = jax.ShapeDtypeStruct
    vmem = pl.BlockSpec(memory_space=pltpu.VMEM)
    hbm = pl.BlockSpec(memory_space=pl.ANY)
    count = 22 + 2 * ((results[0].shape[0] - HALO) // LAST_PART)
    return pl.pallas_call(
        last_kernel,
        out_shape=[shape(a.shape, a.dtype) for a in results],
        in_specs=[hbm] * 22 + [vmem, vmem],
        out_specs=[hbm] * 22,
        scratch_shapes=[pltpu.VMEM(a.shape, a.dtype) for a in results]
        + [pltpu.SemaphoreType.DMA((count,)), pltpu.SemaphoreType.DMA((count,))],
        compiler_params=pltpu.CompilerParams(vmem_limit_bytes=60 * MIB),
        name="last",
    )(*results, out_back, in_back)


def on_device(
    tokens,
    cotangent,
    segment,
    keep_mask,
    attn_master,
    out_master,
    in_master,
    back_master,
    vec_master,
    attn_first,
    out_first,
    in_first,
    back_first,
    vec_first,
    attn_second,
    out_second,
    in_second,
    back_second,
    vec_second,
):
    seq = lax.axis_index("seq")
    seq_count = lax.axis_size("seq")
    both = ("batch", "seq")
    rows = tokens.shape[1]
    masters = (attn_master, out_master, in_master, back_master, vec_master)
    firsts = (attn_first, out_first, in_first, back_first, vec_first)
    seconds = (attn_second, out_second, in_second, back_second, vec_second)
    direct = seq_count == DEPTH and lax.axis_size("batch") == 2 * PLANE
    forward = [(i, i + 1) for i in range(seq_count - 1)]
    backward = [(i + 1, i) for i in range(seq_count - 1)]
    if direct:
        *results, out_back, grad_back = whole(
            masters, firsts, seconds, tokens, cotangent, segment, keep_mask
        )
        for i in range(17, 21):
            results[i] = results[i].reshape(-1, results[i].shape[-1])
        ends = last(results, out_back, grad_back)
        return (ends[0][None], ends[1][None], *ends[2:])
    low = [w.astype(bf16) for w in masters]
    low[4] = jnp.pad(low[4].T, ((0, 0), (0, 128 - low[4].shape[0])))
    attn_w, out_w, in_w, back_w, vec_t = (
        lax.all_gather(w, both, axis=0, tiled=True) for w in low
    )
    x_halo, e_halo, seg_halo, keep_halo = (
        lax.ppermute(a, "seq", forward)
        for a in (
            tokens[0, rows - HALO :], cotangent[0, rows - HALO :],
            segment[:, rows - 128 :], keep_mask[:, rows - 128 :],
        )
    )
    xs, es, xt, qt, kt, vt, c, lse = attn_forward(
        seq_count, tokens, cotangent, x_halo, e_halo, segment, keep_mask, seg_halo, keep_halo,
        attn_w, vec_t,
    )
    z, dh, dr, gwo, gw1, gw2, gvec, gb1 = feed(xs, c, es, out_w, in_w, back_w, vec_t)
    out, out_halo, grad_in, grad_in_halo, gwa, gbias = attn_backward(
        seq_count, xt, qt, kt, vt, lse, dr, dh, z, attn_w, out_w
    )
    grads = (gwa, gwo, gw1, gw2)
    grad_vec = jnp.concatenate(
        [gbias[:1, :D], gbias[:1, 2 * D :], gvec[2:8], gb1[0].reshape(FF // D, D)], 0
    )
    sums = [lax.psum_scatter(g.astype(f32), both, scatter_dimension=0, tiled=True) for g in grads]
    sums.append(lax.psum_scatter(grad_vec, both, scatter_dimension=1, tiled=True))
    new = [
        adam_update(masters[i], firsts[i], seconds[i], sums[i], learn_rates[i]) for i in range(5)
    ]

    def own_columns(i):
        whole = lax.all_gather(new[i][2].astype(bf16), both, axis=1 if i == 4 else 0, tiled=True)
        count = whole.shape[1] // seq_count
        return lax.dynamic_slice_in_dim(whole, seq * count, count, 1)

    results = [out, grad_in] + [new[i][part] for part in range(3) for i in range(5)]
    results += [own_columns(i) for i in range(5)]
    out_back = lax.ppermute(out_halo, "seq", backward)
    grad_back = lax.ppermute(grad_in_halo, "seq", backward)
    ends = last(results, out_back, grad_back)
    return (ends[0][None], ends[1][None], *ends[2:])


def solution(mesh):
    stream = P("batch", "seq", None)
    rows = P(("batch", "seq"), None)
    vector = P(None, ("batch", "seq"))
    five = (rows, rows, rows, rows, vector)
    return jax.shard_map(
        on_device,
        mesh=mesh,
        in_specs=(stream, stream, P("batch", "seq"), P("batch", "seq")) + five * 3,
        out_specs=(stream, stream) + five * 3 + (P(None, "seq"),) * 5,
        check_vma=False,
    )
```

```python
import functools
import math

import jax
import jax.numpy as jnp
from jax import lax
from jax.experimental import pallas as pl
from jax.experimental.pallas import tpu as pltpu
from jax.sharding import PartitionSpec as P

D = 512
HEADS = 8
HEAD_DIM = 64
FF = 2048
STEP = 10
PAIR = 255
SLOT = 256
HALO = 64
TILES = 4
TAIL = 64
PIECE = TAIL // TILES
TILE = 2 * SLOT + PIECE
ROWS = TILES * TILE
LANES = 8 * SLOT + 128
AUG = 16
MIB = 1 << 20

norm_epsilon = 1e-05
beta_first = 0.9
beta_second = 0.999
adam_epsilon = 1e-08
weight_decay = 0.01
learn_rates = (0.03, 0.2, 0.03, 0.02, 0.5)
big = 1e30

f32 = jnp.float32
bf16 = jnp.bfloat16


def dot(a, b, ca, cb):
    return lax.dot_general(a, b, (((ca,), (cb,)), ((), ())), preferred_element_type=f32)


def adam_update(master, first, second, gradient, rate):
    first_new = beta_first * first + (1.0 - beta_first) * gradient
    second_new = beta_second * second + (1.0 - beta_second) * gradient * gradient
    first_hat = first_new / (1.0 - beta_first**STEP)
    second_hat = second_new / (1.0 - beta_second**STEP)
    master_new = master - rate * (
        first_hat / (jnp.sqrt(second_hat) + adam_epsilon) + weight_decay * master
    )
    return (first_new, second_new, master_new)


def slot_row(j):
    return pl.multiple_of((j // 2) * TILE + (j % 2) * SLOT, 16)


def first_row(j, seq):
    return HALO + PAIR * j - 8 * seq


def staged(ref, start):
    base = pl.multiple_of((start // 16) * 16, 16)
    rest = start - base
    wide = ref[pl.ds(base, SLOT + 16), :].astype(f32)
    wide = jnp.where(rest >= 8, wide[8:], wide[:-8])
    shift = rest % 8
    groups = (SLOT + 8) // 8
    wide = wide.reshape(groups, 8, D)
    turned = pltpu.roll(wide, lax.rem(8 - shift, 8), 1)
    place = lax.broadcasted_iota(jnp.int32, (groups - 1, 8, D), 1)
    block = jnp.where(place < 8 - shift, turned[:-1], turned[1:]).reshape(SLOT, D)
    row = lax.broadcasted_iota(jnp.int32, (SLOT, D), 0)
    return jnp.where(row < PAIR, block, 0.0).astype(bf16)


def unstage(ref, start, block):
    base = pl.multiple_of((start // 8) * 8, 8)
    shift = start - base
    turned = pltpu.roll(block.reshape(SLOT // 8, 8, D), shift, 1)
    place = lax.broadcasted_iota(jnp.int32, (1, 8, D), 1)
    keep = ref[pl.ds(base, 8), :].reshape(1, 8, D)
    low = jnp.concatenate([keep, turned], 0)
    high = jnp.concatenate([turned, turned[-1:]], 0)
    place = lax.broadcasted_iota(jnp.int32, low.shape, 1)
    ref[pl.ds(base, SLOT + 8), :] = jnp.where(place < shift, low, high).reshape(SLOT + 8, D)


def stage_slot(ref, start, out_ref, row):
    base = pl.multiple_of((start // 16) * 16, 16)
    rest = start - base
    shift = rest % 8
    groups = (SLOT + 8) // 8
    place = lax.broadcasted_iota(jnp.int32, (groups - 1, 8, 128), 1)
    number = lax.broadcasted_iota(jnp.int32, (groups - 1, 8, 128), 0) * 8 + place
    for g in range(D // 128):
        cols = slice(g * 128, (g + 1) * 128)
        wide = ref[pl.ds(base, SLOT + 16), cols].astype(f32)
        wide = jnp.where(rest >= 8, wide[8:], wide[:-8]).reshape(groups, 8, 128)
        turned = pltpu.roll(wide, lax.rem(8 - shift, 8), 1)
        block = jnp.where(place < 8 - shift, turned[:-1], turned[1:])
        block = jnp.where(number < PAIR, block, 0.0)
        out_ref[pl.ds(row, SLOT), cols] = block.reshape(SLOT, 128).astype(bf16)


def unstage_slot(ref, start, column):
    base = pl.multiple_of((start // 8) * 8, 8)
    shift = start - base
    for g in range(D // 128):
        cols = slice(g * 128, (g + 1) * 128)
        turned = pltpu.roll(column(g).reshape(SLOT // 8, 8, 128), shift, 1)
        keep = ref[pl.ds(base, 8), cols].reshape(1, 8, 128)
        low = jnp.concatenate([keep, turned], 0)
        high = jnp.concatenate([turned, turned[-1:]], 0)
        place = lax.broadcasted_iota(jnp.int32, low.shape, 1)
        ref[pl.ds(base, SLOT + 8), cols] = jnp.where(place < shift, low, high).reshape(SLOT + 8, 128)


def tail_rows(ref, count, is_last):
    kept = ref[HALO + 2048 - count : HALO + 2048, :].astype(f32)
    if count < TAIL:
        kept = jnp.concatenate([kept, jnp.zeros((TAIL - count, D), f32)], 0)
    return jnp.where(is_last, kept, 0.0).astype(bf16)


def tag_rows(tag, pair):
    width = tag.shape[1]
    number = tag // 2 - 2 * pair
    kept = tag % 2
    row = lax.broadcasted_iota(jnp.int32, (AUG, width), 0)
    match = row == number
    query = jnp.where(match, 1.0, 0.0).astype(bf16)
    key = jnp.where(match & (kept == 1), 0.0, -big)
    key = jnp.where(row < 4, key, 0.0).astype(bf16)
    return query, key


def attn_forward_kernel(
    seq_count, tok_ref, cot_ref, tok_halo, cot_halo, seg_ref, keep_ref, seg_halo, keep_halo,
    w_ref, vec_ref,
    xs_ref, es_ref, xt_ref, qt_ref, kt_ref, vt_ref, c_ref, lse_ref,
    wt_ref, x_ref, e_ref, tag_ref, sems,
):
    seq = lax.axis_index("seq")
    is_last = seq == seq_count - 1
    rows = tok_ref.shape[1]
    loads = []
    for i, (whole, halo, ext) in enumerate(((tok_ref, tok_halo, x_ref), (cot_ref, cot_halo, e_ref))):
        loads.append(pltpu.make_async_copy(whole.at[0], ext.at[pl.ds(HALO, rows)], sems.at[2 * i]))
        loads.append(pltpu.make_async_copy(halo, ext.at[pl.ds(0, HALO)], sems.at[2 * i + 1]))
    for load in loads:
        load.start()
    for part in range(3):
        wt_ref[part * D : (part + 1) * D, :] = w_ref[:, part * D : (part + 1) * D].T
    tag_ref[...] = jnp.zeros_like(tag_ref)
    edge = seg_halo[...] * 2 + keep_halo[...]
    tag_ref[:, :HALO] = jnp.broadcast_to(edge[:, 128 - HALO :], (8, HALO))
    tag_ref[:, HALO : HALO + rows] = jnp.broadcast_to(seg_ref[...] * 2 + keep_ref[...], (8, rows))
    query_bias = vec_ref[:, 0:1].astype(f32)
    value_bias = vec_ref[:, 1:2].astype(f32)
    for load in loads:
        load.wait()

    def block(xb, tag, pair, lane, width):
        lanes = pl.ds(lane, width)
        xt_ref[:D, lanes] = xb.T
        q = dot(wt_ref[:D, :], xb, 1, 1) + query_bias
        q = (q.astype(bf16).astype(f32) * HEAD_DIM**-0.5).astype(bf16)
        k = dot(wt_ref[D : 2 * D, :], xb, 1, 1).astype(bf16)
        v = (dot(wt_ref[2 * D :, :], xb, 1, 1) + value_bias).astype(bf16)
        query_tag, key_tag = tag_rows(tag, pair)
        vt_ref[:, lanes] = v
        context = []
        for h in range(HEADS):
            rows = slice(h * HEAD_DIM, (h + 1) * HEAD_DIM)
            qh = jnp.concatenate([q[rows], query_tag], 0)
            kh = jnp.concatenate([k[rows], key_tag], 0)
            qt_ref[h, :, lanes] = qh
            kt_ref[h, :, lanes] = kh
            s = dot(kh, qh, 0, 0)
            top = jnp.max(s, axis=0, keepdims=True)
            ex = jnp.exp(s - top)
            total = jnp.sum(ex, axis=0, keepdims=True)
            lse_ref[h : h + 1, lanes] = top + jnp.log(total)
            a = (ex * (1.0 / total)).astype(bf16)
            context.append(dot(v[rows], a, 1, 0))
        return jnp.concatenate(context, 0).astype(bf16).T

    def one(j, carry):
        start = first_row(j, seq)
        row = slot_row(j)
        xb = staged(x_ref, start)
        xs_ref[pl.ds(row, SLOT), :] = xb
        es_ref[pl.ds(row, SLOT), :] = staged(e_ref, start)
        wide = tag_ref[:, pl.ds(pl.multiple_of(j * SLOT, 128), SLOT + 128)]
        width = SLOT + 128
        tag = pltpu.roll(wide, width - (start - j * SLOT), 1)[:1, :SLOT]
        c_ref[pl.ds(row, SLOT), :] = block(
            xb, tag, 8 * seq + j, pl.multiple_of(j * SLOT, 128), SLOT
        )
        return carry

    lax.fori_loop(0, 8, one, 0)
    count = 8 * seq_count
    xt_ref[:, 8 * SLOT :] = jnp.zeros((D + AUG, 128), bf16)
    xb = tail_rows(x_ref, count, is_last)
    eb = tail_rows(e_ref, count, is_last)
    tag = tag_ref[:1, 2048:2176]
    tag = pltpu.roll(tag_ref[:, 2048:2176], 128 - (64 - count), 1)[:1, :TAIL] if count < 64 else tag[:, :TAIL]
    place = lax.broadcasted_iota(jnp.int32, (1, TAIL), 1)
    tag = jnp.where(place < count, tag, (2 * 8 * seq_count + 3) * 2)
    cb = block(xb, tag, 8 * seq_count, 8 * SLOT, TAIL)
    for t in range(TILES):
        rows = slice(t * PIECE, (t + 1) * PIECE)
        at = slice(t * TILE + 2 * SLOT, (t + 1) * TILE)
        xs_ref[at, :] = xb[rows]
        es_ref[at, :] = eb[rows]
        c_ref[at, :] = cb[rows]
    ones = lax.broadcasted_iota(jnp.int32, (AUG, LANES), 0) == 0
    xt_ref[D:, :] = jnp.where(ones, 1.0, 0.0).astype(bf16)


def attn_forward(seq_count, tokens, cotangent, *others):
    shape = jax.ShapeDtypeStruct
    vmem = pl.BlockSpec(memory_space=pltpu.VMEM)
    hbm = pl.BlockSpec(memory_space=pl.ANY)
    return pl.pallas_call(
        functools.partial(attn_forward_kernel, seq_count),
        out_shape=(
            shape((ROWS, D), bf16),
            shape((ROWS, D), bf16),
            shape((D + AUG, LANES), bf16),
            shape((HEADS, HEAD_DIM + AUG, LANES), bf16),
            shape((HEADS, HEAD_DIM + AUG, LANES), bf16),
            shape((D, LANES), bf16),
            shape((ROWS, D), bf16),
            shape((HEADS, LANES), f32),
        ),
        in_specs=[hbm, hbm] + [vmem] * len(others),
        out_specs=[vmem] * 8,
        scratch_shapes=[
            pltpu.VMEM((3 * D, D), bf16),
            pltpu.VMEM((HALO + tokens.shape[1], D), bf16),
            pltpu.VMEM((HALO + tokens.shape[1], D), bf16),
            pltpu.VMEM((8, LANES), jnp.int32),
            pltpu.SemaphoreType.DMA((4,)),
        ],
        compiler_params=pltpu.CompilerParams(vmem_limit_bytes=56 * MIB),
        name="attn_forward",
    )(tokens, cotangent, *others)


def feed_kernel(
    xs_ref, c_ref, es_ref, wo_ref, w1_ref, w2_ref, vect_ref,
    z_ref, dh_ref, dr_ref, gwo_ref, gw1_ref, gw2_ref, gvec_ref, gb1_ref,
    u_ref, g_ref, awo_ref, aw1_ref, aw2_ref, vec_ref,
):
    step = pl.program_id(0)

    @pl.when(step == 0)
    def _():
        awo_ref[...] = jnp.zeros_like(awo_ref)
        aw1_ref[...] = jnp.zeros_like(aw1_ref)
        aw2_ref[...] = jnp.zeros_like(aw2_ref)
        gvec_ref[...] = jnp.zeros_like(gvec_ref)
        gb1_ref[...] = jnp.zeros_like(gb1_ref)
        vec_ref[...] = vect_ref[...].astype(f32).T

    def mean(v):
        return jnp.mean(v, axis=-1, keepdims=True)

    def row_sum(v):
        return jnp.sum(v, axis=0, keepdims=True)

    bo, b2, g1, c1, g2, c2 = (vec_ref[i : i + 1, :] for i in range(2, 8))
    h1 = xs_ref[...].astype(f32) + (dot(c_ref[...], wo_ref[...], 1, 0) + bo)
    mid = h1 - mean(h1)
    inv1 = lax.rsqrt(mean(mid * mid) + norm_epsilon)
    n1 = mid * inv1
    y = n1 * g1 + c1
    yb = y.astype(bf16)
    chunk = D
    f = None
    for k in range(FF // chunk):
        cols = slice(k * chunk, (k + 1) * chunk)
        u = dot(yb, w1_ref[:, cols], 1, 0) + vec_ref[8 + k : 9 + k, :]
        cdf = 0.5 * (1.0 + lax.erf(u * 0.7071067811865476))
        gk = (u * cdf).astype(bf16)
        u_ref[:, cols] = cdf + u * jnp.exp(u * u * -0.5) * 0.3989422804014327
        g_ref[:, cols] = gk
        part = dot(gk, w2_ref[cols, :], 1, 0)
        f = part if f is None else f + part
    h2 = y + (f + b2)
    mid2 = h2 - mean(h2)
    inv2 = lax.rsqrt(mean(mid2 * mid2) + norm_epsilon)
    n2 = mid2 * inv2
    z_ref[...] = (n2 * g2 + c2).astype(bf16)
    e = es_ref[...].astype(f32)
    gvec_ref[7:8, :] += row_sum(e)
    gvec_ref[6:7, :] += row_sum(e * n2)
    eg = e * g2
    dh2 = (eg - mean(eg) - n2 * mean(eg * n2)) * inv2
    df = dh2.astype(bf16)
    gvec_ref[3:4, :] += row_sum(df.astype(f32))
    dft = df.T
    ybt = yb.T
    dy = dh2
    for k in range(FF // chunk):
        cols = slice(k * chunk, (k + 1) * chunk)
        aw2_ref[:, cols] += dot(dft, g_ref[:, cols], 1, 0)
        dg = dot(df, w2_ref[cols, :], 1, 1)
        du = (dg * u_ref[:, cols]).astype(bf16)
        gb1_ref[:1, cols] += row_sum(du.astype(f32))
        aw1_ref[:, cols] += dot(ybt, du, 1, 0)
        dy = dy + dot(du, w1_ref[:, cols], 1, 1)
    gvec_ref[5:6, :] += row_sum(dy)
    gvec_ref[4:5, :] += row_sum(dy * n1)
    eg = dy * g1
    dh1 = (eg - mean(eg) - n1 * mean(eg * n1)) * inv1
    dh_ref[...] = dh1
    dr = dh1.astype(bf16)
    dr_ref[...] = dr
    gvec_ref[2:3, :] += row_sum(dr.astype(f32))
    awo_ref[...] += dot(c_ref[...].T, dr, 1, 0)

    @pl.when(step == TILES - 1)
    def _():
        gwo_ref[...] = awo_ref[...].astype(bf16)
        gw1_ref[...] = aw1_ref[...].astype(bf16)
        for k in range(FF // chunk):
            cols = slice(k * chunk, (k + 1) * chunk)
            gw2_ref[cols, :] = aw2_ref[:, cols].astype(bf16).T


def feed(xs, c, es, wo, w1, w2, vec_t):
    shape = jax.ShapeDtypeStruct
    tile = pl.BlockSpec((TILE, D), lambda i: (i, 0))

    def whole(*dims):
        return pl.BlockSpec(dims, lambda i: (0,) * len(dims), pipeline_mode=pl.Buffered(1))

    return pl.pallas_call(
        feed_kernel,
        grid=(TILES,),
        out_shape=(
            shape((ROWS, D), bf16),
            shape((ROWS, D), f32),
            shape((ROWS, D), bf16),
            shape((D, D), bf16),
            shape((D, FF), bf16),
            shape((FF, D), bf16),
            shape((8, D), f32),
            shape((8, FF), f32),
        ),
        in_specs=[tile, tile, tile, whole(D, D), whole(D, FF), whole(FF, D), whole(D, 128)],
        out_specs=[tile, tile, tile, whole(D, D), whole(D, FF), whole(FF, D), whole(8, D), whole(8, FF)],
        scratch_shapes=[
            pltpu.VMEM((TILE, FF), f32),
            pltpu.VMEM((TILE, FF), bf16),
            pltpu.VMEM((D, D), f32),
            pltpu.VMEM((D, FF), f32),
            pltpu.VMEM((D, FF), f32),
            pltpu.VMEM((128, D), f32),
        ],
        compiler_params=pltpu.CompilerParams(vmem_limit_bytes=60 * MIB),
        name="feed",
    )(xs, c, es, wo, w1, w2, vec_t)


def attn_backward_kernel(
    seq_count, xt_ref, qt_ref, kt_ref, vt_ref, lse_ref, dr_ref, dh_ref, z_ref, w_ref, wo_ref,
    out_ref, out_halo_ref, in_ref, in_halo_ref, gwa_ref, gbias_ref,
    dpt_ref, ext_ref,
):
    seq = lax.axis_index("seq")
    is_last = seq == seq_count - 1

    def block(dr, lane, width):
        lanes = pl.ds(lane, width)
        dct = dot(wo_ref[...], dr, 1, 1).astype(bf16)
        for h in range(HEADS):
            rows = slice(h * HEAD_DIM, (h + 1) * HEAD_DIM)
            qh = qt_ref[h, :, lanes]
            kh = kt_ref[h, :, lanes]
            vh = vt_ref[rows, lanes]
            dch = dct[rows]
            a = jnp.exp(dot(kh, qh, 0, 0) - lse_ref[h : h + 1, lanes])
            da = dot(vh, dch, 0, 0)
            ada = a * da
            ds = (ada - a * jnp.sum(ada, axis=0, keepdims=True)).astype(bf16)
            dv = dot(dch, a.astype(bf16), 1, 1)
            dk = dot(qh[:HEAD_DIM], ds, 1, 1)
            dq = dot(kh[:HEAD_DIM], ds, 1, 0) * HEAD_DIM**-0.5
            dpt_ref[rows, lanes] = dq.astype(bf16)
            dpt_ref[slice(D + h * HEAD_DIM, D + (h + 1) * HEAD_DIM), lanes] = dk.astype(bf16)
            dpt_ref[slice(2 * D + h * HEAD_DIM, 2 * D + (h + 1) * HEAD_DIM), lanes] = dv.astype(bf16)
        return dot(w_ref[...], dpt_ref[:, lanes], 1, 0).T

    dpt_ref[:, 8 * SLOT :] = jnp.zeros((3 * D, 128), bf16)

    def one(j, carry):
        row = slot_row(j)
        grad = block(dr_ref[pl.ds(row, SLOT), :], pl.multiple_of(j * SLOT, 128), SLOT)
        unstage(ext_ref, first_row(j, seq), grad + dh_ref[pl.ds(row, SLOT), :])
        return carry

    lax.fori_loop(0, 8, one, 0)
    count = 8 * seq_count

    def tail_of(ref):
        return jnp.concatenate(
            [ref[t * TILE + 2 * SLOT : (t + 1) * TILE, :] for t in range(TILES)], 0
        )

    grad = block(tail_of(dr_ref), 8 * SLOT, TAIL) + tail_of(dh_ref)

    @pl.when(is_last)
    def _():
        ext_ref[HALO + 2048 - count : HALO + 2048, :] = grad[:count]

    in_halo_ref[...] = ext_ref[:HALO, :]
    in_ref[...] = ext_ref[HALO : HALO + 2048, :]

    def two(j, carry):
        unstage(ext_ref, first_row(j, seq), z_ref[pl.ds(slot_row(j), SLOT), :].astype(f32))
        return carry

    lax.fori_loop(0, 8, two, 0)
    tail = tail_of(z_ref).astype(f32)

    @pl.when(is_last)
    def _():
        ext_ref[HALO + 2048 - count : HALO + 2048, :] = tail[:count]

    out_halo_ref[...] = ext_ref[:HALO, :].astype(bf16)
    out_ref[...] = ext_ref[HALO : HALO + 2048, :].astype(bf16)
    for part in range(3):
        cols = slice(part * D, (part + 1) * D)
        g = dot(xt_ref[...], dpt_ref[cols, :], 1, 1)
        gwa_ref[:, cols] = g[:D].astype(bf16)
        gbias_ref[:, cols] = g[D : D + 8]


def attn_backward(seq_count, *operands):
    shape = jax.ShapeDtypeStruct
    return pl.pallas_call(
        functools.partial(attn_backward_kernel, seq_count),
        out_shape=(
            shape((2048, D), bf16),
            shape((HALO, D), bf16),
            shape((2048, D), f32),
            shape((HALO, D), f32),
            shape((D, 3 * D), bf16),
            shape((8, 3 * D), f32),
        ),
        in_specs=[pl.BlockSpec(memory_space=pltpu.VMEM)] * len(operands),
        out_specs=[pl.BlockSpec(memory_space=pltpu.VMEM)] * 6,
        scratch_shapes=[
            pltpu.VMEM((3 * D, LANES), bf16),
            pltpu.VMEM((HALO + 2048 + 16, D), f32),
        ],
        compiler_params=pltpu.CompilerParams(vmem_limit_bytes=60 * MIB),
        name="attn_backward",
    )(*operands)


MESH = pl.DeviceIdType.MESH
PLANE = 4
DEPTH = 4


class Place:
    def __init__(self):
        self.batch = lax.axis_index("batch")
        self.z = lax.axis_index("seq")
        self.core = self.batch % 2
        self.plane = self.batch // 2

    def plane_at(self, k):
        x = (self.plane % 2 + k % 2) % 2
        y = (self.plane // 2 + k // 2) % 2
        return y * 2 + x

    def in_plane(self, k, other=0):
        core = self.core if other == 0 else 1 - self.core
        return {"batch": self.plane_at(k) * 2 + core, "seq": self.z}

    def depth_at(self, k):
        return (self.z + k) % DEPTH

    def in_depth(self, k):
        return {"batch": self.batch, "seq": self.depth_at(k)}

    def sibling(self):
        return {"batch": self.plane * 2 + 1 - self.core, "seq": self.z}

    def greet(self):
        barrier = pltpu.get_barrier_semaphore()
        for k in range(1, 4):
            pl.semaphore_signal(barrier, inc=1, device_id=self.in_plane(k), device_id_type=MESH)
            pl.semaphore_signal(barrier, inc=1, device_id=self.in_depth(k), device_id_type=MESH)
            pl.semaphore_signal(barrier, inc=1, device_id=self.in_plane(k, 1), device_id_type=MESH)
        pl.semaphore_signal(barrier, inc=1, device_id=self.sibling(), device_id_type=MESH)
        pl.semaphore_wait(barrier, 10)


def remote(src, dst, send, recv, device):
    return pltpu.make_async_remote_copy(
        src_ref=src, dst_ref=dst, send_sem=send, recv_sem=recv, device_id=device, device_id_type=MESH
    )


LOW, HIGH = pl.ds(0, DEPTH // 2), pl.ds(DEPTH // 2, DEPTH // 2)


class Gather:
    def __init__(self, place, whole, send, recv, parts=None):
        self.place, self.whole, self.send, self.recv, self.parts = place, whole, send, recv, parts

    def block(self, k):
        return self.whole.at[self.place.plane_at(k) * 2 + self.place.core]

    def copy(self, n, source, target, device):
        return remote(source, target, self.send.at[n], self.recv.at[n], device)

    def depth(self, k):
        at = self.place
        here = self.whole.at[at.batch, at.z]
        source = here if self.parts is None else self.parts.at[at.depth_at(k)]
        return self.copy(k - 1, source, here, at.in_depth(k))

    def plane(self, k):
        return self.copy(2 + k, self.block(0), self.block(0), self.place.in_plane(k))

    def across(self, k):
        half = self.block(k).at[LOW if k == 1 else HIGH]
        return self.copy(4 + k, half, half, self.place.in_plane(3 - k))

    def core(self, k):
        return self.copy(7 + k, self.block(k), self.block(k), self.place.sibling())

    def first(self):
        for k in range(1, 4):
            self.depth(k).start()

    def second(self):
        for k in range(1, 4):
            self.depth(k).wait_recv()
        for k in (1, 2):
            self.plane(k).start()
        self.core(0).start()

    def third(self):
        for k in (1, 2):
            self.plane(k).wait_recv()
            self.across(k).start()
            self.core(k).start()

    def fourth(self):
        for k in (1, 2):
            self.across(k).wait_recv()
        self.core(3).start()

    def finish(self):
        for k in range(4):
            self.core(k).wait_recv()
        for k in range(1, 4):
            self.depth(k).wait_send()
        for k in (1, 2):
            self.plane(k).wait_send()
            self.across(k).wait_send()
        for k in range(4):
            self.core(k).wait_send()


class Spread(Gather):
    def step(self, k, other):
        device = self.place.in_plane(k, other) if k else self.place.sibling()
        return self.copy(2 * k + other + 3 if k else 3, self.block(0), self.block(0), device)

    def steps(self):
        return [self.step(0, 0)] + [self.step(k, other) for k in range(1, 4) for other in range(2)]

    def second(self):
        for k in range(1, 4):
            self.depth(k).wait_recv()
        for copy in self.steps():
            copy.start()

    def finish(self):
        for copy in self.steps():
            copy.wait_recv()
        for k in range(1, 4):
            self.depth(k).wait_send()
        for copy in self.steps():
            copy.wait_send()


class Scatter:
    def __init__(self, place, grad, twin, near, far, along, send, recv):
        self.place, self.grad, self.twin = place, grad, twin
        self.near, self.far, self.along, self.send, self.recv = near, far, along, send, recv
        shape = grad.shape
        if len(shape) == 4:
            self.at = lambda p, c: grad.at[p * 2 + c]
        else:
            self.at = lambda p, c: grad.at[p, c]

    def block(self, k):
        return self.at(self.place.plane_at(k), self.place.core)

    def copy(self, n, source, target, device):
        return remote(source, target, self.send.at[n], self.recv.at[n], device)

    def core(self, p):
        source = self.at(p, 1 - self.place.core)
        return self.copy(p, source, self.twin.at[p], self.place.sibling())

    def plane(self, n):
        k, half = ((1, LOW), (3, LOW), (2, HIGH), (3, HIGH))[n]
        target = self.near.at[n]
        return self.copy(4 + n, self.block(k).at[half], target, self.place.in_plane(1 + n // 2))

    def across(self, n):
        k, half = ((2, LOW), (1, HIGH))[n]
        return self.copy(8 + n, self.block(k).at[half], self.far.at[n], self.place.in_plane(2 - n))

    def depth(self, k):
        source = self.block(0).at[self.place.depth_at(k)]
        return self.copy(9 + k, source, self.along.at[k - 1], self.place.in_depth(k))

    def first(self):
        for p in range(PLANE):
            self.core(p).start()

    def second(self):
        for p in range(PLANE):
            self.core(p).wait_recv()
        own = self.place.core

        def one(p, carry):
            mine = self.at(p, own)
            mine[...] = (mine[...].astype(f32) + self.twin[p].astype(f32)).astype(mine.dtype)
            return carry

        lax.fori_loop(0, PLANE, one, 0)
        for n in range(4):
            self.plane(n).start()

    def third(self):
        for n in range(4):
            self.plane(n).wait_recv()
        for n, (k, base) in enumerate(((2, 0), (1, 2))):
            mine = self.block(k)

            def one(q, carry):
                total = mine[base + q].astype(f32) + self.near[2 * n + 1, q].astype(f32)
                mine[base + q] = total.astype(mine.dtype)
                return carry

            lax.fori_loop(0, 2, one, 0)
            self.across(n).start()

    def fourth(self):
        for n in range(2):
            self.across(n).wait_recv()
        mine = self.block(0)

        def one(i, carry):
            n, q = i // 2, i % 2
            total = mine[i].astype(f32) + self.near[2 * n, q].astype(f32) + self.far[n, q].astype(f32)
            mine[i] = total.astype(mine.dtype)
            return carry

        lax.fori_loop(0, DEPTH, one, 0)
        for k in range(1, 4):
            self.depth(k).start()

    def total(self):
        for k in range(1, 4):
            self.depth(k).wait_recv()
        total = self.block(0)[self.place.z].astype(f32)
        for k in range(3):
            total = total + self.along[k].astype(f32)
        return total

    def finish(self):
        for p in range(PLANE):
            self.core(p).wait_send()
        for n in range(4):
            self.plane(n).wait_send()
        for n in range(2):
            self.across(n).wait_send()
        for k in range(1, 4):
            self.depth(k).wait_send()


def turned(ref, value):
    ref[...] = jnp.zeros_like(ref)
    ref[: value.shape[0], : value.shape[1]] = value
    return ref[...].T


def heads_of(block, h):
    return block[h * HEAD_DIM : (h + 1) * HEAD_DIM]


def only_head(block, h):
    zero = jnp.zeros((HEAD_DIM, block.shape[1]), block.dtype)
    mine = heads_of(block, h)
    return jnp.concatenate([mine, zero] if h % 2 == 0 else [zero, mine], 0)


def pair_of(block, h):
    at = h // 2 * 2 * HEAD_DIM
    return block[:, at : at + 2 * HEAD_DIM]


def mask_parts(tag, pair):
    query, key = tag_rows(tag, pair)
    width = tag.shape[1]
    zero = jnp.zeros((128 - AUG, width), bf16)
    return jnp.concatenate([key, zero], 0).T, jnp.concatenate([query, zero], 0)


class Slots:
    def __init__(self, tag_ref, seq, seq_count):
        self.tag_ref, self.seq, self.count = tag_ref, seq, 8 * seq_count
        self.last_pair = 8 * seq_count

    def tag(self, j):
        wide = self.tag_ref[:, pl.ds(pl.multiple_of(j * SLOT, 128), SLOT + 128)]
        offset = HALO - 8 * self.seq - j
        return pltpu.roll(wide, SLOT + 128 - offset, 1)[:1, :SLOT]

    def tail_tag(self):
        tag = self.tag_ref[:, 2048:2176]
        if self.count < TAIL:
            tag = pltpu.roll(tag, 128 - (TAIL - self.count), 1)
        place = lax.broadcasted_iota(jnp.int32, (1, TAIL), 1)
        return jnp.where(place < self.count, tag[:1, :TAIL], 2 * (2 * self.last_pair + 3))

    def tail(self, ref):
        return jnp.concatenate(
            [ref[t * TILE + 2 * SLOT : (t + 1) * TILE, :] for t in range(TILES)], 0
        )

    def set_tail(self, ref, value):
        for t in range(TILES):
            ref[t * TILE + 2 * SLOT : (t + 1) * TILE, :] = value[t * PIECE : (t + 1) * PIECE]


def halves_of(width):
    step = min(width, 128)
    return [slice(i, i + step) for i in range(0, width, step)]


def pair_stack(values, *rest):
    zero = jnp.zeros_like(values[0])
    left = jnp.concatenate([values[0], zero, *rest], 0)
    right = jnp.concatenate([zero, values[1], *rest], 0)
    return left, right


def forward_block(
    xb, tag, pair, lanes, put, wt_ref, biases, xt_ref, qt_ref, kt_ref, vt_ref, lse_ref, s_ref, a_ref,
    kn_ref, ct_ref,
):
    width = xb.shape[0]
    parts = ((kt_ref, None), (qt_ref, biases[0]), (vt_ref, biases[1]))

    def project(n):
        at = (1, 0, 2)[n]
        p = dot(wt_ref[at * D : (at + 1) * D, :], xb, 1, 1)
        s_ref[2 * n, :, :width] = p[:SLOT]
        s_ref[2 * n + 1, :, :width] = p[SLOT:]

    def keep(n):
        out_ref, bias = parts[n]
        for h in range(HEADS):
            at = h % 4 * HEAD_DIM
            value = s_ref[2 * n + h // 4, at : at + HEAD_DIM, :width]
            rows = slice(h * HEAD_DIM, (h + 1) * HEAD_DIM)
            if bias is not None:
                value = value + bias[rows]
            value = value.astype(bf16)
            if n == 1:
                value = (value.astype(f32) * HEAD_DIM**-0.5).astype(bf16)
            out_ref[rows, lanes] = value

    masks = []

    def turn():
        kn_ref[:width, :] = kt_ref[:, lanes].T
        masks.extend(mask_parts(tag, pair))

    def rows_of(h):
        return slice(h * HEAD_DIM, (h + 1) * HEAD_DIM)

    def scores(p):
        key_mask, query_mask = masks
        left = jnp.concatenate([kn_ref[:width, p * 128 : (p + 1) * 128], key_mask], 1)
        both = pair_stack([qt_ref[rows_of(2 * p + i), lanes] for i in range(2)], query_mask)
        if width % 128 == 0:
            s = dot(left, jnp.concatenate(both, 1), 1, 0)
            s_ref[2 * p], s_ref[2 * p + 1] = s[:, :width], s[:, width:]
        else:
            for i in range(2):
                s_ref[2 * p + i, :width, :width] = dot(left, both[i], 1, 0)

    def weigh(p):
        for h in (2 * p, 2 * p + 1):
            for half in halves_of(width):
                s = s_ref[h, :width, half]
                top = jnp.max(s, axis=0, keepdims=True)
                ex = jnp.exp(s - top)
                total = jnp.sum(ex, axis=0, keepdims=True)
                a_ref[h, :width, half] = (ex * (1.0 / total)).astype(bf16)
                at = pl.ds(pl.multiple_of(lanes.start + half.start, 128), half.stop - half.start)
                lse_ref[h : h + 1, at] = top + jnp.log(total)

    def collect(p):
        for h in (2 * p, 2 * p + 1):
            c = dot(vt_ref[rows_of(h), lanes], a_ref[h, :width, :width], 1, 0)
            ct_ref[rows_of(h), :width] = c.astype(bf16)

    def close():
        xt_ref[:D, lanes] = xb.T
        put(ct_ref[:, :width].T)

    call = functools.partial
    ahead = [
        call(project, 0), call(project, 1), call(keep, 0), turn, call(project, 2), call(keep, 1),
        call(keep, 2),
    ]
    return ahead, (scores, weigh, collect), [close]


def together(*blocks):
    for phases in zip(*(block[0] for block in blocks)):
        for phase in phases:
            phase()
    count = len(blocks)

    def stage(n):
        return lambda i: blocks[i % count][1][n](i // count)

    skewed(HEADS // 2 * count, stage(0), stage(1), stage(2))
    for phases in zip(*(block[2] for block in blocks)):
        for phase in phases:
            phase()


def skewed(count, *stages):
    for i in range(count + len(stages) - 1):
        for n, stage in enumerate(stages):
            if 0 <= i - n < count:
                stage(i - n)


def backward_block(
    dr, c, tag, pair, lanes, wo, qt_ref, kt_ref, vt_ref, lse_ref, dpt_ref, s_ref, da_ref, a_ref,
    ds_ref, kn_ref, vn_ref, dct_ref, ct_ref,
):
    width = dr.shape[0]
    masks = []

    def turn():
        kn_ref[:width, :] = kt_ref[:, lanes].T
        vn_ref[:width, :] = vt_ref[:, lanes].T
        masks.extend(mask_parts(tag, pair))

    def spread():
        dct_ref[:, :width] = dot(wo, dr, 1, 1).astype(bf16)
        ct_ref[:, :width] = c.T

    def rows_of(h):
        return slice(h * HEAD_DIM, (h + 1) * HEAD_DIM)

    def scores(p):
        at = slice(p * 128, (p + 1) * 128)
        key_mask, query_mask = masks
        left = jnp.concatenate([kn_ref[:width, at], key_mask], 1)
        both = pair_stack([qt_ref[rows_of(2 * p + i), lanes] for i in range(2)], query_mask)
        both_d = pair_stack([dct_ref[rows_of(2 * p + i), :width] for i in range(2)])
        right = vn_ref[:width, at]
        if width % 128 == 0:
            s = dot(left, jnp.concatenate(both, 1), 1, 0)
            u = 2 * (p % 2)
            s_ref[u], s_ref[u + 1] = s[:, :width], s[:, width:]
            da = dot(right, jnp.concatenate(both_d, 1), 1, 0)
            da_ref[u], da_ref[u + 1] = da[:, :width], da[:, width:]
        else:
            for i in range(2):
                s_ref[2 * (p % 2) + i, :width, :width] = dot(left, both[i], 1, 0)
                da_ref[2 * (p % 2) + i, :width, :width] = dot(right, both_d[i], 1, 0)

    def weigh(p):
        for h in (2 * p, 2 * p + 1):
            rows = rows_of(h)
            for half in halves_of(width):
                at = pl.ds(pl.multiple_of(lanes.start + half.start, 128), half.stop - half.start)
                product = ct_ref[rows, half].astype(f32) * dct_ref[rows, half].astype(f32)
                delta = jnp.sum(product, axis=0, keepdims=True)
                lse = lse_ref[h : h + 1, at]
                for first in range(0, width, 64):
                    keys = slice(first, first + 64)
                    a = jnp.exp(s_ref[h % 4, keys, half] - lse)
                    a_ref[h % 4, keys, half] = a.astype(bf16)
                    ds_ref[h % 4, keys, half] = (a * (da_ref[h % 4, keys, half] - delta)).astype(bf16)

    def collect(p):
        for h in (2 * p, 2 * p + 1):
            rows = rows_of(h)
            ds = ds_ref[h % 4, :width, :width]
            dv = dot(dct_ref[rows, :width], a_ref[h % 4, :width, :width], 1, 1)
            dk = dot(qt_ref[rows, lanes], ds, 1, 1)
            dq = dot(kt_ref[rows, lanes], ds, 1, 0) * HEAD_DIM**-0.5
            dpt_ref[rows, lanes] = dq.astype(bf16)
            dpt_ref[slice(D + rows.start, D + rows.stop), lanes] = dk.astype(bf16)
            dpt_ref[slice(2 * D + rows.start, 2 * D + rows.stop), lanes] = dv.astype(bf16)

    return [turn, spread], (scores, weigh, collect), []


def mean(v):
    return jnp.mean(v, axis=-1, keepdims=True)


def row_sum(v):
    return jnp.sum(v, axis=0, keepdims=True)


def flat(value):
    return value.reshape(-1, value.shape[-1])


BLOCK = 48
MAIN = 2 * SLOT


def eights(v):
    return jnp.sum(v.reshape(-1, 8, v.shape[-1]), axis=0)


def feed_tile(
    t, xs_ref, c_ref, es_ref, wo_ref, w1_ref, w2_ref, vec_ref, dh_ref, gvec_ref,
    acc_ref, other_ref, n1_ref, inv_ref, yb_ref, df_ref, u_ref, g_ref, back_ready, tails,
    awo_ref, aw1_ref, aw2_ref,
):
    first = pl.multiple_of(t * TILE, 16)
    rows = pl.ds(first, TILE)
    piece = pl.ds(pl.multiple_of(t * PIECE, 16), PIECE)
    g_tail, du_tail, df_tail, yb_tail = tails
    bo, b2, g1, c1, g2, c2 = (vec_ref[i : i + 1, :] for i in range(2, 8))
    per = FF // D
    blocks = [slice(i, i + BLOCK) for i in range(0, TILE, BLOCK)]

    def at(block):
        return pl.ds(pl.multiple_of(first + block.start, 16), BLOCK)

    acc_ref[...] = dot(c_ref[rows, :], flat(wo_ref[...]), 1, 0)
    for block in blocks:
        h1 = xs_ref[at(block), :].astype(f32) + (acc_ref[block, :] + bo)
        mid = h1 - mean(h1)
        inv1 = lax.rsqrt(mean(mid * mid) + norm_epsilon)
        n1 = mid * inv1
        n1_ref[block, :] = n1
        inv_ref[block, :] = jnp.broadcast_to(inv1, (BLOCK, 128))
        yb_ref[block, :] = (n1 * g1 + c1).astype(bf16)

    pads = (acc_ref, other_ref)

    def w2_part(k):
        return flat(w2_ref[8 // per * k : 8 // per * (k + 1)])

    def w1_part(k):
        return flat(w1_ref[:, :, :, k * D : (k + 1) * D])

    def up(k):
        pads[k % 2][...] = dot(yb_ref[...], w1_part(k), 1, 0)

    def activate(k):
        cols = slice(k * D, (k + 1) * D)
        b1 = vec_ref[8 + k : 9 + k, :]
        for block in blocks:
            u = pads[k % 2][block, :] + b1
            cdf = 0.5 + 0.5 * lax.erf(u * 0.7071067811865476)
            g_ref[k * TILE + block.start : k * TILE + block.stop, :] = (u * cdf).astype(bf16)
            bell = jnp.exp2(u * u * (-0.5 * math.log2(math.e)) - 0.5 * math.log2(2.0 * math.pi))
            u_ref[block, cols] = cdf + u * bell

    def down(k):
        part = dot(g_ref[k * TILE : (k + 1) * TILE, :], w2_part(k), 1, 0)
        if k == 0:
            dh_ref[rows, :] = part
        else:
            dh_ref[rows, :] += part

    up(0)
    up(1)
    activate(0)
    pl.when(t == 0)(back_ready)
    for k in range(per):
        if k + 2 < per:
            up(k + 2)
        down(k)
        if k + 1 < per:
            activate(k + 1)
    sums = [jnp.zeros((8, D), f32)] * 3
    for block in blocks:
        h2 = (n1_ref[block, :] * g1 + c1) + (dh_ref[at(block), :] + b2)
        mid2 = h2 - mean(h2)
        inv2 = lax.rsqrt(mean(mid2 * mid2) + norm_epsilon)
        n2 = mid2 * inv2
        xs_ref[at(block), :] = (n2 * g2 + c2).astype(bf16)
        e = es_ref[at(block), :].astype(f32)
        en = e * n2
        eg = e * g2
        dh2 = (eg - mean(eg) - n2 * mean(eg * n2)) * inv2
        dh_ref[at(block), :] = dh2
        df = dh2.astype(bf16)
        df_ref[block, :] = df
        sums = [sums[0] + eights(e), sums[1] + eights(en), sums[2] + eights(df.astype(f32))]
    for i, value in zip((7, 6, 3), sums):
        gvec_ref[i : i + 1, :] += row_sum(value)
    dft = df_ref[:MAIN, :].T
    ybt = yb_ref[:MAIN, :].T
    df_tail[piece, :] = df_ref[MAIN:, :]
    yb_tail[piece, :] = yb_ref[MAIN:, :]

    def up_back(k):
        pads[k % 2][...] = dot(df_ref[...], w2_part(k), 1, 1)

    def activate_back(k):
        cols = slice(k * D, (k + 1) * D)
        here = slice(k * TILE, k * TILE + MAIN)
        at_tail = pl.ds(pl.multiple_of(k * TAIL + t * PIECE, 16), PIECE)
        aw2_ref[:, cols] += dot(dft, g_ref[here, :], 1, 0)
        g_tail[at_tail, :] = g_ref[here.stop : here.stop + PIECE, :]
        total = jnp.zeros((8, D), f32)
        for block in blocks:
            du = (pads[k % 2][block, :] * u_ref[block, cols]).astype(bf16)
            g_ref[k * TILE + block.start : k * TILE + block.stop, :] = du
            total = total + eights(du.astype(f32))
        gvec_ref[8 + k : 9 + k, :] += row_sum(total)

    def down_back(k):
        cols = slice(k * D, (k + 1) * D)
        here = slice(k * TILE, k * TILE + MAIN)
        at_tail = pl.ds(pl.multiple_of(k * TAIL + t * PIECE, 16), PIECE)
        aw1_ref[:, cols] += dot(ybt, g_ref[here, :], 1, 0)
        du_tail[at_tail, :] = g_ref[here.stop : here.stop + PIECE, :]
        part = dot(g_ref[k * TILE : (k + 1) * TILE, :], w1_part(k), 1, 1)
        dh_ref[rows, :] += part

    skewed(per, up_back, activate_back, down_back)
    sums = [jnp.zeros((8, D), f32)] * 3
    for block in blocks:
        dy = dh_ref[at(block), :]
        n1 = n1_ref[block, :]
        eg = dy * g1
        dh1 = (eg - mean(eg) - n1 * mean(eg * n1)) * inv_ref[block, :1]
        dh_ref[at(block), :] = dh1
        dr = dh1.astype(bf16)
        es_ref[at(block), :] = dr
        sums = [sums[0] + eights(dy), sums[1] + eights(dy * n1), sums[2] + eights(dr.astype(f32))]
    for i, value in zip((5, 4, 2), sums):
        gvec_ref[i : i + 1, :] += row_sum(value)
    main = pl.ds(first, MAIN)
    awo_ref[...] += dot(c_ref[main, :].T, es_ref[main, :], 1, 0)


def whole_kernel(*refs):
    refs = list(refs)

    def take(count):
        taken = refs[:count]
        del refs[:count]
        return taken

    state_in = take(15)
    tok_ref, cot_ref, seg_ref, keep_ref = take(4)
    out_ref, in_ref = take(2)
    state_out = take(15)
    copy_out = take(5)
    out_back, in_back = take(2)
    state = take(15)
    masters, firsts, seconds = state[:5], state[5:10], state[10:]
    weights = take(5)
    wa_ref, wo_ref, w1_ref, w2_ref, wv_ref = weights
    xs_ref, es_ref, xt_ref, qt_ref, kt_ref, vt_ref, c_ref, lse_ref, dh_ref, tag_ref = take(10)
    ext_ref, seg_halo, keep_halo = take(3)
    square, gvec_ref, gwa_ref, gwo_ref, grad_vec, halo_out, halo_in = take(7)
    twins, nears, fars, alongs = take(5), take(5), take(5), take(5)
    parts, copies, whole_vec = take(4), take(5), take(1)[0]
    (
        state_sems, load_sems, gather_send, gather_recv, edge_send, edge_recv,
        sum_send, sum_recv, copy_send, copy_recv, store_sems,
    ) = refs
    place = Place()
    seq, seq_count = place.z, DEPTH
    is_last = seq == seq_count - 1
    slots = Slots(tag_ref, seq, seq_count)
    rows = tok_ref.shape[1]
    ext_x, ext_e = ext_ref.at[pl.ds(0, HALO + rows)], ext_ref.at[pl.ds(HALO + rows, HALO + rows)]

    loads = [pltpu.make_async_copy(state_in[i], state[i], state_sems.at[i]) for i in range(15)]
    for load in loads:
        load.start()
    big_loads = [
        pltpu.make_async_copy(src.at[0], dst.at[pl.ds(HALO, rows)], load_sems.at[i])
        for i, (src, dst) in enumerate(((tok_ref, ext_x), (cot_ref, ext_e)))
    ]
    for load in big_loads:
        load.start()
    place.greet()
    edge = [
        remote(src, dst, edge_send.at[i], edge_recv.at[i], place.in_depth(1))
        for i, (src, dst) in enumerate((
            (tok_ref.at[0, pl.ds(rows - HALO, HALO)], ext_x.at[pl.ds(0, HALO)]),
            (cot_ref.at[0, pl.ds(rows - HALO, HALO)], ext_e.at[pl.ds(0, HALO)]),
            (seg_ref.at[:, pl.ds(rows - 128, 128)], seg_halo),
            (keep_ref.at[:, pl.ds(rows - 128, 128)], keep_halo),
        ))
    ]
    gathers = [Gather(place, weights[i], gather_send.at[i], gather_recv.at[i]) for i in range(5)]

    def put(i):
        shard = turned(square, masters[4][...])[: masters[4].shape[1]] if i == 4 else masters[i][...]
        weights[i][place.batch, place.z] = shard.astype(bf16)

    for i in (0, 4):
        loads[i].wait()
        put(i)
        gathers[i].first()
    for copy in edge:
        copy.start()
    for i in (1, 2, 3):
        loads[i].wait()
        put(i)
    gathers[1].first()
    for load in big_loads:
        load.wait()
    for copy in edge:
        copy.wait()
    tag_ref[...] = jnp.zeros_like(tag_ref)
    rim = seg_halo[...] * 2 + keep_halo[...]
    tag_ref[:, :HALO] = jnp.broadcast_to(rim[:, 128 - HALO :], (8, HALO))
    tag_ref[:, HALO : HALO + rows] = jnp.broadcast_to(seg_ref[...] * 2 + keep_ref[...], (8, rows))

    def stage_one(j, carry):
        start = first_row(j, seq)
        row = slot_row(j)
        stage_slot(ext_x, start, xs_ref, row)
        stage_slot(ext_e, start, es_ref, row)
        return carry

    gathers[0].second()
    gathers[2].first()
    gathers[4].second()
    gathers[1].second()
    lax.fori_loop(0, 8, stage_one, 0)
    slots.set_tail(xs_ref, tail_rows(ext_x, slots.count, is_last))
    slots.set_tail(es_ref, tail_rows(ext_e, slots.count, is_last))
    gathers[0].third()
    gathers[4].third()
    xt_ref[:, 8 * SLOT :] = jnp.zeros((D + AUG, 128), bf16)
    ones = lax.broadcasted_iota(jnp.int32, (AUG, LANES), 0) == 0
    xt_ref[D:, :] = jnp.where(ones, 1.0, 0.0).astype(bf16)
    gathers[2].second()
    gathers[3].first()
    gathers[0].fourth()
    gathers[4].fourth()
    gathers[1].third()
    gathers[0].finish()
    gathers[4].finish()

    def forward(wt_ref, s_ref, a_ref, kn_ref, ct_ref):
        for part in range(3):
            wt_ref[part * D : (part + 1) * D, :] = flat(
                wa_ref[:, :, :, part * D : (part + 1) * D]
            ).T
        vec_t = flat(wv_ref[...])
        biases = (vec_t[:, 0:1].astype(f32), vec_t[:, 1:2].astype(f32))

        def block(n, xb, tag, pair, lanes, put):
            return forward_block(
                xb, tag, pair, lanes, put, wt_ref, biases, xt_ref, qt_ref, kt_ref, vt_ref, lse_ref,
                s_ref.at[n], a_ref.at[n], kn_ref.at[n], ct_ref.at[n],
            )

        def two(i, carry):
            for step, event in (
                (1, gathers[1].fourth), (1, gathers[2].third), (2, gathers[3].second),
                (3, gathers[2].fourth),
            ):
                pl.when(i == step)(event)

            def slot(n):
                j = 2 * i + n
                at = pl.ds(slot_row(j), SLOT)
                lanes = pl.ds(pl.multiple_of(j * SLOT, 128), SLOT)

                def put(value):
                    c_ref[at, :] = value

                return block(n, xs_ref[at, :], slots.tag(j), 8 * seq + j, lanes, put)

            together(slot(0), slot(1))
            return carry

        lax.fori_loop(0, 4, two, 0)
        together(
            block(
                0, slots.tail(xs_ref), slots.tail_tag(), slots.last_pair, pl.ds(8 * SLOT, TAIL),
                functools.partial(slots.set_tail, c_ref),
            )
        )

    pl.run_scoped(
        forward,
        pltpu.VMEM((3 * D, D), bf16),
        pltpu.VMEM((2, HEADS, SLOT, SLOT), f32),
        pltpu.VMEM((2, HEADS, SLOT, SLOT), bf16),
        pltpu.VMEM((2, SLOT, D), bf16),
        pltpu.VMEM((2, D, SLOT), bf16),
    )
    for i in (1, 2):
        gathers[i].finish()
    gathers[3].third()

    def back_ready():
        gathers[3].fourth()
        gathers[3].finish()

    grads = [gwa_ref, gwo_ref, w1_ref, w2_ref, grad_vec]
    scatters = [
        Scatter(
            place, grads[i], twins[i], nears[i], fars[i], alongs[i], sum_send.at[i], sum_recv.at[i]
        )
        for i in range(5)
    ]

    def feed_all(
        vec_ref, acc_ref, other_ref, n1_ref, inv_ref, u_ref, awo_ref, aw1_ref, aw2_ref
    ):
        used = 0
        views = []
        for count in (4 * TILE, TILE, TILE, TAIL, TAIL, 4 * TAIL, 4 * TAIL):
            views.append(ext_ref.at[pl.ds(used, count)])
            used += count
        g_ref, yb_ref, df_ref, yb_tail, df_tail, g_tail, du_tail = views
        for ref in (awo_ref, aw1_ref, aw2_ref, gvec_ref):
            ref[...] = jnp.zeros_like(ref)
        vec_ref[...] = flat(wv_ref[...]).astype(f32).T[:16]

        def one(t, carry):
            feed_tile(
                t, xs_ref, c_ref, es_ref, wo_ref, w1_ref, w2_ref, vec_ref, dh_ref, gvec_ref, acc_ref,
                other_ref, n1_ref, inv_ref, yb_ref, df_ref, u_ref, g_ref, back_ready,
                (g_tail, du_tail, df_tail, yb_tail),
                awo_ref, aw1_ref, aw2_ref,
            )
            return carry

        lax.fori_loop(0, TILES, one, 0)
        for k in range(FF // D):
            cols = slice(k * D, (k + 1) * D)
            at = slice(k * TAIL, (k + 1) * TAIL)
            aw2_ref[:, cols] += dot(df_tail[...].T, g_tail[at, :], 1, 0)
            aw1_ref[:, cols] += dot(yb_tail[...].T, du_tail[at, :], 1, 0)
        awo_ref[...] += dot(slots.tail(c_ref).T, slots.tail(es_ref), 1, 0)
        def convert(i, carry):
            value = aw2_ref[:, pl.ds(pl.multiple_of(i * 128, 128), 128)].astype(bf16).T
            w2_ref[i // 2, pl.ds(i % 2 * 2, 2)] = value.reshape(2, -1, D)
            return carry

        def convert_rows(i, carry):
            value = aw1_ref[pl.ds(pl.multiple_of(i * 64, 64), 64), :].astype(bf16)
            w1_ref[i] = value.reshape(DEPTH, -1, FF)
            gwo_ref[i // 2, i % 2] = (
                awo_ref[pl.ds(pl.multiple_of(i * 64, 64), 64), :].astype(bf16).reshape(DEPTH, -1, D)
            )
            return carry

        lax.fori_loop(0, FF // 128, convert, 0)
        scatters[3].first()
        lax.fori_loop(0, 8, convert_rows, 0)
        scatters[2].first()
        scatters[1].first()

    pl.run_scoped(
        feed_all,
        pltpu.VMEM((16, D), f32),
        pltpu.VMEM((TILE, D), f32),
        pltpu.VMEM((TILE, D), f32),
        pltpu.VMEM((TILE, D), f32),
        pltpu.VMEM((TILE, 128), f32),
        pltpu.VMEM((TILE, FF), f32),
        pltpu.VMEM((D, D), f32),
        pltpu.VMEM((D, FF), f32),
        pltpu.VMEM((D, FF), f32),
    )
    for load in loads[5:]:
        load.wait()
    copy_gathers = [
        kind(place, copies[i], copy_send.at[i], copy_recv.at[i], parts[i])
        for i, kind in enumerate((Spread, Spread, Gather, Gather))
    ]
    copy_gathers.append(Spread(place, whole_vec, copy_send.at[4], copy_recv.at[4]))
    stores = []

    def store(src, dst):
        stores.append(pltpu.make_async_copy(src, dst, store_sems.at[len(stores)]))
        stores[-1].start()

    def update(i):
        total = scatters[i].total()
        if i == 4:
            square[...] = jnp.zeros_like(square)
            square[: total.shape[0], :] = total
            here, cols = masters[4].shape
            total = square[...].T[:here, :cols]
        new = adam_update(masters[i][...], firsts[i][...], seconds[i][...], total, learn_rates[i])
        firsts[i][...], seconds[i][...], masters[i][...] = new
        if i == 4:
            shard = turned(square, new[2])[: new[2].shape[1]].astype(bf16)
            whole_vec[place.batch, place.z] = shard
        else:
            low = new[2].astype(bf16)
            width = low.shape[1] // DEPTH
            for q in range(DEPTH):
                parts[i][q] = low[:, q * width : (q + 1) * width]
            copies[i][place.batch, place.z] = parts[i][place.z]
        copy_gathers[i].first()

    def backward(dpt_ref):
        dpt_ref[:, 8 * SLOT :] = jnp.zeros((3 * D, 128), bf16)

        def attention(s_ref, da_ref, a_ref, ds_ref, kn_ref, vn_ref, dct_ref, ct_ref):
            wo = flat(wo_ref[...])
            pads = (s_ref, da_ref, a_ref, ds_ref, kn_ref, vn_ref, dct_ref, ct_ref)

            def block(n, dr, c, tag, pair, lanes):
                return backward_block(
                    dr, c, tag, pair, lanes, wo, qt_ref, kt_ref, vt_ref, lse_ref, dpt_ref,
                    *(pad.at[n] for pad in pads),
                )

            def two(i, carry):
                for step, event in (
                    (0, scatters[3].second), (1, scatters[2].second), (2, scatters[3].third),
                    (3, scatters[1].second),
                ):
                    pl.when(i == step)(event)

                def slot(n):
                    j = 2 * i + n
                    at = pl.ds(slot_row(j), SLOT)
                    lanes = pl.ds(pl.multiple_of(j * SLOT, 128), SLOT)
                    return block(n, es_ref[at, :], c_ref[at, :], slots.tag(j), 8 * seq + j, lanes)

                together(slot(0), slot(1))
                return carry

            lax.fori_loop(0, 4, two, 0)
            together(
                block(
                    0, slots.tail(es_ref), slots.tail(c_ref), slots.tail_tag(), slots.last_pair,
                    pl.ds(8 * SLOT, TAIL),
                )
            )

        pl.run_scoped(
            attention,
            *[pltpu.VMEM((2, 4, SLOT, SLOT), f32)] * 2,
            *[pltpu.VMEM((2, 4, SLOT, SLOT), bf16)] * 2,
            *[pltpu.VMEM((2, SLOT, D), bf16)] * 2,
            *[pltpu.VMEM((2, D, SLOT), bf16)] * 2,
        )
        pl.run_scoped(
            functools.partial(finish, dpt_ref),
            pltpu.VMEM((HALO + rows + 16, D), f32),
            pltpu.VMEM((4, SLOT, SLOT), f32),
        )

    def finish(dpt_ref, ext_ref, s_ref):
        low_ref = ext_e
        for part in range(3):
            cols = slice(part * D, (part + 1) * D)
            g = dot(xt_ref[...], dpt_ref[cols, :], 1, 1)
            gwa_ref[:, :, :, :, cols] = g[:D].astype(bf16).reshape(PLANE, 2, DEPTH, -1, D)
            if part != 1:
                gvec_ref[part // 2 : part // 2 + 1, :] = g[D : D + 1]
        grad_vec[...] = gvec_ref[...].T.reshape(grad_vec.shape)
        scatters[0].first()
        scatters[4].first()
        scatters[2].third()

        def output_one(j, carry):
            at = pl.ds(slot_row(j), SLOT)
            unstage_slot(
                ext_ref, first_row(j, seq),
                lambda g: xs_ref[at, g * 128 : (g + 1) * 128].astype(f32),
            )
            return carry

        def close(value):
            @pl.when(is_last)
            def _():
                ext_ref[HALO + rows - slots.count : HALO + rows, :] = value[: slots.count]

        lax.fori_loop(0, 8, output_one, 0)
        close(slots.tail(xs_ref).astype(f32))
        scatters[0].second()
        scatters[4].second()
        scatters[3].fourth()
        scatters[1].third()
        low_ref[...] = ext_ref[: HALO + rows, :].astype(bf16)
        halo_out[...] = low_ref[:HALO, :]
        edge_back[0].start()
        store(low_ref.at[pl.ds(HALO, rows)], out_ref)
        wa = flat(wa_ref[...])

        def input_block(lanes):
            return dot(wa, dpt_ref[:, lanes], 1, 0).T

        def input_two(i, carry):
            for step, event in (
                (0, scatters[2].fourth), (1, scatters[0].third), (1, scatters[4].third),
                (2, scatters[1].fourth), (2, functools.partial(update, 3)),
                (3, scatters[0].fourth), (3, scatters[4].fourth),
            ):
                pl.when(i == step)(event)

            def product(n):
                lanes = pl.ds(pl.multiple_of((2 * i + n) * SLOT, 128), SLOT)
                grad = dot(wa, dpt_ref[:, lanes], 1, 0)
                s_ref[2 * n], s_ref[2 * n + 1] = grad[:SLOT], grad[SLOT:]

            def put_back(n):
                j = 2 * i + n
                at = pl.ds(slot_row(j), SLOT)

                def column(g):
                    part = s_ref[2 * n + g // 2, g % 2 * 128 : g % 2 * 128 + 128, :].T
                    return part + dh_ref[at, g * 128 : (g + 1) * 128]

                unstage_slot(ext_ref, first_row(j, seq), column)

            skewed(2, product, put_back)
            return carry

        lax.fori_loop(0, 4, input_two, 0)
        close(input_block(pl.ds(8 * SLOT, TAIL)) + slots.tail(dh_ref))
        halo_in[...] = ext_ref[:HALO, :]
        edge_back[1].start()
        store(ext_ref.at[pl.ds(HALO, rows)], in_ref)
        copy_gathers[3].second()
        update(2)
        update(1)
        copy_gathers[2].second()
        update(4)
        update(0)
        copy_gathers[3].third()
        copy_gathers[2].third()
        copy_gathers[1].second()
        copy_gathers[4].second()
        copy_gathers[0].second()
        copy_gathers[3].fourth()
        copy_gathers[2].fourth()
        for i in range(5):
            for n, kind in enumerate((firsts, seconds, masters)):
                store(kind[i], state_out[5 * n + i])
        for i in (3, 2, 1, 4, 0):
            copy_gathers[i].finish()
            scatters[i].finish()
        here = masters[4].shape[0]
        mine = jnp.concatenate([whole_vec[seq * 2 + q // 4, q % 4] for q in range(8)], 0)
        copies[4][...] = mine.astype(f32).T[:here].astype(bf16)
        for i in range(5):
            store(copies[i], copy_out[i])
        for copy in stores:
            copy.wait()
        for copy in edge_back:
            copy.wait()

    edge_back = [
        remote(halo_out, out_back, edge_send.at[4], edge_recv.at[4], place.in_depth(3)),
        remote(halo_in, in_back, edge_send.at[5], edge_recv.at[5], place.in_depth(3)),
    ]
    pl.run_scoped(backward, pltpu.VMEM((3 * D, LANES), bf16))


def whole(masters, firsts, seconds, tokens, cotangent, segment, keep):
    shape = jax.ShapeDtypeStruct
    vmem = pl.BlockSpec(memory_space=pltpu.VMEM)
    hbm = pl.BlockSpec(memory_space=pl.ANY)
    state = (*masters, *firsts, *seconds)
    rows = tokens.shape[1]
    r = masters[0].shape[0]
    shapes = ((r, 3 * D), (r, D), (r, FF), (4 * r, D))
    copies = [((8, DEPTH, s[0], s[1] // DEPTH), bf16) for s in shapes]
    copies.append(((masters[4].shape[0], 128), bf16))
    halos = [((HALO, D), bf16), ((HALO, D), f32)]
    out_shape = [
        shape((rows, D), bf16),
        shape((rows, D), f32),
        *[shape(s.shape, f32) for i in range(3) for s in masters],
        *[shape(*c) for c in copies],
        *[shape(*h) for h in halos],
    ]
    five = [(s, bf16) for s in shapes] + [((r, 128), f32)]
    tall = ROWS
    scratch = [pltpu.VMEM(s.shape, f32) for s in state]
    scratch += [pltpu.VMEM((8, DEPTH) + s, bf16) for s in (*shapes, (r, 128))]
    scratch += [
        pltpu.VMEM((tall, D), bf16),
        pltpu.VMEM((tall, D), bf16),
        pltpu.VMEM((D + AUG, LANES), bf16),
        pltpu.VMEM((D, LANES), bf16),
        pltpu.VMEM((D, LANES), bf16),
        pltpu.VMEM((D, LANES), bf16),
        pltpu.VMEM((tall, D), bf16),
        pltpu.VMEM((HEADS, LANES), f32),
        pltpu.VMEM((tall, D), f32),
        pltpu.VMEM((8, LANES), jnp.int32),
        pltpu.VMEM((2 * (HALO + rows), D), bf16),
        pltpu.VMEM((1, 128), jnp.int32),
        pltpu.VMEM((1, 128), jnp.int32),
        pltpu.VMEM((128, 128), f32),
        pltpu.VMEM((128, D), f32),
        pltpu.VMEM((PLANE, 2, DEPTH) + shapes[0], bf16),
        pltpu.VMEM((PLANE, 2, DEPTH) + shapes[1], bf16),
        pltpu.VMEM((PLANE, 2, DEPTH, r, 128), f32),
        *[pltpu.VMEM(*h) for h in halos],
    ]
    for lead in ((PLANE, DEPTH), (4, DEPTH // 2), (2, DEPTH // 2), (3,)):
        scratch += [pltpu.VMEM(lead + s, t) for s, t in five]
    scratch += [pltpu.VMEM((DEPTH, s[0], s[1] // DEPTH), bf16) for s in shapes]
    scratch += [pltpu.VMEM(*c) for c in copies]
    scratch.append(pltpu.VMEM((8, DEPTH, r, 128), bf16))
    dma = pltpu.SemaphoreType.DMA
    scratch += [
        dma((15,)), dma((2,)), dma((5, 11)), dma((5, 11)), dma((6,)), dma((6,)),
        dma((5, 13)), dma((5, 13)), dma((5, 11)), dma((5, 11)), dma((22,)),
    ]
    return pl.pallas_call(
        whole_kernel,
        out_shape=out_shape,
        in_specs=[hbm] * 17 + [vmem] * 2,
        out_specs=[hbm] * 22 + [vmem] * 2,
        scratch_shapes=scratch,
        compiler_params=pltpu.CompilerParams(
            collective_id=0, has_side_effects=True, vmem_limit_bytes=63 * MIB
        ),
        name="whole",
    )(*state, tokens, cotangent, segment, keep)


LAST_PART = 496


def last_kernel(*refs):
    results, backs, ends = refs[:22], refs[22:24], refs[24:46]
    lows, (load_sems, store_sems) = refs[46:68], refs[68:]
    rows = results[0].shape[0]
    seq = lax.axis_index("seq")
    rim = pl.ds(rows - HALO, HALO)
    places = [(i, rim) for i in range(2)]
    places += [
        (i, pl.ds(first, LAST_PART))
        for i in range(2)
        for first in range(0, rows - HALO, LAST_PART)
    ]
    places += [(i, pl.ds(0, results[i].shape[0])) for i in range(2, 22)]
    loads = [
        pltpu.make_async_copy(results[i].at[at], lows[i].at[at], load_sems.at[n])
        for n, (i, at) in enumerate(places)
    ]
    stores = [
        pltpu.make_async_copy(lows[i].at[at], ends[i].at[at], store_sems.at[n])
        for n, (i, at) in enumerate(places)
    ]
    for load in loads:
        load.start()
    place = lax.broadcasted_iota(jnp.int32, (HALO, 1), 0)
    theirs = (place >= HALO - 8 * (seq + 1)) & (seq < lax.axis_size("seq") - 1)
    for n, (i, at) in enumerate(places):
        loads[n].wait()
        if n < 2:
            own = lows[i][rim, :].astype(f32)
            lows[i][rim, :] = jnp.where(theirs, backs[i][...].astype(f32), own).astype(lows[i].dtype)
        stores[n].start()
    for store in stores:
        store.wait()


def last(results, out_back, in_back):
    shape = jax.ShapeDtypeStruct
    vmem = pl.BlockSpec(memory_space=pltpu.VMEM)
    hbm = pl.BlockSpec(memory_space=pl.ANY)
    count = 22 + 2 * ((results[0].shape[0] - HALO) // LAST_PART)
    return pl.pallas_call(
        last_kernel,
        out_shape=[shape(a.shape, a.dtype) for a in results],
        in_specs=[hbm] * 22 + [vmem, vmem],
        out_specs=[hbm] * 22,
        scratch_shapes=[pltpu.VMEM(a.shape, a.dtype) for a in results]
        + [pltpu.SemaphoreType.DMA((count,)), pltpu.SemaphoreType.DMA((count,))],
        compiler_params=pltpu.CompilerParams(vmem_limit_bytes=60 * MIB),
        name="last",
    )(*results, out_back, in_back)


def on_device(
    tokens,
    cotangent,
    segment,
    keep_mask,
    attn_master,
    out_master,
    in_master,
    back_master,
    vec_master,
    attn_first,
    out_first,
    in_first,
    back_first,
    vec_first,
    attn_second,
    out_second,
    in_second,
    back_second,
    vec_second,
):
    seq = lax.axis_index("seq")
    seq_count = lax.axis_size("seq")
    both = ("batch", "seq")
    rows = tokens.shape[1]
    masters = (attn_master, out_master, in_master, back_master, vec_master)
    firsts = (attn_first, out_first, in_first, back_first, vec_first)
    seconds = (attn_second, out_second, in_second, back_second, vec_second)
    direct = seq_count == DEPTH and lax.axis_size("batch") == 2 * PLANE
    forward = [(i, i + 1) for i in range(seq_count - 1)]
    backward = [(i + 1, i) for i in range(seq_count - 1)]
    if direct:
        *results, out_back, grad_back = whole(
            masters, firsts, seconds, tokens, cotangent, segment, keep_mask
        )
        for i in range(17, 21):
            results[i] = results[i].reshape(-1, results[i].shape[-1])
        ends = last(results, out_back, grad_back)
        return (ends[0][None], ends[1][None], *ends[2:])
    low = [w.astype(bf16) for w in masters]
    low[4] = jnp.pad(low[4].T, ((0, 0), (0, 128 - low[4].shape[0])))
    attn_w, out_w, in_w, back_w, vec_t = (
        lax.all_gather(w, both, axis=0, tiled=True) for w in low
    )
    x_halo, e_halo, seg_halo, keep_halo = (
        lax.ppermute(a, "seq", forward)
        for a in (
            tokens[0, rows - HALO :], cotangent[0, rows - HALO :],
            segment[:, rows - 128 :], keep_mask[:, rows - 128 :],
        )
    )
    xs, es, xt, qt, kt, vt, c, lse = attn_forward(
        seq_count, tokens, cotangent, x_halo, e_halo, segment, keep_mask, seg_halo, keep_halo,
        attn_w, vec_t,
    )
    z, dh, dr, gwo, gw1, gw2, gvec, gb1 = feed(xs, c, es, out_w, in_w, back_w, vec_t)
    out, out_halo, grad_in, grad_in_halo, gwa, gbias = attn_backward(
        seq_count, xt, qt, kt, vt, lse, dr, dh, z, attn_w, out_w
    )
    grads = (gwa, gwo, gw1, gw2)
    grad_vec = jnp.concatenate(
        [gbias[:1, :D], gbias[:1, 2 * D :], gvec[2:8], gb1[0].reshape(FF // D, D)], 0
    )
    sums = [lax.psum_scatter(g.astype(f32), both, scatter_dimension=0, tiled=True) for g in grads]
    sums.append(lax.psum_scatter(grad_vec, both, scatter_dimension=1, tiled=True))
    new = [
        adam_update(masters[i], firsts[i], seconds[i], sums[i], learn_rates[i]) for i in range(5)
    ]

    def own_columns(i):
        whole = lax.all_gather(new[i][2].astype(bf16), both, axis=1 if i == 4 else 0, tiled=True)
        count = whole.shape[1] // seq_count
        return lax.dynamic_slice_in_dim(whole, seq * count, count, 1)

    results = [out, grad_in] + [new[i][part] for part in range(3) for i in range(5)]
    results += [own_columns(i) for i in range(5)]
    out_back = lax.ppermute(out_halo, "seq", backward)
    grad_back = lax.ppermute(grad_in_halo, "seq", backward)
    ends = last(results, out_back, grad_back)
    return (ends[0][None], ends[1][None], *ends[2:])


def solution(mesh):
    stream = P("batch", "seq", None)
    rows = P(("batch", "seq"), None)
    vector = P(None, ("batch", "seq"))
    five = (rows, rows, rows, rows, vector)
    return jax.shard_map(
        on_device,
        mesh=mesh,
        in_specs=(stream, stream, P("batch", "seq"), P("batch", "seq")) + five * 3,
        out_specs=(stream, stream) + five * 3 + (P(None, "seq"),) * 5,
        check_vma=False,
    )
```

```python
import functools
import math

import jax
import jax.numpy as jnp
from jax import lax
from jax.experimental import pallas as pl
from jax.experimental.pallas import tpu as pltpu
from jax.sharding import PartitionSpec as P

D = 512
HEADS = 8
HEAD_DIM = 64
FF = 2048
STEP = 10
PAIR = 255
SLOT = 256
HALO = 64
TILES = 4
TAIL = 64
PIECE = TAIL // TILES
TILE = 2 * SLOT + PIECE
ROWS = TILES * TILE
LANES = 8 * SLOT + 128
AUG = 16
MIB = 1 << 20

norm_epsilon = 1e-05
beta_first = 0.9
beta_second = 0.999
adam_epsilon = 1e-08
weight_decay = 0.01
learn_rates = (0.03, 0.2, 0.03, 0.02, 0.5)
big = 1e30

f32 = jnp.float32
bf16 = jnp.bfloat16


def dot(a, b, ca, cb):
    return lax.dot_general(a, b, (((ca,), (cb,)), ((), ())), preferred_element_type=f32)


def adam_update(master, first, second, gradient, rate):
    first_new = beta_first * first + (1.0 - beta_first) * gradient
    second_new = beta_second * second + (1.0 - beta_second) * gradient * gradient
    first_hat = first_new / (1.0 - beta_first**STEP)
    second_hat = second_new / (1.0 - beta_second**STEP)
    master_new = master - rate * (
        first_hat / (jnp.sqrt(second_hat) + adam_epsilon) + weight_decay * master
    )
    return (first_new, second_new, master_new)


def slot_row(j):
    return pl.multiple_of((j // 2) * TILE + (j % 2) * SLOT, 16)


def first_row(j, seq):
    return HALO + PAIR * j - 8 * seq


def staged(ref, start):
    base = pl.multiple_of((start // 16) * 16, 16)
    rest = start - base
    wide = ref[pl.ds(base, SLOT + 16), :].astype(f32)
    wide = jnp.where(rest >= 8, wide[8:], wide[:-8])
    shift = rest % 8
    groups = (SLOT + 8) // 8
    wide = wide.reshape(groups, 8, D)
    turned = pltpu.roll(wide, lax.rem(8 - shift, 8), 1)
    place = lax.broadcasted_iota(jnp.int32, (groups - 1, 8, D), 1)
    block = jnp.where(place < 8 - shift, turned[:-1], turned[1:]).reshape(SLOT, D)
    row = lax.broadcasted_iota(jnp.int32, (SLOT, D), 0)
    return jnp.where(row < PAIR, block, 0.0).astype(bf16)


def unstage(ref, start, block):
    base = pl.multiple_of((start // 8) * 8, 8)
    shift = start - base
    turned = pltpu.roll(block.reshape(SLOT // 8, 8, D), shift, 1)
    place = lax.broadcasted_iota(jnp.int32, (1, 8, D), 1)
    keep = ref[pl.ds(base, 8), :].reshape(1, 8, D)
    low = jnp.concatenate([keep, turned], 0)
    high = jnp.concatenate([turned, turned[-1:]], 0)
    place = lax.broadcasted_iota(jnp.int32, low.shape, 1)
    ref[pl.ds(base, SLOT + 8), :] = jnp.where(place < shift, low, high).reshape(SLOT + 8, D)


def stage_slot(ref, start, out_ref, row):
    base = pl.multiple_of((start // 16) * 16, 16)
    rest = start - base
    shift = rest % 8
    groups = (SLOT + 8) // 8
    place = lax.broadcasted_iota(jnp.int32, (groups - 1, 8, 128), 1)
    number = lax.broadcasted_iota(jnp.int32, (groups - 1, 8, 128), 0) * 8 + place
    for g in range(D // 128):
        cols = slice(g * 128, (g + 1) * 128)
        wide = ref[pl.ds(base, SLOT + 16), cols].astype(f32)
        wide = jnp.where(rest >= 8, wide[8:], wide[:-8]).reshape(groups, 8, 128)
        turned = pltpu.roll(wide, lax.rem(8 - shift, 8), 1)
        block = jnp.where(place < 8 - shift, turned[:-1], turned[1:])
        block = jnp.where(number < PAIR, block, 0.0)
        out_ref[pl.ds(row, SLOT), cols] = block.reshape(SLOT, 128).astype(bf16)


def unstage_slot(ref, start, column):
    base = pl.multiple_of((start // 8) * 8, 8)
    shift = start - base
    for g in range(D // 128):
        cols = slice(g * 128, (g + 1) * 128)
        turned = pltpu.roll(column(g).reshape(SLOT // 8, 8, 128), shift, 1)
        keep = ref[pl.ds(base, 8), cols].reshape(1, 8, 128)
        low = jnp.concatenate([keep, turned], 0)
        high = jnp.concatenate([turned, turned[-1:]], 0)
        place = lax.broadcasted_iota(jnp.int32, low.shape, 1)
        ref[pl.ds(base, SLOT + 8), cols] = jnp.where(place < shift, low, high).reshape(SLOT + 8, 128)


def tail_rows(ref, count, is_last):
    kept = ref[HALO + 2048 - count : HALO + 2048, :].astype(f32)
    if count < TAIL:
        kept = jnp.concatenate([kept, jnp.zeros((TAIL - count, D), f32)], 0)
    return jnp.where(is_last, kept, 0.0).astype(bf16)


def tag_rows(tag, pair):
    width = tag.shape[1]
    number = tag // 2 - 2 * pair
    kept = tag % 2
    row = lax.broadcasted_iota(jnp.int32, (AUG, width), 0)
    match = row == number
    query = jnp.where(match, 1.0, 0.0).astype(bf16)
    key = jnp.where(match & (kept == 1), 0.0, -big)
    key = jnp.where(row < 4, key, 0.0).astype(bf16)
    return query, key


def attn_forward_kernel(
    seq_count, tok_ref, cot_ref, tok_halo, cot_halo, seg_ref, keep_ref, seg_halo, keep_halo,
    w_ref, vec_ref,
    xs_ref, es_ref, xt_ref, qt_ref, kt_ref, vt_ref, c_ref, lse_ref,
    wt_ref, x_ref, e_ref, tag_ref, sems,
):
    seq = lax.axis_index("seq")
    is_last = seq == seq_count - 1
    rows = tok_ref.shape[1]
    loads = []
    for i, (whole, halo, ext) in enumerate(((tok_ref, tok_halo, x_ref), (cot_ref, cot_halo, e_ref))):
        loads.append(pltpu.make_async_copy(whole.at[0], ext.at[pl.ds(HALO, rows)], sems.at[2 * i]))
        loads.append(pltpu.make_async_copy(halo, ext.at[pl.ds(0, HALO)], sems.at[2 * i + 1]))
    for load in loads:
        load.start()
    for part in range(3):
        wt_ref[part * D : (part + 1) * D, :] = w_ref[:, part * D : (part + 1) * D].T
    tag_ref[...] = jnp.zeros_like(tag_ref)
    edge = seg_halo[...] * 2 + keep_halo[...]
    tag_ref[:, :HALO] = jnp.broadcast_to(edge[:, 128 - HALO :], (8, HALO))
    tag_ref[:, HALO : HALO + rows] = jnp.broadcast_to(seg_ref[...] * 2 + keep_ref[...], (8, rows))
    query_bias = vec_ref[:, 0:1].astype(f32)
    value_bias = vec_ref[:, 1:2].astype(f32)
    for load in loads:
        load.wait()

    def block(xb, tag, pair, lane, width):
        lanes = pl.ds(lane, width)
        xt_ref[:D, lanes] = xb.T
        q = dot(wt_ref[:D, :], xb, 1, 1) + query_bias
        q = (q.astype(bf16).astype(f32) * HEAD_DIM**-0.5).astype(bf16)
        k = dot(wt_ref[D : 2 * D, :], xb, 1, 1).astype(bf16)
        v = (dot(wt_ref[2 * D :, :], xb, 1, 1) + value_bias).astype(bf16)
        query_tag, key_tag = tag_rows(tag, pair)
        vt_ref[:, lanes] = v
        context = []
        for h in range(HEADS):
            rows = slice(h * HEAD_DIM, (h + 1) * HEAD_DIM)
            qh = jnp.concatenate([q[rows], query_tag], 0)
            kh = jnp.concatenate([k[rows], key_tag], 0)
            qt_ref[h, :, lanes] = qh
            kt_ref[h, :, lanes] = kh
            s = dot(kh, qh, 0, 0)
            top = jnp.max(s, axis=0, keepdims=True)
            ex = jnp.exp(s - top)
            total = jnp.sum(ex, axis=0, keepdims=True)
            lse_ref[h : h + 1, lanes] = top + jnp.log(total)
            a = (ex * (1.0 / total)).astype(bf16)
            context.append(dot(v[rows], a, 1, 0))
        return jnp.concatenate(context, 0).astype(bf16).T

    def one(j, carry):
        start = first_row(j, seq)
        row = slot_row(j)
        xb = staged(x_ref, start)
        xs_ref[pl.ds(row, SLOT), :] = xb
        es_ref[pl.ds(row, SLOT), :] = staged(e_ref, start)
        wide = tag_ref[:, pl.ds(pl.multiple_of(j * SLOT, 128), SLOT + 128)]
        width = SLOT + 128
        tag = pltpu.roll(wide, width - (start - j * SLOT), 1)[:1, :SLOT]
        c_ref[pl.ds(row, SLOT), :] = block(
            xb, tag, 8 * seq + j, pl.multiple_of(j * SLOT, 128), SLOT
        )
        return carry

    lax.fori_loop(0, 8, one, 0)
    count = 8 * seq_count
    xt_ref[:, 8 * SLOT :] = jnp.zeros((D + AUG, 128), bf16)
    xb = tail_rows(x_ref, count, is_last)
    eb = tail_rows(e_ref, count, is_last)
    tag = tag_ref[:1, 2048:2176]
    tag = pltpu.roll(tag_ref[:, 2048:2176], 128 - (64 - count), 1)[:1, :TAIL] if count < 64 else tag[:, :TAIL]
    place = lax.broadcasted_iota(jnp.int32, (1, TAIL), 1)
    tag = jnp.where(place < count, tag, (2 * 8 * seq_count + 3) * 2)
    cb = block(xb, tag, 8 * seq_count, 8 * SLOT, TAIL)
    for t in range(TILES):
        rows = slice(t * PIECE, (t + 1) * PIECE)
        at = slice(t * TILE + 2 * SLOT, (t + 1) * TILE)
        xs_ref[at, :] = xb[rows]
        es_ref[at, :] = eb[rows]
        c_ref[at, :] = cb[rows]
    ones = lax.broadcasted_iota(jnp.int32, (AUG, LANES), 0) == 0
    xt_ref[D:, :] = jnp.where(ones, 1.0, 0.0).astype(bf16)


def attn_forward(seq_count, tokens, cotangent, *others):
    shape = jax.ShapeDtypeStruct
    vmem = pl.BlockSpec(memory_space=pltpu.VMEM)
    hbm = pl.BlockSpec(memory_space=pl.ANY)
    return pl.pallas_call(
        functools.partial(attn_forward_kernel, seq_count),
        out_shape=(
            shape((ROWS, D), bf16),
            shape((ROWS, D), bf16),
            shape((D + AUG, LANES), bf16),
            shape((HEADS, HEAD_DIM + AUG, LANES), bf16),
            shape((HEADS, HEAD_DIM + AUG, LANES), bf16),
            shape((D, LANES), bf16),
            shape((ROWS, D), bf16),
            shape((HEADS, LANES), f32),
        ),
        in_specs=[hbm, hbm] + [vmem] * len(others),
        out_specs=[vmem] * 8,
        scratch_shapes=[
            pltpu.VMEM((3 * D, D), bf16),
            pltpu.VMEM((HALO + tokens.shape[1], D), bf16),
            pltpu.VMEM((HALO + tokens.shape[1], D), bf16),
            pltpu.VMEM((8, LANES), jnp.int32),
            pltpu.SemaphoreType.DMA((4,)),
        ],
        compiler_params=pltpu.CompilerParams(vmem_limit_bytes=56 * MIB),
        name="attn_forward",
    )(tokens, cotangent, *others)


def feed_kernel(
    xs_ref, c_ref, es_ref, wo_ref, w1_ref, w2_ref, vect_ref,
    z_ref, dh_ref, dr_ref, gwo_ref, gw1_ref, gw2_ref, gvec_ref, gb1_ref,
    u_ref, g_ref, awo_ref, aw1_ref, aw2_ref, vec_ref,
):
    step = pl.program_id(0)

    @pl.when(step == 0)
    def _():
        awo_ref[...] = jnp.zeros_like(awo_ref)
        aw1_ref[...] = jnp.zeros_like(aw1_ref)
        aw2_ref[...] = jnp.zeros_like(aw2_ref)
        gvec_ref[...] = jnp.zeros_like(gvec_ref)
        gb1_ref[...] = jnp.zeros_like(gb1_ref)
        vec_ref[...] = vect_ref[...].astype(f32).T

    def mean(v):
        return jnp.mean(v, axis=-1, keepdims=True)

    def row_sum(v):
        return jnp.sum(v, axis=0, keepdims=True)

    bo, b2, g1, c1, g2, c2 = (vec_ref[i : i + 1, :] for i in range(2, 8))
    h1 = xs_ref[...].astype(f32) + (dot(c_ref[...], wo_ref[...], 1, 0) + bo)
    mid = h1 - mean(h1)
    inv1 = lax.rsqrt(mean(mid * mid) + norm_epsilon)
    n1 = mid * inv1
    y = n1 * g1 + c1
    yb = y.astype(bf16)
    chunk = D
    f = None
    for k in range(FF // chunk):
        cols = slice(k * chunk, (k + 1) * chunk)
        u = dot(yb, w1_ref[:, cols], 1, 0) + vec_ref[8 + k : 9 + k, :]
        cdf = 0.5 * (1.0 + lax.erf(u * 0.7071067811865476))
        gk = (u * cdf).astype(bf16)
        u_ref[:, cols] = cdf + u * jnp.exp(u * u * -0.5) * 0.3989422804014327
        g_ref[:, cols] = gk
        part = dot(gk, w2_ref[cols, :], 1, 0)
        f = part if f is None else f + part
    h2 = y + (f + b2)
    mid2 = h2 - mean(h2)
    inv2 = lax.rsqrt(mean(mid2 * mid2) + norm_epsilon)
    n2 = mid2 * inv2
    z_ref[...] = (n2 * g2 + c2).astype(bf16)
    e = es_ref[...].astype(f32)
    gvec_ref[7:8, :] += row_sum(e)
    gvec_ref[6:7, :] += row_sum(e * n2)
    eg = e * g2
    dh2 = (eg - mean(eg) - n2 * mean(eg * n2)) * inv2
    df = dh2.astype(bf16)
    gvec_ref[3:4, :] += row_sum(df.astype(f32))
    dft = df.T
    ybt = yb.T
    dy = dh2
    for k in range(FF // chunk):
        cols = slice(k * chunk, (k + 1) * chunk)
        aw2_ref[:, cols] += dot(dft, g_ref[:, cols], 1, 0)
        dg = dot(df, w2_ref[cols, :], 1, 1)
        du = (dg * u_ref[:, cols]).astype(bf16)
        gb1_ref[:1, cols] += row_sum(du.astype(f32))
        aw1_ref[:, cols] += dot(ybt, du, 1, 0)
        dy = dy + dot(du, w1_ref[:, cols], 1, 1)
    gvec_ref[5:6, :] += row_sum(dy)
    gvec_ref[4:5, :] += row_sum(dy * n1)
    eg = dy * g1
    dh1 = (eg - mean(eg) - n1 * mean(eg * n1)) * inv1
    dh_ref[...] = dh1
    dr = dh1.astype(bf16)
    dr_ref[...] = dr
    gvec_ref[2:3, :] += row_sum(dr.astype(f32))
    awo_ref[...] += dot(c_ref[...].T, dr, 1, 0)

    @pl.when(step == TILES - 1)
    def _():
        gwo_ref[...] = awo_ref[...].astype(bf16)
        gw1_ref[...] = aw1_ref[...].astype(bf16)
        for k in range(FF // chunk):
            cols = slice(k * chunk, (k + 1) * chunk)
            gw2_ref[cols, :] = aw2_ref[:, cols].astype(bf16).T


def feed(xs, c, es, wo, w1, w2, vec_t):
    shape = jax.ShapeDtypeStruct
    tile = pl.BlockSpec((TILE, D), lambda i: (i, 0))

    def whole(*dims):
        return pl.BlockSpec(dims, lambda i: (0,) * len(dims), pipeline_mode=pl.Buffered(1))

    return pl.pallas_call(
        feed_kernel,
        grid=(TILES,),
        out_shape=(
            shape((ROWS, D), bf16),
            shape((ROWS, D), f32),
            shape((ROWS, D), bf16),
            shape((D, D), bf16),
            shape((D, FF), bf16),
            shape((FF, D), bf16),
            shape((8, D), f32),
            shape((8, FF), f32),
        ),
        in_specs=[tile, tile, tile, whole(D, D), whole(D, FF), whole(FF, D), whole(D, 128)],
        out_specs=[tile, tile, tile, whole(D, D), whole(D, FF), whole(FF, D), whole(8, D), whole(8, FF)],
        scratch_shapes=[
            pltpu.VMEM((TILE, FF), f32),
            pltpu.VMEM((TILE, FF), bf16),
            pltpu.VMEM((D, D), f32),
            pltpu.VMEM((D, FF), f32),
            pltpu.VMEM((D, FF), f32),
            pltpu.VMEM((128, D), f32),
        ],
        compiler_params=pltpu.CompilerParams(vmem_limit_bytes=60 * MIB),
        name="feed",
    )(xs, c, es, wo, w1, w2, vec_t)


def attn_backward_kernel(
    seq_count, xt_ref, qt_ref, kt_ref, vt_ref, lse_ref, dr_ref, dh_ref, z_ref, w_ref, wo_ref,
    out_ref, out_halo_ref, in_ref, in_halo_ref, gwa_ref, gbias_ref,
    dpt_ref, ext_ref,
):
    seq = lax.axis_index("seq")
    is_last = seq == seq_count - 1

    def block(dr, lane, width):
        lanes = pl.ds(lane, width)
        dct = dot(wo_ref[...], dr, 1, 1).astype(bf16)
        for h in range(HEADS):
            rows = slice(h * HEAD_DIM, (h + 1) * HEAD_DIM)
            qh = qt_ref[h, :, lanes]
            kh = kt_ref[h, :, lanes]
            vh = vt_ref[rows, lanes]
            dch = dct[rows]
            a = jnp.exp(dot(kh, qh, 0, 0) - lse_ref[h : h + 1, lanes])
            da = dot(vh, dch, 0, 0)
            ada = a * da
            ds = (ada - a * jnp.sum(ada, axis=0, keepdims=True)).astype(bf16)
            dv = dot(dch, a.astype(bf16), 1, 1)
            dk = dot(qh[:HEAD_DIM], ds, 1, 1)
            dq = dot(kh[:HEAD_DIM], ds, 1, 0) * HEAD_DIM**-0.5
            dpt_ref[rows, lanes] = dq.astype(bf16)
            dpt_ref[slice(D + h * HEAD_DIM, D + (h + 1) * HEAD_DIM), lanes] = dk.astype(bf16)
            dpt_ref[slice(2 * D + h * HEAD_DIM, 2 * D + (h + 1) * HEAD_DIM), lanes] = dv.astype(bf16)
        return dot(w_ref[...], dpt_ref[:, lanes], 1, 0).T

    dpt_ref[:, 8 * SLOT :] = jnp.zeros((3 * D, 128), bf16)

    def one(j, carry):
        row = slot_row(j)
        grad = block(dr_ref[pl.ds(row, SLOT), :], pl.multiple_of(j * SLOT, 128), SLOT)
        unstage(ext_ref, first_row(j, seq), grad + dh_ref[pl.ds(row, SLOT), :])
        return carry

    lax.fori_loop(0, 8, one, 0)
    count = 8 * seq_count

    def tail_of(ref):
        return jnp.concatenate(
            [ref[t * TILE + 2 * SLOT : (t + 1) * TILE, :] for t in range(TILES)], 0
        )

    grad = block(tail_of(dr_ref), 8 * SLOT, TAIL) + tail_of(dh_ref)

    @pl.when(is_last)
    def _():
        ext_ref[HALO + 2048 - count : HALO + 2048, :] = grad[:count]

    in_halo_ref[...] = ext_ref[:HALO, :]
    in_ref[...] = ext_ref[HALO : HALO + 2048, :]

    def two(j, carry):
        unstage(ext_ref, first_row(j, seq), z_ref[pl.ds(slot_row(j), SLOT), :].astype(f32))
        return carry

    lax.fori_loop(0, 8, two, 0)
    tail = tail_of(z_ref).astype(f32)

    @pl.when(is_last)
    def _():
        ext_ref[HALO + 2048 - count : HALO + 2048, :] = tail[:count]

    out_halo_ref[...] = ext_ref[:HALO, :].astype(bf16)
    out_ref[...] = ext_ref[HALO : HALO + 2048, :].astype(bf16)
    for part in range(3):
        cols = slice(part * D, (part + 1) * D)
        g = dot(xt_ref[...], dpt_ref[cols, :], 1, 1)
        gwa_ref[:, cols] = g[:D].astype(bf16)
        gbias_ref[:, cols] = g[D : D + 8]


def attn_backward(seq_count, *operands):
    shape = jax.ShapeDtypeStruct
    return pl.pallas_call(
        functools.partial(attn_backward_kernel, seq_count),
        out_shape=(
            shape((2048, D), bf16),
            shape((HALO, D), bf16),
            shape((2048, D), f32),
            shape((HALO, D), f32),
            shape((D, 3 * D), bf16),
            shape((8, 3 * D), f32),
        ),
        in_specs=[pl.BlockSpec(memory_space=pltpu.VMEM)] * len(operands),
        out_specs=[pl.BlockSpec(memory_space=pltpu.VMEM)] * 6,
        scratch_shapes=[
            pltpu.VMEM((3 * D, LANES), bf16),
            pltpu.VMEM((HALO + 2048 + 16, D), f32),
        ],
        compiler_params=pltpu.CompilerParams(vmem_limit_bytes=60 * MIB),
        name="attn_backward",
    )(*operands)


MESH = pl.DeviceIdType.MESH
PLANE = 4
DEPTH = 4


class Place:
    def __init__(self):
        self.batch = lax.axis_index("batch")
        self.z = lax.axis_index("seq")
        self.core = self.batch % 2
        self.plane = self.batch // 2

    def plane_at(self, k):
        x = (self.plane % 2 + k % 2) % 2
        y = (self.plane // 2 + k // 2) % 2
        return y * 2 + x

    def in_plane(self, k, other=0):
        core = self.core if other == 0 else 1 - self.core
        return {"batch": self.plane_at(k) * 2 + core, "seq": self.z}

    def depth_at(self, k):
        return (self.z + k) % DEPTH

    def in_depth(self, k):
        return {"batch": self.batch, "seq": self.depth_at(k)}

    def sibling(self):
        return {"batch": self.plane * 2 + 1 - self.core, "seq": self.z}

    def greet(self):
        barrier = pltpu.get_barrier_semaphore()
        for k in range(1, 4):
            pl.semaphore_signal(barrier, inc=1, device_id=self.in_plane(k), device_id_type=MESH)
            pl.semaphore_signal(barrier, inc=1, device_id=self.in_depth(k), device_id_type=MESH)
            pl.semaphore_signal(barrier, inc=1, device_id=self.in_plane(k, 1), device_id_type=MESH)
        pl.semaphore_signal(barrier, inc=1, device_id=self.sibling(), device_id_type=MESH)
        pl.semaphore_wait(barrier, 10)


def remote(src, dst, send, recv, device):
    return pltpu.make_async_remote_copy(
        src_ref=src, dst_ref=dst, send_sem=send, recv_sem=recv, device_id=device, device_id_type=MESH
    )


LOW, HIGH = pl.ds(0, DEPTH // 2), pl.ds(DEPTH // 2, DEPTH // 2)


class Gather:
    def __init__(self, place, whole, send, recv, parts=None):
        self.place, self.whole, self.send, self.recv, self.parts = place, whole, send, recv, parts

    def block(self, k):
        return self.whole.at[self.place.plane_at(k) * 2 + self.place.core]

    def copy(self, n, source, target, device):
        return remote(source, target, self.send.at[n], self.recv.at[n], device)

    def depth(self, k):
        at = self.place
        here = self.whole.at[at.batch, at.z]
        source = here if self.parts is None else self.parts.at[at.depth_at(k)]
        return self.copy(k - 1, source, here, at.in_depth(k))

    def plane(self, k):
        return self.copy(2 + k, self.block(0), self.block(0), self.place.in_plane(k))

    def across(self, k):
        half = self.block(k).at[LOW if k == 1 else HIGH]
        return self.copy(4 + k, half, half, self.place.in_plane(3 - k))

    def core(self, k):
        return self.copy(7 + k, self.block(k), self.block(k), self.place.sibling())

    def first(self):
        for k in range(1, 4):
            self.depth(k).start()

    def second(self):
        for k in range(1, 4):
            self.depth(k).wait_recv()
        for k in (1, 2):
            self.plane(k).start()
        self.core(0).start()

    def third(self):
        for k in (1, 2):
            self.plane(k).wait_recv()
            self.across(k).start()
            self.core(k).start()

    def fourth(self):
        for k in (1, 2):
            self.across(k).wait_recv()
        self.core(3).start()

    def finish(self):
        for k in range(4):
            self.core(k).wait_recv()
        for k in range(1, 4):
            self.depth(k).wait_send()
        for k in (1, 2):
            self.plane(k).wait_send()
            self.across(k).wait_send()
        for k in range(4):
            self.core(k).wait_send()


class Spread(Gather):
    def step(self, k, other):
        device = self.place.in_plane(k, other) if k else self.place.sibling()
        return self.copy(2 * k + other + 3 if k else 3, self.block(0), self.block(0), device)

    def steps(self):
        return [self.step(0, 0)] + [self.step(k, other) for k in range(1, 4) for other in range(2)]

    def second(self):
        for k in range(1, 4):
            self.depth(k).wait_recv()
        for copy in self.steps():
            copy.start()

    def finish(self):
        for copy in self.steps():
            copy.wait_recv()
        for k in range(1, 4):
            self.depth(k).wait_send()
        for copy in self.steps():
            copy.wait_send()


class Scatter:
    def __init__(self, place, grad, twin, near, far, along, send, recv):
        self.place, self.grad, self.twin = place, grad, twin
        self.near, self.far, self.along, self.send, self.recv = near, far, along, send, recv
        shape = grad.shape
        if len(shape) == 4:
            self.at = lambda p, c: grad.at[p * 2 + c]
        else:
            self.at = lambda p, c: grad.at[p, c]

    def block(self, k):
        return self.at(self.place.plane_at(k), self.place.core)

    def copy(self, n, source, target, device):
        return remote(source, target, self.send.at[n], self.recv.at[n], device)

    def core(self, p):
        source = self.at(p, 1 - self.place.core)
        return self.copy(p, source, self.twin.at[p], self.place.sibling())

    def plane(self, n):
        k, half = ((1, LOW), (3, LOW), (2, HIGH), (3, HIGH))[n]
        target = self.near.at[n]
        return self.copy(4 + n, self.block(k).at[half], target, self.place.in_plane(1 + n // 2))

    def across(self, n):
        k, half = ((2, LOW), (1, HIGH))[n]
        return self.copy(8 + n, self.block(k).at[half], self.far.at[n], self.place.in_plane(2 - n))

    def depth(self, k):
        source = self.block(0).at[self.place.depth_at(k)]
        return self.copy(9 + k, source, self.along.at[k - 1], self.place.in_depth(k))

    def first(self):
        for p in range(PLANE):
            self.core(p).start()

    def second(self):
        for p in range(PLANE):
            self.core(p).wait_recv()
        own = self.place.core

        def one(p, carry):
            mine = self.at(p, own)
            mine[...] = (mine[...].astype(f32) + self.twin[p].astype(f32)).astype(mine.dtype)
            return carry

        lax.fori_loop(0, PLANE, one, 0)
        for n in range(4):
            self.plane(n).start()

    def third(self):
        for n in range(4):
            self.plane(n).wait_recv()
        for n, (k, base) in enumerate(((2, 0), (1, 2))):
            mine = self.block(k)

            def one(q, carry):
                total = mine[base + q].astype(f32) + self.near[2 * n + 1, q].astype(f32)
                mine[base + q] = total.astype(mine.dtype)
                return carry

            lax.fori_loop(0, 2, one, 0)
            self.across(n).start()

    def fourth(self):
        for n in range(2):
            self.across(n).wait_recv()
        mine = self.block(0)

        def one(i, carry):
            n, q = i // 2, i % 2
            total = mine[i].astype(f32) + self.near[2 * n, q].astype(f32) + self.far[n, q].astype(f32)
            mine[i] = total.astype(mine.dtype)
            return carry

        lax.fori_loop(0, DEPTH, one, 0)
        for k in range(1, 4):
            self.depth(k).start()

    def total(self):
        for k in range(1, 4):
            self.depth(k).wait_recv()
        total = self.block(0)[self.place.z].astype(f32)
        for k in range(3):
            total = total + self.along[k].astype(f32)
        return total

    def finish(self):
        for p in range(PLANE):
            self.core(p).wait_send()
        for n in range(4):
            self.plane(n).wait_send()
        for n in range(2):
            self.across(n).wait_send()
        for k in range(1, 4):
            self.depth(k).wait_send()


def turned(ref, value):
    ref[...] = jnp.zeros_like(ref)
    ref[: value.shape[0], : value.shape[1]] = value
    return ref[...].T


def heads_of(block, h):
    return block[h * HEAD_DIM : (h + 1) * HEAD_DIM]


def only_head(block, h):
    zero = jnp.zeros((HEAD_DIM, block.shape[1]), block.dtype)
    mine = heads_of(block, h)
    return jnp.concatenate([mine, zero] if h % 2 == 0 else [zero, mine], 0)


def pair_of(block, h):
    at = h // 2 * 2 * HEAD_DIM
    return block[:, at : at + 2 * HEAD_DIM]


def mask_parts(tag, pair):
    query, key = tag_rows(tag, pair)
    width = tag.shape[1]
    zero = jnp.zeros((128 - AUG, width), bf16)
    return jnp.concatenate([key, zero], 0).T, jnp.concatenate([query, zero], 0)


class Slots:
    def __init__(self, tag_ref, seq, seq_count):
        self.tag_ref, self.seq, self.count = tag_ref, seq, 8 * seq_count
        self.last_pair = 8 * seq_count

    def tag(self, j):
        wide = self.tag_ref[:, pl.ds(pl.multiple_of(j * SLOT, 128), SLOT + 128)]
        offset = HALO - 8 * self.seq - j
        return pltpu.roll(wide, SLOT + 128 - offset, 1)[:1, :SLOT]

    def tail_tag(self):
        tag = self.tag_ref[:, 2048:2176]
        if self.count < TAIL:
            tag = pltpu.roll(tag, 128 - (TAIL - self.count), 1)
        place = lax.broadcasted_iota(jnp.int32, (1, TAIL), 1)
        return jnp.where(place < self.count, tag[:1, :TAIL], 2 * (2 * self.last_pair + 3))

    def tail(self, ref):
        return jnp.concatenate(
            [ref[t * TILE + 2 * SLOT : (t + 1) * TILE, :] for t in range(TILES)], 0
        )

    def set_tail(self, ref, value):
        for t in range(TILES):
            ref[t * TILE + 2 * SLOT : (t + 1) * TILE, :] = value[t * PIECE : (t + 1) * PIECE]


def halves_of(width):
    step = min(width, 128)
    return [slice(i, i + step) for i in range(0, width, step)]


def pair_stack(values, *rest):
    zero = jnp.zeros_like(values[0])
    left = jnp.concatenate([values[0], zero, *rest], 0)
    right = jnp.concatenate([zero, values[1], *rest], 0)
    return left, right


def forward_block(
    xb, tag, pair, lanes, put, wt_ref, biases, xt_ref, qt_ref, kt_ref, vt_ref, lse_ref, s_ref, a_ref,
    kn_ref, ct_ref,
):
    width = xb.shape[0]
    parts = ((kt_ref, None), (qt_ref, biases[0]), (vt_ref, biases[1]))

    def project(n):
        at = (1, 0, 2)[n]
        p = dot(wt_ref[at * D : (at + 1) * D, :], xb, 1, 1)
        s_ref[2 * n, :, :width] = p[:SLOT]
        s_ref[2 * n + 1, :, :width] = p[SLOT:]

    def keep(n):
        out_ref, bias = parts[n]
        for h in range(HEADS):
            at = h % 4 * HEAD_DIM
            value = s_ref[2 * n + h // 4, at : at + HEAD_DIM, :width]
            rows = slice(h * HEAD_DIM, (h + 1) * HEAD_DIM)
            if bias is not None:
                value = value + bias[rows]
            value = value.astype(bf16)
            if n == 1:
                value = (value.astype(f32) * HEAD_DIM**-0.5).astype(bf16)
            out_ref[rows, lanes] = value

    masks = []

    def turn():
        kn_ref[:width, :] = kt_ref[:, lanes].T
        masks.extend(mask_parts(tag, pair))

    def rows_of(h):
        return slice(h * HEAD_DIM, (h + 1) * HEAD_DIM)

    def scores(p):
        key_mask, query_mask = masks
        left = jnp.concatenate([kn_ref[:width, p * 128 : (p + 1) * 128], key_mask], 1)
        both = pair_stack([qt_ref[rows_of(2 * p + i), lanes] for i in range(2)], query_mask)
        if width % 128 == 0:
            s = dot(left, jnp.concatenate(both, 1), 1, 0)
            s_ref[2 * p], s_ref[2 * p + 1] = s[:, :width], s[:, width:]
        else:
            for i in range(2):
                s_ref[2 * p + i, :width, :width] = dot(left, both[i], 1, 0)

    def weigh(p):
        for h in (2 * p, 2 * p + 1):
            for half in halves_of(width):
                s = s_ref[h, :width, half]
                top = jnp.max(s, axis=0, keepdims=True)
                ex = jnp.exp(s - top)
                total = jnp.sum(ex, axis=0, keepdims=True)
                a_ref[h, :width, half] = (ex * (1.0 / total)).astype(bf16)
                at = pl.ds(pl.multiple_of(lanes.start + half.start, 128), half.stop - half.start)
                lse_ref[h : h + 1, at] = top + jnp.log(total)

    def collect(p):
        for h in (2 * p, 2 * p + 1):
            c = dot(vt_ref[rows_of(h), lanes], a_ref[h, :width, :width], 1, 0)
            ct_ref[rows_of(h), :width] = c.astype(bf16)

    def close():
        xt_ref[:D, lanes] = xb.T
        put(ct_ref[:, :width].T)

    call = functools.partial
    ahead = [
        call(project, 0), call(project, 1), call(keep, 0), turn, call(project, 2), call(keep, 1),
        call(keep, 2),
    ]
    return ahead, (scores, weigh, collect), [close]


def together(*blocks):
    for phases in zip(*(block[0] for block in blocks)):
        for phase in phases:
            phase()
    count = len(blocks)

    def stage(n):
        return lambda i: blocks[i % count][1][n](i // count)

    skewed(HEADS // 2 * count, stage(0), stage(1), stage(2))
    for phases in zip(*(block[2] for block in blocks)):
        for phase in phases:
            phase()


def skewed(count, *stages):
    for i in range(count + len(stages) - 1):
        for n, stage in enumerate(stages):
            if 0 <= i - n < count:
                stage(i - n)


def backward_block(
    dr, c, tag, pair, lanes, wo, qt_ref, kt_ref, vt_ref, lse_ref, dpt_ref, s_ref, da_ref, a_ref,
    ds_ref, kn_ref, vn_ref, dct_ref, ct_ref,
):
    width = dr.shape[0]
    masks = []

    def turn():
        kn_ref[:width, :] = kt_ref[:, lanes].T
        vn_ref[:width, :] = vt_ref[:, lanes].T
        masks.extend(mask_parts(tag, pair))

    def spread():
        dct_ref[:, :width] = dot(wo, dr, 1, 1).astype(bf16)
        ct_ref[:, :width] = c.T

    def rows_of(h):
        return slice(h * HEAD_DIM, (h + 1) * HEAD_DIM)

    def scores(p):
        at = slice(p * 128, (p + 1) * 128)
        key_mask, query_mask = masks
        left = jnp.concatenate([kn_ref[:width, at], key_mask], 1)
        both = pair_stack([qt_ref[rows_of(2 * p + i), lanes] for i in range(2)], query_mask)
        both_d = pair_stack([dct_ref[rows_of(2 * p + i), :width] for i in range(2)])
        right = vn_ref[:width, at]
        if width % 128 == 0:
            s = dot(left, jnp.concatenate(both, 1), 1, 0)
            u = 2 * (p % 2)
            s_ref[u], s_ref[u + 1] = s[:, :width], s[:, width:]
            da = dot(right, jnp.concatenate(both_d, 1), 1, 0)
            da_ref[u], da_ref[u + 1] = da[:, :width], da[:, width:]
        else:
            for i in range(2):
                s_ref[2 * (p % 2) + i, :width, :width] = dot(left, both[i], 1, 0)
                da_ref[2 * (p % 2) + i, :width, :width] = dot(right, both_d[i], 1, 0)

    def weigh(p):
        for h in (2 * p, 2 * p + 1):
            rows = rows_of(h)
            for half in halves_of(width):
                at = pl.ds(pl.multiple_of(lanes.start + half.start, 128), half.stop - half.start)
                product = ct_ref[rows, half].astype(f32) * dct_ref[rows, half].astype(f32)
                delta = jnp.sum(product, axis=0, keepdims=True)
                lse = lse_ref[h : h + 1, at]
                for first in range(0, width, 64):
                    keys = slice(first, first + 64)
                    a = jnp.exp(s_ref[h % 4, keys, half] - lse)
                    a_ref[h % 4, keys, half] = a.astype(bf16)
                    ds_ref[h % 4, keys, half] = (a * (da_ref[h % 4, keys, half] - delta)).astype(bf16)

    def collect(p):
        for h in (2 * p, 2 * p + 1):
            rows = rows_of(h)
            ds = ds_ref[h % 4, :width, :width]
            dv = dot(dct_ref[rows, :width], a_ref[h % 4, :width, :width], 1, 1)
            dk = dot(qt_ref[rows, lanes], ds, 1, 1)
            dq = dot(kt_ref[rows, lanes], ds, 1, 0) * HEAD_DIM**-0.5
            dpt_ref[rows, lanes] = dq.astype(bf16)
            dpt_ref[slice(D + rows.start, D + rows.stop), lanes] = dk.astype(bf16)
            dpt_ref[slice(2 * D + rows.start, 2 * D + rows.stop), lanes] = dv.astype(bf16)

    return [turn, spread], (scores, weigh, collect), []


def mean(v):
    return jnp.mean(v, axis=-1, keepdims=True)


def row_sum(v):
    return jnp.sum(v, axis=0, keepdims=True)


def flat(value):
    return value.reshape(-1, value.shape[-1])


BLOCK = 48
MAIN = 2 * SLOT


def eights(v):
    return jnp.sum(v.reshape(-1, 8, v.shape[-1]), axis=0)


def feed_tile(
    t, xs_ref, c_ref, es_ref, wo_ref, w1_ref, w2_ref, vec_ref, dh_ref, gvec_ref,
    acc_ref, other_ref, n1_ref, inv_ref, yb_ref, df_ref, u_ref, g_ref, back_ready, tails,
    awo_ref, aw1_ref, aw2_ref,
):
    first = pl.multiple_of(t * TILE, 16)
    rows = pl.ds(first, TILE)
    piece = pl.ds(pl.multiple_of(t * PIECE, 16), PIECE)
    g_tail, du_tail, df_tail, yb_tail = tails
    bo, b2, g1, c1, g2, c2 = (vec_ref[i : i + 1, :] for i in range(2, 8))
    per = FF // D
    blocks = [slice(i, i + BLOCK) for i in range(0, TILE, BLOCK)]

    def at(block):
        return pl.ds(pl.multiple_of(first + block.start, 16), BLOCK)

    acc_ref[...] = dot(c_ref[rows, :], flat(wo_ref[...]), 1, 0)
    for block in blocks:
        h1 = xs_ref[at(block), :].astype(f32) + (acc_ref[block, :] + bo)
        mid = h1 - mean(h1)
        inv1 = lax.rsqrt(mean(mid * mid) + norm_epsilon)
        n1 = mid * inv1
        n1_ref[block, :] = n1
        inv_ref[block, :] = jnp.broadcast_to(inv1, (BLOCK, 128))
        yb_ref[block, :] = (n1 * g1 + c1).astype(bf16)

    pads = (acc_ref, other_ref)

    def w2_part(k):
        return flat(w2_ref[8 // per * k : 8 // per * (k + 1)])

    def w1_part(k):
        return flat(w1_ref[:, :, :, k * D : (k + 1) * D])

    def up(k):
        pads[k % 2][...] = dot(yb_ref[...], w1_part(k), 1, 0)

    def activate(k):
        cols = slice(k * D, (k + 1) * D)
        b1 = vec_ref[8 + k : 9 + k, :]
        for block in blocks:
            u = pads[k % 2][block, :] + b1
            cdf = 0.5 + 0.5 * lax.erf(u * 0.7071067811865476)
            g_ref[k * TILE + block.start : k * TILE + block.stop, :] = (u * cdf).astype(bf16)
            bell = jnp.exp2(u * u * (-0.5 * math.log2(math.e)) - 0.5 * math.log2(2.0 * math.pi))
            u_ref[block, cols] = cdf + u * bell

    def down(k):
        part = dot(g_ref[k * TILE : (k + 1) * TILE, :], w2_part(k), 1, 0)
        if k == 0:
            dh_ref[rows, :] = part
        else:
            dh_ref[rows, :] += part

    up(0)
    up(1)
    activate(0)
    pl.when(t == 0)(back_ready)
    for k in range(per):
        if k + 2 < per:
            up(k + 2)
        down(k)
        if k + 1 < per:
            activate(k + 1)
    sums = [jnp.zeros((8, D), f32)] * 3
    for block in blocks:
        h2 = (n1_ref[block, :] * g1 + c1) + (dh_ref[at(block), :] + b2)
        mid2 = h2 - mean(h2)
        inv2 = lax.rsqrt(mean(mid2 * mid2) + norm_epsilon)
        n2 = mid2 * inv2
        xs_ref[at(block), :] = (n2 * g2 + c2).astype(bf16)
        e = es_ref[at(block), :].astype(f32)
        en = e * n2
        eg = e * g2
        dh2 = (eg - mean(eg) - n2 * mean(eg * n2)) * inv2
        dh_ref[at(block), :] = dh2
        df = dh2.astype(bf16)
        df_ref[block, :] = df
        sums = [sums[0] + eights(e), sums[1] + eights(en), sums[2] + eights(df.astype(f32))]
    for i, value in zip((7, 6, 3), sums):
        gvec_ref[i : i + 1, :] += row_sum(value)
    dft = df_ref[:MAIN, :].T
    ybt = yb_ref[:MAIN, :].T
    df_tail[piece, :] = df_ref[MAIN:, :]
    yb_tail[piece, :] = yb_ref[MAIN:, :]

    def up_back(k):
        pads[k % 2][...] = dot(df_ref[...], w2_part(k), 1, 1)

    def activate_back(k):
        cols = slice(k * D, (k + 1) * D)
        here = slice(k * TILE, k * TILE + MAIN)
        at_tail = pl.ds(pl.multiple_of(k * TAIL + t * PIECE, 16), PIECE)
        aw2_ref[:, cols] += dot(dft, g_ref[here, :], 1, 0)
        g_tail[at_tail, :] = g_ref[here.stop : here.stop + PIECE, :]
        total = jnp.zeros((8, D), f32)
        for block in blocks:
            du = (pads[k % 2][block, :] * u_ref[block, cols]).astype(bf16)
            g_ref[k * TILE + block.start : k * TILE + block.stop, :] = du
            total = total + eights(du.astype(f32))
        gvec_ref[8 + k : 9 + k, :] += row_sum(total)

    def down_back(k):
        cols = slice(k * D, (k + 1) * D)
        here = slice(k * TILE, k * TILE + MAIN)
        at_tail = pl.ds(pl.multiple_of(k * TAIL + t * PIECE, 16), PIECE)
        aw1_ref[:, cols] += dot(ybt, g_ref[here, :], 1, 0)
        du_tail[at_tail, :] = g_ref[here.stop : here.stop + PIECE, :]
        part = dot(g_ref[k * TILE : (k + 1) * TILE, :], w1_part(k), 1, 1)
        dh_ref[rows, :] += part

    skewed(per, up_back, activate_back, down_back)
    sums = [jnp.zeros((8, D), f32)] * 3
    for block in blocks:
        dy = dh_ref[at(block), :]
        n1 = n1_ref[block, :]
        eg = dy * g1
        dh1 = (eg - mean(eg) - n1 * mean(eg * n1)) * inv_ref[block, :1]
        dh_ref[at(block), :] = dh1
        dr = dh1.astype(bf16)
        es_ref[at(block), :] = dr
        sums = [sums[0] + eights(dy), sums[1] + eights(dy * n1), sums[2] + eights(dr.astype(f32))]
    for i, value in zip((5, 4, 2), sums):
        gvec_ref[i : i + 1, :] += row_sum(value)
    main = pl.ds(first, MAIN)
    awo_ref[...] += dot(c_ref[main, :].T, es_ref[main, :], 1, 0)


def whole_kernel(*refs):
    refs = list(refs)

    def take(count):
        taken = refs[:count]
        del refs[:count]
        return taken

    state_in = take(15)
    tok_ref, cot_ref, seg_ref, keep_ref = take(4)
    out_ref, in_ref = take(2)
    state_out = take(5)
    copy_out = take(5)
    out_back, in_back = take(2)
    packed = take(5)
    firsts, seconds, masters = ([p.at[n] for p in packed] for n in range(3))
    state = masters + firsts + seconds
    weights = take(5)
    wa_ref, wo_ref, w1_ref, w2_ref, wv_ref = weights
    xs_ref, es_ref, xt_ref, qt_ref, kt_ref, vt_ref, c_ref, lse_ref, dh_ref, tag_ref = take(10)
    ext_ref, seg_halo, keep_halo = take(3)
    square, gvec_ref, gwa_ref, gwo_ref, grad_vec, halo_out, halo_in = take(7)
    twins, nears, fars, alongs = take(5), take(5), take(5), take(5)
    parts, copies, whole_vec = take(4), take(5), take(1)[0]
    (
        state_sems, load_sems, gather_send, gather_recv, edge_send, edge_recv,
        sum_send, sum_recv, copy_send, copy_recv, store_sems,
    ) = refs
    place = Place()
    seq, seq_count = place.z, DEPTH
    is_last = seq == seq_count - 1
    slots = Slots(tag_ref, seq, seq_count)
    rows = tok_ref.shape[1]
    ext_x, ext_e = ext_ref.at[pl.ds(0, HALO + rows)], ext_ref.at[pl.ds(HALO + rows, HALO + rows)]

    loads = [pltpu.make_async_copy(state_in[i], state[i], state_sems.at[i]) for i in range(15)]
    for load in loads:
        load.start()
    big_loads = [
        pltpu.make_async_copy(src.at[0], dst.at[pl.ds(HALO, rows)], load_sems.at[i])
        for i, (src, dst) in enumerate(((tok_ref, ext_x), (cot_ref, ext_e)))
    ]
    for load in big_loads:
        load.start()
    place.greet()
    edge = [
        remote(src, dst, edge_send.at[i], edge_recv.at[i], place.in_depth(1))
        for i, (src, dst) in enumerate((
            (tok_ref.at[0, pl.ds(rows - HALO, HALO)], ext_x.at[pl.ds(0, HALO)]),
            (cot_ref.at[0, pl.ds(rows - HALO, HALO)], ext_e.at[pl.ds(0, HALO)]),
            (seg_ref.at[:, pl.ds(rows - 128, 128)], seg_halo),
            (keep_ref.at[:, pl.ds(rows - 128, 128)], keep_halo),
        ))
    ]
    gathers = [Gather(place, weights[i], gather_send.at[i], gather_recv.at[i]) for i in range(5)]

    def put(i):
        shard = turned(square, masters[4][...])[: masters[4].shape[1]] if i == 4 else masters[i][...]
        weights[i][place.batch, place.z] = shard.astype(bf16)

    for i in (0, 4):
        loads[i].wait()
        put(i)
        gathers[i].first()
    for copy in edge:
        copy.start()
    for i in (1, 2, 3):
        loads[i].wait()
        put(i)
    gathers[1].first()
    for load in big_loads:
        load.wait()
    for copy in edge:
        copy.wait()
    tag_ref[...] = jnp.zeros_like(tag_ref)
    rim = seg_halo[...] * 2 + keep_halo[...]
    tag_ref[:, :HALO] = jnp.broadcast_to(rim[:, 128 - HALO :], (8, HALO))
    tag_ref[:, HALO : HALO + rows] = jnp.broadcast_to(seg_ref[...] * 2 + keep_ref[...], (8, rows))

    def stage_one(j, carry):
        start = first_row(j, seq)
        row = slot_row(j)
        stage_slot(ext_x, start, xs_ref, row)
        stage_slot(ext_e, start, es_ref, row)
        return carry

    gathers[0].second()
    gathers[2].first()
    gathers[4].second()
    gathers[1].second()
    lax.fori_loop(0, 8, stage_one, 0)
    slots.set_tail(xs_ref, tail_rows(ext_x, slots.count, is_last))
    slots.set_tail(es_ref, tail_rows(ext_e, slots.count, is_last))
    gathers[0].third()
    gathers[4].third()
    xt_ref[:, 8 * SLOT :] = jnp.zeros((D + AUG, 128), bf16)
    ones = lax.broadcasted_iota(jnp.int32, (AUG, LANES), 0) == 0
    xt_ref[D:, :] = jnp.where(ones, 1.0, 0.0).astype(bf16)
    gathers[2].second()
    gathers[3].first()
    gathers[0].fourth()
    gathers[4].fourth()
    gathers[1].third()
    gathers[0].finish()
    gathers[4].finish()
    gathers[3].second()

    def forward(wt_ref, s_ref, a_ref, kn_ref, ct_ref):
        for part in range(3):
            wt_ref[part * D : (part + 1) * D, :] = flat(
                wa_ref[:, :, :, part * D : (part + 1) * D]
            ).T
        vec_t = flat(wv_ref[...])
        biases = (vec_t[:, 0:1].astype(f32), vec_t[:, 1:2].astype(f32))

        def block(n, xb, tag, pair, lanes, put):
            return forward_block(
                xb, tag, pair, lanes, put, wt_ref, biases, xt_ref, qt_ref, kt_ref, vt_ref, lse_ref,
                s_ref.at[n], a_ref.at[n], kn_ref.at[n], ct_ref.at[n],
            )

        def two(i, carry):
            for step, event in (
                (1, gathers[1].fourth), (1, gathers[2].third), (3, gathers[2].fourth),
                (3, gathers[3].third),
            ):
                pl.when(i == step)(event)

            def slot(n):
                j = 2 * i + n
                at = pl.ds(slot_row(j), SLOT)
                lanes = pl.ds(pl.multiple_of(j * SLOT, 128), SLOT)

                def put(value):
                    c_ref[at, :] = value

                return block(n, xs_ref[at, :], slots.tag(j), 8 * seq + j, lanes, put)

            together(slot(0), slot(1))
            return carry

        lax.fori_loop(0, 4, two, 0)
        together(
            block(
                0, slots.tail(xs_ref), slots.tail_tag(), slots.last_pair, pl.ds(8 * SLOT, TAIL),
                functools.partial(slots.set_tail, c_ref),
            )
        )

    pl.run_scoped(
        forward,
        pltpu.VMEM((3 * D, D), bf16),
        pltpu.VMEM((2, HEADS, SLOT, SLOT), f32),
        pltpu.VMEM((2, HEADS, SLOT, SLOT), bf16),
        pltpu.VMEM((2, SLOT, D), bf16),
        pltpu.VMEM((2, D, SLOT), bf16),
    )
    for i in (1, 2):
        gathers[i].finish()
    gathers[3].fourth()

    def back_ready():
        gathers[3].finish()

    grads = [gwa_ref, gwo_ref, w1_ref, w2_ref, grad_vec]
    scatters = [
        Scatter(
            place, grads[i], twins[i], nears[i], fars[i], alongs[i], sum_send.at[i], sum_recv.at[i]
        )
        for i in range(5)
    ]

    def feed_all(
        vec_ref, acc_ref, other_ref, n1_ref, inv_ref, u_ref, awo_ref, aw1_ref, aw2_ref
    ):
        used = 0
        views = []
        for count in (4 * TILE, TILE, TILE, TAIL, TAIL, 4 * TAIL, 4 * TAIL):
            views.append(ext_ref.at[pl.ds(used, count)])
            used += count
        g_ref, yb_ref, df_ref, yb_tail, df_tail, g_tail, du_tail = views
        for ref in (awo_ref, aw1_ref, aw2_ref, gvec_ref):
            ref[...] = jnp.zeros_like(ref)
        vec_ref[...] = flat(wv_ref[...]).astype(f32).T[:16]

        def one(t, carry):
            feed_tile(
                t, xs_ref, c_ref, es_ref, wo_ref, w1_ref, w2_ref, vec_ref, dh_ref, gvec_ref, acc_ref,
                other_ref, n1_ref, inv_ref, yb_ref, df_ref, u_ref, g_ref, back_ready,
                (g_tail, du_tail, df_tail, yb_tail),
                awo_ref, aw1_ref, aw2_ref,
            )
            return carry

        lax.fori_loop(0, TILES, one, 0)
        for k in range(FF // D):
            cols = slice(k * D, (k + 1) * D)
            at = slice(k * TAIL, (k + 1) * TAIL)
            aw2_ref[:, cols] += dot(df_tail[...].T, g_tail[at, :], 1, 0)
            aw1_ref[:, cols] += dot(yb_tail[...].T, du_tail[at, :], 1, 0)
        awo_ref[...] += dot(slots.tail(c_ref).T, slots.tail(es_ref), 1, 0)
        def convert(i, carry):
            value = aw2_ref[:, pl.ds(pl.multiple_of(i * 128, 128), 128)].astype(bf16).T
            w2_ref[i // 2, pl.ds(i % 2 * 2, 2)] = value.reshape(2, -1, D)
            return carry

        def convert_rows(i, carry):
            value = aw1_ref[pl.ds(pl.multiple_of(i * 64, 64), 64), :].astype(bf16)
            w1_ref[i] = value.reshape(DEPTH, -1, FF)
            gwo_ref[i // 2, i % 2] = (
                awo_ref[pl.ds(pl.multiple_of(i * 64, 64), 64), :].astype(bf16).reshape(DEPTH, -1, D)
            )
            return carry

        lax.fori_loop(0, FF // 128, convert, 0)
        scatters[3].first()
        lax.fori_loop(0, 8, convert_rows, 0)
        scatters[2].first()
        scatters[1].first()

    pl.run_scoped(
        feed_all,
        pltpu.VMEM((16, D), f32),
        pltpu.VMEM((TILE, D), f32),
        pltpu.VMEM((TILE, D), f32),
        pltpu.VMEM((TILE, D), f32),
        pltpu.VMEM((TILE, 128), f32),
        pltpu.VMEM((TILE, FF), f32),
        pltpu.VMEM((D, D), f32),
        pltpu.VMEM((D, FF), f32),
        pltpu.VMEM((D, FF), f32),
    )
    for load in loads[5:]:
        load.wait()
    copy_gathers = [
        kind(place, copies[i], copy_send.at[i], copy_recv.at[i], parts[i])
        for i, kind in enumerate((Spread, Spread, Gather, Gather))
    ]
    copy_gathers.append(Spread(place, whole_vec, copy_send.at[4], copy_recv.at[4]))
    stores = []

    def store(src, dst):
        stores.append(pltpu.make_async_copy(src, dst, store_sems.at[len(stores)]))
        stores[-1].start()

    def update(i):
        total = scatters[i].total()
        if i == 4:
            square[...] = jnp.zeros_like(square)
            square[: total.shape[0], :] = total
            here, cols = masters[4].shape
            total = square[...].T[:here, :cols]
        new = adam_update(masters[i][...], firsts[i][...], seconds[i][...], total, learn_rates[i])
        firsts[i][...], seconds[i][...], masters[i][...] = new
        if i == 4:
            shard = turned(square, new[2])[: new[2].shape[1]].astype(bf16)
            whole_vec[place.batch, place.z] = shard
        else:
            low = new[2].astype(bf16)
            width = low.shape[1] // DEPTH
            for q in range(DEPTH):
                parts[i][q] = low[:, q * width : (q + 1) * width]
            copies[i][place.batch, place.z] = parts[i][place.z]
        copy_gathers[i].first()

    def backward(dpt_ref):
        dpt_ref[:, 8 * SLOT :] = jnp.zeros((3 * D, 128), bf16)

        def attention(s_ref, da_ref, a_ref, ds_ref, kn_ref, vn_ref, dct_ref, ct_ref):
            wo = flat(wo_ref[...])
            pads = (s_ref, da_ref, a_ref, ds_ref, kn_ref, vn_ref, dct_ref, ct_ref)

            def block(n, dr, c, tag, pair, lanes):
                return backward_block(
                    dr, c, tag, pair, lanes, wo, qt_ref, kt_ref, vt_ref, lse_ref, dpt_ref,
                    *(pad.at[n] for pad in pads),
                )

            def two(i, carry):
                for step, event in (
                    (1, scatters[3].second), (1, scatters[2].second), (3, scatters[3].third),
                    (3, scatters[1].second),
                ):
                    pl.when(i == step)(event)

                def slot(n):
                    j = 2 * i + n
                    at = pl.ds(slot_row(j), SLOT)
                    lanes = pl.ds(pl.multiple_of(j * SLOT, 128), SLOT)
                    return block(n, es_ref[at, :], c_ref[at, :], slots.tag(j), 8 * seq + j, lanes)

                together(slot(0), slot(1))
                return carry

            lax.fori_loop(0, 4, two, 0)
            together(
                block(
                    0, slots.tail(es_ref), slots.tail(c_ref), slots.tail_tag(), slots.last_pair,
                    pl.ds(8 * SLOT, TAIL),
                )
            )

        pl.run_scoped(
            attention,
            *[pltpu.VMEM((2, 4, SLOT, SLOT), f32)] * 2,
            *[pltpu.VMEM((2, 4, SLOT, SLOT), bf16)] * 2,
            *[pltpu.VMEM((2, SLOT, D), bf16)] * 2,
            *[pltpu.VMEM((2, D, SLOT), bf16)] * 2,
        )
        pl.run_scoped(
            functools.partial(finish, dpt_ref),
            pltpu.VMEM((HALO + rows + 16, D), f32),
            pltpu.VMEM((4, SLOT, SLOT), f32),
        )

    def finish(dpt_ref, ext_ref, s_ref):
        low_ref = ext_e
        for part in range(3):
            cols = slice(part * D, (part + 1) * D)
            g = dot(xt_ref[...], dpt_ref[cols, :], 1, 1)
            gwa_ref[:, :, :, :, cols] = g[:D].astype(bf16).reshape(PLANE, 2, DEPTH, -1, D)
            if part != 1:
                gvec_ref[part // 2 : part // 2 + 1, :] = g[D : D + 1]
        grad_vec[...] = gvec_ref[...].T.reshape(grad_vec.shape)
        scatters[0].first()
        scatters[4].first()
        scatters[2].third()

        def output_one(j, carry):
            at = pl.ds(slot_row(j), SLOT)
            unstage_slot(
                ext_ref, first_row(j, seq),
                lambda g: xs_ref[at, g * 128 : (g + 1) * 128].astype(f32),
            )
            return carry

        def close(value):
            @pl.when(is_last)
            def _():
                ext_ref[HALO + rows - slots.count : HALO + rows, :] = value[: slots.count]

        lax.fori_loop(0, 8, output_one, 0)
        close(slots.tail(xs_ref).astype(f32))
        scatters[0].second()
        scatters[4].second()
        scatters[3].fourth()
        scatters[1].third()
        low_ref[...] = ext_ref[: HALO + rows, :].astype(bf16)
        halo_out[...] = low_ref[:HALO, :]
        edge_back[0].start()
        store(low_ref.at[pl.ds(HALO, rows)], out_ref)
        wa = flat(wa_ref[...])

        def input_block(lanes):
            return dot(wa, dpt_ref[:, lanes], 1, 0).T

        def input_two(i, carry):
            for step, event in (
                (1, scatters[2].fourth), (2, scatters[1].fourth), (2, functools.partial(update, 3)),
                (3, scatters[0].third), (3, scatters[4].third),
            ):
                pl.when(i == step)(event)

            def product(n):
                lanes = pl.ds(pl.multiple_of((2 * i + n) * SLOT, 128), SLOT)
                grad = dot(wa, dpt_ref[:, lanes], 1, 0)
                s_ref[2 * n], s_ref[2 * n + 1] = grad[:SLOT], grad[SLOT:]

            def put_back(n):
                j = 2 * i + n
                at = pl.ds(slot_row(j), SLOT)

                def column(g):
                    part = s_ref[2 * n + g // 2, g % 2 * 128 : g % 2 * 128 + 128, :].T
                    return part + dh_ref[at, g * 128 : (g + 1) * 128]

                unstage_slot(ext_ref, first_row(j, seq), column)

            skewed(2, product, put_back)
            return carry

        lax.fori_loop(0, 4, input_two, 0)
        close(input_block(pl.ds(8 * SLOT, TAIL)) + slots.tail(dh_ref))
        halo_in[...] = ext_ref[:HALO, :]
        edge_back[1].start()
        store(ext_ref.at[pl.ds(HALO, rows)], in_ref)
        update(2)
        copy_gathers[3].second()
        scatters[0].fourth()
        scatters[4].fourth()
        update(1)
        copy_gathers[2].second()
        update(4)
        update(0)
        copy_gathers[3].third()
        copy_gathers[2].third()
        copy_gathers[1].second()
        copy_gathers[4].second()
        copy_gathers[0].second()
        copy_gathers[3].fourth()
        copy_gathers[2].fourth()
        for i in range(5):
            store(packed[i], state_out[i])
        for i in (3, 2, 1, 4, 0):
            copy_gathers[i].finish()
            scatters[i].finish()
        here = masters[4].shape[0]
        mine = jnp.concatenate([whole_vec[seq * 2 + q // 4, q % 4] for q in range(8)], 0)
        copies[4][...] = mine.astype(f32).T[:here].astype(bf16)
        for i in range(5):
            store(copies[i], copy_out[i])
        for copy in stores:
            copy.wait()
        for copy in edge_back:
            copy.wait()

    edge_back = [
        remote(halo_out, out_back, edge_send.at[4], edge_recv.at[4], place.in_depth(3)),
        remote(halo_in, in_back, edge_send.at[5], edge_recv.at[5], place.in_depth(3)),
    ]
    pl.run_scoped(backward, pltpu.VMEM((3 * D, LANES), bf16))


def whole(masters, firsts, seconds, tokens, cotangent, segment, keep):
    shape = jax.ShapeDtypeStruct
    vmem = pl.BlockSpec(memory_space=pltpu.VMEM)
    hbm = pl.BlockSpec(memory_space=pl.ANY)
    state = (*masters, *firsts, *seconds)
    rows = tokens.shape[1]
    r = masters[0].shape[0]
    shapes = ((r, 3 * D), (r, D), (r, FF), (4 * r, D))
    copies = [((8, DEPTH, s[0], s[1] // DEPTH), bf16) for s in shapes]
    copies.append(((masters[4].shape[0], 128), bf16))
    halos = [((HALO, D), bf16), ((HALO, D), f32)]
    out_shape = [
        shape((rows, D), bf16),
        shape((rows, D), f32),
        *[shape((3,) + s.shape, f32) for s in masters],
        *[shape(*c) for c in copies],
        *[shape(*h) for h in halos],
    ]
    five = [(s, bf16) for s in shapes] + [((r, 128), f32)]
    tall = ROWS
    scratch = [pltpu.VMEM((3,) + s.shape, f32) for s in masters]
    scratch += [pltpu.VMEM((8, DEPTH) + s, bf16) for s in (*shapes, (r, 128))]
    scratch += [
        pltpu.VMEM((tall, D), bf16),
        pltpu.VMEM((tall, D), bf16),
        pltpu.VMEM((D + AUG, LANES), bf16),
        pltpu.VMEM((D, LANES), bf16),
        pltpu.VMEM((D, LANES), bf16),
        pltpu.VMEM((D, LANES), bf16),
        pltpu.VMEM((tall, D), bf16),
        pltpu.VMEM((HEADS, LANES), f32),
        pltpu.VMEM((tall, D), f32),
        pltpu.VMEM((8, LANES), jnp.int32),
        pltpu.VMEM((2 * (HALO + rows), D), bf16),
        pltpu.VMEM((1, 128), jnp.int32),
        pltpu.VMEM((1, 128), jnp.int32),
        pltpu.VMEM((128, 128), f32),
        pltpu.VMEM((128, D), f32),
        pltpu.VMEM((PLANE, 2, DEPTH) + shapes[0], bf16),
        pltpu.VMEM((PLANE, 2, DEPTH) + shapes[1], bf16),
        pltpu.VMEM((PLANE, 2, DEPTH, r, 128), f32),
        *[pltpu.VMEM(*h) for h in halos],
    ]
    for lead in ((PLANE, DEPTH), (4, DEPTH // 2), (2, DEPTH // 2), (3,)):
        scratch += [pltpu.VMEM(lead + s, t) for s, t in five]
    scratch += [pltpu.VMEM((DEPTH, s[0], s[1] // DEPTH), bf16) for s in shapes]
    scratch += [pltpu.VMEM(*c) for c in copies]
    scratch.append(pltpu.VMEM((8, DEPTH, r, 128), bf16))
    dma = pltpu.SemaphoreType.DMA
    scratch += [
        dma((15,)), dma((2,)), dma((5, 11)), dma((5, 11)), dma((6,)), dma((6,)),
        dma((5, 13)), dma((5, 13)), dma((5, 11)), dma((5, 11)), dma((12,)),
    ]
    return pl.pallas_call(
        whole_kernel,
        out_shape=out_shape,
        in_specs=[hbm] * 17 + [vmem] * 2,
        out_specs=[hbm] * 12 + [vmem] * 2,
        scratch_shapes=scratch,
        compiler_params=pltpu.CompilerParams(
            collective_id=0, has_side_effects=True, vmem_limit_bytes=63 * MIB
        ),
        name="whole",
    )(*state, tokens, cotangent, segment, keep)


LAST_PART = 496


def last_kernel(*refs):
    results, backs, ends = refs[:12], refs[12:14], refs[14:36]
    lows, (load_sems, store_sems) = refs[36:48], refs[48:]
    rows = results[0].shape[0]
    seq = lax.axis_index("seq")
    rim = pl.ds(rows - HALO, HALO)
    places = [(i, rim) for i in range(2)]
    places += [
        (i, pl.ds(first, LAST_PART))
        for i in (1, 0)
        for first in range(0, rows - HALO, LAST_PART)
    ]
    places += [(i, pl.ds(0, results[i].shape[0])) for i in range(2, 12)]
    loads = [
        pltpu.make_async_copy(results[i].at[at], lows[i].at[at], load_sems.at[n])
        for n, (i, at) in enumerate(places)
    ]
    for load in loads:
        load.start()
    place = lax.broadcasted_iota(jnp.int32, (HALO, 1), 0)
    theirs = (place >= HALO - 8 * (seq + 1)) & (seq < lax.axis_size("seq") - 1)
    stores = []
    for n, (i, at) in enumerate(places):
        loads[n].wait()
        if n < 2:
            own = lows[i][rim, :].astype(f32)
            lows[i][rim, :] = jnp.where(theirs, backs[i][...].astype(f32), own).astype(lows[i].dtype)
        if i < 2:
            pairs = [(lows[i].at[at], ends[i].at[at])]
        elif i < 7:
            pairs = [(lows[i].at[part], ends[2 + 5 * part + i - 2]) for part in range(3)]
        else:
            pairs = [(lows[i], ends[10 + i])]
        for source, target in pairs:
            stores.append(pltpu.make_async_copy(source, target, store_sems.at[len(stores)]))
            stores[-1].start()
    for store in stores:
        store.wait()


def last(results, out_back, in_back):
    shape = jax.ShapeDtypeStruct
    vmem = pl.BlockSpec(memory_space=pltpu.VMEM)
    hbm = pl.BlockSpec(memory_space=pl.ANY)
    loads = 12 + 2 * ((results[0].shape[0] - HALO) // LAST_PART)
    ends = list(results[:2])
    for part in range(3):
        ends += [shape(a.shape[1:], a.dtype) for a in results[2:7]]
    ends += results[7:]
    return pl.pallas_call(
        last_kernel,
        out_shape=[shape(a.shape, a.dtype) for a in ends],
        in_specs=[hbm] * 12 + [vmem, vmem],
        out_specs=[hbm] * 22,
        scratch_shapes=[pltpu.VMEM(a.shape, a.dtype) for a in results]
        + [pltpu.SemaphoreType.DMA((loads,)), pltpu.SemaphoreType.DMA((loads + 10,))],
        compiler_params=pltpu.CompilerParams(vmem_limit_bytes=60 * MIB),
        name="last",
    )(*results, out_back, in_back)


def on_device(
    tokens,
    cotangent,
    segment,
    keep_mask,
    attn_master,
    out_master,
    in_master,
    back_master,
    vec_master,
    attn_first,
    out_first,
    in_first,
    back_first,
    vec_first,
    attn_second,
    out_second,
    in_second,
    back_second,
    vec_second,
):
    seq = lax.axis_index("seq")
    seq_count = lax.axis_size("seq")
    both = ("batch", "seq")
    rows = tokens.shape[1]
    masters = (attn_master, out_master, in_master, back_master, vec_master)
    firsts = (attn_first, out_first, in_first, back_first, vec_first)
    seconds = (attn_second, out_second, in_second, back_second, vec_second)
    direct = seq_count == DEPTH and lax.axis_size("batch") == 2 * PLANE
    forward = [(i, i + 1) for i in range(seq_count - 1)]
    backward = [(i + 1, i) for i in range(seq_count - 1)]
    if direct:
        *results, out_back, grad_back = whole(
            masters, firsts, seconds, tokens, cotangent, segment, keep_mask
        )
        for i in range(7, 11):
            results[i] = results[i].reshape(-1, results[i].shape[-1])
        ends = last(results, out_back, grad_back)
        return (ends[0][None], ends[1][None], *ends[2:])
    low = [w.astype(bf16) for w in masters]
    low[4] = jnp.pad(low[4].T, ((0, 0), (0, 128 - low[4].shape[0])))
    attn_w, out_w, in_w, back_w, vec_t = (
        lax.all_gather(w, both, axis=0, tiled=True) for w in low
    )
    x_halo, e_halo, seg_halo, keep_halo = (
        lax.ppermute(a, "seq", forward)
        for a in (
            tokens[0, rows - HALO :], cotangent[0, rows - HALO :],
            segment[:, rows - 128 :], keep_mask[:, rows - 128 :],
        )
    )
    xs, es, xt, qt, kt, vt, c, lse = attn_forward(
        seq_count, tokens, cotangent, x_halo, e_halo, segment, keep_mask, seg_halo, keep_halo,
        attn_w, vec_t,
    )
    z, dh, dr, gwo, gw1, gw2, gvec, gb1 = feed(xs, c, es, out_w, in_w, back_w, vec_t)
    out, out_halo, grad_in, grad_in_halo, gwa, gbias = attn_backward(
        seq_count, xt, qt, kt, vt, lse, dr, dh, z, attn_w, out_w
    )
    grads = (gwa, gwo, gw1, gw2)
    grad_vec = jnp.concatenate(
        [gbias[:1, :D], gbias[:1, 2 * D :], gvec[2:8], gb1[0].reshape(FF // D, D)], 0
    )
    sums = [lax.psum_scatter(g.astype(f32), both, scatter_dimension=0, tiled=True) for g in grads]
    sums.append(lax.psum_scatter(grad_vec, both, scatter_dimension=1, tiled=True))
    new = [
        adam_update(masters[i], firsts[i], seconds[i], sums[i], learn_rates[i]) for i in range(5)
    ]

    def own_columns(i):
        whole = lax.all_gather(new[i][2].astype(bf16), both, axis=1 if i == 4 else 0, tiled=True)
        count = whole.shape[1] // seq_count
        return lax.dynamic_slice_in_dim(whole, seq * count, count, 1)

    results = [out, grad_in] + [jnp.stack(new[i]) for i in range(5)]
    results += [own_columns(i) for i in range(5)]
    out_back = lax.ppermute(out_halo, "seq", backward)
    grad_back = lax.ppermute(grad_in_halo, "seq", backward)
    ends = last(results, out_back, grad_back)
    return (ends[0][None], ends[1][None], *ends[2:])


def solution(mesh):
    stream = P("batch", "seq", None)
    rows = P(("batch", "seq"), None)
    vector = P(None, ("batch", "seq"))
    five = (rows, rows, rows, rows, vector)
    return jax.shard_map(
        on_device,
        mesh=mesh,
        in_specs=(stream, stream, P("batch", "seq"), P("batch", "seq")) + five * 3,
        out_specs=(stream, stream) + five * 3 + (P(None, "seq"),) * 5,
        check_vma=False,
    )
```

```python
import functools
import math

import jax
import jax.numpy as jnp
from jax import lax
from jax.experimental import pallas as pl
from jax.experimental.pallas import tpu as pltpu
from jax.sharding import PartitionSpec as P

D = 512
HEADS = 8
HEAD_DIM = 64
FF = 2048
STEP = 10
PAIR = 255
SLOT = 256
HALO = 64
TILES = 4
TAIL = 64
PIECE = TAIL // TILES
TILE = 2 * SLOT + PIECE
ROWS = TILES * TILE
LANES = 8 * SLOT + 128
AUG = 16
MIB = 1 << 20

norm_epsilon = 1e-05
beta_first = 0.9
beta_second = 0.999
adam_epsilon = 1e-08
weight_decay = 0.01
learn_rates = (0.03, 0.2, 0.03, 0.02, 0.5)
big = 1e30

f32 = jnp.float32
bf16 = jnp.bfloat16


def dot(a, b, ca, cb):
    return lax.dot_general(a, b, (((ca,), (cb,)), ((), ())), preferred_element_type=f32)


def adam_update(master, first, second, gradient, rate):
    first_new = beta_first * first + (1.0 - beta_first) * gradient
    second_new = beta_second * second + (1.0 - beta_second) * gradient * gradient
    first_hat = first_new / (1.0 - beta_first**STEP)
    second_hat = second_new / (1.0 - beta_second**STEP)
    master_new = master - rate * (
        first_hat / (jnp.sqrt(second_hat) + adam_epsilon) + weight_decay * master
    )
    return (first_new, second_new, master_new)


def slot_row(j):
    if isinstance(j, int):
        return (j // 2) * TILE + (j % 2) * SLOT
    return pl.multiple_of((j // 2) * TILE + (j % 2) * SLOT, 16)


def first_row(j, seq):
    return HALO + PAIR * j - 8 * seq


def staged(ref, start):
    base = pl.multiple_of((start // 16) * 16, 16)
    rest = start - base
    wide = ref[pl.ds(base, SLOT + 16), :].astype(f32)
    wide = jnp.where(rest >= 8, wide[8:], wide[:-8])
    shift = rest % 8
    groups = (SLOT + 8) // 8
    wide = wide.reshape(groups, 8, D)
    turned = pltpu.roll(wide, lax.rem(8 - shift, 8), 1)
    place = lax.broadcasted_iota(jnp.int32, (groups - 1, 8, D), 1)
    block = jnp.where(place < 8 - shift, turned[:-1], turned[1:]).reshape(SLOT, D)
    row = lax.broadcasted_iota(jnp.int32, (SLOT, D), 0)
    return jnp.where(row < PAIR, block, 0.0).astype(bf16)


def unstage(ref, start, block):
    base = pl.multiple_of((start // 8) * 8, 8)
    shift = start - base
    turned = pltpu.roll(block.reshape(SLOT // 8, 8, D), shift, 1)
    place = lax.broadcasted_iota(jnp.int32, (1, 8, D), 1)
    keep = ref[pl.ds(base, 8), :].reshape(1, 8, D)
    low = jnp.concatenate([keep, turned], 0)
    high = jnp.concatenate([turned, turned[-1:]], 0)
    place = lax.broadcasted_iota(jnp.int32, low.shape, 1)
    ref[pl.ds(base, SLOT + 8), :] = jnp.where(place < shift, low, high).reshape(SLOT + 8, D)


def stage_slot(ref, start, out_ref, row):
    base = pl.multiple_of((start // 16) * 16, 16)
    rest = start - base
    shift = rest % 8
    groups = (SLOT + 8) // 8
    place = lax.broadcasted_iota(jnp.int32, (groups - 1, 8, 128), 1)
    number = lax.broadcasted_iota(jnp.int32, (groups - 1, 8, 128), 0) * 8 + place
    for g in range(D // 128):
        cols = slice(g * 128, (g + 1) * 128)
        wide = ref[pl.ds(base, SLOT + 16), cols].astype(f32)
        wide = jnp.where(rest >= 8, wide[8:], wide[:-8]).reshape(groups, 8, 128)
        turned = pltpu.roll(wide, lax.rem(8 - shift, 8), 1)
        block = jnp.where(place < 8 - shift, turned[:-1], turned[1:])
        block = jnp.where(number < PAIR, block, 0.0)
        out_ref[pl.ds(row, SLOT), cols] = block.reshape(SLOT, 128).astype(bf16)


def unstage_slot(ref, start, column):
    base = pl.multiple_of((start // 8) * 8, 8)
    shift = start - base
    for g in range(D // 128):
        cols = slice(g * 128, (g + 1) * 128)
        turned = pltpu.roll(column(g).reshape(SLOT // 8, 8, 128), shift, 1)
        keep = ref[pl.ds(base, 8), cols].reshape(1, 8, 128)
        low = jnp.concatenate([keep, turned], 0)
        high = jnp.concatenate([turned, turned[-1:]], 0)
        place = lax.broadcasted_iota(jnp.int32, low.shape, 1)
        ref[pl.ds(base, SLOT + 8), cols] = jnp.where(place < shift, low, high).reshape(SLOT + 8, 128)


def tail_rows(ref, count, is_last):
    kept = ref[HALO + 2048 - count : HALO + 2048, :].astype(f32)
    if count < TAIL:
        kept = jnp.concatenate([kept, jnp.zeros((TAIL - count, D), f32)], 0)
    return jnp.where(is_last, kept, 0.0).astype(bf16)


def tag_rows(tag, pair):
    width = tag.shape[1]
    number = tag // 2 - 2 * pair
    kept = tag % 2
    row = lax.broadcasted_iota(jnp.int32, (AUG, width), 0)
    match = row == number
    query = jnp.where(match, 1.0, 0.0).astype(bf16)
    key = jnp.where(match & (kept == 1), 0.0, -big)
    key = jnp.where(row < 4, key, 0.0).astype(bf16)
    return query, key


def attn_forward_kernel(
    seq_count, tok_ref, cot_ref, tok_halo, cot_halo, seg_ref, keep_ref, seg_halo, keep_halo,
    w_ref, vec_ref,
    xs_ref, es_ref, xt_ref, qt_ref, kt_ref, vt_ref, c_ref, lse_ref,
    wt_ref, x_ref, e_ref, tag_ref, sems,
):
    seq = lax.axis_index("seq")
    is_last = seq == seq_count - 1
    rows = tok_ref.shape[1]
    loads = []
    for i, (whole, halo, ext) in enumerate(((tok_ref, tok_halo, x_ref), (cot_ref, cot_halo, e_ref))):
        loads.append(pltpu.make_async_copy(whole.at[0], ext.at[pl.ds(HALO, rows)], sems.at[2 * i]))
        loads.append(pltpu.make_async_copy(halo, ext.at[pl.ds(0, HALO)], sems.at[2 * i + 1]))
    for load in loads:
        load.start()
    for part in range(3):
        wt_ref[part * D : (part + 1) * D, :] = w_ref[:, part * D : (part + 1) * D].T
    tag_ref[...] = jnp.zeros_like(tag_ref)
    edge = seg_halo[...] * 2 + keep_halo[...]
    tag_ref[:, :HALO] = jnp.broadcast_to(edge[:, 128 - HALO :], (8, HALO))
    tag_ref[:, HALO : HALO + rows] = jnp.broadcast_to(seg_ref[...] * 2 + keep_ref[...], (8, rows))
    query_bias = vec_ref[:, 0:1].astype(f32)
    value_bias = vec_ref[:, 1:2].astype(f32)
    for load in loads:
        load.wait()

    def block(xb, tag, pair, lane, width):
        lanes = pl.ds(lane, width)
        xt_ref[:D, lanes] = xb.T
        q = dot(wt_ref[:D, :], xb, 1, 1) + query_bias
        q = (q.astype(bf16).astype(f32) * HEAD_DIM**-0.5).astype(bf16)
        k = dot(wt_ref[D : 2 * D, :], xb, 1, 1).astype(bf16)
        v = (dot(wt_ref[2 * D :, :], xb, 1, 1) + value_bias).astype(bf16)
        query_tag, key_tag = tag_rows(tag, pair)
        vt_ref[:, lanes] = v
        context = []
        for h in range(HEADS):
            rows = slice(h * HEAD_DIM, (h + 1) * HEAD_DIM)
            qh = jnp.concatenate([q[rows], query_tag], 0)
            kh = jnp.concatenate([k[rows], key_tag], 0)
            qt_ref[h, :, lanes] = qh
            kt_ref[h, :, lanes] = kh
            s = dot(kh, qh, 0, 0)
            top = jnp.max(s, axis=0, keepdims=True)
            ex = jnp.exp(s - top)
            total = jnp.sum(ex, axis=0, keepdims=True)
            lse_ref[h : h + 1, lanes] = top + jnp.log(total)
            a = (ex * (1.0 / total)).astype(bf16)
            context.append(dot(v[rows], a, 1, 0))
        return jnp.concatenate(context, 0).astype(bf16).T

    def one(j, carry):
        start = first_row(j, seq)
        row = slot_row(j)
        xb = staged(x_ref, start)
        xs_ref[pl.ds(row, SLOT), :] = xb
        es_ref[pl.ds(row, SLOT), :] = staged(e_ref, start)
        wide = tag_ref[:, pl.ds(pl.multiple_of(j * SLOT, 128), SLOT + 128)]
        width = SLOT + 128
        tag = pltpu.roll(wide, width - (start - j * SLOT), 1)[:1, :SLOT]
        c_ref[pl.ds(row, SLOT), :] = block(
            xb, tag, 8 * seq + j, pl.multiple_of(j * SLOT, 128), SLOT
        )
        return carry

    lax.fori_loop(0, 8, one, 0)
    count = 8 * seq_count
    xt_ref[:, 8 * SLOT :] = jnp.zeros((D + AUG, 128), bf16)
    xb = tail_rows(x_ref, count, is_last)
    eb = tail_rows(e_ref, count, is_last)
    tag = tag_ref[:1, 2048:2176]
    tag = pltpu.roll(tag_ref[:, 2048:2176], 128 - (64 - count), 1)[:1, :TAIL] if count < 64 else tag[:, :TAIL]
    place = lax.broadcasted_iota(jnp.int32, (1, TAIL), 1)
    tag = jnp.where(place < count, tag, (2 * 8 * seq_count + 3) * 2)
    cb = block(xb, tag, 8 * seq_count, 8 * SLOT, TAIL)
    for t in range(TILES):
        rows = slice(t * PIECE, (t + 1) * PIECE)
        at = slice(t * TILE + 2 * SLOT, (t + 1) * TILE)
        xs_ref[at, :] = xb[rows]
        es_ref[at, :] = eb[rows]
        c_ref[at, :] = cb[rows]
    ones = lax.broadcasted_iota(jnp.int32, (AUG, LANES), 0) == 0
    xt_ref[D:, :] = jnp.where(ones, 1.0, 0.0).astype(bf16)


def attn_forward(seq_count, tokens, cotangent, *others):
    shape = jax.ShapeDtypeStruct
    vmem = pl.BlockSpec(memory_space=pltpu.VMEM)
    hbm = pl.BlockSpec(memory_space=pl.ANY)
    return pl.pallas_call(
        functools.partial(attn_forward_kernel, seq_count),
        out_shape=(
            shape((ROWS, D), bf16),
            shape((ROWS, D), bf16),
            shape((D + AUG, LANES), bf16),
            shape((HEADS, HEAD_DIM + AUG, LANES), bf16),
            shape((HEADS, HEAD_DIM + AUG, LANES), bf16),
            shape((D, LANES), bf16),
            shape((ROWS, D), bf16),
            shape((HEADS, LANES), f32),
        ),
        in_specs=[hbm, hbm] + [vmem] * len(others),
        out_specs=[vmem] * 8,
        scratch_shapes=[
            pltpu.VMEM((3 * D, D), bf16),
            pltpu.VMEM((HALO + tokens.shape[1], D), bf16),
            pltpu.VMEM((HALO + tokens.shape[1], D), bf16),
            pltpu.VMEM((8, LANES), jnp.int32),
            pltpu.SemaphoreType.DMA((4,)),
        ],
        compiler_params=pltpu.CompilerParams(vmem_limit_bytes=56 * MIB),
        name="attn_forward",
    )(tokens, cotangent, *others)


def feed_kernel(
    xs_ref, c_ref, es_ref, wo_ref, w1_ref, w2_ref, vect_ref,
    z_ref, dh_ref, dr_ref, gwo_ref, gw1_ref, gw2_ref, gvec_ref, gb1_ref,
    u_ref, g_ref, awo_ref, aw1_ref, aw2_ref, vec_ref,
):
    step = pl.program_id(0)

    @pl.when(step == 0)
    def _():
        awo_ref[...] = jnp.zeros_like(awo_ref)
        aw1_ref[...] = jnp.zeros_like(aw1_ref)
        aw2_ref[...] = jnp.zeros_like(aw2_ref)
        gvec_ref[...] = jnp.zeros_like(gvec_ref)
        gb1_ref[...] = jnp.zeros_like(gb1_ref)
        vec_ref[...] = vect_ref[...].astype(f32).T

    def mean(v):
        return jnp.mean(v, axis=-1, keepdims=True)

    def row_sum(v):
        return jnp.sum(v, axis=0, keepdims=True)

    bo, b2, g1, c1, g2, c2 = (vec_ref[i : i + 1, :] for i in range(2, 8))
    h1 = xs_ref[...].astype(f32) + (dot(c_ref[...], wo_ref[...], 1, 0) + bo)
    mid = h1 - mean(h1)
    inv1 = lax.rsqrt(mean(mid * mid) + norm_epsilon)
    n1 = mid * inv1
    y = n1 * g1 + c1
    yb = y.astype(bf16)
    chunk = D
    f = None
    for k in range(FF // chunk):
        cols = slice(k * chunk, (k + 1) * chunk)
        u = dot(yb, w1_ref[:, cols], 1, 0) + vec_ref[8 + k : 9 + k, :]
        cdf = 0.5 * (1.0 + lax.erf(u * 0.7071067811865476))
        gk = (u * cdf).astype(bf16)
        u_ref[:, cols] = cdf + u * jnp.exp(u * u * -0.5) * 0.3989422804014327
        g_ref[:, cols] = gk
        part = dot(gk, w2_ref[cols, :], 1, 0)
        f = part if f is None else f + part
    h2 = y + (f + b2)
    mid2 = h2 - mean(h2)
    inv2 = lax.rsqrt(mean(mid2 * mid2) + norm_epsilon)
    n2 = mid2 * inv2
    z_ref[...] = (n2 * g2 + c2).astype(bf16)
    e = es_ref[...].astype(f32)
    gvec_ref[7:8, :] += row_sum(e)
    gvec_ref[6:7, :] += row_sum(e * n2)
    eg = e * g2
    dh2 = (eg - mean(eg) - n2 * mean(eg * n2)) * inv2
    df = dh2.astype(bf16)
    gvec_ref[3:4, :] += row_sum(df.astype(f32))
    dft = df.T
    ybt = yb.T
    dy = dh2
    for k in range(FF // chunk):
        cols = slice(k * chunk, (k + 1) * chunk)
        aw2_ref[:, cols] += dot(dft, g_ref[:, cols], 1, 0)
        dg = dot(df, w2_ref[cols, :], 1, 1)
        du = (dg * u_ref[:, cols]).astype(bf16)
        gb1_ref[:1, cols] += row_sum(du.astype(f32))
        aw1_ref[:, cols] += dot(ybt, du, 1, 0)
        dy = dy + dot(du, w1_ref[:, cols], 1, 1)
    gvec_ref[5:6, :] += row_sum(dy)
    gvec_ref[4:5, :] += row_sum(dy * n1)
    eg = dy * g1
    dh1 = (eg - mean(eg) - n1 * mean(eg * n1)) * inv1
    dh_ref[...] = dh1
    dr = dh1.astype(bf16)
    dr_ref[...] = dr
    gvec_ref[2:3, :] += row_sum(dr.astype(f32))
    awo_ref[...] += dot(c_ref[...].T, dr, 1, 0)

    @pl.when(step == TILES - 1)
    def _():
        gwo_ref[...] = awo_ref[...].astype(bf16)
        gw1_ref[...] = aw1_ref[...].astype(bf16)
        for k in range(FF // chunk):
            cols = slice(k * chunk, (k + 1) * chunk)
            gw2_ref[cols, :] = aw2_ref[:, cols].astype(bf16).T


def feed(xs, c, es, wo, w1, w2, vec_t):
    shape = jax.ShapeDtypeStruct
    tile = pl.BlockSpec((TILE, D), lambda i: (i, 0))

    def whole(*dims):
        return pl.BlockSpec(dims, lambda i: (0,) * len(dims), pipeline_mode=pl.Buffered(1))

    return pl.pallas_call(
        feed_kernel,
        grid=(TILES,),
        out_shape=(
            shape((ROWS, D), bf16),
            shape((ROWS, D), f32),
            shape((ROWS, D), bf16),
            shape((D, D), bf16),
            shape((D, FF), bf16),
            shape((FF, D), bf16),
            shape((8, D), f32),
            shape((8, FF), f32),
        ),
        in_specs=[tile, tile, tile, whole(D, D), whole(D, FF), whole(FF, D), whole(D, 128)],
        out_specs=[tile, tile, tile, whole(D, D), whole(D, FF), whole(FF, D), whole(8, D), whole(8, FF)],
        scratch_shapes=[
            pltpu.VMEM((TILE, FF), f32),
            pltpu.VMEM((TILE, FF), bf16),
            pltpu.VMEM((D, D), f32),
            pltpu.VMEM((D, FF), f32),
            pltpu.VMEM((D, FF), f32),
            pltpu.VMEM((128, D), f32),
        ],
        compiler_params=pltpu.CompilerParams(vmem_limit_bytes=60 * MIB),
        name="feed",
    )(xs, c, es, wo, w1, w2, vec_t)


def attn_backward_kernel(
    seq_count, xt_ref, qt_ref, kt_ref, vt_ref, lse_ref, dr_ref, dh_ref, z_ref, w_ref, wo_ref,
    out_ref, out_halo_ref, in_ref, in_halo_ref, gwa_ref, gbias_ref,
    dpt_ref, ext_ref,
):
    seq = lax.axis_index("seq")
    is_last = seq == seq_count - 1

    def block(dr, lane, width):
        lanes = pl.ds(lane, width)
        dct = dot(wo_ref[...], dr, 1, 1).astype(bf16)
        for h in range(HEADS):
            rows = slice(h * HEAD_DIM, (h + 1) * HEAD_DIM)
            qh = qt_ref[h, :, lanes]
            kh = kt_ref[h, :, lanes]
            vh = vt_ref[rows, lanes]
            dch = dct[rows]
            a = jnp.exp(dot(kh, qh, 0, 0) - lse_ref[h : h + 1, lanes])
            da = dot(vh, dch, 0, 0)
            ada = a * da
            ds = (ada - a * jnp.sum(ada, axis=0, keepdims=True)).astype(bf16)
            dv = dot(dch, a.astype(bf16), 1, 1)
            dk = dot(qh[:HEAD_DIM], ds, 1, 1)
            dq = dot(kh[:HEAD_DIM], ds, 1, 0) * HEAD_DIM**-0.5
            dpt_ref[rows, lanes] = dq.astype(bf16)
            dpt_ref[slice(D + h * HEAD_DIM, D + (h + 1) * HEAD_DIM), lanes] = dk.astype(bf16)
            dpt_ref[slice(2 * D + h * HEAD_DIM, 2 * D + (h + 1) * HEAD_DIM), lanes] = dv.astype(bf16)
        return dot(w_ref[...], dpt_ref[:, lanes], 1, 0).T

    dpt_ref[:, 8 * SLOT :] = jnp.zeros((3 * D, 128), bf16)

    def one(j, carry):
        row = slot_row(j)
        grad = block(dr_ref[pl.ds(row, SLOT), :], pl.multiple_of(j * SLOT, 128), SLOT)
        unstage(ext_ref, first_row(j, seq), grad + dh_ref[pl.ds(row, SLOT), :])
        return carry

    lax.fori_loop(0, 8, one, 0)
    count = 8 * seq_count

    def tail_of(ref):
        return jnp.concatenate(
            [ref[t * TILE + 2 * SLOT : (t + 1) * TILE, :] for t in range(TILES)], 0
        )

    grad = block(tail_of(dr_ref), 8 * SLOT, TAIL) + tail_of(dh_ref)

    @pl.when(is_last)
    def _():
        ext_ref[HALO + 2048 - count : HALO + 2048, :] = grad[:count]

    in_halo_ref[...] = ext_ref[:HALO, :]
    in_ref[...] = ext_ref[HALO : HALO + 2048, :]

    def two(j, carry):
        unstage(ext_ref, first_row(j, seq), z_ref[pl.ds(slot_row(j), SLOT), :].astype(f32))
        return carry

    lax.fori_loop(0, 8, two, 0)
    tail = tail_of(z_ref).astype(f32)

    @pl.when(is_last)
    def _():
        ext_ref[HALO + 2048 - count : HALO + 2048, :] = tail[:count]

    out_halo_ref[...] = ext_ref[:HALO, :].astype(bf16)
    out_ref[...] = ext_ref[HALO : HALO + 2048, :].astype(bf16)
    for part in range(3):
        cols = slice(part * D, (part + 1) * D)
        g = dot(xt_ref[...], dpt_ref[cols, :], 1, 1)
        gwa_ref[:, cols] = g[:D].astype(bf16)
        gbias_ref[:, cols] = g[D : D + 8]


def attn_backward(seq_count, *operands):
    shape = jax.ShapeDtypeStruct
    return pl.pallas_call(
        functools.partial(attn_backward_kernel, seq_count),
        out_shape=(
            shape((2048, D), bf16),
            shape((HALO, D), bf16),
            shape((2048, D), f32),
            shape((HALO, D), f32),
            shape((D, 3 * D), bf16),
            shape((8, 3 * D), f32),
        ),
        in_specs=[pl.BlockSpec(memory_space=pltpu.VMEM)] * len(operands),
        out_specs=[pl.BlockSpec(memory_space=pltpu.VMEM)] * 6,
        scratch_shapes=[
            pltpu.VMEM((3 * D, LANES), bf16),
            pltpu.VMEM((HALO + 2048 + 16, D), f32),
        ],
        compiler_params=pltpu.CompilerParams(vmem_limit_bytes=60 * MIB),
        name="attn_backward",
    )(*operands)


MESH = pl.DeviceIdType.MESH
PLANE = 4
DEPTH = 4


class Place:
    def __init__(self):
        self.batch = lax.axis_index("batch")
        self.z = lax.axis_index("seq")
        self.core = self.batch % 2
        self.plane = self.batch // 2

    def plane_at(self, k):
        x = (self.plane % 2 + k % 2) % 2
        y = (self.plane // 2 + k // 2) % 2
        return y * 2 + x

    def in_plane(self, k, other=0):
        core = self.core if other == 0 else 1 - self.core
        return {"batch": self.plane_at(k) * 2 + core, "seq": self.z}

    def depth_at(self, k):
        return (self.z + k) % DEPTH

    def in_depth(self, k):
        return {"batch": self.batch, "seq": self.depth_at(k)}

    def sibling(self):
        return {"batch": self.plane * 2 + 1 - self.core, "seq": self.z}

    def greet(self):
        barrier = pltpu.get_barrier_semaphore()
        for k in range(1, 4):
            pl.semaphore_signal(barrier, inc=1, device_id=self.in_plane(k), device_id_type=MESH)
            pl.semaphore_signal(barrier, inc=1, device_id=self.in_depth(k), device_id_type=MESH)
            pl.semaphore_signal(barrier, inc=1, device_id=self.in_plane(k, 1), device_id_type=MESH)
        pl.semaphore_signal(barrier, inc=1, device_id=self.sibling(), device_id_type=MESH)

    def greeted(self):
        pl.semaphore_wait(pltpu.get_barrier_semaphore(), 10)


def remote(src, dst, send, recv, device):
    return pltpu.make_async_remote_copy(
        src_ref=src, dst_ref=dst, send_sem=send, recv_sem=recv, device_id=device, device_id_type=MESH
    )


LOW, HIGH = pl.ds(0, DEPTH // 2), pl.ds(DEPTH // 2, DEPTH // 2)


class Gather:
    def __init__(self, place, whole, send, recv, parts=None):
        self.place, self.whole, self.send, self.recv, self.parts = place, whole, send, recv, parts

    def block(self, k):
        return self.whole.at[self.place.plane_at(k) * 2 + self.place.core]

    def copy(self, n, source, target, device):
        return remote(source, target, self.send.at[n], self.recv.at[n], device)

    def depth(self, k):
        at = self.place
        here = self.whole.at[at.batch, at.z]
        source = here if self.parts is None else self.parts.at[at.depth_at(k)]
        return self.copy(k - 1, source, here, at.in_depth(k))

    def plane(self, k):
        return self.copy(2 + k, self.block(0), self.block(0), self.place.in_plane(k))

    def across(self, k):
        half = self.block(k).at[LOW if k == 1 else HIGH]
        return self.copy(4 + k, half, half, self.place.in_plane(3 - k))

    def core(self, k):
        return self.copy(7 + k, self.block(k), self.block(k), self.place.sibling())

    def first(self):
        for k in range(1, 4):
            self.depth(k).start()

    def second(self):
        for k in range(1, 4):
            self.depth(k).wait_recv()
        for k in (1, 2):
            self.plane(k).start()
        self.core(0).start()

    def third(self):
        for k in (1, 2):
            self.plane(k).wait_recv()
            self.across(k).start()
            self.core(k).start()

    def fourth(self):
        for k in (1, 2):
            self.across(k).wait_recv()
        self.core(3).start()

    def finish(self):
        for k in range(4):
            self.core(k).wait_recv()
        for k in range(1, 4):
            self.depth(k).wait_send()
        for k in (1, 2):
            self.plane(k).wait_send()
            self.across(k).wait_send()
        for k in range(4):
            self.core(k).wait_send()


class Spread(Gather):
    def step(self, k, other):
        device = self.place.in_plane(k, other) if k else self.place.sibling()
        return self.copy(2 * k + other + 3 if k else 3, self.block(0), self.block(0), device)

    def steps(self):
        return [self.step(0, 0)] + [self.step(k, other) for k in range(1, 4) for other in range(2)]

    def second(self):
        for k in range(1, 4):
            self.depth(k).wait_recv()
        for copy in self.steps():
            copy.start()

    def finish(self):
        for copy in self.steps():
            copy.wait_recv()
        for k in range(1, 4):
            self.depth(k).wait_send()
        for copy in self.steps():
            copy.wait_send()


class Scatter:
    def __init__(self, place, grad, twin, near, far, along, send, recv):
        self.place, self.grad, self.twin = place, grad, twin
        self.near, self.far, self.along, self.send, self.recv = near, far, along, send, recv
        shape = grad.shape
        if len(shape) == 4:
            self.at = lambda p, c: grad.at[p * 2 + c]
        else:
            self.at = lambda p, c: grad.at[p, c]

    def block(self, k):
        return self.at(self.place.plane_at(k), self.place.core)

    def copy(self, n, source, target, device):
        return remote(source, target, self.send.at[n], self.recv.at[n], device)

    def core(self, p):
        source = self.at(p, 1 - self.place.core)
        return self.copy(p, source, self.twin.at[p], self.place.sibling())

    def plane(self, n):
        k, half = ((1, LOW), (3, LOW), (2, HIGH), (3, HIGH))[n]
        target = self.near.at[n]
        return self.copy(4 + n, self.block(k).at[half], target, self.place.in_plane(1 + n // 2))

    def across(self, n):
        k, half = ((2, LOW), (1, HIGH))[n]
        return self.copy(8 + n, self.block(k).at[half], self.far.at[n], self.place.in_plane(2 - n))

    def depth(self, k):
        source = self.block(0).at[self.place.depth_at(k)]
        return self.copy(9 + k, source, self.along.at[k - 1], self.place.in_depth(k))

    def first(self):
        for p in range(PLANE):
            self.core(p).start()

    def second(self):
        for p in range(PLANE):
            self.core(p).wait_recv()
        own = self.place.core

        def one(p, carry):
            mine = self.at(p, own)
            mine[...] = (mine[...].astype(f32) + self.twin[p].astype(f32)).astype(mine.dtype)
            return carry

        lax.fori_loop(0, PLANE, one, 0)
        for n in range(4):
            self.plane(n).start()

    def third(self):
        for n in range(4):
            self.plane(n).wait_recv()
        for n, (k, base) in enumerate(((2, 0), (1, 2))):
            mine = self.block(k)

            def one(q, carry):
                total = mine[base + q].astype(f32) + self.near[2 * n + 1, q].astype(f32)
                mine[base + q] = total.astype(mine.dtype)
                return carry

            lax.fori_loop(0, 2, one, 0)
            self.across(n).start()

    def fourth(self):
        for n in range(2):
            self.across(n).wait_recv()
        mine = self.block(0)

        def one(i, carry):
            n, q = i // 2, i % 2
            total = mine[i].astype(f32) + self.near[2 * n, q].astype(f32) + self.far[n, q].astype(f32)
            mine[i] = total.astype(mine.dtype)
            return carry

        lax.fori_loop(0, DEPTH, one, 0)
        for k in range(1, 4):
            self.depth(k).start()

    def total(self):
        for k in range(1, 4):
            self.depth(k).wait_recv()
        total = self.block(0)[self.place.z].astype(f32)
        for k in range(3):
            total = total + self.along[k].astype(f32)
        return total

    def finish(self):
        for p in range(PLANE):
            self.core(p).wait_send()
        for n in range(4):
            self.plane(n).wait_send()
        for n in range(2):
            self.across(n).wait_send()
        for k in range(1, 4):
            self.depth(k).wait_send()


def turned(ref, value):
    ref[...] = jnp.zeros_like(ref)
    ref[: value.shape[0], : value.shape[1]] = value
    return ref[...].T


def heads_of(block, h):
    return block[h * HEAD_DIM : (h + 1) * HEAD_DIM]


def only_head(block, h):
    zero = jnp.zeros((HEAD_DIM, block.shape[1]), block.dtype)
    mine = heads_of(block, h)
    return jnp.concatenate([mine, zero] if h % 2 == 0 else [zero, mine], 0)


def pair_of(block, h):
    at = h // 2 * 2 * HEAD_DIM
    return block[:, at : at + 2 * HEAD_DIM]


def mask_parts(tag, pair):
    query, key = tag_rows(tag, pair)
    width = tag.shape[1]
    zero = jnp.zeros((128 - AUG, width), bf16)
    return jnp.concatenate([key, zero], 0).T, jnp.concatenate([query, zero], 0)


class Slots:
    def __init__(self, tag_ref, seq, seq_count):
        self.tag_ref, self.seq, self.count = tag_ref, seq, 8 * seq_count
        self.last_pair = 8 * seq_count

    def tag(self, j):
        wide = self.tag_ref[:, pl.ds(lanes_of(j).start, SLOT + 128)]
        offset = HALO - 8 * self.seq - j
        return pltpu.roll(wide, SLOT + 128 - offset, 1)[:1, :SLOT]

    def tail_tag(self):
        tag = self.tag_ref[:, 2048:2176]
        if self.count < TAIL:
            tag = pltpu.roll(tag, 128 - (TAIL - self.count), 1)
        place = lax.broadcasted_iota(jnp.int32, (1, TAIL), 1)
        return jnp.where(place < self.count, tag[:1, :TAIL], 2 * (2 * self.last_pair + 3))

    def tail(self, ref):
        return jnp.concatenate(
            [ref[t * TILE + 2 * SLOT : (t + 1) * TILE, :] for t in range(TILES)], 0
        )

    def set_tail(self, ref, value):
        for t in range(TILES):
            ref[t * TILE + 2 * SLOT : (t + 1) * TILE, :] = value[t * PIECE : (t + 1) * PIECE]


def part_of(lanes, half):
    start = lanes.start + half.start
    if not isinstance(start, int):
        start = pl.multiple_of(start, 128)
    return pl.ds(start, half.stop - half.start)


def halves_of(width):
    step = min(width, 128)
    return [slice(i, i + step) for i in range(0, width, step)]


def pair_stack(values, *rest):
    zero = jnp.zeros_like(values[0])
    left = jnp.concatenate([values[0], zero, *rest], 0)
    right = jnp.concatenate([zero, values[1], *rest], 0)
    return left, right


def forward_block(
    xb, tag, pair, lanes, put, wt_ref, biases, xt_ref, qt_ref, kt_ref, vt_ref, lse_ref, s_ref, a_ref,
    kn_ref, ct_ref,
):
    width = xb.shape[0]
    parts = ((kt_ref, None), (qt_ref, biases[0]), (vt_ref, biases[1]))

    def project(n):
        at = (1, 0, 2)[n]
        p = dot(wt_ref[at * D : (at + 1) * D, :], xb, 1, 1)
        s_ref[2 * n, :, :width] = p[:SLOT]
        s_ref[2 * n + 1, :, :width] = p[SLOT:]

    def keep(n):
        out_ref, bias = parts[n]
        for h in range(HEADS):
            at = h % 4 * HEAD_DIM
            value = s_ref[2 * n + h // 4, at : at + HEAD_DIM, :width]
            rows = slice(h * HEAD_DIM, (h + 1) * HEAD_DIM)
            if bias is not None:
                value = value + bias[rows]
            value = value.astype(bf16)
            if n == 1:
                value = (value.astype(f32) * HEAD_DIM**-0.5).astype(bf16)
            out_ref[rows, lanes] = value

    masks = []

    def turn():
        kn_ref[:width, :] = kt_ref[:, lanes].T
        masks.extend(mask_parts(tag, pair))

    def rows_of(h):
        return slice(h * HEAD_DIM, (h + 1) * HEAD_DIM)

    def scores(p):
        key_mask, query_mask = masks
        left = jnp.concatenate([kn_ref[:width, p * 128 : (p + 1) * 128], key_mask], 1)
        both = pair_stack([qt_ref[rows_of(2 * p + i), lanes] for i in range(2)], query_mask)
        if width % 128 == 0:
            s = dot(left, jnp.concatenate(both, 1), 1, 0)
            s_ref[2 * p], s_ref[2 * p + 1] = s[:, :width], s[:, width:]
        else:
            for i in range(2):
                s_ref[2 * p + i, :width, :width] = dot(left, both[i], 1, 0)

    def weigh(p):
        for h in (2 * p, 2 * p + 1):
            for half in halves_of(width):
                s = s_ref[h, :width, half]
                top = jnp.max(s, axis=0, keepdims=True)
                ex = jnp.exp(s - top)
                total = jnp.sum(ex, axis=0, keepdims=True)
                a_ref[h, :width, half] = (ex * (1.0 / total)).astype(bf16)
                at = part_of(lanes, half)
                lse_ref[h : h + 1, at] = top + jnp.log(total)

    def collect(p):
        for h in (2 * p, 2 * p + 1):
            c = dot(vt_ref[rows_of(h), lanes], a_ref[h, :width, :width], 1, 0)
            ct_ref[rows_of(h), :width] = c.astype(bf16)

    def close():
        xt_ref[:D, lanes] = xb.T
        put(ct_ref[:, :width].T)

    call = functools.partial
    ahead = [
        call(project, 0), call(project, 1), call(keep, 0), turn, call(project, 2), call(keep, 1),
        call(keep, 2),
    ]
    return ahead, (scores, weigh, collect), [close]


def when(condition, event):
    if isinstance(condition, bool):
        if condition:
            event()
    else:
        pl.when(condition)(event)


def lanes_of(j):
    start = j * SLOT
    return pl.ds(start if isinstance(j, int) else pl.multiple_of(start, 128), SLOT)


def together(*blocks):
    for phases in zip(*(block[0] for block in blocks)):
        for phase in phases:
            phase()
    count = len(blocks)

    def stage(n):
        return lambda i: blocks[i % count][1][n](i // count)

    skewed(HEADS // 2 * count, stage(0), stage(1), stage(2))
    for phases in zip(*(block[2] for block in blocks)):
        for phase in phases:
            phase()


def skewed(count, *stages):
    for i in range(count + len(stages) - 1):
        for n, stage in enumerate(stages):
            if 0 <= i - n < count:
                stage(i - n)


def backward_block(
    dr, c, tag, pair, lanes, wo, qt_ref, kt_ref, vt_ref, lse_ref, dpt_ref, s_ref, da_ref, a_ref,
    ds_ref, kn_ref, vn_ref, dct_ref, ct_ref,
):
    width = dr.shape[0]
    masks = []

    def turn():
        kn_ref[:width, :] = kt_ref[:, lanes].T
        vn_ref[:width, :] = vt_ref[:, lanes].T
        masks.extend(mask_parts(tag, pair))

    def spread():
        dct_ref[:, :width] = dot(wo, dr, 1, 1).astype(bf16)
        ct_ref[:, :width] = c.T

    def rows_of(h):
        return slice(h * HEAD_DIM, (h + 1) * HEAD_DIM)

    def scores(p):
        at = slice(p * 128, (p + 1) * 128)
        key_mask, query_mask = masks
        left = jnp.concatenate([kn_ref[:width, at], key_mask], 1)
        both = pair_stack([qt_ref[rows_of(2 * p + i), lanes] for i in range(2)], query_mask)
        both_d = pair_stack([dct_ref[rows_of(2 * p + i), :width] for i in range(2)])
        right = vn_ref[:width, at]
        if width % 128 == 0:
            s = dot(left, jnp.concatenate(both, 1), 1, 0)
            u = 2 * (p % 2)
            s_ref[u], s_ref[u + 1] = s[:, :width], s[:, width:]
            da = dot(right, jnp.concatenate(both_d, 1), 1, 0)
            da_ref[u], da_ref[u + 1] = da[:, :width], da[:, width:]
        else:
            for i in range(2):
                s_ref[2 * (p % 2) + i, :width, :width] = dot(left, both[i], 1, 0)
                da_ref[2 * (p % 2) + i, :width, :width] = dot(right, both_d[i], 1, 0)

    def weigh(p):
        for h in (2 * p, 2 * p + 1):
            rows = rows_of(h)
            for half in halves_of(width):
                at = part_of(lanes, half)
                product = ct_ref[rows, half].astype(f32) * dct_ref[rows, half].astype(f32)
                delta = jnp.sum(product, axis=0, keepdims=True)
                lse = lse_ref[h : h + 1, at]
                for first in range(0, width, 64):
                    keys = slice(first, first + 64)
                    a = jnp.exp(s_ref[h % 4, keys, half] - lse)
                    a_ref[h % 4, keys, half] = a.astype(bf16)
                    ds_ref[h % 4, keys, half] = (a * (da_ref[h % 4, keys, half] - delta)).astype(bf16)

    def collect(p):
        for h in (2 * p, 2 * p + 1):
            rows = rows_of(h)
            ds = ds_ref[h % 4, :width, :width]
            dv = dot(dct_ref[rows, :width], a_ref[h % 4, :width, :width], 1, 1)
            dk = dot(qt_ref[rows, lanes], ds, 1, 1)
            dq = dot(kt_ref[rows, lanes], ds, 1, 0) * HEAD_DIM**-0.5
            dpt_ref[rows, lanes] = dq.astype(bf16)
            dpt_ref[slice(D + rows.start, D + rows.stop), lanes] = dk.astype(bf16)
            dpt_ref[slice(2 * D + rows.start, 2 * D + rows.stop), lanes] = dv.astype(bf16)

    return [turn, spread], (scores, weigh, collect), []


def mean(v):
    return jnp.mean(v, axis=-1, keepdims=True)


def row_sum(v):
    return jnp.sum(v, axis=0, keepdims=True)


def flat(value):
    return value.reshape(-1, value.shape[-1])


BLOCK = 48
MAIN = 2 * SLOT


def eights(v):
    return jnp.sum(v.reshape(-1, 8, v.shape[-1]), axis=0)


def feed_tile(
    t, xs_ref, c_ref, es_ref, wo_ref, w1_ref, w2_ref, vec_ref, dh_ref, gvec_ref,
    acc_ref, other_ref, n1_ref, inv_ref, yb_ref, df_ref, u_ref, g_ref, back_ready, tails,
    awo_ref, aw1_ref, aw2_ref,
):
    first = pl.multiple_of(t * TILE, 16)
    rows = pl.ds(first, TILE)
    piece = pl.ds(pl.multiple_of(t * PIECE, 16), PIECE)
    g_tail, du_tail, df_tail, yb_tail = tails
    bo, b2, g1, c1, g2, c2 = (vec_ref[i : i + 1, :] for i in range(2, 8))
    per = FF // D
    blocks = [slice(i, i + BLOCK) for i in range(0, TILE, BLOCK)]

    def at(block):
        return pl.ds(pl.multiple_of(first + block.start, 16), BLOCK)

    acc_ref[...] = dot(c_ref[rows, :], flat(wo_ref[...]), 1, 0)
    for block in blocks:
        h1 = xs_ref[at(block), :].astype(f32) + (acc_ref[block, :] + bo)
        mid = h1 - mean(h1)
        inv1 = lax.rsqrt(mean(mid * mid) + norm_epsilon)
        n1 = mid * inv1
        n1_ref[block, :] = n1
        inv_ref[block, :] = jnp.broadcast_to(inv1, (BLOCK, 128))
        yb_ref[block, :] = (n1 * g1 + c1).astype(bf16)

    pads = (acc_ref, other_ref)

    def w2_part(k):
        return flat(w2_ref[8 // per * k : 8 // per * (k + 1)])

    def w1_part(k):
        return flat(w1_ref[:, :, :, k * D : (k + 1) * D])

    def up(k):
        pads[k % 2][...] = dot(yb_ref[...], w1_part(k), 1, 0)

    def activate(k):
        cols = slice(k * D, (k + 1) * D)
        b1 = vec_ref[8 + k : 9 + k, :]
        for block in blocks:
            u = pads[k % 2][block, :] + b1
            cdf = 0.5 + 0.5 * lax.erf(u * 0.7071067811865476)
            g_ref[k * TILE + block.start : k * TILE + block.stop, :] = (u * cdf).astype(bf16)
            bell = jnp.exp2(u * u * (-0.5 * math.log2(math.e)) - 0.5 * math.log2(2.0 * math.pi))
            u_ref[block, cols] = cdf + u * bell

    def down(k):
        part = dot(g_ref[k * TILE : (k + 1) * TILE, :], w2_part(k), 1, 0)
        if k == 0:
            dh_ref[rows, :] = part
        else:
            dh_ref[rows, :] += part

    up(0)
    up(1)
    activate(0)
    pl.when(t == 0)(back_ready)
    for k in range(per):
        if k + 2 < per:
            up(k + 2)
        down(k)
        if k + 1 < per:
            activate(k + 1)
    sums = [jnp.zeros((8, D), f32)] * 3
    for block in blocks:
        h2 = (n1_ref[block, :] * g1 + c1) + (dh_ref[at(block), :] + b2)
        mid2 = h2 - mean(h2)
        inv2 = lax.rsqrt(mean(mid2 * mid2) + norm_epsilon)
        n2 = mid2 * inv2
        xs_ref[at(block), :] = (n2 * g2 + c2).astype(bf16)
        e = es_ref[at(block), :].astype(f32)
        en = e * n2
        eg = e * g2
        dh2 = (eg - mean(eg) - n2 * mean(eg * n2)) * inv2
        dh_ref[at(block), :] = dh2
        df = dh2.astype(bf16)
        df_ref[block, :] = df
        sums = [sums[0] + eights(e), sums[1] + eights(en), sums[2] + eights(df.astype(f32))]
    for i, value in zip((7, 6, 3), sums):
        gvec_ref[i : i + 1, :] += row_sum(value)
    dft = df_ref[:MAIN, :].T
    ybt = yb_ref[:MAIN, :].T
    df_tail[piece, :] = df_ref[MAIN:, :]
    yb_tail[piece, :] = yb_ref[MAIN:, :]

    def up_back(k):
        pads[k % 2][...] = dot(df_ref[...], w2_part(k), 1, 1)

    def activate_back(k):
        cols = slice(k * D, (k + 1) * D)
        here = slice(k * TILE, k * TILE + MAIN)
        at_tail = pl.ds(pl.multiple_of(k * TAIL + t * PIECE, 16), PIECE)
        aw2_ref[:, cols] += dot(dft, g_ref[here, :], 1, 0)
        g_tail[at_tail, :] = g_ref[here.stop : here.stop + PIECE, :]
        total = jnp.zeros((8, D), f32)
        for block in blocks:
            du = (pads[k % 2][block, :] * u_ref[block, cols]).astype(bf16)
            g_ref[k * TILE + block.start : k * TILE + block.stop, :] = du
            total = total + eights(du.astype(f32))
        gvec_ref[8 + k : 9 + k, :] += row_sum(total)

    def down_back(k):
        cols = slice(k * D, (k + 1) * D)
        here = slice(k * TILE, k * TILE + MAIN)
        at_tail = pl.ds(pl.multiple_of(k * TAIL + t * PIECE, 16), PIECE)
        aw1_ref[:, cols] += dot(ybt, g_ref[here, :], 1, 0)
        du_tail[at_tail, :] = g_ref[here.stop : here.stop + PIECE, :]
        part = dot(g_ref[k * TILE : (k + 1) * TILE, :], w1_part(k), 1, 1)
        dh_ref[rows, :] += part

    skewed(per, up_back, activate_back, down_back)
    sums = [jnp.zeros((8, D), f32)] * 3
    for block in blocks:
        dy = dh_ref[at(block), :]
        n1 = n1_ref[block, :]
        eg = dy * g1
        dh1 = (eg - mean(eg) - n1 * mean(eg * n1)) * inv_ref[block, :1]
        dh_ref[at(block), :] = dh1
        dr = dh1.astype(bf16)
        es_ref[at(block), :] = dr
        sums = [sums[0] + eights(dy), sums[1] + eights(dy * n1), sums[2] + eights(dr.astype(f32))]
    for i, value in zip((5, 4, 2), sums):
        gvec_ref[i : i + 1, :] += row_sum(value)
    main = pl.ds(first, MAIN)
    awo_ref[...] += dot(c_ref[main, :].T, es_ref[main, :], 1, 0)


def whole_kernel(*refs):
    refs = list(refs)

    def take(count):
        taken = refs[:count]
        del refs[:count]
        return taken

    state_in = take(15)
    tok_ref, cot_ref, seg_ref, keep_ref = take(4)
    out_ref, in_ref = take(2)
    state_out = take(5)
    copy_out = take(5)
    out_back, in_back = take(2)
    packed = take(5)
    firsts, seconds, masters = ([p.at[n] for p in packed] for n in range(3))
    state = masters + firsts + seconds
    weights = take(5)
    wa_ref, wo_ref, w1_ref, w2_ref, wv_ref = weights
    xs_ref, es_ref, xt_ref, qt_ref, kt_ref, vt_ref, c_ref, lse_ref, dh_ref, tag_ref = take(10)
    ext_ref, seg_halo, keep_halo = take(3)
    square, gvec_ref, gwa_ref, gwo_ref, grad_vec, halo_out, halo_in = take(7)
    twins, nears, fars, alongs = take(5), take(5), take(5), take(5)
    parts, copies, whole_vec = take(4), take(5), take(1)[0]
    (
        state_sems, load_sems, gather_send, gather_recv, edge_send, edge_recv,
        sum_send, sum_recv, copy_send, copy_recv, store_sems,
    ) = refs
    place = Place()
    place.greet()
    seq, seq_count = place.z, DEPTH
    is_last = seq == seq_count - 1
    slots = Slots(tag_ref, seq, seq_count)
    rows = tok_ref.shape[1]
    ext_x, ext_e = ext_ref.at[pl.ds(0, HALO + rows)], ext_ref.at[pl.ds(HALO + rows, HALO + rows)]

    loads = [pltpu.make_async_copy(state_in[i], state[i], state_sems.at[i]) for i in range(15)]
    for load in loads:
        load.start()
    big_loads = [
        pltpu.make_async_copy(src.at[0], dst.at[pl.ds(HALO, rows)], load_sems.at[i])
        for i, (src, dst) in enumerate(((tok_ref, ext_x), (cot_ref, ext_e)))
    ]
    for load in big_loads:
        load.start()
    place.greeted()
    edge = [
        remote(src, dst, edge_send.at[i], edge_recv.at[i], place.in_depth(1))
        for i, (src, dst) in enumerate((
            (tok_ref.at[0, pl.ds(rows - HALO, HALO)], ext_x.at[pl.ds(0, HALO)]),
            (cot_ref.at[0, pl.ds(rows - HALO, HALO)], ext_e.at[pl.ds(0, HALO)]),
            (seg_ref.at[:, pl.ds(rows - 128, 128)], seg_halo),
            (keep_ref.at[:, pl.ds(rows - 128, 128)], keep_halo),
        ))
    ]
    gathers = [Gather(place, weights[i], gather_send.at[i], gather_recv.at[i]) for i in range(5)]

    def put(i):
        shard = turned(square, masters[4][...])[: masters[4].shape[1]] if i == 4 else masters[i][...]
        weights[i][place.batch, place.z] = shard.astype(bf16)

    for i in (0, 4):
        loads[i].wait()
        put(i)
        gathers[i].first()
    for copy in edge:
        copy.start()
    for i in (1, 2, 3):
        loads[i].wait()
        put(i)
    gathers[1].first()
    for load in big_loads:
        load.wait()
    for copy in edge:
        copy.wait()
    tag_ref[...] = jnp.zeros_like(tag_ref)
    rim = seg_halo[...] * 2 + keep_halo[...]
    tag_ref[:, :HALO] = jnp.broadcast_to(rim[:, 128 - HALO :], (8, HALO))
    tag_ref[:, HALO : HALO + rows] = jnp.broadcast_to(seg_ref[...] * 2 + keep_ref[...], (8, rows))

    def stage_one(j, carry):
        start = first_row(j, seq)
        row = slot_row(j)
        stage_slot(ext_x, start, xs_ref, row)
        stage_slot(ext_e, start, es_ref, row)
        return carry

    gathers[0].second()
    gathers[2].first()
    gathers[4].second()
    gathers[1].second()
    lax.fori_loop(0, 8, stage_one, 0)
    slots.set_tail(xs_ref, tail_rows(ext_x, slots.count, is_last))
    slots.set_tail(es_ref, tail_rows(ext_e, slots.count, is_last))
    gathers[0].third()
    gathers[4].third()
    xt_ref[:, 8 * SLOT :] = jnp.zeros((D + AUG, 128), bf16)
    ones = lax.broadcasted_iota(jnp.int32, (AUG, LANES), 0) == 0
    xt_ref[D:, :] = jnp.where(ones, 1.0, 0.0).astype(bf16)
    gathers[2].second()
    gathers[3].first()
    gathers[0].fourth()
    gathers[4].fourth()
    gathers[1].third()
    gathers[0].finish()
    gathers[4].finish()
    gathers[3].second()

    def forward(wt_ref, s_ref, a_ref, kn_ref, ct_ref):
        for part in range(3):
            wt_ref[part * D : (part + 1) * D, :] = flat(
                wa_ref[:, :, :, part * D : (part + 1) * D]
            ).T
        vec_t = flat(wv_ref[...])
        biases = (vec_t[:, 0:1].astype(f32), vec_t[:, 1:2].astype(f32))

        def block(n, xb, tag, pair, lanes, put):
            return forward_block(
                xb, tag, pair, lanes, put, wt_ref, biases, xt_ref, qt_ref, kt_ref, vt_ref, lse_ref,
                s_ref.at[n], a_ref.at[n], kn_ref.at[n], ct_ref.at[n],
            )

        def two(i, carry, *more):
            for step, event in (
                (1, gathers[1].fourth), (1, gathers[2].third), (3, gathers[2].fourth),
                (3, gathers[3].third),
            ):
                when(i == step, event)

            def slot(n):
                j = 2 * i + n
                at = pl.ds(slot_row(j), SLOT)
                lanes = lanes_of(j)

                def put(value):
                    c_ref[at, :] = value

                return block(n, xs_ref[at, :], slots.tag(j), 8 * seq + j, lanes, put)

            together(slot(0), slot(1), *more)
            return carry

        lax.fori_loop(0, 3, two, 0)
        tail = block(
            2, slots.tail(xs_ref), slots.tail_tag(), slots.last_pair, pl.ds(8 * SLOT, TAIL),
            functools.partial(slots.set_tail, c_ref),
        )
        two(3, 0, tail)

    pl.run_scoped(
        forward,
        pltpu.VMEM((3 * D, D), bf16),
        pltpu.VMEM((3, HEADS, SLOT, SLOT), f32),
        pltpu.VMEM((3, HEADS, SLOT, SLOT), bf16),
        pltpu.VMEM((3, SLOT, D), bf16),
        pltpu.VMEM((3, D, SLOT), bf16),
    )
    for i in (1, 2):
        gathers[i].finish()
    gathers[3].fourth()

    def back_ready():
        gathers[3].finish()

    grads = [gwa_ref, gwo_ref, w1_ref, w2_ref, grad_vec]
    scatters = [
        Scatter(
            place, grads[i], twins[i], nears[i], fars[i], alongs[i], sum_send.at[i], sum_recv.at[i]
        )
        for i in range(5)
    ]

    def feed_all(
        vec_ref, acc_ref, other_ref, n1_ref, inv_ref, u_ref, awo_ref, aw1_ref, aw2_ref
    ):
        used = 0
        views = []
        for count in (4 * TILE, TILE, TILE, TAIL, TAIL, 4 * TAIL, 4 * TAIL):
            views.append(ext_ref.at[pl.ds(used, count)])
            used += count
        g_ref, yb_ref, df_ref, yb_tail, df_tail, g_tail, du_tail = views
        for ref in (awo_ref, aw1_ref, aw2_ref, gvec_ref):
            ref[...] = jnp.zeros_like(ref)
        vec_ref[...] = flat(wv_ref[...]).astype(f32).T[:16]

        def one(t, carry):
            feed_tile(
                t, xs_ref, c_ref, es_ref, wo_ref, w1_ref, w2_ref, vec_ref, dh_ref, gvec_ref, acc_ref,
                other_ref, n1_ref, inv_ref, yb_ref, df_ref, u_ref, g_ref, back_ready,
                (g_tail, du_tail, df_tail, yb_tail),
                awo_ref, aw1_ref, aw2_ref,
            )
            return carry

        lax.fori_loop(0, TILES, one, 0)
        for k in range(FF // D):
            cols = slice(k * D, (k + 1) * D)
            at = slice(k * TAIL, (k + 1) * TAIL)
            aw2_ref[:, cols] += dot(df_tail[...].T, g_tail[at, :], 1, 0)
            aw1_ref[:, cols] += dot(yb_tail[...].T, du_tail[at, :], 1, 0)
        awo_ref[...] += dot(slots.tail(c_ref).T, slots.tail(es_ref), 1, 0)
        def convert(i, carry):
            value = aw2_ref[:, pl.ds(pl.multiple_of(i * 128, 128), 128)].astype(bf16).T
            w2_ref[i // 2, pl.ds(i % 2 * 2, 2)] = value.reshape(2, -1, D)
            return carry

        def convert_rows(i, carry):
            value = aw1_ref[pl.ds(pl.multiple_of(i * 64, 64), 64), :].astype(bf16)
            w1_ref[i] = value.reshape(DEPTH, -1, FF)
            gwo_ref[i // 2, i % 2] = (
                awo_ref[pl.ds(pl.multiple_of(i * 64, 64), 64), :].astype(bf16).reshape(DEPTH, -1, D)
            )
            return carry

        lax.fori_loop(0, FF // 128, convert, 0)
        scatters[3].first()
        lax.fori_loop(0, 8, convert_rows, 0)
        scatters[2].first()
        scatters[1].first()

    pl.run_scoped(
        feed_all,
        pltpu.VMEM((16, D), f32),
        pltpu.VMEM((TILE, D), f32),
        pltpu.VMEM((TILE, D), f32),
        pltpu.VMEM((TILE, D), f32),
        pltpu.VMEM((TILE, 128), f32),
        pltpu.VMEM((TILE, FF), f32),
        pltpu.VMEM((D, D), f32),
        pltpu.VMEM((D, FF), f32),
        pltpu.VMEM((D, FF), f32),
    )
    for load in loads[5:]:
        load.wait()
    copy_gathers = [
        kind(place, copies[i], copy_send.at[i], copy_recv.at[i], parts[i])
        for i, kind in enumerate((Spread, Spread, Gather, Gather))
    ]
    copy_gathers.append(Spread(place, whole_vec, copy_send.at[4], copy_recv.at[4]))
    stores = []

    def store(src, dst):
        stores.append(pltpu.make_async_copy(src, dst, store_sems.at[len(stores)]))
        stores[-1].start()

    def update(i):
        total = scatters[i].total()
        if i == 4:
            square[...] = jnp.zeros_like(square)
            square[: total.shape[0], :] = total
            here, cols = masters[4].shape
            total = square[...].T[:here, :cols]
        new = adam_update(masters[i][...], firsts[i][...], seconds[i][...], total, learn_rates[i])
        firsts[i][...], seconds[i][...], masters[i][...] = new
        if i == 4:
            shard = turned(square, new[2])[: new[2].shape[1]].astype(bf16)
            whole_vec[place.batch, place.z] = shard
        else:
            low = new[2].astype(bf16)
            width = low.shape[1] // DEPTH
            for q in range(DEPTH):
                parts[i][q] = low[:, q * width : (q + 1) * width]
            copies[i][place.batch, place.z] = parts[i][place.z]
        copy_gathers[i].first()

    def backward(dpt_ref):
        dpt_ref[:, 8 * SLOT :] = jnp.zeros((3 * D, 128), bf16)

        def attention(s_ref, da_ref, a_ref, ds_ref, kn_ref, vn_ref, dct_ref, ct_ref):
            wo = flat(wo_ref[...])
            pads = (s_ref, da_ref, a_ref, ds_ref, kn_ref, vn_ref, dct_ref, ct_ref)

            def block(n, dr, c, tag, pair, lanes):
                return backward_block(
                    dr, c, tag, pair, lanes, wo, qt_ref, kt_ref, vt_ref, lse_ref, dpt_ref,
                    *(pad.at[n] for pad in pads),
                )

            def two(i, carry):
                for step, event in (
                    (1, scatters[3].second), (1, scatters[2].second), (3, scatters[3].third),
                    (3, scatters[1].second),
                ):
                    pl.when(i == step)(event)

                def slot(n):
                    j = 2 * i + n
                    at = pl.ds(slot_row(j), SLOT)
                    lanes = pl.ds(pl.multiple_of(j * SLOT, 128), SLOT)
                    return block(n, es_ref[at, :], c_ref[at, :], slots.tag(j), 8 * seq + j, lanes)

                together(slot(0), slot(1))
                return carry

            lax.fori_loop(0, 4, two, 0)
            together(
                block(
                    0, slots.tail(es_ref), slots.tail(c_ref), slots.tail_tag(), slots.last_pair,
                    pl.ds(8 * SLOT, TAIL),
                )
            )

        pl.run_scoped(
            attention,
            *[pltpu.VMEM((2, 4, SLOT, SLOT), f32)] * 2,
            *[pltpu.VMEM((2, 4, SLOT, SLOT), bf16)] * 2,
            *[pltpu.VMEM((2, SLOT, D), bf16)] * 2,
            *[pltpu.VMEM((2, D, SLOT), bf16)] * 2,
        )
        pl.run_scoped(
            functools.partial(finish, dpt_ref),
            pltpu.VMEM((HALO + rows + 16, D), f32),
            pltpu.VMEM((4, SLOT, SLOT), f32),
        )

    def finish(dpt_ref, ext_ref, s_ref):
        low_ref = ext_e
        for part in range(3):
            cols = slice(part * D, (part + 1) * D)
            g = dot(xt_ref[...], dpt_ref[cols, :], 1, 1)
            gwa_ref[:, :, :, :, cols] = g[:D].astype(bf16).reshape(PLANE, 2, DEPTH, -1, D)
            if part != 1:
                gvec_ref[part // 2 : part // 2 + 1, :] = g[D : D + 1]
        grad_vec[...] = gvec_ref[...].T.reshape(grad_vec.shape)
        scatters[0].first()
        scatters[4].first()
        scatters[2].third()

        def output_one(j, carry):
            at = pl.ds(slot_row(j), SLOT)
            unstage_slot(
                ext_ref, first_row(j, seq),
                lambda g: xs_ref[at, g * 128 : (g + 1) * 128].astype(f32),
            )
            return carry

        def close(value):
            @pl.when(is_last)
            def _():
                ext_ref[HALO + rows - slots.count : HALO + rows, :] = value[: slots.count]

        lax.fori_loop(0, 8, output_one, 0)
        close(slots.tail(xs_ref).astype(f32))
        scatters[0].second()
        scatters[4].second()
        scatters[3].fourth()
        scatters[1].third()
        low_ref[...] = ext_ref[: HALO + rows, :].astype(bf16)
        halo_out[...] = low_ref[:HALO, :]
        edge_back[0].start()
        store(low_ref.at[pl.ds(HALO, rows)], out_ref)
        wa = flat(wa_ref[...])

        def input_block(lanes):
            return dot(wa, dpt_ref[:, lanes], 1, 0).T

        def input_two(i, carry):
            for step, event in (
                (1, scatters[2].fourth), (2, scatters[1].fourth), (2, functools.partial(update, 3)),
                (3, scatters[0].third), (3, scatters[4].third),
            ):
                pl.when(i == step)(event)

            def product(n):
                lanes = pl.ds(pl.multiple_of((2 * i + n) * SLOT, 128), SLOT)
                grad = dot(wa, dpt_ref[:, lanes], 1, 0)
                s_ref[2 * n], s_ref[2 * n + 1] = grad[:SLOT], grad[SLOT:]

            def put_back(n):
                j = 2 * i + n
                at = pl.ds(slot_row(j), SLOT)

                def column(g):
                    part = s_ref[2 * n + g // 2, g % 2 * 128 : g % 2 * 128 + 128, :].T
                    return part + dh_ref[at, g * 128 : (g + 1) * 128]

                unstage_slot(ext_ref, first_row(j, seq), column)

            skewed(2, product, put_back)
            return carry

        lax.fori_loop(0, 4, input_two, 0)
        close(input_block(pl.ds(8 * SLOT, TAIL)) + slots.tail(dh_ref))
        halo_in[...] = ext_ref[:HALO, :]
        edge_back[1].start()
        store(ext_ref.at[pl.ds(HALO, rows)], in_ref)
        update(2)
        copy_gathers[3].second()
        scatters[0].fourth()
        scatters[4].fourth()
        update(1)
        copy_gathers[2].second()
        update(4)
        update(0)
        copy_gathers[3].third()
        copy_gathers[2].third()
        copy_gathers[1].second()
        copy_gathers[4].second()
        copy_gathers[0].second()
        copy_gathers[3].fourth()
        copy_gathers[2].fourth()
        for i in range(5):
            store(packed[i], state_out[i])
        for i in (3, 2, 1, 4, 0):
            copy_gathers[i].finish()
            scatters[i].finish()
        here = masters[4].shape[0]
        mine = jnp.concatenate([whole_vec[seq * 2 + q // 4, q % 4] for q in range(8)], 0)
        copies[4][...] = mine.astype(f32).T[:here].astype(bf16)
        for i in range(5):
            store(copies[i], copy_out[i])
        for copy in stores:
            copy.wait()
        for copy in edge_back:
            copy.wait()

    edge_back = [
        remote(halo_out, out_back, edge_send.at[4], edge_recv.at[4], place.in_depth(3)),
        remote(halo_in, in_back, edge_send.at[5], edge_recv.at[5], place.in_depth(3)),
    ]
    pl.run_scoped(backward, pltpu.VMEM((3 * D, LANES), bf16))


def whole(masters, firsts, seconds, tokens, cotangent, segment, keep):
    shape = jax.ShapeDtypeStruct
    vmem = pl.BlockSpec(memory_space=pltpu.VMEM)
    hbm = pl.BlockSpec(memory_space=pl.ANY)
    state = (*masters, *firsts, *seconds)
    rows = tokens.shape[1]
    r = masters[0].shape[0]
    shapes = ((r, 3 * D), (r, D), (r, FF), (4 * r, D))
    copies = [((8, DEPTH, s[0], s[1] // DEPTH), bf16) for s in shapes]
    copies.append(((masters[4].shape[0], 128), bf16))
    halos = [((HALO, D), bf16), ((HALO, D), f32)]
    out_shape = [
        shape((rows, D), bf16),
        shape((rows, D), f32),
        *[shape((3,) + s.shape, f32) for s in masters],
        *[shape(*c) for c in copies],
        *[shape(*h) for h in halos],
    ]
    five = [(s, bf16) for s in shapes] + [((r, 128), f32)]
    tall = ROWS
    scratch = [pltpu.VMEM((3,) + s.shape, f32) for s in masters]
    scratch += [pltpu.VMEM((8, DEPTH) + s, bf16) for s in (*shapes, (r, 128))]
    scratch += [
        pltpu.VMEM((tall, D), bf16),
        pltpu.VMEM((tall, D), bf16),
        pltpu.VMEM((D + AUG, LANES), bf16),
        pltpu.VMEM((D, LANES), bf16),
        pltpu.VMEM((D, LANES), bf16),
        pltpu.VMEM((D, LANES), bf16),
        pltpu.VMEM((tall, D), bf16),
        pltpu.VMEM((HEADS, LANES), f32),
        pltpu.VMEM((tall, D), f32),
        pltpu.VMEM((8, LANES), jnp.int32),
        pltpu.VMEM((2 * (HALO + rows), D), bf16),
        pltpu.VMEM((1, 128), jnp.int32),
        pltpu.VMEM((1, 128), jnp.int32),
        pltpu.VMEM((128, 128), f32),
        pltpu.VMEM((128, D), f32),
        pltpu.VMEM((PLANE, 2, DEPTH) + shapes[0], bf16),
        pltpu.VMEM((PLANE, 2, DEPTH) + shapes[1], bf16),
        pltpu.VMEM((PLANE, 2, DEPTH, r, 128), f32),
        *[pltpu.VMEM(*h) for h in halos],
    ]
    for lead in ((PLANE, DEPTH), (4, DEPTH // 2), (2, DEPTH // 2), (3,)):
        scratch += [pltpu.VMEM(lead + s, t) for s, t in five]
    scratch += [pltpu.VMEM((DEPTH, s[0], s[1] // DEPTH), bf16) for s in shapes]
    scratch += [pltpu.VMEM(*c) for c in copies]
    scratch.append(pltpu.VMEM((8, DEPTH, r, 128), bf16))
    dma = pltpu.SemaphoreType.DMA
    scratch += [
        dma((15,)), dma((2,)), dma((5, 11)), dma((5, 11)), dma((6,)), dma((6,)),
        dma((5, 13)), dma((5, 13)), dma((5, 11)), dma((5, 11)), dma((12,)),
    ]
    return pl.pallas_call(
        whole_kernel,
        out_shape=out_shape,
        in_specs=[hbm] * 17 + [vmem] * 2,
        out_specs=[hbm] * 12 + [vmem] * 2,
        scratch_shapes=scratch,
        compiler_params=pltpu.CompilerParams(
            collective_id=0, has_side_effects=True, vmem_limit_bytes=63 * MIB
        ),
        name="whole",
    )(*state, tokens, cotangent, segment, keep)


LAST_PART = 496


def last_kernel(*refs):
    results, backs, ends = refs[:12], refs[12:14], refs[14:36]
    lows, (load_sems, store_sems) = refs[36:48], refs[48:]
    rows = results[0].shape[0]
    seq = lax.axis_index("seq")
    rim = pl.ds(rows - HALO, HALO)
    places = [(i, rim) for i in range(2)]
    places += [
        (i, pl.ds(first, LAST_PART))
        for i in (1, 0)
        for first in range(0, rows - HALO, LAST_PART)
    ]
    places += [(i, pl.ds(0, results[i].shape[0])) for i in range(2, 12)]
    loads = [
        pltpu.make_async_copy(results[i].at[at], lows[i].at[at], load_sems.at[n])
        for n, (i, at) in enumerate(places)
    ]
    for load in loads:
        load.start()
    place = lax.broadcasted_iota(jnp.int32, (HALO, 1), 0)
    theirs = (place >= HALO - 8 * (seq + 1)) & (seq < lax.axis_size("seq") - 1)
    stores = []
    for n, (i, at) in enumerate(places):
        loads[n].wait()
        if n < 2:
            own = lows[i][rim, :].astype(f32)
            lows[i][rim, :] = jnp.where(theirs, backs[i][...].astype(f32), own).astype(lows[i].dtype)
        if i < 2:
            pairs = [(lows[i].at[at], ends[i].at[at])]
        elif i < 7:
            pairs = [(lows[i].at[part], ends[2 + 5 * part + i - 2]) for part in range(3)]
        else:
            pairs = [(lows[i], ends[10 + i])]
        for source, target in pairs:
            stores.append(pltpu.make_async_copy(source, target, store_sems.at[len(stores)]))
            stores[-1].start()
    for store in stores:
        store.wait()


def last(results, out_back, in_back):
    shape = jax.ShapeDtypeStruct
    vmem = pl.BlockSpec(memory_space=pltpu.VMEM)
    hbm = pl.BlockSpec(memory_space=pl.ANY)
    loads = 12 + 2 * ((results[0].shape[0] - HALO) // LAST_PART)
    ends = list(results[:2])
    for part in range(3):
        ends += [shape(a.shape[1:], a.dtype) for a in results[2:7]]
    ends += results[7:]
    return pl.pallas_call(
        last_kernel,
        out_shape=[shape(a.shape, a.dtype) for a in ends],
        in_specs=[hbm] * 12 + [vmem, vmem],
        out_specs=[hbm] * 22,
        scratch_shapes=[pltpu.VMEM(a.shape, a.dtype) for a in results]
        + [pltpu.SemaphoreType.DMA((loads,)), pltpu.SemaphoreType.DMA((loads + 10,))],
        compiler_params=pltpu.CompilerParams(vmem_limit_bytes=60 * MIB),
        name="last",
    )(*results, out_back, in_back)


def on_device(
    tokens,
    cotangent,
    segment,
    keep_mask,
    attn_master,
    out_master,
    in_master,
    back_master,
    vec_master,
    attn_first,
    out_first,
    in_first,
    back_first,
    vec_first,
    attn_second,
    out_second,
    in_second,
    back_second,
    vec_second,
):
    seq = lax.axis_index("seq")
    seq_count = lax.axis_size("seq")
    both = ("batch", "seq")
    rows = tokens.shape[1]
    masters = (attn_master, out_master, in_master, back_master, vec_master)
    firsts = (attn_first, out_first, in_first, back_first, vec_first)
    seconds = (attn_second, out_second, in_second, back_second, vec_second)
    direct = seq_count == DEPTH and lax.axis_size("batch") == 2 * PLANE
    forward = [(i, i + 1) for i in range(seq_count - 1)]
    backward = [(i + 1, i) for i in range(seq_count - 1)]
    if direct:
        *results, out_back, grad_back = whole(
            masters, firsts, seconds, tokens, cotangent, segment, keep_mask
        )
        for i in range(7, 11):
            results[i] = results[i].reshape(-1, results[i].shape[-1])
        ends = last(results, out_back, grad_back)
        return (ends[0][None], ends[1][None], *ends[2:])
    low = [w.astype(bf16) for w in masters]
    low[4] = jnp.pad(low[4].T, ((0, 0), (0, 128 - low[4].shape[0])))
    attn_w, out_w, in_w, back_w, vec_t = (
        lax.all_gather(w, both, axis=0, tiled=True) for w in low
    )
    x_halo, e_halo, seg_halo, keep_halo = (
        lax.ppermute(a, "seq", forward)
        for a in (
            tokens[0, rows - HALO :], cotangent[0, rows - HALO :],
            segment[:, rows - 128 :], keep_mask[:, rows - 128 :],
        )
    )
    xs, es, xt, qt, kt, vt, c, lse = attn_forward(
        seq_count, tokens, cotangent, x_halo, e_halo, segment, keep_mask, seg_halo, keep_halo,
        attn_w, vec_t,
    )
    z, dh, dr, gwo, gw1, gw2, gvec, gb1 = feed(xs, c, es, out_w, in_w, back_w, vec_t)
    out, out_halo, grad_in, grad_in_halo, gwa, gbias = attn_backward(
        seq_count, xt, qt, kt, vt, lse, dr, dh, z, attn_w, out_w
    )
    grads = (gwa, gwo, gw1, gw2)
    grad_vec = jnp.concatenate(
        [gbias[:1, :D], gbias[:1, 2 * D :], gvec[2:8], gb1[0].reshape(FF // D, D)], 0
    )
    sums = [lax.psum_scatter(g.astype(f32), both, scatter_dimension=0, tiled=True) for g in grads]
    sums.append(lax.psum_scatter(grad_vec, both, scatter_dimension=1, tiled=True))
    new = [
        adam_update(masters[i], firsts[i], seconds[i], sums[i], learn_rates[i]) for i in range(5)
    ]

    def own_columns(i):
        whole = lax.all_gather(new[i][2].astype(bf16), both, axis=1 if i == 4 else 0, tiled=True)
        count = whole.shape[1] // seq_count
        return lax.dynamic_slice_in_dim(whole, seq * count, count, 1)

    results = [out, grad_in] + [jnp.stack(new[i]) for i in range(5)]
    results += [own_columns(i) for i in range(5)]
    out_back = lax.ppermute(out_halo, "seq", backward)
    grad_back = lax.ppermute(grad_in_halo, "seq", backward)
    ends = last(results, out_back, grad_back)
    return (ends[0][None], ends[1][None], *ends[2:])


def solution(mesh):
    stream = P("batch", "seq", None)
    rows = P(("batch", "seq"), None)
    vector = P(None, ("batch", "seq"))
    five = (rows, rows, rows, rows, vector)
    return jax.shard_map(
        on_device,
        mesh=mesh,
        in_specs=(stream, stream, P("batch", "seq"), P("batch", "seq")) + five * 3,
        out_specs=(stream, stream) + five * 3 + (P(None, "seq"),) * 5,
        check_vma=False,
    )
```
